128 devices in a mesh: dp: 4 (over z), ctx: 8 (over y_lo, x), tensor: 4 (over y_hi, core).
Axes of the slice: x: 4, y: 4 (y_hi: 2, y_lo: 2; y = y_hi * 2 + y_lo), z: 4, core: 2. Of those that a mesh axis runs over, the one named last changes fastest.
Arguments:
- inputs: bfloat16 [4, 2048, 2048], P('dp', 'ctx'), may hold values from -6 to 6
- segments: int32 [4, 2048], P('dp', 'ctx'), may hold values from 0 to 8, as said below
- w_query: bfloat16 [2048, 2048], P(None, 'tensor'), may hold values from -0.125 to 0.125
- w_key: bfloat16 [2048, 2048], P(None, 'tensor'), may hold values from -0.125 to 0.125
- w_value: bfloat16 [2048, 2048], P(None, 'tensor'), may hold values from -0.125 to 0.125
- w_out: bfloat16 [2048, 2048], P('tensor'), may hold values from -0.125 to 0.125
- q_gain: float32 [16, 128], P('tensor'), may hold values from 0.25 to 1.75
- k_gain: float32 [16, 128], P('tensor'), may hold values from 0.25 to 1.75
- attn_gain: float32 [2048], replicated, may hold values from 0.25 to 1.75
- w_gate: bfloat16 [2048, 8192], P(None, 'tensor'), may hold values from -0.125 to 0.125
- w_up: bfloat16 [2048, 8192], P(None, 'tensor'), may hold values from -0.125 to 0.125
- w_down: bfloat16 [8192, 2048], P('tensor'), may hold values from -0.0625 to 0.0625
- mlp_gain: float32 [2048], replicated, may hold values from 0.25 to 1.75
- cotangent: bfloat16 [4, 2048, 2048], P('dp', 'ctx'), may hold values from -6 to 6
Outputs:
- outputs: bfloat16 [4, 2048, 2048], P('dp', 'ctx')
- input_grad: bfloat16 [4, 2048, 2048], P('dp', 'ctx')
- grad_query: float32 [2048, 2048], P(('dp', 'ctx'), 'tensor')
- grad_key: float32 [2048, 2048], P(('dp', 'ctx'), 'tensor')
- grad_value: float32 [2048, 2048], P(('dp', 'ctx'), 'tensor')
- grad_out: float32 [2048, 2048], P('tensor', ('dp', 'ctx'))
- grad_q_gain: float32 [16, 128], P('tensor', ('dp', 'ctx'))
- grad_k_gain: float32 [16, 128], P('tensor', ('dp', 'ctx'))
- grad_attn_gain: float32 [2048], P(('dp', 'ctx'))
- grad_gate: float32 [2048, 8192], P(('dp', 'ctx'), 'tensor')
- grad_up: float32 [2048, 8192], P(('dp', 'ctx'), 'tensor')
- grad_down: float32 [8192, 2048], P('tensor', ('dp', 'ctx'))
- grad_mlp_gain: float32 [2048], P(('dp', 'ctx'))
The draws below stay inside these ranges and needn't reach their ends.
Inputs may be any that keep to these rules, and one draw needn't show every extreme that they name: `segments`: never falling along a sequence; 0 at each sequence's first token and 8 at its last.
All inputs are finite; a program needn't handle non-finite values.
Results may differ from the reference program's by a relative error of at most 0.035.
Values may be sent and summed in bfloat16 or wider, within the bound.
A program may use at most 192 MiB of HBM per device.

```python
import math
from functools import partial
import jax
import jax.numpy as jnp
from jax import lax

D = 2048
HEADS = 16
HD = 128
FF = 8192
CUTS = 8
LENGTH = 2048
SHARD = 256
BATCH = 4


def draw_segments(key, part):
    key = jax.random.fold_in(key, 7)
    key_spread, key_late, key_pick = jax.random.split(key, 3)
    boundary = jax.random.randint(key_spread, (BATCH, CUTS), 1, LENGTH)
    late_cuts = jax.random.randint(key_late, (BATCH, CUTS), LENGTH - SHARD // 2, LENGTH)
    chosen = jax.random.randint(key_pick, (), 0, BATCH)
    picked = jnp.arange(BATCH)[:, None] == chosen
    boundary = jnp.where(picked, late_cuts, boundary)
    positions = jnp.arange(LENGTH)
    return jnp.sum((positions[None, :, None] >= boundary[:, None, :]).astype(jnp.int32), axis=2).astype(jnp.int32)


def strengthened(values, stream_key, source, target, parts, factor):
    def block_of(position):
        return (jnp.arange(values.shape[position]) // (values.shape[position] // parts)).reshape((-1,) + (1,) * (values.ndim - 1 - position))

    one_side = jax.random.permutation(stream_key, parts)[block_of(target)]
    far = (block_of(target) + parts // 2) % parts
    return jnp.where((block_of(source) == one_side) | (block_of(source) == far), factor * values, values)


def block_scale(key, shape, cuts, low, top_value):
    level = 1.0
    for dim, parts in cuts:
        steps = jax.random.uniform(jax.random.fold_in(jax.random.fold_in(key, 6), dim), (parts,), jnp.float32, low / len(cuts), top_value / len(cuts))
        level = level * jnp.repeat(jnp.exp(steps), shape[dim] // parts).reshape((-1,) + (1,) * (len(shape) - 1 - dim))
    return level


def scatter_about(rng, extent, width, bound, cuts=(), kind=jnp.bfloat16):
    factor_of = block_scale(rng, extent, cuts, -0.22, 0.18) if cuts else 1.0
    drawn = jax.random.normal(rng, extent, jnp.float32) * width * factor_of
    return jnp.minimum(jnp.maximum(drawn, -bound), bound).astype(kind)


def bell_draw_with(own_key, extent, width, most, cuts, heavy, kind=jnp.bfloat16):
    drawn = width * jax.random.normal(own_key, extent, jnp.float32)
    if cuts:
        drawn = drawn * block_scale(own_key, extent, cuts, -0.22, 0.18)
    return jnp.clip(strengthened(drawn, jax.random.fold_in(own_key, 3), *heavy), -most, most).astype(kind)


def setup_inputs(seed: int = 0) -> dict:
    seeds = jax.random.split(jax.random.key(seed), 15)
    inputs = bell_draw_with(seeds[0], (BATCH, LENGTH, D), 1.0, 6.0, ((0, 4), (1, 8)), (1, 2, 8, 2.0))
    segments = draw_segments(jax.random.fold_in(seeds[14], 71), 0)
    w_query = scatter_about(seeds[2], (D, D), D ** -0.5, 0.125, ((1, 4),))
    w_key = scatter_about(seeds[3], (D, D), D ** -0.5, 0.125, ((1, 4),))
    w_value = scatter_about(seeds[4], (D, D), D ** -0.5, 0.125, ((1, 4),))
    w_out = scatter_about(seeds[5], (D, D), D ** -0.5, 0.125, ((0, 4),))
    q_gain = jnp.clip(1.0 + 0.15 * jax.random.normal(seeds[6], (HEADS, HD), jnp.float32), 0.25, 1.75)
    k_gain = jnp.clip(1.0 + 0.15 * jax.random.normal(seeds[7], (HEADS, HD), jnp.float32), 0.25, 1.75)
    attn_gain = jnp.clip(1.0 + 0.15 * jax.random.normal(seeds[8], (D,), jnp.float32), 0.25, 1.75)
    w_gate = scatter_about(seeds[9], (D, FF), D ** -0.5, 0.125, ((1, 4),))
    w_up = scatter_about(seeds[10], (D, FF), D ** -0.5, 0.125, ((1, 4),))
    w_down = scatter_about(seeds[11], (FF, D), FF ** -0.5, 0.0625, ((0, 4),))
    mlp_gain = jnp.clip(1.0 + 0.15 * jax.random.normal(seeds[12], (D,), jnp.float32), 0.25, 1.75)
    cotangent = bell_draw_with(seeds[13], (BATCH, LENGTH, D), 1.0, 6.0, ((0, 4), (1, 8)), (1, 2, 8, 2.0))
    return dict(inputs=inputs, segments=segments, w_query=w_query, w_key=w_key, w_value=w_value, w_out=w_out, q_gain=q_gain, k_gain=k_gain, attn_gain=attn_gain, w_gate=w_gate, w_up=w_up, w_down=w_down, mlp_gain=mlp_gain, cotangent=cotangent)


@jax.custom_vjp
def low(v):
    return lax.optimization_barrier(v.astype(jnp.bfloat16)).astype(jnp.float32)

@jax.custom_vjp
def low_back(v):
    return v

def low_keep(v):
    return (low(v), None)

def low_pass(kept, grad):
    return (grad,)

def back_keep(v):
    return (v, None)

def back_low(kept, grad):
    return (low(grad),)
low.defvjp(low_keep, low_pass)
low_back.defvjp(back_keep, back_low)
epsilon = 1e-06
highest = lax.Precision.HIGHEST

def product(left, right):
    return jnp.dot(left, right, precision=highest, preferred_element_type=jnp.float32)

def rms_apply(values_in, gain_row):
    return values_in * lax.rsqrt(lax.optimization_barrier(jnp.mean(values_in * values_in, axis=-1, keepdims=True)) + epsilon) * gain_row

def attend_block(key_heads, value_heads, seg_keys, element):
    block_queries, block_segments, first_row = element
    count = block_queries.shape[0]
    scores = jnp.einsum('qhd,khd->hqk', block_queries, key_heads, precision=highest) * HD ** (-0.5)
    scores = low_back(scores)
    query_place = first_row + jnp.arange(count, dtype=jnp.int32)
    key_place = jnp.arange(key_heads.shape[0], dtype=jnp.int32)
    counted = (key_place[None, :] <= query_place[:, None]) & (seg_keys[None, :] == block_segments[:, None])
    scores = jnp.where(counted[None], scores, -1e+30)
    probs = low(jax.nn.softmax(scores, axis=-1))
    return jnp.einsum('hqk,khd->qhd', probs, value_heads, precision=highest)

def block_forward(features, w_query, w_key, w_value, w_out, q_gain, k_gain, attn_gain, w_gate, w_up, w_down, mlp_gain, seg_row):
    length = features.shape[0]
    q_raw = low_back(product(features, w_query))
    k_raw = low_back(product(features, w_key))
    values = low_back(low(product(features, w_value)))
    queries = low(rms_apply(q_raw, q_gain.reshape(-1)))
    keys = low(rms_apply(k_raw, k_gain.reshape(-1)))
    block_rows = math.gcd(length, 512)
    blocks = length // block_rows
    query_blocks = queries.reshape(blocks, block_rows, HEADS, HD)
    segment_blocks = seg_row.reshape(blocks, block_rows)
    first_rows = jnp.arange(blocks, dtype=jnp.int32) * block_rows
    key_heads = keys.reshape(length, HEADS, HD)
    value_heads = values.reshape(length, HEADS, HD)
    attend = jax.checkpoint(partial(attend_block, key_heads, value_heads, seg_row))
    attended = lax.map(attend, (query_blocks, segment_blocks, first_rows)).reshape(length, HEADS * HD)
    attended = low_back(low(attended))
    attn_out = low_back(product(attended, w_out))
    hidden_state = features + rms_apply(attn_out, attn_gain)
    hidden_low = low(hidden_state)
    gate = low_back(product(hidden_low, w_gate))
    upward = low_back(product(hidden_low, w_up))
    mixed = low(jax.nn.silu(gate) * upward)
    mlp_out = low_back(product(mixed, w_down))
    return hidden_state + rms_apply(mlp_out, mlp_gain)

def reference(inputs, segments, w_query, w_key, w_value, w_out, q_gain, k_gain, attn_gain, w_gate, w_up, w_down, mlp_gain, cotangent):
    weights = tuple((weight.astype(jnp.float32) for weight in (w_query, w_key, w_value, w_out, q_gain, k_gain, attn_gain, w_gate, w_up, w_down, mlp_gain)))

    def one_sequence(totals, element):
        feature_row, seg_row, cot_row = element

        def forward(features, *params):
            return block_forward(features, *params, seg_row)
        result, pullback = jax.vjp(forward, feature_row.astype(jnp.float32), *weights)
        grads = pullback(cot_row.astype(jnp.float32))
        new_totals = tuple((total + grad for total, grad in zip(totals, grads[1:])))
        return (new_totals, (result.astype(jnp.bfloat16), grads[0].astype(jnp.bfloat16)))
    zero_grads = tuple((jnp.zeros(weight.shape, jnp.float32) for weight in weights))
    totals, (outputs, input_grad) = lax.scan(one_sequence, zero_grads, (inputs, segments, cotangent))
    return (outputs, input_grad) + totals
```

```python
import functools
import jax
import jax.numpy as jnp
from jax import lax
from jax.experimental import pallas as pl
from jax.experimental.pallas import tpu as pltpu
from jax.sharding import PartitionSpec as P

MESH = pl.DeviceIdType.MESH
F32 = jnp.float32
BF16 = jnp.bfloat16
EPS = 1e-06
T = 256
D = 2048
HD = 128
OWN = 64
NC = 4
CW = D // NC
VMEM = pl.BlockSpec(memory_space=pltpu.VMEM)
ANY = pl.BlockSpec(memory_space=pl.ANY)


def place():
    t = lax.axis_index("tensor")
    ctx = lax.axis_index("ctx")
    return t // 2, lax.rem(t, 2), ctx // 4, lax.rem(ctx, 4)


def core_peer(yh, core):
    return {"tensor": yh * 2 + (1 - core)}


def far_peer(yh, core):
    return {"tensor": (1 - yh) * 2 + core}


def remote(src, dst, send_sem, recv_sem, device):
    return pltpu.make_async_remote_copy(
        src_ref=src,
        dst_ref=dst,
        send_sem=send_sem,
        recv_sem=recv_sem,
        device_id=device,
        device_id_type=MESH,
    )


def greet(devices):
    barrier = pltpu.get_barrier_semaphore()
    for device in devices:
        pl.semaphore_signal(barrier, inc=1, device_id=device, device_id_type=MESH)
    pl.semaphore_wait(barrier, len(devices))


def rows_of(index, count):
    return pl.ds(pl.multiple_of(index * count, count), count)


def reduce_rows(part, near, far, out_low, acc, sems):
    yh, core, _, _ = place()
    near_send, near_recv, far_send, far_recv = sems
    near_copies, far_copies = [], []
    for j in range(NC):
        cols = pl.ds(j * CW, CW)
        for slot, row in ((0, (1 - yh) * 2 + (1 - core)), (1, yh * 2 + (1 - core))):
            copy = remote(
                part.at[rows_of(row, OWN), cols],
                near.at[slot, :, cols],
                near_send.at[slot, j],
                near_recv.at[slot, j],
                core_peer(yh, core),
            )
            copy.start()
            near_copies.append(copy)
    for j in range(NC):
        cols = pl.ds(j * CW, CW)
        near_copies[2 * j].wait_recv()
        out_low[:, cols] = (
            part[rows_of((1 - yh) * 2 + core, OWN), cols].astype(F32)
            + near[0, :, cols].astype(F32)
        ).astype(BF16)
        copy = remote(
            out_low.at[:, cols], far.at[:, cols], far_send.at[j], far_recv.at[j], far_peer(yh, core)
        )
        copy.start()
        far_copies.append(copy)
    for j in range(NC):
        cols = pl.ds(j * CW, CW)
        near_copies[2 * j + 1].wait_recv()
        acc[:, cols] = part[rows_of(yh * 2 + core, OWN), cols].astype(F32) + near[
            1, :, cols
        ].astype(F32)
    for j in range(NC):
        cols = pl.ds(j * CW, CW)
        far_copies[j].wait_recv()
        acc[:, cols] = acc[:, cols] + far[:, cols].astype(F32)
    for copy in near_copies + far_copies:
        copy.wait_send()


def gather_rows(out, sems):
    yh, core, _, _ = place()
    own_send, own_recv, far_send, far_recv, on_send, on_recv = sems
    mine, other = rows_of(yh * 2 + core, OWN), rows_of((1 - yh) * 2 + core, OWN)
    far_copies, own_copies, on_copies = [], [], []
    for j in range(NC):
        block = out.at[mine, pl.ds(j * CW, CW)]
        copy = remote(block, block, far_send.at[j], far_recv.at[j], far_peer(yh, core))
        copy.start()
        far_copies.append(copy)
    for j in range(NC):
        block = out.at[mine, pl.ds(j * CW, CW)]
        copy = remote(block, block, own_send.at[j], own_recv.at[j], core_peer(yh, core))
        copy.start()
        own_copies.append(copy)
    for j in range(NC):
        far_copies[j].wait_recv()
        block = out.at[other, pl.ds(j * CW, CW)]
        copy = remote(block, block, on_send.at[j], on_recv.at[j], core_peer(yh, core))
        copy.start()
        on_copies.append(copy)
    for copy in own_copies + on_copies:
        copy.wait_recv()
    for copy in far_copies + own_copies + on_copies:
        copy.wait_send()


REDUCE_SCRATCH = [
    pltpu.VMEM((2, OWN, D), BF16),
    pltpu.VMEM((OWN, D), BF16),
    pltpu.VMEM((OWN, D), BF16),
    pltpu.VMEM((OWN, D), F32),
    pltpu.SemaphoreType.DMA((2, NC)),
    pltpu.SemaphoreType.DMA((2, NC)),
    pltpu.SemaphoreType.DMA((NC,)),
    pltpu.SemaphoreType.DMA((NC,)),
]
GATHER_SCRATCH = [pltpu.SemaphoreType.DMA((NC,))] * 6


def summed(part, near, far, out_low, acc, *sems):
    yh, core, _, _ = place()
    greet([core_peer(yh, core), far_peer(yh, core)])
    reduce_rows(part, near, far, out_low, acc, sems[:4])
    return rows_of(yh * 2 + core, OWN)


def norm_scale(v):
    return lax.rsqrt(jnp.mean(v * v, axis=1, keepdims=True) + EPS)


def norm_back(v, r, g, dy):
    column_sum = jnp.sum(dy * g * v, axis=1, keepdims=True)
    return r * g * dy - v * (r * r * r) * (column_sum / D)


def attn_out_kernel(part, features, gain, out, attn_own, hidden_own, *scratch):
    reduce, gather = scratch[:8], scratch[8:14]
    mine = summed(part, *reduce)
    v = reduce[3][...]
    hidden = features[mine, :].astype(F32) + v * norm_scale(v) * gain[...]
    out[mine, :] = hidden.astype(BF16)
    attn_own[...] = v
    hidden_own[...] = hidden
    gather_rows(out, gather)


def mlp_out_kernel(part, hidden_own, cotangent, gain, out, result_own, gain_grad, *scratch):
    reduce, gather = scratch[:8], scratch[8:14]
    mine = summed(part, *reduce)
    v = reduce[3][...]
    z = norm_scale(v)
    dy = cotangent[mine, :].astype(F32)
    g = gain[...]
    out[mine, :] = norm_back(v, z, g, dy).astype(BF16)
    result_own[...] = (hidden_own[...] + v * z * g).astype(BF16)
    gain_grad[...] = jnp.sum(dy * v * z, axis=0, keepdims=True)
    gather_rows(out, gather)


def mlp_back_kernel(part, attn_own, cotangent, gain, out, d_hidden_own, gain_grad, *scratch):
    reduce, gather = scratch[:8], scratch[8:14]
    mine = summed(part, *reduce)
    dy = cotangent[mine, :].astype(F32) + reduce[3][...]
    v = attn_own[...]
    a = norm_scale(v)
    g = gain[...]
    out[mine, :] = norm_back(v, a, g, dy).astype(BF16)
    d_hidden_own[...] = dy
    gain_grad[...] = jnp.sum(dy * v * a, axis=0, keepdims=True)
    gather_rows(out, gather)


def input_grad_kernel(part, d_hidden_own, out, *scratch):
    reduce, gather = scratch[:8], scratch[8:14]
    mine = summed(part, *reduce)
    out[mine, :] = (d_hidden_own[...] + reduce[3][...]).astype(BF16)
    gather_rows(out, gather)


def tensor_call(kernel, name, collective_id, operands, outs):
    return pl.pallas_call(
        kernel,
        name=name,
        out_shape=[jax.ShapeDtypeStruct(shape, kind) for shape, kind in outs],
        in_specs=[VMEM] * len(operands),
        out_specs=[VMEM] * len(outs),
        scratch_shapes=REDUCE_SCRATCH + GATHER_SCRATCH,
        compiler_params=pltpu.CompilerParams(
            collective_id=collective_id, has_side_effects=True, vmem_limit_bytes=24 * 2**20
        ),
    )(*operands)


def row_device(yl, x):
    return {"ctx": yl * 4 + x}


def all_peers(yh, core, yl, x):
    peers = [core_peer(yh, core), far_peer(yh, core)]
    peers += [row_device(yl, lax.rem(x + s, 4)) for s in (1, 2, 3)]
    peers += [row_device(1 - yl, lax.rem(x + s, 4)) for s in range(4)]
    return peers


def tensor_sum(own, near, far, send, recv):
    yh, core, _, _ = place()
    copy = remote(own.at[0], near, send.at[0], recv.at[0], core_peer(yh, core))
    copy.start()
    copy.wait_recv()
    own[1] = own[0] + near[...]
    again = remote(own.at[1], far, send.at[1], recv.at[1], far_peer(yh, core))
    again.start()
    again.wait_recv()
    total = own[1] + far[...]
    copy.wait_send()
    again.wait_send()
    return total


def two_columns(first, second):
    lane = lax.broadcasted_iota(jnp.int32, (T, HD), 1)
    return jnp.where(lane < HD // 2, first, second)


def dot(a, b, dims):
    return lax.dot_general(a, b, (dims, ((), ())), preferred_element_type=F32)


class Spread:
    def __init__(self, src, dst, sems):
        self.src, self.dst = src, dst
        self.send, self.recv, self.down_send, self.down_recv = sems

    def row_copy(self, s):
        _, _, yl, x = place()
        h = lax.rem(x + s, 4)
        return remote(
            self.src.at[:, pl.ds(pl.multiple_of(h * HD, HD), HD)],
            self.dst.at[rows_of(yl * 4 + x, T)],
            self.send.at[s],
            self.recv.at[s],
            row_device(yl, h),
        )

    def down_copy(self, s):
        _, _, yl, x = place()
        h = lax.rem(x + s, 4)
        return remote(
            self.src.at[:, pl.ds(pl.multiple_of(h * HD, HD), HD)],
            self.dst.at[rows_of(x, T)],
            self.down_send.at[s],
            self.down_recv.at[s],
            row_device(1, h),
        )


def keep_own(src, dst, block):
    _, _, _, x = place()
    dst[rows_of(block, T), :] = src[:, pl.ds(pl.multiple_of(x * HD, HD), HD)]


def attend_kernel(
    q_raw, k_raw, value, seg, q_gain, k_gain,
    attended, q_head, k_head, v_head, probs_out, scale_out,
    seg_all, q_low, k_low, sums, near, far, result,
    v_sems, k_sems, q_send, q_recv, s_send, s_recv, sum_send, sum_recv, a_send, a_recv,
):
    yh, core, yl, x = place()
    greet(all_peers(yh, core, yl, x))
    me = yl * 4 + x
    v_sems = [v_sems.at[i] for i in range(4)]
    k_sems = [k_sems.at[i] for i in range(4)]
    values = Spread(value, v_head, v_sems)
    keys = Spread(k_low, k_head, k_sems)

    @pl.when(yl == 0)
    def _():
        for s in range(4):
            values.down_copy(s).start()

    for s in (1, 2, 3):
        values.row_copy(s).start()
    seg_all[me] = jnp.broadcast_to(seg[...].astype(F32), (8, T))

    def seg_copy(s):
        dx, dy = s % 4, s // 4
        to = row_device(lax.rem(yl + dy, 2), lax.rem(x + dx, 4))
        return remote(seg_all.at[me], seg_all.at[me], s_send.at[s], s_recv.at[s], to)

    for s in range(1, 8):
        seg_copy(s).start()

    qr, kr = q_raw[...], k_raw[...]
    sums[0] = two_columns(
        jnp.sum(qr * qr, axis=1, keepdims=True), jnp.sum(kr * kr, axis=1, keepdims=True)
    )
    keep_own(value, v_head, me)
    scales = lax.rsqrt(tensor_sum(sums, near, far, sum_send, sum_recv) / D + EPS)
    scale_out[...] = scales
    k_low[...] = (kr * scales[:, HD // 2 : HD // 2 + 1] * k_gain[...]).astype(BF16)

    @pl.when(yl == 0)
    def _():
        for s in range(4):
            keys.down_copy(s).start()

    for s in (1, 2, 3):
        keys.row_copy(s).start()
    q_low[...] = (qr * scales[:, :1] * q_gain[...]).astype(BF16)

    def q_copy(s):
        h = lax.rem(x + s, 4)
        return remote(
            q_low.at[:, pl.ds(pl.multiple_of(h * HD, HD), HD)],
            q_head.at[rows_of(x, T)],
            q_send.at[s],
            q_recv.at[s],
            row_device(yl, h),
        )

    for s in (1, 2, 3):
        q_copy(s).start()
    keep_own(k_low, k_head, me)
    keep_own(q_low, q_head, x)
    for s in range(1, 8):
        seg_copy(s).wait()
    for s in (1, 2, 3):
        values.row_copy(s).wait()
        keys.row_copy(s).wait()
        q_copy(s).wait()

    @pl.when(yl == 0)
    def _():
        for s in range(4):
            values.down_copy(s).wait_send()
            keys.down_copy(s).wait_send()

    @pl.when(yl == 1)
    def _():
        for s in range(4):
            values.down_copy(s).wait_recv()
            keys.down_copy(s).wait_recv()

    lane = lax.broadcasted_iota(jnp.int32, (8, HD), 0)
    pick = jnp.where(lane == 0, 1.0, 0.0)

    def attend(row, i):
        blocks = row * 4 + i + 1
        width = blocks * T
        q = q_head[i * T : (i + 1) * T, :]
        scores = dot(q, k_head[:width, :], ((1,), (1,))) * HD ** (-0.5)
        own_seg = dot(seg_all[row * 4 + i], pick, ((0,), (0,)))[:, :1]
        seg_keys = jnp.concatenate([seg_all[b, :1, :] for b in range(blocks)], axis=1)
        q_place = lax.broadcasted_iota(jnp.int32, (T, width), 0) + (blocks - 1) * T
        k_place = lax.broadcasted_iota(jnp.int32, (T, width), 1)
        counted = (k_place <= q_place) & (seg_keys == own_seg)
        scores = jnp.where(counted, scores, -1e30)
        exps = jnp.exp(scores - jnp.max(scores, axis=1, keepdims=True))
        probs = (exps * (1.0 / jnp.sum(exps, axis=1, keepdims=True))).astype(BF16)
        probs_out[i, :, :width] = probs
        result[i] = dot(probs, v_head[:width, :], ((1,), (0,))).astype(BF16)

    def back_copy(i):
        return remote(
            result.at[i],
            attended.at[:, pl.ds(pl.multiple_of(x * HD, HD), HD)],
            a_send.at[i],
            a_recv.at[x],
            row_device(yl, i),
        )

    for i in range(4):
        for row in range(2):

            @pl.when(yl == row)
            def _():
                attend(row, i)

        @pl.when(x == i)
        def _():
            attended[:, i * HD : (i + 1) * HD] = result[i]

        @pl.when(x != i)
        def _():
            back_copy(i).start()

    for h in range(4):

        @pl.when(x != h)
        def _():
            back_copy(h).wait_send()
            remote(
                result.at[h],
                attended.at[:, h * HD : (h + 1) * HD],
                a_send.at[h],
                a_recv.at[h],
                row_device(yl, h),
            ).wait_recv()


def attend(q_raw, k_raw, value, seg, q_gain, k_gain):
    dma = pltpu.SemaphoreType.DMA
    operands = (q_raw, k_raw, value, seg, q_gain, k_gain)
    outs = [
        ((T, 4 * HD), BF16),
        ((4 * T, HD), BF16),
        ((8 * T, HD), BF16),
        ((8 * T, HD), BF16),
        ((4, T, 8 * T), BF16),
        ((T, HD), F32),
    ]
    return pl.pallas_call(
        attend_kernel,
        name="attend",
        out_shape=[jax.ShapeDtypeStruct(shape, kind) for shape, kind in outs],
        in_specs=[VMEM] * len(operands),
        out_specs=[VMEM] * len(outs),
        scratch_shapes=[
            pltpu.VMEM((8, 8, T), F32),
            pltpu.VMEM((T, 4 * HD), BF16),
            pltpu.VMEM((T, 4 * HD), BF16),
            pltpu.VMEM((2, T, HD), F32),
            pltpu.VMEM((T, HD), F32),
            pltpu.VMEM((T, HD), F32),
            pltpu.VMEM((4, T, HD), BF16),
            dma((4, 4)),
            dma((4, 4)),
            dma((4,)),
            dma((4,)),
            dma((8,)),
            dma((8,)),
            dma((2,)),
            dma((2,)),
            dma((4,)),
            dma((4,)),
        ],
        compiler_params=pltpu.CompilerParams(
            collective_id=5, has_side_effects=True, vmem_limit_bytes=40 * 2**20
        ),
    )(*operands)


def attend_back_kernel(
    d_attended, q_head, k_head, v_head, probs_in, q_raw, k_raw, scales_in, q_gain, k_gain,
    d_q_low, d_k_low, d_v_low, q_gain_grad, k_gain_grad,
    d_out, dq_send_buf, dk_send_buf, dv_send_buf, dk_acc, dv_acc, dq_got, dk_got, dv_got,
    sums, near, far,
    o_send, o_recv, dq_send, dq_recv, dk_send, dk_recv, dv_send, dv_recv, sum_send, sum_recv,
):
    yh, core, yl, x = place()
    greet(all_peers(yh, core, yl, x))
    scale = HD ** (-0.5)

    def o_copy(s):
        h = lax.rem(x + s, 4)
        return remote(
            d_attended.at[:, pl.ds(pl.multiple_of(h * HD, HD), HD)],
            d_out.at[rows_of(x, T)],
            o_send.at[s],
            o_recv.at[s],
            row_device(yl, h),
        )

    for s in (1, 2, 3):
        o_copy(s).start()
    keep_own(d_attended, d_out, x)
    dk_acc[...] = jnp.zeros_like(dk_acc)
    dv_acc[...] = jnp.zeros_like(dv_acc)
    for s in (1, 2, 3):
        o_copy(s).wait()

    def back(row, i):
        width = (row * 4 + i + 1) * T
        q = q_head[i * T : (i + 1) * T, :]
        do = d_out[i * T : (i + 1) * T, :]
        probs_low = probs_in[i, :, :width]
        probs = probs_low.astype(F32)
        d_probs = dot(do, v_head[:width, :], ((1,), (1,)))
        delta = jnp.sum(probs * d_probs, axis=1, keepdims=True)
        d_scores = (probs * (d_probs - delta)).astype(BF16)
        dq_send_buf[i] = (dot(d_scores, k_head[:width, :], ((1,), (0,))) * scale).astype(BF16)
        dk_acc[:width, :] += dot(d_scores, q, ((0,), (0,)))
        dv_acc[:width, :] += dot(probs_low, do, ((0,), (0,)))

    def dq_copy(i):
        return remote(
            dq_send_buf.at[i], dq_got.at[x], dq_send.at[i], dq_recv.at[x], row_device(yl, i)
        )

    for i in range(4):
        for row in range(2):

            @pl.when(yl == row)
            def _():
                back(row, i)

        @pl.when(x == i)
        def _():
            dq_got[i] = dq_send_buf[i]

        @pl.when(x != i)
        def _():
            dq_copy(i).start()

    def kv_copy(j, buf, got, send, recv):
        return remote(
            buf.at[j], got.at[yl, x], send.at[j], recv.at[yl, x], row_device(j // 4, j % 4)
        )

    dk_args = (dk_send_buf, dk_got, dk_send, dk_recv)
    dv_args = (dv_send_buf, dv_got, dv_send, dv_recv)
    for j in range(8):
        dk_send_buf[j] = (dk_acc[j * T : (j + 1) * T, :] * scale).astype(BF16)
        dv_send_buf[j] = dv_acc[j * T : (j + 1) * T, :].astype(BF16)
        here = (yl == j // 4) & (x == j % 4)

        @pl.when(here)
        def _():
            dk_got[j // 4, j % 4] = dk_send_buf[j]
            dv_got[j // 4, j % 4] = dv_send_buf[j]

        sends = (yl >= j // 4) & ~here

        @pl.when(sends)
        def _():
            kv_copy(j, *dk_args).start()
            kv_copy(j, *dv_args).start()

    for h in range(4):

        @pl.when(x != h)
        def _():
            dq_copy(h).wait_send()
            remote(
                dq_send_buf.at[h], dq_got.at[h], dq_send.at[h], dq_recv.at[h], row_device(yl, h)
            ).wait_recv()

        for row in range(2):
            comes = (row >= yl) & ~((yl == row) & (x == h))

            @pl.when(comes)
            def _():
                for buf, got, send, recv in (dk_args, dv_args):
                    remote(
                        buf.at[0],
                        got.at[row, h],
                        send.at[0],
                        recv.at[row, h],
                        row_device(row, h),
                    ).wait_recv()

    for j in range(8):
        here = (yl == j // 4) & (x == j % 4)
        sends = (yl >= j // 4) & ~here

        @pl.when(sends)
        def _():
            kv_copy(j, *dk_args).wait_send()
            kv_copy(j, *dv_args).wait_send()

    @pl.when(yl == 1)
    def _():
        for h in range(4):
            dk_got[0, h] = jnp.zeros((T, HD), BF16)
            dv_got[0, h] = jnp.zeros((T, HD), BF16)

    q_sum = jnp.zeros((T, 1), F32)
    k_sum = jnp.zeros((T, 1), F32)
    for h in range(4):
        cols = slice(h * HD, (h + 1) * HD)
        dq = dq_got[h].astype(F32)
        dk = dk_got[0, h].astype(F32) + dk_got[1, h].astype(F32)
        d_v_low[:, cols] = (dv_got[0, h].astype(F32) + dv_got[1, h].astype(F32)).astype(BF16)
        q_sum += jnp.sum(dq * q_raw[:, cols] * q_gain[:, cols], axis=1, keepdims=True)
        k_sum += jnp.sum(dk * k_raw[:, cols] * k_gain[:, cols], axis=1, keepdims=True)
    sums[0] = two_columns(q_sum, k_sum)
    total = tensor_sum(sums, near, far, sum_send, sum_recv)
    qs, ks = scales_in[:, :1], scales_in[:, HD // 2 : HD // 2 + 1]
    q_coef = qs * qs * qs * (total[:, :1] / D)
    k_coef = ks * ks * ks * (total[:, HD // 2 : HD // 2 + 1] / D)
    for h in range(4):
        cols = slice(h * HD, (h + 1) * HD)
        dq = dq_got[h].astype(F32)
        dk = dk_got[0, h].astype(F32) + dk_got[1, h].astype(F32)
        qr, kr = q_raw[:, cols], k_raw[:, cols]
        d_q_low[:, cols] = (qs * q_gain[:, cols] * dq - qr * q_coef).astype(BF16)
        d_k_low[:, cols] = (ks * k_gain[:, cols] * dk - kr * k_coef).astype(BF16)
        q_gain_grad[:, cols] = jnp.sum(dq * qr * qs, axis=0, keepdims=True)
        k_gain_grad[:, cols] = jnp.sum(dk * kr * ks, axis=0, keepdims=True)


def attend_back(d_attended, saved, q_raw, k_raw, scales, q_gain, k_gain):
    dma = pltpu.SemaphoreType.DMA
    operands = (d_attended, *saved, q_raw, k_raw, scales, q_gain, k_gain)
    outs = [
        ((T, 4 * HD), BF16),
        ((T, 4 * HD), BF16),
        ((T, 4 * HD), BF16),
        ((1, 4 * HD), F32),
        ((1, 4 * HD), F32),
    ]
    return pl.pallas_call(
        attend_back_kernel,
        name="attend_back",
        out_shape=[jax.ShapeDtypeStruct(shape, kind) for shape, kind in outs],
        in_specs=[VMEM] * len(operands),
        out_specs=[VMEM] * len(outs),
        scratch_shapes=[
            pltpu.VMEM((4 * T, HD), BF16),
            pltpu.VMEM((4, T, HD), BF16),
            pltpu.VMEM((8, T, HD), BF16),
            pltpu.VMEM((8, T, HD), BF16),
            pltpu.VMEM((8 * T, HD), F32),
            pltpu.VMEM((8 * T, HD), F32),
            pltpu.VMEM((4, T, HD), BF16),
            pltpu.VMEM((2, 4, T, HD), BF16),
            pltpu.VMEM((2, 4, T, HD), BF16),
            pltpu.VMEM((2, T, HD), F32),
            pltpu.VMEM((T, HD), F32),
            pltpu.VMEM((T, HD), F32),
            dma((4,)),
            dma((4,)),
            dma((4,)),
            dma((4,)),
            dma((8,)),
            dma((2, 4)),
            dma((8,)),
            dma((2, 4)),
            dma((2,)),
            dma((2,)),
        ],
        compiler_params=pltpu.CompilerParams(
            collective_id=6, has_side_effects=True, vmem_limit_bytes=40 * 2**20
        ),
    )(*operands)


X_GROUPS = [[0, 1, 2, 3], [4, 5, 6, 7]]
Y_GROUPS = [[0, 4], [1, 5], [2, 6], [3, 7]]


def grad_kernel(pairs, *refs):
    ins, out = refs[:-1], refs[-1]
    at = 0
    for n, (left, right, width) in enumerate(pairs):
        product = dot(ins[left][...], ins[right][...], ((0,), (0,))).astype(BF16)
        for y in range(2):
            for x in range(4):
                out[x, 0, y, :, at : at + width] = product[(y * 4 + x) * 64 : (y * 4 + x + 1) * 64]
        at += width


def partial_grads(name, lefts, rights, pairs):
    rows = 4 * T
    total = sum(width for _, _, width in pairs)
    n = len(lefts)
    in_specs = [pl.BlockSpec((rows, D // 4), lambda i: (0, i)) for _ in lefts]
    in_specs += [pl.BlockSpec(right.shape, lambda i: (0, 0)) for right in rights]
    return pl.pallas_call(
        functools.partial(grad_kernel, [(a, n + b, w) for a, b, w in pairs]),
        name=name,
        grid=(4,),
        out_shape=jax.ShapeDtypeStruct((4, 4, 2, 64, total), BF16),
        in_specs=in_specs,
        out_specs=pl.BlockSpec((4, 1, 2, 64, total), lambda i: (0, i, 0, 0, 0)),
        compiler_params=pltpu.CompilerParams(vmem_limit_bytes=40 * 2**20),
        cost_estimate=pl.CostEstimate(
            flops=2 * rows * D * total,
            bytes_accessed=2 * rows * (D * n + total) + 2 * D * total,
            transcendentals=0,
        ),
    )(*lefts, *rights)


def quarters(arrays):
    return jnp.concatenate(
        [a.reshape(T, 4, a.shape[1] // 4).transpose(1, 0, 2) for a in arrays], axis=2
    )


def over_dp(blocks):
    return lax.all_to_all(blocks, "dp", 0, 0, tiled=True)


def scatter_grads(partial):
    width = partial.shape[-1]
    got = lax.all_to_all(partial, "ctx", 0, 0, axis_index_groups=X_GROUPS, tiled=True)
    total = jnp.sum(got.astype(F32), axis=0).astype(BF16)
    swapped = lax.all_to_all(
        total.transpose(1, 0, 2, 3), "ctx", 0, 0, axis_index_groups=Y_GROUPS, tiled=True
    )
    total = jnp.sum(swapped.astype(F32), axis=0).astype(BF16)
    return over_dp(total).astype(F32).transpose(1, 0, 2)


def per_device(
    inputs, segments, w_query, w_key, w_value, w_out, q_gain, k_gain, attn_gain,
    w_gate, w_up, w_down, mlp_gain, cotangent,
):
    features, top = inputs[0], cotangent[0]
    q_row, k_row = q_gain.reshape(1, -1), k_gain.reshape(1, -1)
    a_row, m_row = attn_gain.reshape(1, -1), mlp_gain.reshape(1, -1)

    def matmul(a, w):
        return jnp.dot(a, w, preferred_element_type=F32)

    def matmul_t(a, w):
        return lax.dot_general(a, w, (((1,), (1,)), ((), ())), preferred_element_type=F32)

    q_raw = matmul(features, w_query)
    k_raw = matmul(features, w_key)
    value = matmul(features, w_value).astype(BF16)
    attended, *saved, scales = attend(q_raw, k_raw, value, segments, q_row, k_row)
    part = matmul(attended, w_out).astype(BF16)
    hidden_low, attn_own, hidden_own = tensor_call(
        attn_out_kernel, "attn_out", 1, (part, features, a_row),
        [((T, D), BF16), ((OWN, D), F32), ((OWN, D), F32)],
    )
    gate = matmul(hidden_low, w_gate)
    upward = matmul(hidden_low, w_up)
    sigma = jax.nn.sigmoid(gate)
    activated = gate * sigma
    mixed = (activated * upward).astype(BF16)
    part = matmul(mixed, w_down).astype(BF16)
    d_mlp_low, result_own, mlp_gain_grad = tensor_call(
        mlp_out_kernel, "mlp_out", 2, (part, hidden_own, top, m_row),
        [((T, D), BF16), ((OWN, D), BF16), ((1, D), F32)],
    )
    outputs = lax.all_gather(result_own, "tensor", axis=0, tiled=True)
    d_mixed = matmul_t(d_mlp_low, w_down)
    d_up = (d_mixed * activated).astype(BF16)
    d_gate = (d_mixed * upward * sigma * (1.0 + gate * (1.0 - sigma))).astype(BF16)
    part = (matmul_t(d_gate, w_gate) + matmul_t(d_up, w_up)).astype(BF16)
    d_attn_low, d_hidden_own, attn_gain_grad = tensor_call(
        mlp_back_kernel, "mlp_back", 3, (part, attn_own, top, a_row),
        [((T, D), BF16), ((OWN, D), F32), ((1, D), F32)],
    )
    d_attended = matmul_t(d_attn_low, w_out).astype(BF16)
    d_q, d_k, d_v, q_gain_grad, k_gain_grad = attend_back(
        d_attended, saved, q_raw, k_raw, scales, q_row, k_row
    )
    part = (matmul_t(d_q, w_query) + matmul_t(d_k, w_key) + matmul_t(d_v, w_value)).astype(BF16)
    (input_grad,) = tensor_call(
        input_grad_kernel, "input_grad", 4, (part, d_hidden_own), [((T, D), BF16)]
    )

    def gathered(a):
        return lax.all_gather(a, "dp", axis=0, tiled=True)

    hidden_all, top_all = gathered(hidden_low), gathered(d_mlp_low)
    features_all, attn_all = gathered(features), gathered(d_attn_low)
    right = over_dp(quarters([d_gate, d_up, mixed])).reshape(4 * T, 1536)
    mlp = partial_grads(
        "mlp_grads", [hidden_all, top_all], [right[:, :1024], right[:, 1024:]],
        [(0, 0, 1024), (1, 1, 512)],
    )
    mlp = scatter_grads(mlp)
    right = over_dp(quarters([d_q, d_k, d_v, attended])).reshape(4 * T, 512)
    proj = partial_grads(
        "attn_grads", [features_all, attn_all], [right[:, :384], right[:, 384:]],
        [(0, 0, 384), (1, 1, 128)],
    )
    proj = scatter_grads(proj)

    gains = jnp.stack([attn_gain_grad[0], mlp_gain_grad[0]])
    gains = lax.psum(gains, ("dp", "ctx", "tensor"))
    heads = lax.psum(jnp.stack([q_gain_grad[0], k_gain_grad[0]]), ("dp", "ctx"))
    rank = lax.axis_index("dp") * 8 + lax.axis_index("ctx")
    gains = lax.dynamic_slice_in_dim(gains, rank * 64, 64, 1)
    heads = lax.dynamic_slice_in_dim(heads.reshape(2, 4, HD), rank * 4, 4, 2)

    def joined(block):
        return block.reshape(64, -1)

    return (
        outputs[None],
        input_grad[None],
        joined(proj[:, :, :128]),
        joined(proj[:, :, 128:256]),
        joined(proj[:, :, 256:384]),
        joined(proj[:, :, 384:]).T,
        heads[0],
        heads[1],
        gains[0],
        joined(mlp[:, :, :512]),
        joined(mlp[:, :, 512:1024]),
        joined(mlp[:, :, 1024:]).T,
        gains[1],
    )


def solution(mesh):
    rows, full = P("dp", "ctx", None), P()
    down, across = P("tensor", None), P(None, "tensor")
    in_specs = (
        rows, P("dp", "ctx"), across, across, across, down, down, down, full,
        across, across, down, full, rows,
    )
    split = ("dp", "ctx")
    out_specs = (
        rows, rows, P(split, "tensor"), P(split, "tensor"), P(split, "tensor"), P("tensor", split),
        P("tensor", split), P("tensor", split), P(split), P(split, "tensor"), P(split, "tensor"),
        P("tensor", split), P(split),
    )
    return jax.shard_map(
        per_device, mesh=mesh, in_specs=in_specs, out_specs=out_specs, check_vma=False
    )
```

```python
import functools
import jax
import jax.numpy as jnp
from jax import lax
from jax.experimental import pallas as pl
from jax.experimental.pallas import tpu as pltpu
from jax.sharding import PartitionSpec as P

MESH = pl.DeviceIdType.MESH
F32 = jnp.float32
BF16 = jnp.bfloat16
EPS = 1e-06
T = 256
D = 2048
HD = 128
OWN = 64
NC = 4
CW = D // NC
VMEM = pl.BlockSpec(memory_space=pltpu.VMEM)
ANY = pl.BlockSpec(memory_space=pl.ANY)


def place():
    t = lax.axis_index("tensor")
    ctx = lax.axis_index("ctx")
    return t // 2, lax.rem(t, 2), ctx // 4, lax.rem(ctx, 4)


def peer(dz=0, dy=0, dx=0, dh=0, dc=0):
    yh, core, yl, x = place()
    z = lax.rem(lax.axis_index("dp") + dz, 4)
    ctx = lax.rem(yl + dy, 2) * 4 + lax.rem(x + dx, 4)
    return {"dp": z, "ctx": ctx, "tensor": lax.rem(yh + dh, 2) * 2 + lax.rem(core + dc, 2)}


CORE, FAR = (0, 0, 0, 0, 1), (0, 0, 0, 1, 0)


def along(axis, s):
    return (s, 0, 0, 0, 0) if axis == "z" else (0, 0, s, 0, 0)


def spot(axis):
    return lax.axis_index("dp") if axis == "z" else place()[3]


def remote(src, dst, send_sem, recv_sem, device):
    return pltpu.make_async_remote_copy(
        src_ref=src,
        dst_ref=dst,
        send_sem=send_sem,
        recv_sem=recv_sem,
        device_id=device,
        device_id_type=MESH,
    )


def greet(offsets):
    barrier = pltpu.get_barrier_semaphore()
    for offset in offsets:
        pl.semaphore_signal(barrier, inc=1, device_id=peer(*offset), device_id_type=MESH)
    pl.semaphore_wait(barrier, len(offsets))


def rows_of(index, count):
    return pl.ds(pl.multiple_of(index * count, count), count)


class Move:
    def __init__(self, source, shape, offsets, pairs):
        self.source, self.shape, self.offsets, self.pairs = source, shape, offsets, pairs

    def scratch(self):
        dma = pltpu.SemaphoreType.DMA
        return [dma((len(self.offsets),)), dma((len(self.offsets),)), dma((1,))]

    def copies(self, src, dst, send, recv, local):
        made = []
        at = 0
        for a, b, offset in self.pairs(src, dst):
            if offset is None:
                made.append(pltpu.make_async_copy(a, b, local.at[0]))
            else:
                made.append(remote(a, b, send.at[at], recv.at[at], peer(*offset)))
                at += 1
        return made


def half_move(a, axis):
    half = a.shape[1] // 2
    offsets = [along(axis, s) for s in (1, 2, 3)]

    def pairs(src, dst):
        mine = src.at[:, pl.ds(pl.multiple_of(place()[1] * half, half), half)]
        me = spot(axis)
        return [(mine, dst.at[me], offset) for offset in offsets + [None]]

    return Move(a, (4, T, half), offsets, pairs)


def core_move(a):
    return Move(a, a.shape, [CORE], lambda src, dst: [(src, dst, CORE)])


def quarter_move(b, axis):
    width = b.shape[1] // 4
    offsets = [along(axis, s) for s in (1, 2, 3)]

    def pairs(src, dst):
        me = spot(axis)

        def part(s):
            return src.at[:, pl.ds(pl.multiple_of(lax.rem(me + s, 4) * width, width), width)]

        made = [(part(s), dst.at[me], along(axis, s)) for s in (1, 2, 3)]
        return made + [(part(0), dst.at[me], None)]

    return Move(b, (4, T, width), offsets, pairs)


def full_move(b, axis):
    offsets = [along(axis, s) for s in (1, 2, 3)]

    def pairs(src, dst):
        return [(src, dst.at[spot(axis)], offset) for offset in offsets + [None]]

    return Move(b, (4,) + b.shape, offsets, pairs)


def block_move(p, axis):
    offsets = [along(axis, s) for s in (1, 2, 3)]

    def pairs(src, dst):
        me = spot(axis)
        made = [(src.at[lax.rem(me + s, 4)], dst.at[me], along(axis, s)) for s in (1, 2, 3)]
        return made + [(src.at[me], dst.at[me], None)]

    return Move(p, p.shape, offsets, pairs)


def final_move(p, axis):
    steps = [(dy, s) for dy in range(2) for s in range(4) if dy or s]

    def offset(dy, s):
        return (s, dy, 0, 0, 0) if axis == "z" else (0, dy, s, 0, 0)

    def pairs(src, dst):
        yl, me = place()[2], spot(axis)
        made = [
            (src.at[lax.rem(yl + dy, 2), lax.rem(me + s, 4)], dst.at[yl, me], offset(dy, s))
            for dy, s in steps
        ]
        return made + [(src.at[yl, me], dst.at[yl, me], None)]

    return Move(p, p.shape, [offset(*step) for step in steps], pairs)


def rank_move(p):
    steps = [(dz, dy, dx, 0, 0) for dz in range(4) for dy in range(2) for dx in range(4)][1:]

    def pairs(src, dst):
        _, _, yl, x = place()
        z = lax.axis_index("dp")
        me = z * 8 + yl * 4 + x

        def rank(dz, dy, dx, *_):
            return lax.rem(z + dz, 4) * 8 + lax.rem(yl + dy, 2) * 4 + lax.rem(x + dx, 4)

        made = [(src.at[rank(*step)], dst.at[me], step) for step in steps]
        return made + [(src.at[me], dst.at[me], None)]

    return Move(p, p.shape, steps, pairs)


def call(main, name, collective_id, operands, outs, scratch, offsets, moves, vmem):
    n_in, n_out, n_move, n_scratch = len(operands), len(outs), len(moves), len(scratch)
    offsets = list(dict.fromkeys(offsets + [o for move in moves for o in move.offsets]))

    def kernel(*refs):
        ins, rest = refs[:n_in], refs[n_in:]
        sources, rest = rest[:n_move], rest[n_move:]
        results, rest = rest[:n_out], rest[n_out:]
        targets, rest = rest[:n_move], rest[n_move:]
        own, sems = rest[:n_scratch], rest[n_scratch:]
        greet(offsets)
        copies = []
        for i, move in enumerate(moves):
            copies += move.copies(sources[i], targets[i], *sems[3 * i : 3 * i + 3])
        for copy in copies:
            copy.start()
        if main is not None:
            main(*ins, *results, *own)
        for copy in copies:
            copy.wait()

    move_outs = [(move.shape, move.source.dtype) for move in moves]
    got = pl.pallas_call(
        kernel,
        name=name,
        out_shape=[jax.ShapeDtypeStruct(shape, kind) for shape, kind in outs + move_outs],
        in_specs=[VMEM] * n_in + [ANY] * n_move,
        out_specs=[VMEM] * n_out + [ANY] * n_move,
        scratch_shapes=scratch + [s for move in moves for s in move.scratch()],
        compiler_params=pltpu.CompilerParams(
            collective_id=collective_id, has_side_effects=True, vmem_limit_bytes=vmem * 2**20
        ),
    )(*operands, *[move.source for move in moves])
    return got[:n_out], got[n_out:]


def reduce_rows(part, near, far, out_low, acc, sems):
    yh, core, _, _ = place()
    near_send, near_recv, far_send, far_recv = sems
    near_copies, far_copies = [], []
    for j in range(NC):
        cols = pl.ds(j * CW, CW)
        for slot, row in ((0, (1 - yh) * 2 + (1 - core)), (1, yh * 2 + (1 - core))):
            copy = remote(
                part.at[rows_of(row, OWN), cols],
                near.at[slot, :, cols],
                near_send.at[slot, j],
                near_recv.at[slot, j],
                peer(*CORE),
            )
            copy.start()
            near_copies.append(copy)
    for j in range(NC):
        cols = pl.ds(j * CW, CW)
        near_copies[2 * j].wait_recv()
        out_low[:, cols] = (
            part[rows_of((1 - yh) * 2 + core, OWN), cols].astype(F32)
            + near[0, :, cols].astype(F32)
        ).astype(BF16)
        copy = remote(
            out_low.at[:, cols], far.at[:, cols], far_send.at[j], far_recv.at[j], peer(*FAR)
        )
        copy.start()
        far_copies.append(copy)
    for j in range(NC):
        cols = pl.ds(j * CW, CW)
        near_copies[2 * j + 1].wait_recv()
        acc[:, cols] = part[rows_of(yh * 2 + core, OWN), cols].astype(F32) + near[
            1, :, cols
        ].astype(F32)
    for j in range(NC):
        cols = pl.ds(j * CW, CW)
        far_copies[j].wait_recv()
        acc[:, cols] = acc[:, cols] + far[:, cols].astype(F32)
    for copy in near_copies + far_copies:
        copy.wait_send()


def gather_rows(out, sems):
    yh, core, _, _ = place()
    own_send, own_recv, far_send, far_recv, on_send, on_recv = sems
    mine, other = rows_of(yh * 2 + core, OWN), rows_of((1 - yh) * 2 + core, OWN)
    far_copies, own_copies, on_copies = [], [], []
    for j in range(NC):
        block = out.at[mine, pl.ds(j * CW, CW)]
        copy = remote(block, block, far_send.at[j], far_recv.at[j], peer(*FAR))
        copy.start()
        far_copies.append(copy)
    for j in range(NC):
        block = out.at[mine, pl.ds(j * CW, CW)]
        copy = remote(block, block, own_send.at[j], own_recv.at[j], peer(*CORE))
        copy.start()
        own_copies.append(copy)
    for j in range(NC):
        far_copies[j].wait_recv()
        block = out.at[other, pl.ds(j * CW, CW)]
        copy = remote(block, block, on_send.at[j], on_recv.at[j], peer(*CORE))
        copy.start()
        on_copies.append(copy)
    for copy in own_copies + on_copies:
        copy.wait_recv()
    for copy in far_copies + own_copies + on_copies:
        copy.wait_send()


REDUCE_SCRATCH = [
    pltpu.VMEM((2, OWN, D), BF16),
    pltpu.VMEM((OWN, D), BF16),
    pltpu.VMEM((OWN, D), BF16),
    pltpu.VMEM((OWN, D), F32),
    pltpu.SemaphoreType.DMA((2, NC)),
    pltpu.SemaphoreType.DMA((2, NC)),
    pltpu.SemaphoreType.DMA((NC,)),
    pltpu.SemaphoreType.DMA((NC,)),
]
GATHER_SCRATCH = [pltpu.SemaphoreType.DMA((NC,))] * 6


def summed(part, near, far, out_low, acc, *sems):
    yh, core, _, _ = place()
    reduce_rows(part, near, far, out_low, acc, sems[:4])
    return rows_of(yh * 2 + core, OWN)


def norm_scale(v):
    return lax.rsqrt(jnp.mean(v * v, axis=1, keepdims=True) + EPS)


def norm_back(v, r, g, dy):
    column_sum = jnp.sum(dy * g * v, axis=1, keepdims=True)
    return r * g * dy - v * (r * r * r) * (column_sum / D)


def attn_out_kernel(part, features, gain, out, attn_own, hidden_own, *scratch):
    reduce, gather = scratch[:8], scratch[8:14]
    mine = summed(part, *reduce)
    v = reduce[3][...]
    hidden = features[mine, :].astype(F32) + v * norm_scale(v) * gain[...]
    out[mine, :] = hidden.astype(BF16)
    attn_own[...] = v
    hidden_own[...] = hidden
    gather_rows(out, gather)


def mlp_out_kernel(part, hidden_own, cotangent, gain, out, result_own, gain_grad, *scratch):
    reduce, gather = scratch[:8], scratch[8:14]
    mine = summed(part, *reduce)
    v = reduce[3][...]
    z = norm_scale(v)
    dy = cotangent[mine, :].astype(F32)
    g = gain[...]
    out[mine, :] = norm_back(v, z, g, dy).astype(BF16)
    result_own[...] = (hidden_own[...] + v * z * g).astype(BF16)
    gain_grad[...] = jnp.broadcast_to(jnp.sum(dy * v * z, axis=0, keepdims=True), (8, D))
    gather_rows(out, gather)


def mlp_back_kernel(
    part, attn_own, cotangent, gain, mlp_gain_grad, out, d_hidden_own, gain_grad, *scratch
):
    reduce, gather = scratch[:8], scratch[8:14]
    mine = summed(part, *reduce)
    dy = cotangent[mine, :].astype(F32) + reduce[3][...]
    v = attn_own[...]
    a = norm_scale(v)
    g = gain[...]
    out[mine, :] = norm_back(v, a, g, dy).astype(BF16)
    d_hidden_own[...] = dy
    row = lax.broadcasted_iota(jnp.int32, (8, D), 0)
    attn_grad = jnp.sum(dy * v * a, axis=0, keepdims=True)
    gain_grad[...] = jnp.where(row == 0, attn_grad, mlp_gain_grad[...])
    gather_rows(out, gather)


def input_grad_kernel(part, d_hidden_own, out, *scratch):
    reduce, gather = scratch[:8], scratch[8:14]
    mine = summed(part, *reduce)
    out[mine, :] = (d_hidden_own[...] + reduce[3][...]).astype(BF16)
    gather_rows(out, gather)


def tensor_call(kernel, name, collective_id, operands, outs, moves):
    scratch = REDUCE_SCRATCH + GATHER_SCRATCH
    return call(kernel, name, collective_id, operands, outs, scratch, [CORE, FAR], moves, 24)


def row_device(yl, x):
    return {"ctx": yl * 4 + x}


ATTEND_PEERS = [CORE, FAR] + [(0, dy, dx, 0, 0) for dy in range(2) for dx in range(4) if dy or dx]


def tensor_sum(own, near, far, send, recv):
    yh, core, _, _ = place()
    copy = remote(own.at[0], near, send.at[0], recv.at[0], peer(*CORE))
    copy.start()
    copy.wait_recv()
    own[1] = own[0] + near[...]
    again = remote(own.at[1], far, send.at[1], recv.at[1], peer(*FAR))
    again.start()
    again.wait_recv()
    total = own[1] + far[...]
    copy.wait_send()
    again.wait_send()
    return total


def two_columns(first, second):
    lane = lax.broadcasted_iota(jnp.int32, (T, HD), 1)
    return jnp.where(lane < HD // 2, first, second)


def dot(a, b, dims):
    return lax.dot_general(a, b, (dims, ((), ())), preferred_element_type=F32)


class Spread:
    def __init__(self, src, dst, sems):
        self.src, self.dst = src, dst
        self.send, self.recv, self.down_send, self.down_recv = sems

    def row_copy(self, s):
        _, _, yl, x = place()
        h = lax.rem(x + s, 4)
        return remote(
            self.src.at[:, pl.ds(pl.multiple_of(h * HD, HD), HD)],
            self.dst.at[rows_of(yl * 4 + x, T)],
            self.send.at[s],
            self.recv.at[s],
            row_device(yl, h),
        )

    def down_copy(self, s):
        _, _, yl, x = place()
        h = lax.rem(x + s, 4)
        return remote(
            self.src.at[:, pl.ds(pl.multiple_of(h * HD, HD), HD)],
            self.dst.at[rows_of(x, T)],
            self.down_send.at[s],
            self.down_recv.at[s],
            row_device(1, h),
        )


def keep_own(src, dst, block):
    _, _, _, x = place()
    dst[rows_of(block, T), :] = src[:, pl.ds(pl.multiple_of(x * HD, HD), HD)]


def attend_kernel(
    q_raw, k_raw, value, seg, q_gain, k_gain,
    attended, q_head, k_head, v_head, probs_out, scale_out,
    seg_all, q_low, k_low, sums, near, far, result,
    v_sems, k_sems, q_send, q_recv, s_send, s_recv, sum_send, sum_recv, a_send, a_recv,
):
    yh, core, yl, x = place()
    me = yl * 4 + x
    v_sems = [v_sems.at[i] for i in range(4)]
    k_sems = [k_sems.at[i] for i in range(4)]
    values = Spread(value, v_head, v_sems)
    keys = Spread(k_low, k_head, k_sems)

    @pl.when(yl == 0)
    def _():
        for s in range(4):
            values.down_copy(s).start()

    for s in (1, 2, 3):
        values.row_copy(s).start()
    seg_all[me] = jnp.broadcast_to(seg[...].astype(F32), (8, T))

    def seg_copy(s):
        dx, dy = s % 4, s // 4
        to = row_device(lax.rem(yl + dy, 2), lax.rem(x + dx, 4))
        return remote(seg_all.at[me], seg_all.at[me], s_send.at[s], s_recv.at[s], to)

    for s in range(1, 8):
        seg_copy(s).start()

    qr, kr = q_raw[...], k_raw[...]
    sums[0] = two_columns(
        jnp.sum(qr * qr, axis=1, keepdims=True), jnp.sum(kr * kr, axis=1, keepdims=True)
    )
    keep_own(value, v_head, me)
    scales = lax.rsqrt(tensor_sum(sums, near, far, sum_send, sum_recv) / D + EPS)
    scale_out[...] = scales
    k_low[...] = (kr * scales[:, HD // 2 : HD // 2 + 1] * k_gain[...]).astype(BF16)

    @pl.when(yl == 0)
    def _():
        for s in range(4):
            keys.down_copy(s).start()

    for s in (1, 2, 3):
        keys.row_copy(s).start()
    q_low[...] = (qr * scales[:, :1] * q_gain[...]).astype(BF16)

    def q_copy(s):
        h = lax.rem(x + s, 4)
        return remote(
            q_low.at[:, pl.ds(pl.multiple_of(h * HD, HD), HD)],
            q_head.at[rows_of(x, T)],
            q_send.at[s],
            q_recv.at[s],
            row_device(yl, h),
        )

    for s in (1, 2, 3):
        q_copy(s).start()
    keep_own(k_low, k_head, me)
    keep_own(q_low, q_head, x)
    for s in range(1, 8):
        seg_copy(s).wait()
    for s in (1, 2, 3):
        values.row_copy(s).wait()
        keys.row_copy(s).wait()
        q_copy(s).wait()

    @pl.when(yl == 0)
    def _():
        for s in range(4):
            values.down_copy(s).wait_send()
            keys.down_copy(s).wait_send()

    @pl.when(yl == 1)
    def _():
        for s in range(4):
            values.down_copy(s).wait_recv()
            keys.down_copy(s).wait_recv()

    lane = lax.broadcasted_iota(jnp.int32, (8, HD), 0)
    pick = jnp.where(lane == 0, 1.0, 0.0)

    def attend(row, i):
        blocks = row * 4 + i + 1
        width = blocks * T
        q = q_head[i * T : (i + 1) * T, :]
        scores = dot(q, k_head[:width, :], ((1,), (1,))) * HD ** (-0.5)
        own_seg = dot(seg_all[row * 4 + i], pick, ((0,), (0,)))[:, :1]
        seg_keys = jnp.concatenate([seg_all[b, :1, :] for b in range(blocks)], axis=1)
        q_place = lax.broadcasted_iota(jnp.int32, (T, width), 0) + (blocks - 1) * T
        k_place = lax.broadcasted_iota(jnp.int32, (T, width), 1)
        counted = (k_place <= q_place) & (seg_keys == own_seg)
        scores = jnp.where(counted, scores, -1e30)
        exps = jnp.exp(scores - jnp.max(scores, axis=1, keepdims=True))
        probs = (exps * (1.0 / jnp.sum(exps, axis=1, keepdims=True))).astype(BF16)
        probs_out[i, :, :width] = probs
        result[i] = dot(probs, v_head[:width, :], ((1,), (0,))).astype(BF16)

    def back_copy(i):
        return remote(
            result.at[i],
            attended.at[:, pl.ds(pl.multiple_of(x * HD, HD), HD)],
            a_send.at[i],
            a_recv.at[x],
            row_device(yl, i),
        )

    for i in range(4):
        for row in range(2):

            @pl.when(yl == row)
            def _():
                attend(row, i)

        @pl.when(x == i)
        def _():
            attended[:, i * HD : (i + 1) * HD] = result[i]

        @pl.when(x != i)
        def _():
            back_copy(i).start()

    for h in range(4):

        @pl.when(x != h)
        def _():
            back_copy(h).wait_send()
            remote(
                result.at[h],
                attended.at[:, h * HD : (h + 1) * HD],
                a_send.at[h],
                a_recv.at[h],
                row_device(yl, h),
            ).wait_recv()


def attend(q_raw, k_raw, value, seg, q_gain, k_gain, moves):
    dma = pltpu.SemaphoreType.DMA
    operands = (q_raw, k_raw, value, seg, q_gain, k_gain)
    outs = [
        ((T, 4 * HD), BF16),
        ((4 * T, HD), BF16),
        ((8 * T, HD), BF16),
        ((8 * T, HD), BF16),
        ((4, T, 8 * T), BF16),
        ((T, HD), F32),
    ]
    scratch = [
            pltpu.VMEM((8, 8, T), F32),
            pltpu.VMEM((T, 4 * HD), BF16),
            pltpu.VMEM((T, 4 * HD), BF16),
            pltpu.VMEM((2, T, HD), F32),
            pltpu.VMEM((T, HD), F32),
            pltpu.VMEM((T, HD), F32),
            pltpu.VMEM((4, T, HD), BF16),
            dma((4, 4)),
            dma((4, 4)),
            dma((4,)),
            dma((4,)),
            dma((8,)),
            dma((8,)),
            dma((2,)),
            dma((2,)),
            dma((4,)),
            dma((4,)),
    ]
    return call(attend_kernel, "attend", 5, operands, outs, scratch, ATTEND_PEERS, moves, 40)


def attend_back_kernel(
    d_attended, q_head, k_head, v_head, probs_in, q_raw, k_raw, scales_in, q_gain, k_gain, gains,
    d_q_low, d_k_low, d_v_low, q_gain_grad, k_gain_grad, gains_out,
    d_out, dq_send_buf, dk_send_buf, dv_send_buf, dk_acc, dv_acc, dq_got, dk_got, dv_got,
    sums, near, far,
    o_send, o_recv, dq_send, dq_recv, dk_send, dk_recv, dv_send, dv_recv, sum_send, sum_recv,
    gain_near, gain_far, gain_sum, gain_send, gain_recv,
):
    yh, core, yl, x = place()
    scale = HD ** (-0.5)

    def o_copy(s):
        h = lax.rem(x + s, 4)
        return remote(
            d_attended.at[:, pl.ds(pl.multiple_of(h * HD, HD), HD)],
            d_out.at[rows_of(x, T)],
            o_send.at[s],
            o_recv.at[s],
            row_device(yl, h),
        )

    for s in (1, 2, 3):
        o_copy(s).start()
    gain_near_copy = remote(gains, gain_near, gain_send.at[0], gain_recv.at[0], peer(*CORE))
    gain_near_copy.start()
    keep_own(d_attended, d_out, x)
    dk_acc[...] = jnp.zeros_like(dk_acc)
    dv_acc[...] = jnp.zeros_like(dv_acc)
    for s in (1, 2, 3):
        o_copy(s).wait()

    gain_near_copy.wait()
    gain_sum[...] = gains[...] + gain_near[...]
    gain_far_copy = remote(gain_sum, gain_far, gain_send.at[1], gain_recv.at[1], peer(*FAR))
    gain_far_copy.start()

    def back(row, i):
        width = (row * 4 + i + 1) * T
        q = q_head[i * T : (i + 1) * T, :]
        do = d_out[i * T : (i + 1) * T, :]
        probs_low = probs_in[i, :, :width]
        probs = probs_low.astype(F32)
        d_probs = dot(do, v_head[:width, :], ((1,), (1,)))
        delta = jnp.sum(probs * d_probs, axis=1, keepdims=True)
        d_scores = (probs * (d_probs - delta)).astype(BF16)
        dq_send_buf[i] = (dot(d_scores, k_head[:width, :], ((1,), (0,))) * scale).astype(BF16)
        dk_acc[:width, :] += dot(d_scores, q, ((0,), (0,)))
        dv_acc[:width, :] += dot(probs_low, do, ((0,), (0,)))

    def dq_copy(i):
        return remote(
            dq_send_buf.at[i], dq_got.at[x], dq_send.at[i], dq_recv.at[x], row_device(yl, i)
        )

    for i in range(4):
        for row in range(2):

            @pl.when(yl == row)
            def _():
                back(row, i)

        @pl.when(x == i)
        def _():
            dq_got[i] = dq_send_buf[i]

        @pl.when(x != i)
        def _():
            dq_copy(i).start()

    def kv_copy(j, buf, got, send, recv):
        return remote(
            buf.at[j], got.at[yl, x], send.at[j], recv.at[yl, x], row_device(j // 4, j % 4)
        )

    dk_args = (dk_send_buf, dk_got, dk_send, dk_recv)
    dv_args = (dv_send_buf, dv_got, dv_send, dv_recv)
    for j in range(8):
        dk_send_buf[j] = (dk_acc[j * T : (j + 1) * T, :] * scale).astype(BF16)
        dv_send_buf[j] = dv_acc[j * T : (j + 1) * T, :].astype(BF16)
        here = (yl == j // 4) & (x == j % 4)

        @pl.when(here)
        def _():
            dk_got[j // 4, j % 4] = dk_send_buf[j]
            dv_got[j // 4, j % 4] = dv_send_buf[j]

        sends = (yl >= j // 4) & ~here

        @pl.when(sends)
        def _():
            kv_copy(j, *dk_args).start()
            kv_copy(j, *dv_args).start()

    for h in range(4):

        @pl.when(x != h)
        def _():
            dq_copy(h).wait_send()
            remote(
                dq_send_buf.at[h], dq_got.at[h], dq_send.at[h], dq_recv.at[h], row_device(yl, h)
            ).wait_recv()

        for row in range(2):
            comes = (row >= yl) & ~((yl == row) & (x == h))

            @pl.when(comes)
            def _():
                for buf, got, send, recv in (dk_args, dv_args):
                    remote(
                        buf.at[0],
                        got.at[row, h],
                        send.at[0],
                        recv.at[row, h],
                        row_device(row, h),
                    ).wait_recv()

    for j in range(8):
        here = (yl == j // 4) & (x == j % 4)
        sends = (yl >= j // 4) & ~here

        @pl.when(sends)
        def _():
            kv_copy(j, *dk_args).wait_send()
            kv_copy(j, *dv_args).wait_send()

    @pl.when(yl == 1)
    def _():
        for h in range(4):
            dk_got[0, h] = jnp.zeros((T, HD), BF16)
            dv_got[0, h] = jnp.zeros((T, HD), BF16)

    gain_far_copy.wait()
    gains_out[...] = gain_sum[...] + gain_far[...]
    q_sum = jnp.zeros((T, 1), F32)
    k_sum = jnp.zeros((T, 1), F32)
    for h in range(4):
        cols = slice(h * HD, (h + 1) * HD)
        dq = dq_got[h].astype(F32)
        dk = dk_got[0, h].astype(F32) + dk_got[1, h].astype(F32)
        d_v_low[:, cols] = (dv_got[0, h].astype(F32) + dv_got[1, h].astype(F32)).astype(BF16)
        q_sum += jnp.sum(dq * q_raw[:, cols] * q_gain[:, cols], axis=1, keepdims=True)
        k_sum += jnp.sum(dk * k_raw[:, cols] * k_gain[:, cols], axis=1, keepdims=True)
    sums[0] = two_columns(q_sum, k_sum)
    total = tensor_sum(sums, near, far, sum_send, sum_recv)
    qs, ks = scales_in[:, :1], scales_in[:, HD // 2 : HD // 2 + 1]
    q_coef = qs * qs * qs * (total[:, :1] / D)
    k_coef = ks * ks * ks * (total[:, HD // 2 : HD // 2 + 1] / D)
    for h in range(4):
        cols = slice(h * HD, (h + 1) * HD)
        dq = dq_got[h].astype(F32)
        dk = dk_got[0, h].astype(F32) + dk_got[1, h].astype(F32)
        qr, kr = q_raw[:, cols], k_raw[:, cols]
        d_q_low[:, cols] = (qs * q_gain[:, cols] * dq - qr * q_coef).astype(BF16)
        d_k_low[:, cols] = (ks * k_gain[:, cols] * dk - kr * k_coef).astype(BF16)
        q_gain_grad[:, cols] = jnp.sum(dq * qr * qs, axis=0, keepdims=True)
        k_gain_grad[:, cols] = jnp.sum(dk * kr * ks, axis=0, keepdims=True)


def attend_back(d_attended, saved, q_raw, k_raw, scales, q_gain, k_gain, gains, moves):
    dma = pltpu.SemaphoreType.DMA
    operands = (d_attended, *saved, q_raw, k_raw, scales, q_gain, k_gain, gains)
    outs = [
        ((T, 4 * HD), BF16),
        ((T, 4 * HD), BF16),
        ((T, 4 * HD), BF16),
        ((1, 4 * HD), F32),
        ((1, 4 * HD), F32),
        ((8, D), F32),
    ]
    scratch = [
            pltpu.VMEM((4 * T, HD), BF16),
            pltpu.VMEM((4, T, HD), BF16),
            pltpu.VMEM((8, T, HD), BF16),
            pltpu.VMEM((8, T, HD), BF16),
            pltpu.VMEM((8 * T, HD), F32),
            pltpu.VMEM((8 * T, HD), F32),
            pltpu.VMEM((4, T, HD), BF16),
            pltpu.VMEM((2, 4, T, HD), BF16),
            pltpu.VMEM((2, 4, T, HD), BF16),
            pltpu.VMEM((2, T, HD), F32),
            pltpu.VMEM((T, HD), F32),
            pltpu.VMEM((T, HD), F32),
            dma((4,)),
            dma((4,)),
            dma((4,)),
            dma((4,)),
            dma((8,)),
            dma((2, 4)),
            dma((8,)),
            dma((2, 4)),
            dma((2,)),
            dma((2,)),
            pltpu.VMEM((8, D), F32),
            pltpu.VMEM((8, D), F32),
            pltpu.VMEM((8, D), F32),
            dma((2,)),
            dma((2,)),
    ]
    return call(
        attend_back_kernel, "attend_back", 6, operands, outs, scratch, ATTEND_PEERS, moves, 40
    )


def grad_kernel(layout, core_ref, own_half, other_half, *refs):
    rights, out = refs[:-1], refs[-1]
    ours = pl.program_id(0) // 2 == core_ref[0]

    def product(left):
        at = 0
        for right in rights:
            width = right.shape[2]
            got = dot(
                left[...].reshape(4 * T, D // 4), right[...].reshape(4 * T, width), ((0,), (0,))
            ).astype(BF16)
            for y in range(2):
                for x in range(4):
                    rows = got[(y * 4 + x) * 64 : (y * 4 + x + 1) * 64]
                    if layout == "x":
                        out[x, y, 0, :, at : at + width] = rows
                    else:
                        out[0, y, x, :, at : at + width] = rows
            at += width

    @pl.when(ours)
    def _():
        product(own_half)

    @pl.when(jnp.logical_not(ours))
    def _():
        product(other_half)


def partial_grads(name, layout, own_half, other_half, rights):
    total = sum(right.shape[2] for right in rights)
    core = lax.rem(lax.axis_index("tensor"), 2).reshape(1)
    block = (4, T, D // 4)
    in_specs = [
        pl.BlockSpec(block, lambda i, c: (0, 0, jnp.where(i // 2 == c[0], i % 2, 0))),
        pl.BlockSpec(block, lambda i, c: (0, 0, jnp.where(i // 2 == c[0], 0, i % 2))),
    ]
    in_specs += [pl.BlockSpec(right.shape, lambda i, c: (0, 0, 0)) for right in rights]
    if layout == "x":
        shape, out_block = (4, 2, 4, 64, total), (4, 2, 1, 64, total)
        out_spec = pl.BlockSpec(out_block, lambda i, c: (0, 0, i, 0, 0))
    else:
        shape, out_block = (4, 2, 4, 64, total), (1, 2, 4, 64, total)
        out_spec = pl.BlockSpec(out_block, lambda i, c: (i, 0, 0, 0, 0))
    return pl.pallas_call(
        functools.partial(grad_kernel, layout),
        name=name,
        grid_spec=pltpu.PrefetchScalarGridSpec(
            num_scalar_prefetch=1, grid=(4,), in_specs=in_specs, out_specs=out_spec
        ),
        out_shape=jax.ShapeDtypeStruct(shape, BF16),
        compiler_params=pltpu.CompilerParams(vmem_limit_bytes=40 * 2**20),
        cost_estimate=pl.CostEstimate(
            flops=8 * T * D * total, bytes_accessed=8 * T * (D + total) + 2 * D * total,
            transcendentals=0,
        ),
    )(core, own_half, other_half, *rights)


def add_up(blocks):
    return jnp.sum(blocks.astype(F32), axis=0)


def rows_out(final):
    return add_up(final).transpose(1, 0, 2)


def per_device(
    inputs, segments, w_query, w_key, w_value, w_out, q_gain, k_gain, attn_gain,
    w_gate, w_up, w_down, mlp_gain, cotangent,
):
    features, top = inputs[0], cotangent[0]
    q_row, k_row = q_gain.reshape(1, -1), k_gain.reshape(1, -1)
    a_row, m_row = attn_gain.reshape(1, -1), mlp_gain.reshape(1, -1)

    def matmul(a, w):
        return jnp.dot(a, w, preferred_element_type=F32)

    def matmul_t(a, w):
        return lax.dot_general(a, w, (((1,), (1,)), ((), ())), preferred_element_type=F32)

    q_raw = matmul(features, w_query)
    k_raw = matmul(features, w_key)
    value = matmul(features, w_value).astype(BF16)
    (attended, *saved, scales), _ = attend(q_raw, k_raw, value, segments, q_row, k_row, [])
    part = matmul(attended, w_out).astype(BF16)
    (hidden_low, attn_own, hidden_own), (features_half, attended_all) = tensor_call(
        attn_out_kernel, "attn_out", 1, (part, features, a_row),
        [((T, D), BF16), ((OWN, D), F32), ((OWN, D), F32)],
        [half_move(features, "x"), full_move(attended, "z")],
    )
    gate = matmul(hidden_low, w_gate)
    upward = matmul(hidden_low, w_up)
    sigma = jax.nn.sigmoid(gate)
    activated = gate * sigma
    mixed = (activated * upward).astype(BF16)
    part = matmul(mixed, w_down).astype(BF16)
    (d_mlp_low, result_own, gain_rows), (hidden_half, features_rest) = tensor_call(
        mlp_out_kernel, "mlp_out", 2, (part, hidden_own, top, m_row),
        [((T, D), BF16), ((OWN, D), BF16), ((8, D), F32)],
        [half_move(hidden_low, "z"), core_move(features_half)],
    )
    outputs = lax.all_gather(result_own, "tensor", axis=0, tiled=True)
    d_mixed = matmul_t(d_mlp_low, w_down)
    d_up = (d_mixed * activated).astype(BF16)
    d_gate = (d_mixed * upward * sigma * (1.0 + gate * (1.0 - sigma))).astype(BF16)
    part = (matmul_t(d_gate, w_gate) + matmul_t(d_up, w_up)).astype(BF16)
    (d_attn_low, d_hidden_own, gain_rows), (hidden_rest, gate_right, up_right) = tensor_call(
        mlp_back_kernel, "mlp_back", 3, (part, attn_own, top, a_row, gain_rows),
        [((T, D), BF16), ((OWN, D), F32), ((8, D), F32)],
        [core_move(hidden_half), quarter_move(d_gate, "z"), quarter_move(d_up, "z")],
    )
    d_attended = matmul_t(d_attn_low, w_out).astype(BF16)
    mlp_in = partial_grads("mlp_in", "x", hidden_half, hidden_rest, [gate_right, up_right])
    (d_q, d_k, d_v, q_gain_grad, k_gain_grad, gain_rows), moved = attend_back(
        d_attended, saved, q_raw, k_raw, scales, q_row, k_row, gain_rows,
        [
            block_move(mlp_in, "x"), half_move(d_mlp_low, "z"), quarter_move(mixed, "z"),
            quarter_move(d_attn_low, "z"),
        ],
    )
    mlp_in, top_half, mixed_right, attn_left = moved
    part = (matmul_t(d_q, w_query) + matmul_t(d_k, w_key) + matmul_t(d_v, w_value)).astype(BF16)
    out_grad = lax.dot_general(
        attn_left.reshape(4 * T, 512), attended_all.reshape(4 * T, 512), (((0,), (0,)), ((), ())),
        preferred_element_type=F32,
    ).astype(BF16)
    mlp_in = add_up(mlp_in).astype(BF16)
    (input_grad,), moved = tensor_call(
        input_grad_kernel, "input_grad", 4, (part, d_hidden_own), [((T, D), BF16)],
        [
            quarter_move(d_q, "x"), quarter_move(d_k, "x"), quarter_move(d_v, "x"),
            core_move(top_half), final_move(mlp_in, "z"),
            final_move(out_grad.reshape(2, 4, 64, 512), "x"),
        ],
    )
    *qkv_right, top_rest, mlp_in, out_grad = moved
    qkv = partial_grads("qkv", "z", features_half, features_rest, qkv_right)
    mlp_down = partial_grads("mlp_down", "x", top_half, top_rest, [mixed_right])
    heads = jnp.stack([q_gain_grad, k_gain_grad]).reshape(2, 4, 32, 4).transpose(2, 0, 1, 3)
    tiles = jnp.zeros((32, 8, HD), F32)
    tiles = tiles.at[:, 0:2, :64].set(gain_rows[:2].reshape(2, 32, 64).transpose(1, 0, 2))
    tiles = tiles.at[:, 2:4, :16].set(heads.reshape(32, 2, 16))
    _, (qkv, mlp_down, tiles) = call(
        None, "scatter", 7, (), [], [], [],
        [block_move(qkv, "z"), block_move(mlp_down, "x"), rank_move(tiles)], 16,
    )
    _, (qkv, mlp_down) = call(
        None, "place", 8, (), [], [], [],
        [
            final_move(add_up(qkv).astype(BF16), "x"),
            final_move(add_up(mlp_down).astype(BF16), "z"),
        ], 16,
    )
    gains = add_up(tiles)
    qkv, mlp_in, mlp_down = rows_out(qkv), rows_out(mlp_in), rows_out(mlp_down)
    out_grad = add_up(out_grad.reshape(8, 64, 512))

    def joined(block):
        return block.reshape(64, -1)

    return (
        outputs[None],
        input_grad[None],
        joined(qkv[:, :, :128]),
        joined(qkv[:, :, 128:256]),
        joined(qkv[:, :, 256:]),
        out_grad.T,
        gains[2, :16].reshape(4, 4),
        gains[3, :16].reshape(4, 4),
        gains[0, :64],
        joined(mlp_in[:, :, :512]),
        joined(mlp_in[:, :, 512:]),
        joined(mlp_down).T,
        gains[1, :64],
    )


def solution(mesh):
    rows, full = P("dp", "ctx", None), P()
    down, across = P("tensor", None), P(None, "tensor")
    in_specs = (
        rows, P("dp", "ctx"), across, across, across, down, down, down, full,
        across, across, down, full, rows,
    )
    split = ("dp", "ctx")
    out_specs = (
        rows, rows, P(split, "tensor"), P(split, "tensor"), P(split, "tensor"), P("tensor", split),
        P("tensor", split), P("tensor", split), P(split), P(split, "tensor"), P(split, "tensor"),
        P("tensor", split), P(split),
    )
    return jax.shard_map(
        per_device, mesh=mesh, in_specs=in_specs, out_specs=out_specs, check_vma=False
    )
```

```python
import functools
import jax
import jax.numpy as jnp
from jax import lax
from jax.experimental import pallas as pl
from jax.experimental.pallas import tpu as pltpu
from jax.sharding import PartitionSpec as P

MESH = pl.DeviceIdType.MESH
F32 = jnp.float32
BF16 = jnp.bfloat16
EPS = 1e-06
T = 256
D = 2048
HD = 128
OWN = 64
NC = 4
CW = D // NC
VMEM = pl.BlockSpec(memory_space=pltpu.VMEM)
ANY = pl.BlockSpec(memory_space=pltpu.HBM)


def place():
    t = lax.axis_index("tensor")
    ctx = lax.axis_index("ctx")
    return t // 2, lax.rem(t, 2), ctx // 4, lax.rem(ctx, 4)


def peer(dz=0, dy=0, dx=0, dh=0, dc=0):
    yh, core, yl, x = place()
    z = lax.rem(lax.axis_index("dp") + dz, 4)
    ctx = lax.rem(yl + dy, 2) * 4 + lax.rem(x + dx, 4)
    return {"dp": z, "ctx": ctx, "tensor": lax.rem(yh + dh, 2) * 2 + lax.rem(core + dc, 2)}


CORE, FAR = (0, 0, 0, 0, 1), (0, 0, 0, 1, 0)


def along(axis, s):
    return (s, 0, 0, 0, 0) if axis == "z" else (0, 0, s, 0, 0)


def spot(axis):
    return lax.axis_index("dp") if axis == "z" else place()[3]


def remote(src, dst, send_sem, recv_sem, device):
    return pltpu.make_async_remote_copy(
        src_ref=src,
        dst_ref=dst,
        send_sem=send_sem,
        recv_sem=recv_sem,
        device_id=device,
        device_id_type=MESH,
    )


def greet(offsets):
    barrier = pltpu.get_barrier_semaphore()
    for offset in offsets:
        pl.semaphore_signal(barrier, inc=1, device_id=peer(*offset), device_id_type=MESH)
    pl.semaphore_wait(barrier, len(offsets))


def wait(copies):
    for copy in copies:
        copy.wait()


def dot(a, b, dims):
    return lax.dot_general(a, b, (dims, ((), ())), preferred_element_type=F32)


def rows_of(index, count):
    return pl.ds(pl.multiple_of(index * count, count), count)


class Move:
    def __init__(self, source, shape, offsets, pairs):
        self.source, self.shape, self.offsets, self.pairs = source, shape, offsets, pairs
        self.out = (shape, source.dtype)

    def scratch(self):
        dma = pltpu.SemaphoreType.DMA
        return [dma((len(self.offsets),)), dma((len(self.offsets),)), dma((1,))]

    def copies(self, src, dst, send, recv, local):
        made = []
        at = 0
        for a, b, offset in self.pairs(src, dst):
            if offset is None:
                made.append(pltpu.make_async_copy(a, b, local.at[0]))
            else:
                made.append(remote(a, b, send.at[at], recv.at[at], peer(*offset)))
                at += 1
        return made

    def start(self, src, dst, *sems):
        copies = self.copies(src, dst, *sems)
        for copy in copies:
            copy.start()
        return copies


def half_move(a, axis):
    half = a.shape[1] // 2
    offsets = [along(axis, s) for s in (1, 2, 3)]

    def pairs(src, dst):
        mine = src.at[:, pl.ds(pl.multiple_of(place()[1] * half, half), half)]
        me = spot(axis)
        return [(mine, dst.at[me], offset) for offset in offsets + [None]]

    return Move(a, (4, T, half), offsets, pairs)


def core_move(a):
    return Move(a, a.shape, [CORE], lambda src, dst: [(src, dst, CORE)])


def quarter_move(b, axis):
    width = b.shape[1] // 4
    offsets = [along(axis, s) for s in (1, 2, 3)]

    def pairs(src, dst):
        me = spot(axis)

        def part(s):
            return src.at[:, pl.ds(pl.multiple_of(lax.rem(me + s, 4) * width, width), width)]

        made = [(part(s), dst.at[me], along(axis, s)) for s in (1, 2, 3)]
        return made + [(part(0), dst.at[me], None)]

    return Move(b, (4, T, width), offsets, pairs)


def full_move(b, axis):
    offsets = [along(axis, s) for s in (1, 2, 3)]

    def pairs(src, dst):
        return [(src, dst.at[spot(axis)], offset) for offset in offsets + [None]]

    return Move(b, (4,) + b.shape, offsets, pairs)


def block_move(p, axis):
    offsets = [along(axis, s) for s in (1, 2, 3)]

    def pairs(src, dst):
        me = spot(axis)
        made = [(src.at[lax.rem(me + s, 4)], dst.at[me], along(axis, s)) for s in (1, 2, 3)]
        return made + [(src.at[me], dst.at[me], None)]

    return Move(p, p.shape, offsets, pairs)


def final_move(p, axis):
    steps = [(dy, s) for dy in range(2) for s in range(4) if dy or s]

    def offset(dy, s):
        return (s, dy, 0, 0, 0) if axis == "z" else (0, dy, s, 0, 0)

    def pairs(src, dst):
        yl, me = place()[2], spot(axis)
        made = [
            (src.at[lax.rem(yl + dy, 2), lax.rem(me + s, 4)], dst.at[yl, me], offset(dy, s))
            for dy, s in steps
        ]
        return made + [(src.at[yl, me], dst.at[yl, me], None)]

    return Move(p, p.shape, [offset(*step) for step in steps], pairs)


def rank_move(p):
    steps = [(dz, dy, dx, 0, 0) for dz in range(4) for dy in range(2) for dx in range(4)][1:]

    def pairs(src, dst):
        _, _, yl, x = place()
        z = lax.axis_index("dp")
        me = z * 8 + yl * 4 + x

        def rank(dz, dy, dx, *_):
            return lax.rem(z + dz, 4) * 8 + lax.rem(yl + dy, 2) * 4 + lax.rem(x + dx, 4)

        made = [(src.at[rank(*step)], dst.at[me], step) for step in steps]
        return made + [(src.at[me], dst.at[me], None)]

    return Move(p, p.shape, steps, pairs)


def call(main, name, collective_id, operands, outs, scratch, offsets, moves, vmem):
    n_in, n_out, n_move, n_scratch = len(operands), len(outs), len(moves), len(scratch)
    offsets = list(dict.fromkeys(offsets + [o for move in moves for o in move.offsets]))

    def kernel(*refs):
        ins, rest = refs[:n_in], refs[n_in:]
        sources, rest = rest[:n_move], rest[n_move:]
        results, rest = rest[:n_out], rest[n_out:]
        targets, rest = rest[:n_move], rest[n_move:]
        own, sems = rest[:n_scratch], rest[n_scratch:]
        greet(offsets)
        copies = []
        for i, move in enumerate(moves):
            copies += move.copies(sources[i], targets[i], *sems[3 * i : 3 * i + 3])
        for copy in copies:
            copy.start()
        if main is not None:
            main(*ins, *results, *own)
        for copy in copies:
            copy.wait()

    move_outs = [(move.shape, move.source.dtype) for move in moves]
    got = pl.pallas_call(
        kernel,
        name=name,
        out_shape=[jax.ShapeDtypeStruct(shape, kind) for shape, kind in outs + move_outs],
        in_specs=[VMEM] * n_in + [ANY] * n_move,
        out_specs=[VMEM] * n_out + [ANY] * n_move,
        scratch_shapes=scratch + [s for move in moves for s in move.scratch()],
        compiler_params=pltpu.CompilerParams(
            collective_id=collective_id, has_side_effects=True, vmem_limit_bytes=vmem * 2**20
        ),
    )(*operands, *[move.source for move in moves])
    return got[:n_out], got[n_out:]


class Reduce:
    def __init__(self, part, near, far, out_low, acc, *sems):
        self.part, self.near, self.far, self.out_low, self.acc = part, near, far, out_low, acc
        self.sems = sems
        self.near_copies, self.far_copies = [], []

    def send(self, j):
        yh, core, _, _ = place()
        near_send, near_recv, _, _ = self.sems
        cols = pl.ds(j * CW, CW)
        for slot, row in ((0, (1 - yh) * 2 + (1 - core)), (1, yh * 2 + (1 - core))):
            copy = remote(
                self.part.at[rows_of(row, OWN), cols],
                self.near.at[slot, :, cols],
                near_send.at[slot, j],
                near_recv.at[slot, j],
                peer(*CORE),
            )
            copy.start()
            self.near_copies.append(copy)

    def forward(self, j):
        yh, core, _, _ = place()
        _, _, far_send, far_recv = self.sems
        cols = pl.ds(j * CW, CW)
        self.near_copies[2 * j].wait_recv()
        self.out_low[:, cols] = (
            self.part[rows_of((1 - yh) * 2 + core, OWN), cols].astype(F32)
            + self.near[0, :, cols].astype(F32)
        ).astype(BF16)
        copy = remote(
            self.out_low.at[:, cols], self.far.at[:, cols], far_send.at[j], far_recv.at[j],
            peer(*FAR),
        )
        copy.start()
        self.far_copies.append(copy)

    def finish(self):
        yh, core, _, _ = place()
        for j in range(NC):
            cols = pl.ds(j * CW, CW)
            self.near_copies[2 * j + 1].wait_recv()
            self.acc[:, cols] = self.part[rows_of(yh * 2 + core, OWN), cols].astype(
                F32
            ) + self.near[1, :, cols].astype(F32)
        for j in range(NC):
            cols = pl.ds(j * CW, CW)
            self.far_copies[j].wait_recv()
            self.acc[:, cols] = self.acc[:, cols] + self.far[:, cols].astype(F32)
        for copy in self.near_copies + self.far_copies:
            copy.wait_send()

    def run(self, produce):
        for j in range(NC):
            produce(j)
            self.send(j)
            if j > 0:
                self.forward(j - 1)
        self.forward(NC - 1)
        self.finish()


def gather_rows(out, sems):
    yh, core, _, _ = place()
    own_send, own_recv, far_send, far_recv, on_send, on_recv = sems
    mine, other = rows_of(yh * 2 + core, OWN), rows_of((1 - yh) * 2 + core, OWN)
    far_copies, own_copies, on_copies = [], [], []
    for j in range(NC):
        block = out.at[mine, pl.ds(j * CW, CW)]
        copy = remote(block, block, far_send.at[j], far_recv.at[j], peer(*FAR))
        copy.start()
        far_copies.append(copy)
    for j in range(NC):
        block = out.at[mine, pl.ds(j * CW, CW)]
        copy = remote(block, block, own_send.at[j], own_recv.at[j], peer(*CORE))
        copy.start()
        own_copies.append(copy)
    for j in range(NC):
        far_copies[j].wait_recv()
        block = out.at[other, pl.ds(j * CW, CW)]
        copy = remote(block, block, on_send.at[j], on_recv.at[j], peer(*CORE))
        copy.start()
        on_copies.append(copy)
    for copy in own_copies + on_copies:
        copy.wait_recv()
    for copy in far_copies + own_copies + on_copies:
        copy.wait_send()


REDUCE_SCRATCH = [
    pltpu.VMEM((2, OWN, D), BF16),
    pltpu.VMEM((OWN, D), BF16),
    pltpu.VMEM((OWN, D), BF16),
    pltpu.VMEM((OWN, D), F32),
    pltpu.SemaphoreType.DMA((2, NC)),
    pltpu.SemaphoreType.DMA((2, NC)),
    pltpu.SemaphoreType.DMA((NC,)),
    pltpu.SemaphoreType.DMA((NC,)),
]
GATHER_SCRATCH = [pltpu.SemaphoreType.DMA((NC,))] * 6


def norm_scale(v):
    return lax.rsqrt(jnp.mean(v * v, axis=1, keepdims=True) + EPS)


def norm_back(v, r, g, dy):
    column_sum = jnp.sum(dy * g * v, axis=1, keepdims=True)
    return r * g * dy - v * (r * r * r) * (column_sum / D)


def input_tile(ref, j):
    return ref[:, pl.ds(pl.multiple_of(j * CW, CW), CW)]


def feed_forward_kernel(
    attended, attn_gain, mlp_gain, features, cotangent, w_out, w_gate, w_up, w_down,
    d_attended, d_hidden_own, result_own, gain_rows, d_mlp, mixed, d_attn,
    features_half, features_rest, attended_all, hidden_half, hidden_rest, gate_right, up_right,
    out_vmem, gate_vmem, up_vmem, down_vmem, features_own, top_own, part, hidden, act, slope,
    d_gate, d_up, attn_own, hidden_own, load_sems, *scratch,
):
    reduce, gather, move_sems = scratch[:8], scratch[8:14], scratch[14:]
    yh, core, _, _ = place()
    t = yh * 2 + core
    greet(FF_PEERS)
    moves = {}
    sems = iter([move_sems[i : i + 3] for i in range(0, len(move_sems), 3)])
    for name in FF_MOVES:
        moves[name] = next(sems)

    def begin(name, src, dst):
        return FF_MOVES[name].start(src, dst, *moves[name])

    loads = [
        pltpu.make_async_copy(features.at[rows_of(t, OWN)], features_own, load_sems.at[0]),
        pltpu.make_async_copy(cotangent.at[rows_of(t, OWN)], top_own, load_sems.at[1]),
        pltpu.make_async_copy(w_out, out_vmem, load_sems.at[2]),
        pltpu.make_async_copy(w_gate, gate_vmem, load_sems.at[3]),
        pltpu.make_async_copy(w_up, up_vmem, load_sems.at[4]),
        pltpu.make_async_copy(w_down, down_vmem, load_sems.at[5]),
    ]
    for load in loads:
        load.start()
    loads[2].wait()

    def attn_part(j):
        part[:, j * CW : (j + 1) * CW] = dot(
            attended[...], out_vmem[:, j * CW : (j + 1) * CW], ((1,), (0,))
        ).astype(BF16)

    Reduce(part, *reduce).run(attn_part)
    loads[0].wait()
    v = reduce[3][...]
    state = features_own[...].astype(F32) + v * norm_scale(v) * attn_gain[...]
    hidden[rows_of(t, OWN), :] = state.astype(BF16)
    attn_own[...] = v
    hidden_own[...] = state
    features_copies = begin("features_half", features, features_half)
    attended_copies = begin("attended_all", attended, attended_all)
    gather_rows(hidden, gather)
    hidden_copies = begin("hidden_half", hidden, hidden_half)

    for load in loads[3:]:
        load.wait()

    def hidden_units(j, _):
        cols = pl.ds(pl.multiple_of(j * CW, CW), CW)
        gate = dot(hidden[...], gate_vmem[:, cols], ((1,), (0,)))
        upward = dot(hidden[...], up_vmem[:, cols], ((1,), (0,)))
        sigma = jax.nn.sigmoid(gate)
        activated = gate * sigma
        mixed[:, cols] = (activated * upward).astype(BF16)
        act[:, cols] = activated
        slope[:, cols] = upward * sigma * (1.0 + gate * (1.0 - sigma))
        return 0

    lax.fori_loop(0, NC, hidden_units, 0)

    def mlp_part(j):
        part[:, j * CW : (j + 1) * CW] = dot(
            mixed[...], down_vmem[:, j * CW : (j + 1) * CW], ((1,), (0,))
        ).astype(BF16)

    Reduce(part, *reduce).run(mlp_part)
    loads[1].wait()
    v = reduce[3][...]
    z = norm_scale(v)
    dy = top_own[...].astype(F32)
    g = mlp_gain[...]
    d_mlp[rows_of(t, OWN), :] = norm_back(v, z, g, dy).astype(BF16)
    result_own[...] = (hidden_own[...] + v * z * g).astype(BF16)
    mlp_gain_grad = jnp.sum(dy * v * z, axis=0, keepdims=True)
    gather_rows(d_mlp, gather)

    def hidden_units_back(j, _):
        cols = pl.ds(pl.multiple_of(j * CW, CW), CW)
        d_mixed = dot(d_mlp[...], down_vmem[cols, :], ((1,), (1,)))
        d_up[:, cols] = (d_mixed * act[:, cols]).astype(BF16)
        d_gate[:, cols] = (d_mixed * slope[:, cols]).astype(BF16)
        return 0

    lax.fori_loop(0, NC, hidden_units_back, 0)
    right_copies = begin("gate_right", d_gate, gate_right) + begin("up_right", d_up, up_right)
    wait(features_copies)
    features_copies = begin("features_rest", features_half, features_rest)

    def back_part(j):
        rows = pl.ds(j * CW, CW)
        part[:, j * CW : (j + 1) * CW] = (
            dot(d_gate[...], gate_vmem[rows, :], ((1,), (1,)))
            + dot(d_up[...], up_vmem[rows, :], ((1,), (1,)))
        ).astype(BF16)

    Reduce(part, *reduce).run(back_part)
    wait(hidden_copies)
    hidden_copies = begin("hidden_rest", hidden_half, hidden_rest)
    dy = top_own[...].astype(F32) + reduce[3][...]
    v = attn_own[...]
    a = norm_scale(v)
    g = attn_gain[...]
    d_attn[rows_of(t, OWN), :] = norm_back(v, a, g, dy).astype(BF16)
    d_hidden_own[...] = dy
    row = lax.broadcasted_iota(jnp.int32, (8, D), 0)
    attn_grad = jnp.sum(dy * v * a, axis=0, keepdims=True)
    gain_rows[...] = jnp.where(row == 0, attn_grad, mlp_gain_grad)
    gather_rows(d_attn, gather)
    d_attended[...] = dot(d_attn[...], out_vmem[...], ((1,), (1,))).astype(BF16)
    wait(right_copies + hidden_copies + features_copies + attended_copies)


WIDE = jax.ShapeDtypeStruct((T, D), BF16)
NARROW = jax.ShapeDtypeStruct((T, 4 * HD), BF16)
HALVES = jax.ShapeDtypeStruct((4, T, D // 2), BF16)
FF_MOVES = {
    "features_half": half_move(WIDE, "x"),
    "features_rest": core_move(HALVES),
    "attended_all": full_move(NARROW, "z"),
    "hidden_half": half_move(WIDE, "z"),
    "hidden_rest": core_move(HALVES),
    "gate_right": quarter_move(WIDE, "z"),
    "up_right": quarter_move(WIDE, "z"),
}
FF_PEERS = list(
    dict.fromkeys([CORE, FAR] + [o for move in FF_MOVES.values() for o in move.offsets])
)


def feed_forward(attended, attn_gain, mlp_gain, features, cotangent, w_out, w_gate, w_up, w_down):
    outs = [
        ((T, 4 * HD), BF16),
        ((OWN, D), F32),
        ((OWN, D), BF16),
        ((8, D), F32),
        ((T, D), BF16),
        ((T, D), BF16),
        ((T, D), BF16),
    ]
    move_outs = [move.out for move in FF_MOVES.values()]
    weight, wide = pltpu.VMEM((D, D), BF16), pltpu.VMEM((T, D), BF16)
    own, tall = pltpu.VMEM((OWN, D), F32), pltpu.VMEM((T, D), F32)
    scratch = [pltpu.VMEM((4 * HD, D), BF16), weight, weight, weight]
    scratch += [pltpu.VMEM((OWN, D), BF16)] * 2
    scratch += [wide, wide, tall, tall, wide, wide, own, own, pltpu.SemaphoreType.DMA((6,))]
    scratch += REDUCE_SCRATCH + GATHER_SCRATCH
    scratch += [sem for move in FF_MOVES.values() for sem in move.scratch()]
    return pl.pallas_call(
        feed_forward_kernel,
        name="feed_forward",
        out_shape=[jax.ShapeDtypeStruct(shape, kind) for shape, kind in outs + move_outs],
        in_specs=[VMEM] * 3 + [ANY] * 6,
        out_specs=[VMEM] * len(outs) + [ANY] * len(move_outs),
        scratch_shapes=scratch,
        compiler_params=pltpu.CompilerParams(
            collective_id=1, has_side_effects=True, vmem_limit_bytes=60 * 2**20
        ),
    )(attended, attn_gain, mlp_gain, features, cotangent, w_out, w_gate, w_up, w_down)


def input_grad_kernel(part, d_hidden_own, out, *scratch):
    reduce, gather = scratch[:8], scratch[8:14]
    yh, core, _, _ = place()
    mine = rows_of(yh * 2 + core, OWN)
    Reduce(part, *reduce).run(lambda j: None)
    out[mine, :] = (d_hidden_own[...] + reduce[3][...]).astype(BF16)
    gather_rows(out, gather)


def tensor_call(kernel, name, collective_id, operands, outs, moves):
    scratch = REDUCE_SCRATCH + GATHER_SCRATCH
    return call(kernel, name, collective_id, operands, outs, scratch, [CORE, FAR], moves, 24)


def row_device(yl, x):
    return {"ctx": yl * 4 + x}


ATTEND_PEERS = [CORE, FAR] + [(0, dy, dx, 0, 0) for dy in range(2) for dx in range(4) if dy or dx]


def tensor_sum(own, near, far, send, recv):
    yh, core, _, _ = place()
    copy = remote(own.at[0], near, send.at[0], recv.at[0], peer(*CORE))
    copy.start()
    copy.wait_recv()
    own[1] = own[0] + near[...]
    again = remote(own.at[1], far, send.at[1], recv.at[1], peer(*FAR))
    again.start()
    again.wait_recv()
    total = own[1] + far[...]
    copy.wait_send()
    again.wait_send()
    return total


def two_columns(first, second):
    lane = lax.broadcasted_iota(jnp.int32, (T, HD), 1)
    return jnp.where(lane < HD // 2, first, second)


class Spread:
    def __init__(self, src, dst, sems):
        self.src, self.dst = src, dst
        self.send, self.recv, self.down_send, self.down_recv = sems

    def row_copy(self, s):
        _, _, yl, x = place()
        h = lax.rem(x + s, 4)
        return remote(
            self.src.at[:, pl.ds(pl.multiple_of(h * HD, HD), HD)],
            self.dst.at[rows_of(yl * 4 + x, T)],
            self.send.at[s],
            self.recv.at[s],
            row_device(yl, h),
        )

    def down_copy(self, s):
        _, _, yl, x = place()
        h = lax.rem(x + s, 4)
        return remote(
            self.src.at[:, pl.ds(pl.multiple_of(h * HD, HD), HD)],
            self.dst.at[rows_of(x, T)],
            self.down_send.at[s],
            self.down_recv.at[s],
            row_device(1, h),
        )


def keep_own(src, dst, block):
    _, _, _, x = place()
    dst[rows_of(block, T), :] = src[:, pl.ds(pl.multiple_of(x * HD, HD), HD)]


def attend_kernel(
    q_raw, k_raw, value, seg, q_gain, k_gain,
    attended, q_head, k_head, v_head, probs_out, scale_out,
    seg_all, q_low, k_low, sums, near, far, result,
    v_sems, k_sems, q_send, q_recv, s_send, s_recv, sum_send, sum_recv, a_send, a_recv,
):
    yh, core, yl, x = place()
    me = yl * 4 + x
    v_sems = [v_sems.at[i] for i in range(4)]
    k_sems = [k_sems.at[i] for i in range(4)]
    values = Spread(value, v_head, v_sems)
    keys = Spread(k_low, k_head, k_sems)

    @pl.when(yl == 0)
    def _():
        for s in range(4):
            values.down_copy(s).start()

    for s in (1, 2, 3):
        values.row_copy(s).start()
    seg_all[me] = jnp.broadcast_to(seg[...].astype(F32), (8, T))

    def seg_copy(s):
        dx, dy = s % 4, s // 4
        to = row_device(lax.rem(yl + dy, 2), lax.rem(x + dx, 4))
        return remote(seg_all.at[me], seg_all.at[me], s_send.at[s], s_recv.at[s], to)

    for s in range(1, 8):
        seg_copy(s).start()

    qr, kr = q_raw[...], k_raw[...]
    sums[0] = two_columns(
        jnp.sum(qr * qr, axis=1, keepdims=True), jnp.sum(kr * kr, axis=1, keepdims=True)
    )
    keep_own(value, v_head, me)
    scales = lax.rsqrt(tensor_sum(sums, near, far, sum_send, sum_recv) / D + EPS)
    scale_out[...] = scales
    k_low[...] = (kr * scales[:, HD // 2 : HD // 2 + 1] * k_gain[...]).astype(BF16)

    @pl.when(yl == 0)
    def _():
        for s in range(4):
            keys.down_copy(s).start()

    for s in (1, 2, 3):
        keys.row_copy(s).start()
    q_low[...] = (qr * scales[:, :1] * q_gain[...]).astype(BF16)

    def q_copy(s):
        h = lax.rem(x + s, 4)
        return remote(
            q_low.at[:, pl.ds(pl.multiple_of(h * HD, HD), HD)],
            q_head.at[rows_of(x, T)],
            q_send.at[s],
            q_recv.at[s],
            row_device(yl, h),
        )

    for s in (1, 2, 3):
        q_copy(s).start()
    keep_own(k_low, k_head, me)
    keep_own(q_low, q_head, x)
    for s in range(1, 8):
        seg_copy(s).wait()
    for s in (1, 2, 3):
        values.row_copy(s).wait()
        keys.row_copy(s).wait()
        q_copy(s).wait()

    @pl.when(yl == 0)
    def _():
        for s in range(4):
            values.down_copy(s).wait_send()
            keys.down_copy(s).wait_send()

    @pl.when(yl == 1)
    def _():
        for s in range(4):
            values.down_copy(s).wait_recv()
            keys.down_copy(s).wait_recv()

    lane = lax.broadcasted_iota(jnp.int32, (8, HD), 0)
    pick = jnp.where(lane == 0, 1.0, 0.0)

    def attend(row, i):
        blocks = row * 4 + i + 1
        width = blocks * T
        q = q_head[i * T : (i + 1) * T, :]
        scores = dot(q, k_head[:width, :], ((1,), (1,))) * HD ** (-0.5)
        own_seg = dot(seg_all[row * 4 + i], pick, ((0,), (0,)))[:, :1]
        seg_keys = jnp.concatenate([seg_all[b, :1, :] for b in range(blocks)], axis=1)
        q_place = lax.broadcasted_iota(jnp.int32, (T, width), 0) + (blocks - 1) * T
        k_place = lax.broadcasted_iota(jnp.int32, (T, width), 1)
        counted = (k_place <= q_place) & (seg_keys == own_seg)
        scores = jnp.where(counted, scores, -1e30)
        exps = jnp.exp(scores - jnp.max(scores, axis=1, keepdims=True))
        probs = (exps * (1.0 / jnp.sum(exps, axis=1, keepdims=True))).astype(BF16)
        probs_out[i, :, :width] = probs
        result[i] = dot(probs, v_head[:width, :], ((1,), (0,))).astype(BF16)

    def back_copy(i):
        return remote(
            result.at[i],
            attended.at[:, pl.ds(pl.multiple_of(x * HD, HD), HD)],
            a_send.at[i],
            a_recv.at[x],
            row_device(yl, i),
        )

    for i in range(4):
        for row in range(2):

            @pl.when(yl == row)
            def _():
                attend(row, i)

        @pl.when(x == i)
        def _():
            attended[:, i * HD : (i + 1) * HD] = result[i]

        @pl.when(x != i)
        def _():
            back_copy(i).start()

    for h in range(4):

        @pl.when(x != h)
        def _():
            back_copy(h).wait_send()
            remote(
                result.at[h],
                attended.at[:, h * HD : (h + 1) * HD],
                a_send.at[h],
                a_recv.at[h],
                row_device(yl, h),
            ).wait_recv()


def attend(q_raw, k_raw, value, seg, q_gain, k_gain, moves):
    dma = pltpu.SemaphoreType.DMA
    operands = (q_raw, k_raw, value, seg, q_gain, k_gain)
    outs = [
        ((T, 4 * HD), BF16),
        ((4 * T, HD), BF16),
        ((8 * T, HD), BF16),
        ((8 * T, HD), BF16),
        ((4, T, 8 * T), BF16),
        ((T, HD), F32),
    ]
    scratch = [
            pltpu.VMEM((8, 8, T), F32),
            pltpu.VMEM((T, 4 * HD), BF16),
            pltpu.VMEM((T, 4 * HD), BF16),
            pltpu.VMEM((2, T, HD), F32),
            pltpu.VMEM((T, HD), F32),
            pltpu.VMEM((T, HD), F32),
            pltpu.VMEM((4, T, HD), BF16),
            dma((4, 4)),
            dma((4, 4)),
            dma((4,)),
            dma((4,)),
            dma((8,)),
            dma((8,)),
            dma((2,)),
            dma((2,)),
            dma((4,)),
            dma((4,)),
    ]
    return call(attend_kernel, "attend", 5, operands, outs, scratch, ATTEND_PEERS, moves, 40)


def attend_back_kernel(
    d_attended, q_head, k_head, v_head, probs_in, q_raw, k_raw, scales_in, q_gain, k_gain, gains,
    d_q_low, d_k_low, d_v_low, q_gain_grad, k_gain_grad, gains_out,
    d_out, dq_send_buf, dk_send_buf, dv_send_buf, dk_acc, dv_acc, dq_got, dk_got, dv_got,
    sums, near, far,
    o_send, o_recv, dq_send, dq_recv, dk_send, dk_recv, dv_send, dv_recv, sum_send, sum_recv,
    gain_near, gain_far, gain_sum, gain_send, gain_recv,
):
    yh, core, yl, x = place()
    scale = HD ** (-0.5)

    def o_copy(s):
        h = lax.rem(x + s, 4)
        return remote(
            d_attended.at[:, pl.ds(pl.multiple_of(h * HD, HD), HD)],
            d_out.at[rows_of(x, T)],
            o_send.at[s],
            o_recv.at[s],
            row_device(yl, h),
        )

    for s in (1, 2, 3):
        o_copy(s).start()
    gain_near_copy = remote(gains, gain_near, gain_send.at[0], gain_recv.at[0], peer(*CORE))
    gain_near_copy.start()
    keep_own(d_attended, d_out, x)
    dk_acc[...] = jnp.zeros_like(dk_acc)
    dv_acc[...] = jnp.zeros_like(dv_acc)
    for s in (1, 2, 3):
        o_copy(s).wait()

    gain_near_copy.wait()
    gain_sum[...] = gains[...] + gain_near[...]
    gain_far_copy = remote(gain_sum, gain_far, gain_send.at[1], gain_recv.at[1], peer(*FAR))
    gain_far_copy.start()

    def back(row, i):
        width = (row * 4 + i + 1) * T
        q = q_head[i * T : (i + 1) * T, :]
        do = d_out[i * T : (i + 1) * T, :]
        probs_low = probs_in[i, :, :width]
        probs = probs_low.astype(F32)
        d_probs = dot(do, v_head[:width, :], ((1,), (1,)))
        delta = jnp.sum(probs * d_probs, axis=1, keepdims=True)
        d_scores = (probs * (d_probs - delta)).astype(BF16)
        dq_send_buf[i] = (dot(d_scores, k_head[:width, :], ((1,), (0,))) * scale).astype(BF16)
        dk_acc[:width, :] += dot(d_scores, q, ((0,), (0,)))
        dv_acc[:width, :] += dot(probs_low, do, ((0,), (0,)))

    def dq_copy(i):
        return remote(
            dq_send_buf.at[i], dq_got.at[x], dq_send.at[i], dq_recv.at[x], row_device(yl, i)
        )

    for i in range(4):
        for row in range(2):

            @pl.when(yl == row)
            def _():
                back(row, i)

        @pl.when(x == i)
        def _():
            dq_got[i] = dq_send_buf[i]

        @pl.when(x != i)
        def _():
            dq_copy(i).start()

    def kv_copy(j, buf, got, send, recv):
        return remote(
            buf.at[j], got.at[yl, x], send.at[j], recv.at[yl, x], row_device(j // 4, j % 4)
        )

    dk_args = (dk_send_buf, dk_got, dk_send, dk_recv)
    dv_args = (dv_send_buf, dv_got, dv_send, dv_recv)
    for j in range(8):
        dk_send_buf[j] = (dk_acc[j * T : (j + 1) * T, :] * scale).astype(BF16)
        dv_send_buf[j] = dv_acc[j * T : (j + 1) * T, :].astype(BF16)
        here = (yl == j // 4) & (x == j % 4)

        @pl.when(here)
        def _():
            dk_got[j // 4, j % 4] = dk_send_buf[j]
            dv_got[j // 4, j % 4] = dv_send_buf[j]

        sends = (yl >= j // 4) & ~here

        @pl.when(sends)
        def _():
            kv_copy(j, *dk_args).start()
            kv_copy(j, *dv_args).start()

    for h in range(4):

        @pl.when(x != h)
        def _():
            dq_copy(h).wait_send()
            remote(
                dq_send_buf.at[h], dq_got.at[h], dq_send.at[h], dq_recv.at[h], row_device(yl, h)
            ).wait_recv()

        for row in range(2):
            comes = (row >= yl) & ~((yl == row) & (x == h))

            @pl.when(comes)
            def _():
                for buf, got, send, recv in (dk_args, dv_args):
                    remote(
                        buf.at[0],
                        got.at[row, h],
                        send.at[0],
                        recv.at[row, h],
                        row_device(row, h),
                    ).wait_recv()

    for j in range(8):
        here = (yl == j // 4) & (x == j % 4)
        sends = (yl >= j // 4) & ~here

        @pl.when(sends)
        def _():
            kv_copy(j, *dk_args).wait_send()
            kv_copy(j, *dv_args).wait_send()

    @pl.when(yl == 1)
    def _():
        for h in range(4):
            dk_got[0, h] = jnp.zeros((T, HD), BF16)
            dv_got[0, h] = jnp.zeros((T, HD), BF16)

    gain_far_copy.wait()
    gains_out[...] = gain_sum[...] + gain_far[...]
    q_sum = jnp.zeros((T, 1), F32)
    k_sum = jnp.zeros((T, 1), F32)
    for h in range(4):
        cols = slice(h * HD, (h + 1) * HD)
        dq = dq_got[h].astype(F32)
        dk = dk_got[0, h].astype(F32) + dk_got[1, h].astype(F32)
        d_v_low[:, cols] = (dv_got[0, h].astype(F32) + dv_got[1, h].astype(F32)).astype(BF16)
        q_sum += jnp.sum(dq * q_raw[:, cols] * q_gain[:, cols], axis=1, keepdims=True)
        k_sum += jnp.sum(dk * k_raw[:, cols] * k_gain[:, cols], axis=1, keepdims=True)
    sums[0] = two_columns(q_sum, k_sum)
    total = tensor_sum(sums, near, far, sum_send, sum_recv)
    qs, ks = scales_in[:, :1], scales_in[:, HD // 2 : HD // 2 + 1]
    q_coef = qs * qs * qs * (total[:, :1] / D)
    k_coef = ks * ks * ks * (total[:, HD // 2 : HD // 2 + 1] / D)
    for h in range(4):
        cols = slice(h * HD, (h + 1) * HD)
        dq = dq_got[h].astype(F32)
        dk = dk_got[0, h].astype(F32) + dk_got[1, h].astype(F32)
        qr, kr = q_raw[:, cols], k_raw[:, cols]
        d_q_low[:, cols] = (qs * q_gain[:, cols] * dq - qr * q_coef).astype(BF16)
        d_k_low[:, cols] = (ks * k_gain[:, cols] * dk - kr * k_coef).astype(BF16)
        q_gain_grad[:, cols] = jnp.sum(dq * qr * qs, axis=0, keepdims=True)
        k_gain_grad[:, cols] = jnp.sum(dk * kr * ks, axis=0, keepdims=True)


def attend_back(d_attended, saved, q_raw, k_raw, scales, q_gain, k_gain, gains, moves):
    dma = pltpu.SemaphoreType.DMA
    operands = (d_attended, *saved, q_raw, k_raw, scales, q_gain, k_gain, gains)
    outs = [
        ((T, 4 * HD), BF16),
        ((T, 4 * HD), BF16),
        ((T, 4 * HD), BF16),
        ((1, 4 * HD), F32),
        ((1, 4 * HD), F32),
        ((8, D), F32),
    ]
    scratch = [
            pltpu.VMEM((4 * T, HD), BF16),
            pltpu.VMEM((4, T, HD), BF16),
            pltpu.VMEM((8, T, HD), BF16),
            pltpu.VMEM((8, T, HD), BF16),
            pltpu.VMEM((8 * T, HD), F32),
            pltpu.VMEM((8 * T, HD), F32),
            pltpu.VMEM((4, T, HD), BF16),
            pltpu.VMEM((2, 4, T, HD), BF16),
            pltpu.VMEM((2, 4, T, HD), BF16),
            pltpu.VMEM((2, T, HD), F32),
            pltpu.VMEM((T, HD), F32),
            pltpu.VMEM((T, HD), F32),
            dma((4,)),
            dma((4,)),
            dma((4,)),
            dma((4,)),
            dma((8,)),
            dma((2, 4)),
            dma((8,)),
            dma((2, 4)),
            dma((2,)),
            dma((2,)),
            pltpu.VMEM((8, D), F32),
            pltpu.VMEM((8, D), F32),
            pltpu.VMEM((8, D), F32),
            dma((2,)),
            dma((2,)),
    ]
    return call(
        attend_back_kernel, "attend_back", 6, operands, outs, scratch, ATTEND_PEERS, moves, 40
    )


def grad_kernel(layout, core_ref, own_half, other_half, *refs):
    rights, out = refs[:-1], refs[-1]
    ours = pl.program_id(0) // 2 == core_ref[0]

    def product(left):
        at = 0
        for right in rights:
            width = right.shape[2]
            got = dot(
                left[...].reshape(4 * T, D // 4), right[...].reshape(4 * T, width), ((0,), (0,))
            ).astype(BF16)
            for y in range(2):
                for x in range(4):
                    rows = got[(y * 4 + x) * 64 : (y * 4 + x + 1) * 64]
                    if layout == "x":
                        out[x, y, 0, :, at : at + width] = rows
                    else:
                        out[0, y, x, :, at : at + width] = rows
            at += width

    @pl.when(ours)
    def _():
        product(own_half)

    @pl.when(jnp.logical_not(ours))
    def _():
        product(other_half)


def partial_grads(name, layout, own_half, other_half, rights):
    total = sum(right.shape[2] for right in rights)
    core = lax.rem(lax.axis_index("tensor"), 2).reshape(1)
    block = (4, T, D // 4)
    in_specs = [
        pl.BlockSpec(block, lambda i, c: (0, 0, jnp.where(i // 2 == c[0], i % 2, 0))),
        pl.BlockSpec(block, lambda i, c: (0, 0, jnp.where(i // 2 == c[0], 0, i % 2))),
    ]
    in_specs += [pl.BlockSpec(right.shape, lambda i, c: (0, 0, 0)) for right in rights]
    if layout == "x":
        shape, out_block = (4, 2, 4, 64, total), (4, 2, 1, 64, total)
        out_spec = pl.BlockSpec(out_block, lambda i, c: (0, 0, i, 0, 0))
    else:
        shape, out_block = (4, 2, 4, 64, total), (1, 2, 4, 64, total)
        out_spec = pl.BlockSpec(out_block, lambda i, c: (i, 0, 0, 0, 0))
    return pl.pallas_call(
        functools.partial(grad_kernel, layout),
        name=name,
        grid_spec=pltpu.PrefetchScalarGridSpec(
            num_scalar_prefetch=1, grid=(4,), in_specs=in_specs, out_specs=out_spec
        ),
        out_shape=jax.ShapeDtypeStruct(shape, BF16),
        compiler_params=pltpu.CompilerParams(vmem_limit_bytes=40 * 2**20),
        cost_estimate=pl.CostEstimate(
            flops=8 * T * D * total, bytes_accessed=8 * T * (D + total) + 2 * D * total,
            transcendentals=0,
        ),
    )(core, own_half, other_half, *rights)


def add_up(blocks):
    return jnp.sum(blocks.astype(F32), axis=0)


def rows_out(final):
    return add_up(final).transpose(1, 0, 2)


def per_device(
    inputs, segments, w_query, w_key, w_value, w_out, q_gain, k_gain, attn_gain,
    w_gate, w_up, w_down, mlp_gain, cotangent,
):
    features, top = inputs[0], cotangent[0]
    q_row, k_row = q_gain.reshape(1, -1), k_gain.reshape(1, -1)
    a_row, m_row = attn_gain.reshape(1, -1), mlp_gain.reshape(1, -1)

    def matmul(a, w):
        return jnp.dot(a, w, preferred_element_type=F32)

    def matmul_t(a, w):
        return lax.dot_general(a, w, (((1,), (1,)), ((), ())), preferred_element_type=F32)

    q_raw = matmul(features, w_query)
    k_raw = matmul(features, w_key)
    value = matmul(features, w_value).astype(BF16)
    (attended, *saved, scales), _ = attend(q_raw, k_raw, value, segments, q_row, k_row, [])
    (
        d_attended, d_hidden_own, result_own, gain_rows, d_mlp_low, mixed, d_attn_low,
        features_half, features_rest, attended_all, hidden_half, hidden_rest, gate_right, up_right,
    ) = feed_forward(attended, a_row, m_row, features, top, w_out, w_gate, w_up, w_down)
    outputs = lax.all_gather(result_own, "tensor", axis=0, tiled=True)
    mlp_in = partial_grads("mlp_in", "x", hidden_half, hidden_rest, [gate_right, up_right])
    (d_q, d_k, d_v, q_gain_grad, k_gain_grad, gain_rows), moved = attend_back(
        d_attended, saved, q_raw, k_raw, scales, q_row, k_row, gain_rows,
        [
            block_move(mlp_in, "x"), half_move(d_mlp_low, "z"), quarter_move(mixed, "z"),
            quarter_move(d_attn_low, "z"),
        ],
    )
    mlp_in, top_half, mixed_right, attn_left = moved
    part = (matmul_t(d_q, w_query) + matmul_t(d_k, w_key) + matmul_t(d_v, w_value)).astype(BF16)
    out_grad = lax.dot_general(
        attn_left.reshape(4 * T, 512), attended_all.reshape(4 * T, 512), (((0,), (0,)), ((), ())),
        preferred_element_type=F32,
    ).astype(BF16)
    mlp_in = add_up(mlp_in).astype(BF16)
    (input_grad,), moved = tensor_call(
        input_grad_kernel, "input_grad", 4, (part, d_hidden_own), [((T, D), BF16)],
        [
            quarter_move(d_q, "x"), quarter_move(d_k, "x"), quarter_move(d_v, "x"),
            core_move(top_half), final_move(mlp_in, "z"),
            final_move(out_grad.reshape(2, 4, 64, 512), "x"),
        ],
    )
    *qkv_right, top_rest, mlp_in, out_grad = moved
    qkv = partial_grads("qkv", "z", features_half, features_rest, qkv_right)
    mlp_down = partial_grads("mlp_down", "x", top_half, top_rest, [mixed_right])
    heads = jnp.stack([q_gain_grad, k_gain_grad]).reshape(2, 4, 32, 4).transpose(2, 0, 1, 3)
    tiles = jnp.zeros((32, 8, HD), F32)
    tiles = tiles.at[:, 0:2, :64].set(gain_rows[:2].reshape(2, 32, 64).transpose(1, 0, 2))
    tiles = tiles.at[:, 2:4, :16].set(heads.reshape(32, 2, 16))
    _, (qkv, mlp_down, tiles) = call(
        None, "scatter", 7, (), [], [], [],
        [block_move(qkv, "z"), block_move(mlp_down, "x"), rank_move(tiles)], 16,
    )
    _, (qkv, mlp_down) = call(
        None, "place", 8, (), [], [], [],
        [
            final_move(add_up(qkv).astype(BF16), "x"),
            final_move(add_up(mlp_down).astype(BF16), "z"),
        ], 16,
    )
    gains = add_up(tiles)
    qkv, mlp_in, mlp_down = rows_out(qkv), rows_out(mlp_in), rows_out(mlp_down)
    out_grad = add_up(out_grad.reshape(8, 64, 512))

    def joined(block):
        return block.reshape(64, -1)

    return (
        outputs[None],
        input_grad[None],
        joined(qkv[:, :, :128]),
        joined(qkv[:, :, 128:256]),
        joined(qkv[:, :, 256:]),
        out_grad.T,
        gains[2, :16].reshape(4, 4),
        gains[3, :16].reshape(4, 4),
        gains[0, :64],
        joined(mlp_in[:, :, :512]),
        joined(mlp_in[:, :, 512:]),
        joined(mlp_down).T,
        gains[1, :64],
    )


def solution(mesh):
    rows, full = P("dp", "ctx", None), P()
    down, across = P("tensor", None), P(None, "tensor")
    in_specs = (
        rows, P("dp", "ctx"), across, across, across, down, down, down, full,
        across, across, down, full, rows,
    )
    split = ("dp", "ctx")
    out_specs = (
        rows, rows, P(split, "tensor"), P(split, "tensor"), P(split, "tensor"), P("tensor", split),
        P("tensor", split), P("tensor", split), P(split), P(split, "tensor"), P(split, "tensor"),
        P("tensor", split), P(split),
    )
    return jax.shard_map(
        per_device, mesh=mesh, in_specs=in_specs, out_specs=out_specs, check_vma=False
    )
```

```python
import functools
import jax
import jax.numpy as jnp
from jax import lax
from jax.experimental import pallas as pl
from jax.experimental.pallas import tpu as pltpu
from jax.sharding import PartitionSpec as P

MESH = pl.DeviceIdType.MESH
F32 = jnp.float32
BF16 = jnp.bfloat16
EPS = 1e-06
T = 256
D = 2048
HD = 128
OWN = 64
NC = 4
CW = D // NC
VMEM = pl.BlockSpec(memory_space=pltpu.VMEM)
ANY = pl.BlockSpec(memory_space=pltpu.HBM)


def place():
    t = lax.axis_index("tensor")
    ctx = lax.axis_index("ctx")
    return t // 2, lax.rem(t, 2), ctx // 4, lax.rem(ctx, 4)


def peer(dz=0, dy=0, dx=0, dh=0, dc=0):
    yh, core, yl, x = place()
    z = lax.rem(lax.axis_index("dp") + dz, 4)
    ctx = lax.rem(yl + dy, 2) * 4 + lax.rem(x + dx, 4)
    return {"dp": z, "ctx": ctx, "tensor": lax.rem(yh + dh, 2) * 2 + lax.rem(core + dc, 2)}


CORE, FAR = (0, 0, 0, 0, 1), (0, 0, 0, 1, 0)


def along(axis, s):
    return (s, 0, 0, 0, 0) if axis == "z" else (0, 0, s, 0, 0)


def spot(axis):
    return lax.axis_index("dp") if axis == "z" else place()[3]


def remote(src, dst, send_sem, recv_sem, device):
    return pltpu.make_async_remote_copy(
        src_ref=src,
        dst_ref=dst,
        send_sem=send_sem,
        recv_sem=recv_sem,
        device_id=device,
        device_id_type=MESH,
    )


def greet(offsets):
    barrier = pltpu.get_barrier_semaphore()
    for offset in offsets:
        pl.semaphore_signal(barrier, inc=1, device_id=peer(*offset), device_id_type=MESH)
    pl.semaphore_wait(barrier, len(offsets))


def wait(copies):
    for copy in copies:
        copy.wait()


def dot(a, b, dims):
    return lax.dot_general(a, b, (dims, ((), ())), preferred_element_type=F32)


def rows_of(index, count):
    return pl.ds(pl.multiple_of(index * count, count), count)


class Move:
    def __init__(self, source, shape, offsets, pairs):
        self.source, self.shape, self.offsets, self.pairs = source, shape, offsets, pairs
        self.out = (shape, source.dtype)

    def scratch(self):
        dma = pltpu.SemaphoreType.DMA
        return [dma((len(self.offsets),)), dma((len(self.offsets),)), dma((1,))]

    def copies(self, src, dst, send, recv, local):
        made = []
        at = 0
        for a, b, offset in self.pairs(src, dst):
            if offset is None:
                made.append(pltpu.make_async_copy(a, b, local.at[0]))
            else:
                made.append(remote(a, b, send.at[at], recv.at[at], peer(*offset)))
                at += 1
        return made

    def start(self, src, dst, *sems):
        copies = self.copies(src, dst, *sems)
        for copy in copies:
            copy.start()
        return copies


def half_move(a, axis):
    half = a.shape[1] // 2
    offsets = [along(axis, s) for s in (1, 2, 3)]

    def pairs(src, dst):
        mine = src.at[:, pl.ds(pl.multiple_of(place()[1] * half, half), half)]
        me = spot(axis)
        return [(mine, dst.at[me], offset) for offset in offsets + [None]]

    return Move(a, (4, T, half), offsets, pairs)


def core_move(a):
    return Move(a, a.shape, [CORE], lambda src, dst: [(src, dst, CORE)])


def quarter_move(b, axis):
    width = b.shape[1] // 4
    offsets = [along(axis, s) for s in (1, 2, 3)]

    def pairs(src, dst):
        me = spot(axis)

        def part(s):
            return src.at[:, pl.ds(pl.multiple_of(lax.rem(me + s, 4) * width, width), width)]

        made = [(part(s), dst.at[me], along(axis, s)) for s in (1, 2, 3)]
        return made + [(part(0), dst.at[me], None)]

    return Move(b, (4, T, width), offsets, pairs)


def full_move(b, axis):
    offsets = [along(axis, s) for s in (1, 2, 3)]

    def pairs(src, dst):
        return [(src, dst.at[spot(axis)], offset) for offset in offsets + [None]]

    return Move(b, (4,) + b.shape, offsets, pairs)


def block_move(p, axis):
    offsets = [along(axis, s) for s in (1, 2, 3)]

    def pairs(src, dst):
        me = spot(axis)
        made = [(src.at[lax.rem(me + s, 4)], dst.at[me], along(axis, s)) for s in (1, 2, 3)]
        return made + [(src.at[me], dst.at[me], None)]

    return Move(p, p.shape, offsets, pairs)


def final_move(p, axis):
    steps = [(dy, s) for dy in range(2) for s in range(4) if dy or s]

    def offset(dy, s):
        return (s, dy, 0, 0, 0) if axis == "z" else (0, dy, s, 0, 0)

    def pairs(src, dst):
        yl, me = place()[2], spot(axis)
        made = [
            (src.at[lax.rem(yl + dy, 2), lax.rem(me + s, 4)], dst.at[yl, me], offset(dy, s))
            for dy, s in steps
        ]
        return made + [(src.at[yl, me], dst.at[yl, me], None)]

    return Move(p, p.shape, [offset(*step) for step in steps], pairs)


def rank_move(p):
    steps = [(dz, dy, dx, 0, 0) for dz in range(4) for dy in range(2) for dx in range(4)][1:]

    def pairs(src, dst):
        _, _, yl, x = place()
        z = lax.axis_index("dp")
        me = z * 8 + yl * 4 + x

        def rank(dz, dy, dx, *_):
            return lax.rem(z + dz, 4) * 8 + lax.rem(yl + dy, 2) * 4 + lax.rem(x + dx, 4)

        made = [(src.at[rank(*step)], dst.at[me], step) for step in steps]
        return made + [(src.at[me], dst.at[me], None)]

    return Move(p, p.shape, steps, pairs)


class Names:
    def __init__(self, **names):
        self.__dict__.update(names)


def run_kernel(body, collective_id, small, large, small_outs, large_outs, scratch, vmem):
    ins = [jax.tree.flatten(small), jax.tree.flatten(large)]
    shapes = [
        jax.tree.flatten({name: jax.ShapeDtypeStruct(*out) for name, out in outs.items()})
        for outs in (small_outs, large_outs)
    ]
    own = jax.tree.flatten(scratch)

    def kernel(*refs):
        names, at = {}, 0
        for leaves, tree in ins + shapes + [own]:
            names.update(tree.unflatten(refs[at : at + len(leaves)]))
            at += len(leaves)
        body(Names(**names))

    got = pl.pallas_call(
        kernel,
        name=body.__name__,
        out_shape=shapes[0][0] + shapes[1][0],
        in_specs=[VMEM] * len(ins[0][0]) + [ANY] * len(ins[1][0]),
        out_specs=[VMEM] * len(shapes[0][0]) + [ANY] * len(shapes[1][0]),
        scratch_shapes=own[0],
        compiler_params=pltpu.CompilerParams(
            collective_id=collective_id, has_side_effects=True, vmem_limit_bytes=vmem * 2**20
        ),
    )(*ins[0][0], *ins[1][0])
    n = len(shapes[0][0])
    return Names(**shapes[0][1].unflatten(got[:n]), **shapes[1][1].unflatten(got[n:]))


def move_scratch(moves):
    return {name: move.scratch() for name, move in moves.items()}


def peers_of(moves):
    return [offset for move in moves.values() for offset in move.offsets]


def distinct(offsets):
    return list(dict.fromkeys(offsets))


class Reduce:
    def __init__(self, part, near, far, out_low, acc, *sems):
        self.part, self.near, self.far, self.out_low, self.acc = part, near, far, out_low, acc
        self.sems = sems
        self.near_copies, self.far_copies = [], []

    def send(self, j):
        yh, core, _, _ = place()
        near_send, near_recv, _, _ = self.sems
        cols = pl.ds(j * CW, CW)
        for slot, row in ((0, (1 - yh) * 2 + (1 - core)), (1, yh * 2 + (1 - core))):
            copy = remote(
                self.part.at[rows_of(row, OWN), cols],
                self.near.at[slot, :, cols],
                near_send.at[slot, j],
                near_recv.at[slot, j],
                peer(*CORE),
            )
            copy.start()
            self.near_copies.append(copy)

    def forward(self, j):
        yh, core, _, _ = place()
        _, _, far_send, far_recv = self.sems
        cols = pl.ds(j * CW, CW)
        self.near_copies[2 * j].wait_recv()
        self.out_low[:, cols] = (
            self.part[rows_of((1 - yh) * 2 + core, OWN), cols].astype(F32)
            + self.near[0, :, cols].astype(F32)
        ).astype(BF16)
        copy = remote(
            self.out_low.at[:, cols], self.far.at[:, cols], far_send.at[j], far_recv.at[j],
            peer(*FAR),
        )
        copy.start()
        self.far_copies.append(copy)

    def finish(self):
        yh, core, _, _ = place()
        for j in range(NC):
            cols = pl.ds(j * CW, CW)
            self.near_copies[2 * j + 1].wait_recv()
            self.acc[:, cols] = self.part[rows_of(yh * 2 + core, OWN), cols].astype(
                F32
            ) + self.near[1, :, cols].astype(F32)
        for j in range(NC):
            cols = pl.ds(j * CW, CW)
            self.far_copies[j].wait_recv()
            self.acc[:, cols] = self.acc[:, cols] + self.far[:, cols].astype(F32)
        for copy in self.near_copies + self.far_copies:
            copy.wait_send()

    def begin(self, produce):
        for j in range(NC):
            produce(j)
            self.send(j)
            if j > 0:
                self.forward(j - 1)
        self.forward(NC - 1)

    def run(self, produce):
        self.begin(produce)
        self.finish()


class Gather:
    def __init__(self, out, sems):
        self.out, self.sems = out, sems

    def begin(self):
        yh, core, _, _ = place()
        own_send, own_recv, far_send, far_recv, _, _ = self.sems
        mine = rows_of(yh * 2 + core, OWN)
        self.far_copies, self.own_copies, self.on_copies = [], [], []
        for j in range(NC):
            block = self.out.at[mine, pl.ds(j * CW, CW)]
            copy = remote(block, block, far_send.at[j], far_recv.at[j], peer(*FAR))
            copy.start()
            self.far_copies.append(copy)
        for j in range(NC):
            block = self.out.at[mine, pl.ds(j * CW, CW)]
            copy = remote(block, block, own_send.at[j], own_recv.at[j], peer(*CORE))
            copy.start()
            self.own_copies.append(copy)

    def finish(self):
        yh, core, _, _ = place()
        on_send, on_recv = self.sems[4:]
        other = rows_of((1 - yh) * 2 + core, OWN)
        for j in range(NC):
            self.far_copies[j].wait_recv()
            block = self.out.at[other, pl.ds(j * CW, CW)]
            copy = remote(block, block, on_send.at[j], on_recv.at[j], peer(*CORE))
            copy.start()
            self.on_copies.append(copy)
        for copy in self.own_copies + self.on_copies:
            copy.wait_recv()
        for copy in self.far_copies + self.own_copies + self.on_copies:
            copy.wait_send()


def gather_rows(out, sems):
    gather = Gather(out, sems)
    gather.begin()
    gather.finish()


REDUCE_SCRATCH = [
    pltpu.VMEM((2, OWN, D), BF16),
    pltpu.VMEM((OWN, D), BF16),
    pltpu.VMEM((OWN, D), BF16),
    pltpu.VMEM((OWN, D), F32),
    pltpu.SemaphoreType.DMA((2, NC)),
    pltpu.SemaphoreType.DMA((2, NC)),
    pltpu.SemaphoreType.DMA((NC,)),
    pltpu.SemaphoreType.DMA((NC,)),
]
GATHER_SCRATCH = [pltpu.SemaphoreType.DMA((NC,))] * 6


def norm_scale(v):
    return lax.rsqrt(jnp.mean(v * v, axis=1, keepdims=True) + EPS)


def norm_back(v, r, g, dy):
    column_sum = jnp.sum(dy * g * v, axis=1, keepdims=True)
    return r * g * dy - v * (r * r * r) * (column_sum / D)


def input_tile(ref, j):
    return ref[:, pl.ds(pl.multiple_of(j * CW, CW), CW)]


def feed_forward_kernel(r):
    yh, core, _, _ = place()
    t = yh * 2 + core
    greet(FF_PEERS)

    def begin(name, src, dst):
        return FF_MOVES[name].start(src, dst, *r.moves[name])

    loads = [
        pltpu.make_async_copy(r.features.at[rows_of(t, OWN)], r.features_own, r.load_sems.at[0]),
        pltpu.make_async_copy(r.cotangent.at[rows_of(t, OWN)], r.top_own, r.load_sems.at[1]),
        pltpu.make_async_copy(r.w_out, r.out_vmem, r.load_sems.at[2]),
        pltpu.make_async_copy(r.w_gate, r.gate_vmem, r.load_sems.at[3]),
        pltpu.make_async_copy(r.w_up, r.up_vmem, r.load_sems.at[4]),
        pltpu.make_async_copy(r.w_down, r.down_vmem, r.load_sems.at[5]),
    ]
    for load in loads:
        load.start()
    loads[2].wait()

    def attn_part(j):
        r.part[:, j * CW : (j + 1) * CW] = dot(
            r.attended[...], r.out_vmem[:, j * CW : (j + 1) * CW], ((1,), (0,))
        ).astype(BF16)

    Reduce(r.part, *r.reduce).run(attn_part)
    loads[0].wait()
    v = r.reduce[3][...]
    state = r.features_own[...].astype(F32) + v * norm_scale(v) * r.attn_gain[...]
    r.hidden[rows_of(t, OWN), :] = state.astype(BF16)
    r.attn_own[...] = v
    r.hidden_own[...] = state
    features_copies = begin(FF.features_half, r.features, r.features_half)
    attended_copies = begin(FF.attended_all, r.attended, r.attended_all)
    gather_rows(r.hidden, r.gather)
    hidden_copies = begin(FF.hidden_half, r.hidden, r.hidden_half)

    for load in loads[3:]:
        load.wait()

    def hidden_units(j, _):
        cols = pl.ds(pl.multiple_of(j * CW, CW), CW)
        gate = dot(r.hidden[...], r.gate_vmem[:, cols], ((1,), (0,)))
        upward = dot(r.hidden[...], r.up_vmem[:, cols], ((1,), (0,)))
        sigma = jax.nn.sigmoid(gate)
        activated = gate * sigma
        r.mixed[:, cols] = (activated * upward).astype(BF16)
        r.act[:, cols] = activated
        r.slope[:, cols] = upward * sigma * (1.0 + gate * (1.0 - sigma))
        return 0

    lax.fori_loop(0, NC, hidden_units, 0)
    mixed_copies = begin(FF.mixed_right, r.mixed, r.mixed_right)

    def mlp_part(j):
        r.part[:, j * CW : (j + 1) * CW] = dot(
            r.mixed[...], r.down_vmem[:, j * CW : (j + 1) * CW], ((1,), (0,))
        ).astype(BF16)

    Reduce(r.part, *r.reduce).run(mlp_part)
    loads[1].wait()
    v = r.reduce[3][...]
    z = norm_scale(v)
    dy = r.top_own[...].astype(F32)
    g = r.mlp_gain[...]
    r.d_mlp[rows_of(t, OWN), :] = norm_back(v, z, g, dy).astype(BF16)
    r.result_own[...] = (r.hidden_own[...] + v * z * g).astype(BF16)
    mlp_gain_grad = jnp.sum(dy * v * z, axis=0, keepdims=True)
    gather_rows(r.d_mlp, r.gather)
    top_copies = begin(FF.top_half, r.d_mlp, r.top_half)

    def hidden_units_back(j, _):
        cols = pl.ds(pl.multiple_of(j * CW, CW), CW)
        d_mixed = dot(r.d_mlp[...], r.down_vmem[cols, :], ((1,), (1,)))
        r.d_up[:, cols] = (d_mixed * r.act[:, cols]).astype(BF16)
        r.d_gate[:, cols] = (d_mixed * r.slope[:, cols]).astype(BF16)
        return 0

    lax.fori_loop(0, NC, hidden_units_back, 0)
    right_copies = begin(FF.gate_right, r.d_gate, r.gate_right) + begin(FF.up_right, r.d_up, r.up_right)
    wait(features_copies)
    features_copies = begin(FF.features_rest, r.features_half, r.features_rest)

    def back_part(j):
        rows = pl.ds(j * CW, CW)
        r.part[:, j * CW : (j + 1) * CW] = (
            dot(r.d_gate[...], r.gate_vmem[rows, :], ((1,), (1,)))
            + dot(r.d_up[...], r.up_vmem[rows, :], ((1,), (1,)))
        ).astype(BF16)

    Reduce(r.part, *r.reduce).run(back_part)
    wait(hidden_copies)
    hidden_copies = begin(FF.hidden_rest, r.hidden_half, r.hidden_rest)
    dy = r.top_own[...].astype(F32) + r.reduce[3][...]
    v = r.attn_own[...]
    a = norm_scale(v)
    g = r.attn_gain[...]
    r.d_attn[rows_of(t, OWN), :] = norm_back(v, a, g, dy).astype(BF16)
    r.d_hidden_own[...] = dy
    row = lax.broadcasted_iota(jnp.int32, (8, D), 0)
    attn_grad = jnp.sum(dy * v * a, axis=0, keepdims=True)
    r.gain_rows[...] = jnp.where(row == 0, attn_grad, mlp_gain_grad)
    gather_rows(r.d_attn, r.gather)
    r.d_attended[...] = dot(r.d_attn[...], r.out_vmem[...], ((1,), (1,))).astype(BF16)
    wait(right_copies + hidden_copies + features_copies + attended_copies)
    wait(mixed_copies + top_copies)


WIDE = jax.ShapeDtypeStruct((T, D), BF16)
NARROW = jax.ShapeDtypeStruct((T, 4 * HD), BF16)
HALVES = jax.ShapeDtypeStruct((4, T, D // 2), BF16)
FF_MOVES = dict(
    features_half=half_move(WIDE, "x"),
    features_rest=core_move(HALVES),
    attended_all=full_move(NARROW, "z"),
    hidden_half=half_move(WIDE, "z"),
    hidden_rest=core_move(HALVES),
    gate_right=quarter_move(WIDE, "z"),
    up_right=quarter_move(WIDE, "z"),
    mixed_right=quarter_move(WIDE, "x"),
    top_half=half_move(WIDE, "x"),
)
FF = Names(**{name: name for name in FF_MOVES})
FF_PEERS = distinct([CORE, FAR] + peers_of(FF_MOVES))


def feed_forward(small, large):
    weight, wide = pltpu.VMEM((D, D), BF16), pltpu.VMEM((T, D), BF16)
    own, tall = pltpu.VMEM((OWN, D), F32), pltpu.VMEM((T, D), F32)
    own_low = pltpu.VMEM((OWN, D), BF16)
    scratch = dict(
        out_vmem=pltpu.VMEM((4 * HD, D), BF16),
        gate_vmem=weight,
        up_vmem=weight,
        down_vmem=weight,
        features_own=own_low,
        top_own=own_low,
        part=wide,
        hidden=wide,
        act=tall,
        slope=tall,
        d_gate=wide,
        d_up=wide,
        d_mlp=wide,
        mixed=wide,
        attn_own=own,
        hidden_own=own,
        load_sems=pltpu.SemaphoreType.DMA((6,)),
        reduce=REDUCE_SCRATCH,
        gather=GATHER_SCRATCH,
        moves=move_scratch(FF_MOVES),
    )
    outs = dict(
        d_attended=((T, 4 * HD), BF16),
        d_hidden_own=((OWN, D), F32),
        result_own=((OWN, D), BF16),
        gain_rows=((8, D), F32),
        d_attn=((T, D), BF16),
    )
    large_outs = {name: move.out for name, move in FF_MOVES.items()}
    return run_kernel(feed_forward_kernel, 1, small, large, outs, large_outs, scratch, 60)


def row_device(yl, x):
    return {"ctx": yl * 4 + x}


ATTEND_PEERS = [CORE, FAR] + [(0, dy, dx, 0, 0) for dy in range(2) for dx in range(4) if dy or dx]


def tensor_sum(own, near, far, send, recv):
    yh, core, _, _ = place()
    copy = remote(own.at[0], near, send.at[0], recv.at[0], peer(*CORE))
    copy.start()
    copy.wait_recv()
    own[1] = own[0] + near[...]
    again = remote(own.at[1], far, send.at[1], recv.at[1], peer(*FAR))
    again.start()
    again.wait_recv()
    total = own[1] + far[...]
    copy.wait_send()
    again.wait_send()
    return total


def two_columns(first, second):
    lane = lax.broadcasted_iota(jnp.int32, (T, HD), 1)
    return jnp.where(lane < HD // 2, first, second)


class Spread:
    def __init__(self, src, dst, sems):
        self.src, self.dst = src, dst
        self.send, self.recv, self.down_send, self.down_recv = sems

    def row_copy(self, s):
        _, _, yl, x = place()
        h = lax.rem(x + s, 4)
        return remote(
            self.src.at[:, pl.ds(pl.multiple_of(h * HD, HD), HD)],
            self.dst.at[rows_of(yl * 4 + x, T)],
            self.send.at[s],
            self.recv.at[s],
            row_device(yl, h),
        )

    def down_copy(self, s):
        _, _, yl, x = place()
        h = lax.rem(x + s, 4)
        return remote(
            self.src.at[:, pl.ds(pl.multiple_of(h * HD, HD), HD)],
            self.dst.at[rows_of(x, T)],
            self.down_send.at[s],
            self.down_recv.at[s],
            row_device(1, h),
        )


def keep_own(src, dst, block):
    _, _, _, x = place()
    dst[rows_of(block, T), :] = src[:, pl.ds(pl.multiple_of(x * HD, HD), HD)]


def attend_kernel(
    q_raw, k_raw, value, seg, q_gain, k_gain,
    attended, q_head, k_head, v_head, probs_out, scale_out,
    seg_all, q_low, k_low, sums, near, far, result,
    v_sems, k_sems, q_send, q_recv, s_send, s_recv, sum_send, sum_recv, a_send, a_recv,
):
    yh, core, yl, x = place()
    me = yl * 4 + x
    v_sems = [v_sems.at[i] for i in range(4)]
    k_sems = [k_sems.at[i] for i in range(4)]
    values = Spread(value, v_head, v_sems)
    keys = Spread(k_low, k_head, k_sems)

    @pl.when(yl == 0)
    def _():
        for s in range(4):
            values.down_copy(s).start()

    for s in (1, 2, 3):
        values.row_copy(s).start()
    seg_all[me] = jnp.broadcast_to(seg[...].astype(F32), (8, T))

    def seg_copy(s):
        dx, dy = s % 4, s // 4
        to = row_device(lax.rem(yl + dy, 2), lax.rem(x + dx, 4))
        return remote(seg_all.at[me], seg_all.at[me], s_send.at[s], s_recv.at[s], to)

    for s in range(1, 8):
        seg_copy(s).start()

    qr, kr = q_raw[...], k_raw[...]
    sums[0] = two_columns(
        jnp.sum(qr * qr, axis=1, keepdims=True), jnp.sum(kr * kr, axis=1, keepdims=True)
    )
    keep_own(value, v_head, me)
    scales = lax.rsqrt(tensor_sum(sums, near, far, sum_send, sum_recv) / D + EPS)
    scale_out[...] = scales
    k_low[...] = (kr * scales[:, HD // 2 : HD // 2 + 1] * k_gain[...]).astype(BF16)

    @pl.when(yl == 0)
    def _():
        for s in range(4):
            keys.down_copy(s).start()

    for s in (1, 2, 3):
        keys.row_copy(s).start()
    q_low[...] = (qr * scales[:, :1] * q_gain[...]).astype(BF16)

    def q_copy(s):
        h = lax.rem(x + s, 4)
        return remote(
            q_low.at[:, pl.ds(pl.multiple_of(h * HD, HD), HD)],
            q_head.at[rows_of(x, T)],
            q_send.at[s],
            q_recv.at[s],
            row_device(yl, h),
        )

    for s in (1, 2, 3):
        q_copy(s).start()
    keep_own(k_low, k_head, me)
    keep_own(q_low, q_head, x)
    for s in range(1, 8):
        seg_copy(s).wait()
    for s in (1, 2, 3):
        values.row_copy(s).wait()
        keys.row_copy(s).wait()
        q_copy(s).wait()

    @pl.when(yl == 0)
    def _():
        for s in range(4):
            values.down_copy(s).wait_send()
            keys.down_copy(s).wait_send()

    @pl.when(yl == 1)
    def _():
        for s in range(4):
            values.down_copy(s).wait_recv()
            keys.down_copy(s).wait_recv()

    lane = lax.broadcasted_iota(jnp.int32, (8, HD), 0)
    pick = jnp.where(lane == 0, 1.0, 0.0)

    def attend(row, i):
        blocks = row * 4 + i + 1
        width = blocks * T
        q = q_head[i * T : (i + 1) * T, :]
        scores = dot(q, k_head[:width, :], ((1,), (1,))) * HD ** (-0.5)
        own_seg = dot(seg_all[row * 4 + i], pick, ((0,), (0,)))[:, :1]
        seg_keys = jnp.concatenate([seg_all[b, :1, :] for b in range(blocks)], axis=1)
        q_place = lax.broadcasted_iota(jnp.int32, (T, width), 0) + (blocks - 1) * T
        k_place = lax.broadcasted_iota(jnp.int32, (T, width), 1)
        counted = (k_place <= q_place) & (seg_keys == own_seg)
        scores = jnp.where(counted, scores, -1e30)
        exps = jnp.exp(scores - jnp.max(scores, axis=1, keepdims=True))
        probs = (exps * (1.0 / jnp.sum(exps, axis=1, keepdims=True))).astype(BF16)
        probs_out[i, :, :width] = probs
        result[i] = dot(probs, v_head[:width, :], ((1,), (0,))).astype(BF16)

    def back_copy(i):
        return remote(
            result.at[i],
            attended.at[:, pl.ds(pl.multiple_of(x * HD, HD), HD)],
            a_send.at[i],
            a_recv.at[x],
            row_device(yl, i),
        )

    for i in range(4):
        for row in range(2):

            @pl.when(yl == row)
            def _():
                attend(row, i)

        @pl.when(x == i)
        def _():
            attended[:, i * HD : (i + 1) * HD] = result[i]

        @pl.when(x != i)
        def _():
            back_copy(i).start()

    for h in range(4):

        @pl.when(x != h)
        def _():
            back_copy(h).wait_send()
            remote(
                result.at[h],
                attended.at[:, h * HD : (h + 1) * HD],
                a_send.at[h],
                a_recv.at[h],
                row_device(yl, h),
            ).wait_recv()


def attend(small):
    dma = pltpu.SemaphoreType.DMA
    outs = dict(
        attended=((T, 4 * HD), BF16),
        q_head=((4 * T, HD), BF16),
        k_head=((8 * T, HD), BF16),
        v_head=((8 * T, HD), BF16),
        probs=((4, T, 8 * T), BF16),
        scales=((T, HD), F32),
    )
    scratch = dict(
        own=[
            pltpu.VMEM((8, 8, T), F32),
            pltpu.VMEM((T, 4 * HD), BF16),
            pltpu.VMEM((T, 4 * HD), BF16),
            pltpu.VMEM((2, T, HD), F32),
            pltpu.VMEM((T, HD), F32),
            pltpu.VMEM((T, HD), F32),
            pltpu.VMEM((4, T, HD), BF16),
            dma((4, 4)),
            dma((4, 4)),
            dma((4,)),
            dma((4,)),
            dma((8,)),
            dma((8,)),
            dma((2,)),
            dma((2,)),
            dma((4,)),
            dma((4,)),
        ]
    )
    return run_kernel(attend_body, 5, small, {}, outs, {}, scratch, 40)


def attend_body(r):
    greet(ATTEND_PEERS)
    attend_kernel(
        r.q_raw, r.k_raw, r.value, r.seg, r.q_gain, r.k_gain,
        r.attended, r.q_head, r.k_head, r.v_head, r.probs, r.scales, *r.own,
    )


def product_rows(left, right):
    return dot(
        left.reshape(4 * T, left.shape[2]), right.reshape(4 * T, right.shape[2]), ((0,), (0,))
    ).astype(BF16)


def blocks_out(partial, slots, send, recv, axis, piece=None):
    me = spot(axis)
    made = []
    for s in (1, 2, 3):
        source, target = partial.at[lax.rem(me + s, 4)], slots.at[s - 1]
        send_sem, recv_sem = send.at[s - 1], recv.at[s - 1]
        if piece is not None:
            source, target = source.at[:, piece], target.at[:, piece]
            send_sem, recv_sem = send.at[s - 1, piece], recv.at[s - 1, piece]
        made.append(remote(source, target, send_sem, recv_sem, peer(*along(axis, s))))
    return made


def add_blocks(total, partial, slots, axis):
    me = spot(axis)
    for y in range(2):
        for j in range(4):
            block = partial[me, y, j].astype(F32)
            for s in range(3):
                block += slots[s, y, j].astype(F32)
            total[y, j] = block.astype(BF16)


HALF_GRID = (2, 4, 64)
BACK_MOVES = dict(
    attn_left=quarter_move(WIDE, "z"),
    q_right=quarter_move(NARROW, "x"),
    k_right=quarter_move(NARROW, "x"),
    v_right=quarter_move(NARROW, "x"),
    mlp_in=final_move(jax.ShapeDtypeStruct(HALF_GRID + (1024,), BF16), "z"),
    mlp_down=final_move(jax.ShapeDtypeStruct(HALF_GRID + (512,), BF16), "x"),
    qkv=final_move(jax.ShapeDtypeStruct(HALF_GRID + (384,), BF16), "x"),
    out=final_move(jax.ShapeDtypeStruct(HALF_GRID + (512,), BF16), "x"),
    tiles=rank_move(jax.ShapeDtypeStruct((32, 16, HD), F32)),
)
BACK = Names(**{name: name for name in BACK_MOVES})
BACK_PEERS = distinct(ATTEND_PEERS + peers_of(BACK_MOVES))


def back_scratch():
    dma = pltpu.SemaphoreType.DMA

    def vmem(*shape, kind=BF16):
        return pltpu.VMEM(shape, kind)

    rows = (2, 4, 64)
    return dict(
        q_head=vmem(4 * T, HD),
        k_head=vmem(8 * T, HD),
        v_head=vmem(8 * T, HD),
        probs=vmem(2, T, 8 * T),
        q_raw=vmem(T, 4 * HD, kind=F32),
        k_raw=vmem(T, 4 * HD, kind=F32),
        scales=vmem(T, HD, kind=F32),
        wq=vmem(D, 4 * HD),
        wk=vmem(D, 4 * HD),
        wv=vmem(D, 4 * HD),
        left=vmem(2, 4, T, D // 2),
        top=vmem(2, 4, T, D // 2),
        gate_right=vmem(4, T, 512),
        up_right=vmem(4, T, 512),
        mixed_right=vmem(4, T, 512),
        attn_left=vmem(4, T, 512),
        attended_all=vmem(4, T, 512),
        q_right=vmem(4, T, HD),
        k_right=vmem(4, T, HD),
        v_right=vmem(4, T, HD),
        in_part=vmem(4, *rows, 1024),
        in_slots=vmem(3, *rows, 1024),
        in_sum=vmem(*rows, 1024),
        down_part=vmem(4, *rows, 512),
        down_slots=vmem(3, *rows, 512),
        down_sum=vmem(*rows, 512),
        qkv_part=vmem(4, *rows, 384),
        qkv_slots=vmem(3, *rows, 384),
        qkv_sum=vmem(*rows, 384),
        out_part=vmem(*rows, 512),
        tile_part=vmem(32, 16, HD, kind=F32),
        d_q=vmem(T, 4 * HD),
        d_k=vmem(T, 4 * HD),
        d_v=vmem(T, 4 * HD),
        part=vmem(T, D),
        d_out=vmem(4 * T, HD),
        dq_buf=vmem(4, T, HD),
        dk_buf=vmem(8, T, HD),
        dv_buf=vmem(8, T, HD),
        dk_acc=vmem(8 * T, HD, kind=F32),
        dv_acc=vmem(8 * T, HD, kind=F32),
        dq_got=vmem(4, T, HD),
        dk_got=vmem(2, 4, T, HD),
        dv_got=vmem(2, 4, T, HD),
        sums=vmem(2, T, HD, kind=F32),
        near=vmem(T, HD, kind=F32),
        far=vmem(T, HD, kind=F32),
        gain_near=vmem(8, D, kind=F32),
        gain_far=vmem(8, D, kind=F32),
        gain_sum=vmem(8, D, kind=F32),
        load_sems=dma((32,)),
        in_send=dma((3, 4)),
        in_recv=dma((3, 4)),
        down_send=dma((3,)),
        down_recv=dma((3,)),
        qkv_send=dma((3,)),
        qkv_recv=dma((3,)),
        o_send=dma((4,)),
        o_recv=dma((4,)),
        dq_send=dma((4,)),
        dq_recv=dma((4,)),
        dk_send=dma((8,)),
        dk_recv=dma((2, 4)),
        dv_send=dma((8,)),
        dv_recv=dma((2, 4)),
        sum_send=dma((2,)),
        sum_recv=dma((2,)),
        gain_send=dma((2,)),
        gain_recv=dma((2,)),
        top_send=dma((1,)),
        top_recv=dma((1,)),
        result_send=dma((3,)),
        result_recv=dma((3,)),
        reduce=REDUCE_SCRATCH,
        gather=GATHER_SCRATCH,
        moves=move_scratch(BACK_MOVES),
    )


def backward_kernel(r):
    yh, core, yl, x = place()
    t = yh * 2 + core
    scale = HD ** (-0.5)
    greet(BACK_PEERS)

    def begin(name, src, dst):
        return BACK_MOVES[name].start(src, dst, *r.moves[name])

    load_count = iter(range(32))

    def load(src, dst):
        copy = pltpu.make_async_copy(src, dst, r.load_sems.at[next(load_count)])
        copy.start()
        return copy

    def o_copy(s):
        h = lax.rem(x + s, 4)
        return remote(
            r.d_attended.at[:, pl.ds(pl.multiple_of(h * HD, HD), HD)],
            r.d_out.at[rows_of(x, T)],
            r.o_send.at[s],
            r.o_recv.at[s],
            row_device(yl, h),
        )

    for s in (1, 2, 3):
        o_copy(s).start()
    hidden0_load = load(r.hidden_half, r.left.at[core])
    gate_right_load = load(r.gate_right_in, r.gate_right)
    up_right_load = load(r.up_right_in, r.up_right)
    hidden1_load = load(r.hidden_rest, r.left.at[1 - core])
    q_head_load = load(r.q_head_in, r.q_head)
    k_head_load = load(r.k_head_in, r.k_head)
    v_head_load = load(r.v_head_in, r.v_head)
    probs_loads = [load(r.probs_in.at[i], r.probs.at[i]) for i in range(2)]
    q_raw_load = load(r.q_raw_in, r.q_raw)
    k_raw_load = load(r.k_raw_in, r.k_raw)
    scales_load = load(r.scales_in, r.scales)
    mixed_right_load = load(r.mixed_right_in, r.mixed_right)
    top_load = load(r.top_half, r.top.at[core])
    attended_all_load = load(r.attended_all_in, r.attended_all)
    w_query_load = load(r.w_query, r.wq)
    w_key_load = load(r.w_key, r.wk)
    w_value_load = load(r.w_value, r.wv)
    gain_near_copy = remote(
        r.gains, r.gain_near, r.gain_send.at[0], r.gain_recv.at[0], peer(*CORE)
    )
    gain_near_copy.start()
    top_copy = remote(
        r.top_half, r.top.at[core], r.top_send.at[0], r.top_recv.at[0], peer(*CORE)
    )
    top_copy.start()
    mine, other = rows_of(t, OWN), rows_of((1 - yh) * 2 + core, OWN)
    result_load = load(r.result_own, r.outputs.at[mine])
    result_copies = [
        remote(
            r.result_own, r.outputs.at[mine], r.result_send.at[n], r.result_recv.at[n], to
        )
        for n, to in enumerate((peer(*FAR), peer(*CORE)))
    ]
    for copy in result_copies:
        copy.start()
    attn_left = begin(BACK.attn_left, r.d_attn, r.attn_left)
    keep_own(r.d_attended, r.d_out, x)
    r.dk_acc[...] = jnp.zeros_like(r.dk_acc)
    r.dv_acc[...] = jnp.zeros_like(r.dv_acc)

    wait([hidden0_load, gate_right_load, up_right_load, hidden1_load])
    in_copies = []

    def in_piece(piece):
        copies = blocks_out(r.in_part, r.in_slots, r.in_send, r.in_recv, "x", piece)
        for copy in copies:
            copy.start()
        in_copies.extend(copies)

    for i in range(4):
        left = r.left[i // 2, :, :, (i % 2) * 512 : (i % 2 + 1) * 512]
        for n, right in enumerate((r.gate_right, r.up_right)):
            got = product_rows(left, right[...])
            for y in range(2):
                for j in range(4):
                    r.in_part[j, y, i, :, n * 512 : (n + 1) * 512] = got[
                        (y * 4 + j) * 64 : (y * 4 + j + 1) * 64
                    ]
        if i < 2:
            in_piece(i)
    features0_load = load(r.features_half, r.left.at[core])
    features1_load = load(r.features_rest, r.left.at[1 - core])
    gain_near_copy.wait()
    r.gain_sum[...] = r.gains[...] + r.gain_near[...]
    gain_far_copy = remote(
        r.gain_sum, r.gain_far, r.gain_send.at[1], r.gain_recv.at[1], peer(*FAR)
    )
    gain_far_copy.start()

    for s in (1, 2, 3):
        o_copy(s).wait()
    wait([q_head_load, k_head_load, v_head_load])

    def back(row, i):
        width = (row * 4 + i + 1) * T
        q = r.q_head[i * T : (i + 1) * T, :]
        do = r.d_out[i * T : (i + 1) * T, :]
        probs_low = r.probs[i % 2, :, :width]
        probs = probs_low.astype(F32)
        d_probs = dot(do, r.v_head[:width, :], ((1,), (1,)))
        delta = jnp.sum(probs * d_probs, axis=1, keepdims=True)
        d_scores = (probs * (d_probs - delta)).astype(BF16)
        r.dq_buf[i] = (dot(d_scores, r.k_head[:width, :], ((1,), (0,))) * scale).astype(BF16)
        r.dk_acc[:width, :] += dot(d_scores, q, ((0,), (0,)))
        r.dv_acc[:width, :] += dot(probs_low, do, ((0,), (0,)))

    def dq_copy(i):
        return remote(
            r.dq_buf.at[i], r.dq_got.at[x], r.dq_send.at[i], r.dq_recv.at[x], row_device(yl, i)
        )

    for i in range(4):
        probs_loads[i].wait()
        for row in range(2):

            @pl.when(yl == row)
            def _():
                back(row, i)

        if i < 2:
            probs_loads.append(load(r.probs_in.at[i + 2], r.probs.at[i]))

        @pl.when(x == i)
        def _():
            r.dq_got[i] = r.dq_buf[i]

        @pl.when(x != i)
        def _():
            dq_copy(i).start()

    def kv_copy(j, buf, got, send, recv):
        return remote(
            buf.at[j], got.at[yl, x], send.at[j], recv.at[yl, x], row_device(j // 4, j % 4)
        )

    dk_args = (r.dk_buf, r.dk_got, r.dk_send, r.dk_recv)
    dv_args = (r.dv_buf, r.dv_got, r.dv_send, r.dv_recv)
    for j in range(8):
        r.dk_buf[j] = (r.dk_acc[j * T : (j + 1) * T, :] * scale).astype(BF16)
        r.dv_buf[j] = r.dv_acc[j * T : (j + 1) * T, :].astype(BF16)
        here = (yl == j // 4) & (x == j % 4)

        @pl.when(here)
        def _():
            r.dk_got[j // 4, j % 4] = r.dk_buf[j]
            r.dv_got[j // 4, j % 4] = r.dv_buf[j]

        sends = (yl >= j // 4) & ~here

        @pl.when(sends)
        def _():
            kv_copy(j, *dk_args).start()
            kv_copy(j, *dv_args).start()

    in_piece(2)
    in_piece(3)

    result_copies[0].wait_recv()
    result_copies.append(
        remote(
            r.outputs.at[other],
            r.outputs.at[other],
            r.result_send.at[2],
            r.result_recv.at[2],
            peer(*CORE),
        )
    )
    result_copies[2].start()

    mixed_right_load.wait()
    top_load.wait()
    top_copy.wait()
    for i in range(4):
        left = r.top[i // 2, :, :, (i % 2) * 512 : (i % 2 + 1) * 512]
        r.down_part[i] = product_rows(left, r.mixed_right[...]).reshape(2, 4, 64, 512)
    down_copies = blocks_out(r.down_part, r.down_slots, r.down_send, r.down_recv, "z")
    for copy in down_copies:
        copy.start()
    attended_all_load.wait()
    wait(attn_left)
    r.out_part[...] = product_rows(r.attn_left[...], r.attended_all[...]).reshape(2, 4, 64, 512)

    for h in range(4):

        @pl.when(x != h)
        def _():
            dq_copy(h).wait_send()
            remote(
                r.dq_buf.at[h], r.dq_got.at[h], r.dq_send.at[h], r.dq_recv.at[h],
                row_device(yl, h),
            ).wait_recv()

        for row in range(2):
            comes = (row >= yl) & ~((yl == row) & (x == h))

            @pl.when(comes)
            def _():
                for buf, got, send, recv in (dk_args, dv_args):
                    remote(
                        buf.at[0],
                        got.at[row, h],
                        send.at[0],
                        recv.at[row, h],
                        row_device(row, h),
                    ).wait_recv()

    for j in range(8):
        here = (yl == j // 4) & (x == j % 4)
        sends = (yl >= j // 4) & ~here

        @pl.when(sends)
        def _():
            kv_copy(j, *dk_args).wait_send()
            kv_copy(j, *dv_args).wait_send()

    @pl.when(yl == 1)
    def _():
        for h in range(4):
            r.dk_got[0, h] = jnp.zeros((T, HD), BF16)
            r.dv_got[0, h] = jnp.zeros((T, HD), BF16)

    wait([q_raw_load, k_raw_load, scales_load])
    q_sum = jnp.zeros((T, 1), F32)
    k_sum = jnp.zeros((T, 1), F32)
    for h in range(4):
        cols = slice(h * HD, (h + 1) * HD)
        dq = r.dq_got[h].astype(F32)
        dk = r.dk_got[0, h].astype(F32) + r.dk_got[1, h].astype(F32)
        r.d_v[:, cols] = (r.dv_got[0, h].astype(F32) + r.dv_got[1, h].astype(F32)).astype(BF16)
        q_sum += jnp.sum(dq * r.q_raw[:, cols] * r.q_gain[:, cols], axis=1, keepdims=True)
        k_sum += jnp.sum(dk * r.k_raw[:, cols] * r.k_gain[:, cols], axis=1, keepdims=True)
    r.sums[0] = two_columns(q_sum, k_sum)
    v_copies = begin(BACK.v_right, r.d_v, r.v_right)
    total = tensor_sum(r.sums, r.near, r.far, r.sum_send, r.sum_recv)
    qs, ks = r.scales[:, :1], r.scales[:, HD // 2 : HD // 2 + 1]
    q_coef = qs * qs * qs * (total[:, :1] / D)
    k_coef = ks * ks * ks * (total[:, HD // 2 : HD // 2 + 1] / D)
    gain_far_copy.wait()
    both = r.gain_sum[...] + r.gain_far[...]
    tile = []
    for h in range(4):
        cols = slice(h * HD, (h + 1) * HD)
        dq = r.dq_got[h].astype(F32)
        dk = r.dk_got[0, h].astype(F32) + r.dk_got[1, h].astype(F32)
        qr, kr = r.q_raw[:, cols], r.k_raw[:, cols]
        r.d_q[:, cols] = (qs * r.q_gain[:, cols] * dq - qr * q_coef).astype(BF16)
        r.d_k[:, cols] = (ks * r.k_gain[:, cols] * dk - kr * k_coef).astype(BF16)
        tile.append((jnp.sum(dq * qr * qs, axis=0, keepdims=True), jnp.sum(dk * kr * ks, axis=0, keepdims=True)))
    qk_copies = begin(BACK.q_right, r.d_q, r.q_right) + begin(BACK.k_right, r.d_k, r.k_right)
    row = lax.broadcasted_iota(jnp.int32, (8, HD), 0)
    top_tile = jnp.zeros((8, HD), F32)
    for h in range(4):
        top_tile = jnp.where(row == h, tile[h][0], top_tile)
        top_tile = jnp.where(row == h + 4, tile[h][1], top_tile)
    for rank in range(32):
        r.tile_part[rank, :8] = top_tile
        r.tile_part[rank, 8:] = both[:, (rank // 2) * HD : (rank // 2 + 1) * HD]
    tile_copies = begin(BACK.tiles, r.tile_part, r.tiles)

    wait([w_query_load, w_key_load, w_value_load])

    def input_part(j):
        rows = pl.ds(j * CW, CW)
        r.part[:, j * CW : (j + 1) * CW] = (
            dot(r.d_q[...], r.wq[rows, :], ((1,), (1,)))
            + dot(r.d_k[...], r.wk[rows, :], ((1,), (1,)))
            + dot(r.d_v[...], r.wv[rows, :], ((1,), (1,)))
        ).astype(BF16)

    reduce = Reduce(r.part, *r.reduce)
    reduce.begin(input_part)
    out_copies = begin(BACK.out, r.out_part, r.out)
    wait(v_copies + qk_copies)
    features0_load.wait()
    features1_load.wait()
    for i in range(4):
        left = r.left[i // 2, :, :, (i % 2) * 512 : (i % 2 + 1) * 512]
        for n, right in enumerate((r.q_right, r.k_right, r.v_right)):
            r.qkv_part[i, :, :, :, n * HD : (n + 1) * HD] = product_rows(left, right[...]).reshape(
                2, 4, 64, HD
            )
    qkv_copies = blocks_out(r.qkv_part, r.qkv_slots, r.qkv_send, r.qkv_recv, "z")
    for copy in qkv_copies:
        copy.start()
    reduce.finish()
    r.input_grad[mine, :] = (r.d_hidden_own[...] + r.reduce[3][...]).astype(BF16)
    gather = Gather(r.input_grad, r.gather)
    gather.begin()

    wait(down_copies)
    add_blocks(r.down_sum, r.down_part, r.down_slots, "z")
    down_final = begin(BACK.mlp_down, r.down_sum, r.mlp_down)
    wait(in_copies)
    add_blocks(r.in_sum, r.in_part, r.in_slots, "x")
    in_final = begin(BACK.mlp_in, r.in_sum, r.mlp_in)
    gather.finish()
    wait(qkv_copies)
    add_blocks(r.qkv_sum, r.qkv_part, r.qkv_slots, "z")
    qkv_final = begin(BACK.qkv, r.qkv_sum, r.qkv)
    result_load.wait()
    result_copies[0].wait_send()
    result_copies[1].wait()
    result_copies[2].wait()
    wait(tile_copies + out_copies + down_final + in_final + qkv_final)


def backward(small, large):
    large_outs = dict(
        outputs=((T, D), BF16),
        tiles=((32, 16, HD), F32),
        mlp_in=(HALF_GRID + (1024,), BF16),
        mlp_down=(HALF_GRID + (512,), BF16),
        qkv=(HALF_GRID + (384,), BF16),
        out=(HALF_GRID + (512,), BF16),
    )
    outs = dict(input_grad=((T, D), BF16))
    return run_kernel(backward_kernel, 6, small, large, outs, large_outs, back_scratch(), 62)


def add_up(blocks):
    return jnp.sum(blocks.astype(F32), axis=0)


def rows_out(final):
    return add_up(final).transpose(1, 0, 2)


def per_device(
    inputs, segments, w_query, w_key, w_value, w_out, q_gain, k_gain, attn_gain,
    w_gate, w_up, w_down, mlp_gain, cotangent,
):
    features, top = inputs[0], cotangent[0]
    q_row, k_row = q_gain.reshape(1, -1), k_gain.reshape(1, -1)
    a_row, m_row = attn_gain.reshape(1, -1), mlp_gain.reshape(1, -1)

    def matmul(a, w):
        return jnp.dot(a, w, preferred_element_type=F32)

    def matmul_t(a, w):
        return lax.dot_general(a, w, (((1,), (1,)), ((), ())), preferred_element_type=F32)

    q_raw = matmul(features, w_query)
    k_raw = matmul(features, w_key)
    value = matmul(features, w_value).astype(BF16)
    att = attend(
        dict(q_raw=q_raw, k_raw=k_raw, value=value, seg=segments, q_gain=q_row, k_gain=k_row)
    )
    ff = feed_forward(
        dict(attended=att.attended, attn_gain=a_row, mlp_gain=m_row),
        dict(
            features=features, cotangent=top, w_out=w_out, w_gate=w_gate, w_up=w_up, w_down=w_down
        ),
    )
    got = backward(
        dict(
            d_attended=ff.d_attended, q_gain=q_row, k_gain=k_row, gains=ff.gain_rows,
            d_hidden_own=ff.d_hidden_own, result_own=ff.result_own,
        ),
        dict(
            q_head_in=att.q_head, k_head_in=att.k_head, v_head_in=att.v_head, probs_in=att.probs,
            q_raw_in=q_raw, k_raw_in=k_raw, scales_in=att.scales,
            w_query=w_query, w_key=w_key, w_value=w_value,
            hidden_half=ff.hidden_half, hidden_rest=ff.hidden_rest, gate_right_in=ff.gate_right,
            up_right_in=ff.up_right, top_half=ff.top_half, mixed_right_in=ff.mixed_right,
            features_half=ff.features_half, features_rest=ff.features_rest,
            attended_all_in=ff.attended_all, d_attn=ff.d_attn,
        ),
    )
    gains = add_up(got.tiles)
    rank = lax.axis_index("dp") * 8 + lax.axis_index("ctx")
    heads = lax.dynamic_slice_in_dim(gains[:8], rank * 4, 4, 1)
    columns = lax.dynamic_slice_in_dim(gains[8:10], lax.rem(rank, 2) * 64, 64, 1)
    qkv, mlp_in, mlp_down = rows_out(got.qkv), rows_out(got.mlp_in), rows_out(got.mlp_down)
    out_grad = add_up(got.out.reshape(8, 64, 512))

    def joined(block):
        return block.reshape(64, -1)

    return (
        got.outputs[None],
        got.input_grad[None],
        joined(qkv[:, :, :128]),
        joined(qkv[:, :, 128:256]),
        joined(qkv[:, :, 256:]),
        out_grad.T,
        heads[:4],
        heads[4:],
        columns[0],
        joined(mlp_in[:, :, :512]),
        joined(mlp_in[:, :, 512:]),
        joined(mlp_down).T,
        columns[1],
    )


def solution(mesh):
    rows, full = P("dp", "ctx", None), P()
    down, across = P("tensor", None), P(None, "tensor")
    in_specs = (
        rows, P("dp", "ctx"), across, across, across, down, down, down, full,
        across, across, down, full, rows,
    )
    split = ("dp", "ctx")
    out_specs = (
        rows, rows, P(split, "tensor"), P(split, "tensor"), P(split, "tensor"), P("tensor", split),
        P("tensor", split), P("tensor", split), P(split), P(split, "tensor"), P(split, "tensor"),
        P("tensor", split), P(split),
    )
    return jax.shard_map(
        per_device, mesh=mesh, in_specs=in_specs, out_specs=out_specs, check_vma=False
    )
```

```python
import functools
import jax
import jax.numpy as jnp
from jax import lax
from jax.experimental import pallas as pl
from jax.experimental.pallas import tpu as pltpu
from jax.sharding import PartitionSpec as P

MESH = pl.DeviceIdType.MESH
F32 = jnp.float32
BF16 = jnp.bfloat16
EPS = 1e-06
T = 256
D = 2048
HD = 128
OWN = 64
NC = 4
CW = D // NC
VMEM = pl.BlockSpec(memory_space=pltpu.VMEM)
ANY = pl.BlockSpec(memory_space=pltpu.HBM)


def place():
    t = lax.axis_index("tensor")
    ctx = lax.axis_index("ctx")
    return t // 2, lax.rem(t, 2), ctx // 4, lax.rem(ctx, 4)


def peer(dz=0, dy=0, dx=0, dh=0, dc=0):
    yh, core, yl, x = place()
    z = lax.rem(lax.axis_index("dp") + dz, 4)
    ctx = lax.rem(yl + dy, 2) * 4 + lax.rem(x + dx, 4)
    return {"dp": z, "ctx": ctx, "tensor": lax.rem(yh + dh, 2) * 2 + lax.rem(core + dc, 2)}


CORE, FAR = (0, 0, 0, 0, 1), (0, 0, 0, 1, 0)


def along(axis, s):
    return (s, 0, 0, 0, 0) if axis == "z" else (0, 0, s, 0, 0)


def spot(axis):
    return lax.axis_index("dp") if axis == "z" else place()[3]


def remote(src, dst, send_sem, recv_sem, device):
    return pltpu.make_async_remote_copy(
        src_ref=src,
        dst_ref=dst,
        send_sem=send_sem,
        recv_sem=recv_sem,
        device_id=device,
        device_id_type=MESH,
    )


def greet(offsets):
    barrier = pltpu.get_barrier_semaphore()
    for offset in offsets:
        pl.semaphore_signal(barrier, inc=1, device_id=peer(*offset), device_id_type=MESH)


def greeted(offsets):
    pl.semaphore_wait(pltpu.get_barrier_semaphore(), len(offsets))


def wait(copies):
    for copy in copies:
        copy.wait()


def dot(a, b, dims):
    return lax.dot_general(a, b, (dims, ((), ())), preferred_element_type=F32)


def rows_of(index, count):
    return pl.ds(pl.multiple_of(index * count, count), count)


class Move:
    def __init__(self, source, shape, offsets, pairs):
        self.source, self.shape, self.offsets, self.pairs = source, shape, offsets, pairs
        self.out = (shape, source.dtype)

    def scratch(self):
        dma = pltpu.SemaphoreType.DMA
        return [dma((len(self.offsets),)), dma((len(self.offsets),)), dma((1,))]

    def copies(self, src, dst, send, recv, local):
        made = []
        at = 0
        for a, b, offset in self.pairs(src, dst):
            if offset is None:
                made.append(pltpu.make_async_copy(a, b, local.at[0]))
            else:
                made.append(remote(a, b, send.at[at], recv.at[at], peer(*offset)))
                at += 1
        return made

    def start(self, src, dst, *sems):
        copies = self.copies(src, dst, *sems)
        for copy in copies:
            copy.start()
        return copies


def half_move(a, axis):
    half = a.shape[1] // 2
    offsets = [along(axis, s) for s in (1, 2, 3)]

    def pairs(src, dst):
        mine = src.at[:, pl.ds(pl.multiple_of(place()[1] * half, half), half)]
        me = spot(axis)
        return [(mine, dst.at[me], offset) for offset in offsets + [None]]

    return Move(a, (4, T, half), offsets, pairs)


def core_move(a):
    return Move(a, a.shape, [CORE], lambda src, dst: [(src, dst, CORE)])


def quarter_move(b, axis):
    width = b.shape[1] // 4
    offsets = [along(axis, s) for s in (1, 2, 3)]

    def pairs(src, dst):
        me = spot(axis)

        def part(s):
            return src.at[:, pl.ds(pl.multiple_of(lax.rem(me + s, 4) * width, width), width)]

        made = [(part(s), dst.at[me], along(axis, s)) for s in (1, 2, 3)]
        return made + [(part(0), dst.at[me], None)]

    return Move(b, (4, T, width), offsets, pairs)


def full_move(b, axis):
    offsets = [along(axis, s) for s in (1, 2, 3)]

    def pairs(src, dst):
        return [(src, dst.at[spot(axis)], offset) for offset in offsets + [None]]

    return Move(b, (4,) + b.shape, offsets, pairs)


def block_move(p, axis):
    offsets = [along(axis, s) for s in (1, 2, 3)]

    def pairs(src, dst):
        me = spot(axis)
        made = [(src.at[lax.rem(me + s, 4)], dst.at[me], along(axis, s)) for s in (1, 2, 3)]
        return made + [(src.at[me], dst.at[me], None)]

    return Move(p, p.shape, offsets, pairs)


def final_move(p, axis):
    steps = [(dy, s) for dy in range(2) for s in range(4) if dy or s]

    def offset(dy, s):
        return (s, dy, 0, 0, 0) if axis == "z" else (0, dy, s, 0, 0)

    def pairs(src, dst):
        yl, me = place()[2], spot(axis)
        made = [
            (src.at[lax.rem(yl + dy, 2), lax.rem(me + s, 4)], dst.at[yl, me], offset(dy, s))
            for dy, s in steps
        ]
        return made + [(src.at[yl, me], dst.at[yl, me], None)]

    return Move(p, p.shape, [offset(*step) for step in steps], pairs)


def rank_move(p):
    steps = [(dz, dy, dx, 0, 0) for dz in range(4) for dy in range(2) for dx in range(4)][1:]

    def pairs(src, dst):
        _, _, yl, x = place()
        z = lax.axis_index("dp")
        me = z * 8 + yl * 4 + x

        def rank(dz, dy, dx, *_):
            return lax.rem(z + dz, 4) * 8 + lax.rem(yl + dy, 2) * 4 + lax.rem(x + dx, 4)

        made = [(src.at[rank(*step)], dst.at[me], step) for step in steps]
        return made + [(src.at[me], dst.at[me], None)]

    return Move(p, p.shape, steps, pairs)


class Names:
    def __init__(self, **names):
        self.__dict__.update(names)


def run_kernel(body, collective_id, small, large, small_outs, large_outs, scratch, vmem):
    ins = [jax.tree.flatten(small), jax.tree.flatten(large)]
    shapes = [
        jax.tree.flatten({name: jax.ShapeDtypeStruct(*out) for name, out in outs.items()})
        for outs in (small_outs, large_outs)
    ]
    own = jax.tree.flatten(scratch)

    def kernel(*refs):
        names, at = {}, 0
        for leaves, tree in ins + shapes + [own]:
            names.update(tree.unflatten(refs[at : at + len(leaves)]))
            at += len(leaves)
        body(Names(**names))

    got = pl.pallas_call(
        kernel,
        name=body.__name__,
        out_shape=shapes[0][0] + shapes[1][0],
        in_specs=[VMEM] * len(ins[0][0]) + [ANY] * len(ins[1][0]),
        out_specs=[VMEM] * len(shapes[0][0]) + [ANY] * len(shapes[1][0]),
        scratch_shapes=own[0],
        compiler_params=pltpu.CompilerParams(
            collective_id=collective_id, has_side_effects=True, vmem_limit_bytes=vmem * 2**20
        ),
    )(*ins[0][0], *ins[1][0])
    n = len(shapes[0][0])
    return Names(**shapes[0][1].unflatten(got[:n]), **shapes[1][1].unflatten(got[n:]))


def move_scratch(moves):
    return {name: move.scratch() for name, move in moves.items()}


def peers_of(moves):
    return [offset for move in moves.values() for offset in move.offsets]


def distinct(offsets):
    return list(dict.fromkeys(offsets))


class Reduce:
    def __init__(self, part, near, far, out_low, acc, *sems):
        self.part, self.near, self.far, self.out_low, self.acc = part, near, far, out_low, acc
        self.sems = sems
        self.near_copies, self.far_copies = [], []

    def send(self, j):
        yh, core, _, _ = place()
        near_send, near_recv, _, _ = self.sems
        cols = pl.ds(j * CW, CW)
        for slot, row in ((0, (1 - yh) * 2 + (1 - core)), (1, yh * 2 + (1 - core))):
            copy = remote(
                self.part.at[rows_of(row, OWN), cols],
                self.near.at[slot, :, cols],
                near_send.at[slot, j],
                near_recv.at[slot, j],
                peer(*CORE),
            )
            copy.start()
            self.near_copies.append(copy)

    def forward(self, j):
        yh, core, _, _ = place()
        _, _, far_send, far_recv = self.sems
        cols = pl.ds(j * CW, CW)
        self.near_copies[2 * j].wait_recv()
        self.out_low[:, cols] = (
            self.part[rows_of((1 - yh) * 2 + core, OWN), cols].astype(F32)
            + self.near[0, :, cols].astype(F32)
        ).astype(BF16)
        copy = remote(
            self.out_low.at[:, cols], self.far.at[:, cols], far_send.at[j], far_recv.at[j],
            peer(*FAR),
        )
        copy.start()
        self.far_copies.append(copy)

    def finish(self):
        yh, core, _, _ = place()
        for j in range(NC):
            cols = pl.ds(j * CW, CW)
            self.near_copies[2 * j + 1].wait_recv()
            self.acc[:, cols] = self.part[rows_of(yh * 2 + core, OWN), cols].astype(
                F32
            ) + self.near[1, :, cols].astype(F32)
        for j in range(NC):
            cols = pl.ds(j * CW, CW)
            self.far_copies[j].wait_recv()
            self.acc[:, cols] = self.acc[:, cols] + self.far[:, cols].astype(F32)
        for copy in self.near_copies + self.far_copies:
            copy.wait_send()

    def begin(self, produce):
        for j in range(NC):
            produce(j)
            self.send(j)
            if j > 0:
                self.forward(j - 1)
        self.forward(NC - 1)

    def run(self, produce):
        self.begin(produce)
        self.finish()


class Gather:
    def __init__(self, out, sems):
        self.out, self.sems = out, sems

    def begin(self):
        yh, core, _, _ = place()
        own_send, own_recv, far_send, far_recv, _, _ = self.sems
        mine = rows_of(yh * 2 + core, OWN)
        self.far_copies, self.own_copies, self.on_copies = [], [], []
        for j in range(NC):
            block = self.out.at[mine, pl.ds(j * CW, CW)]
            copy = remote(block, block, far_send.at[j], far_recv.at[j], peer(*FAR))
            copy.start()
            self.far_copies.append(copy)
        for j in range(NC):
            block = self.out.at[mine, pl.ds(j * CW, CW)]
            copy = remote(block, block, own_send.at[j], own_recv.at[j], peer(*CORE))
            copy.start()
            self.own_copies.append(copy)

    def finish(self):
        yh, core, _, _ = place()
        on_send, on_recv = self.sems[4:]
        other = rows_of((1 - yh) * 2 + core, OWN)
        for j in range(NC):
            self.far_copies[j].wait_recv()
            block = self.out.at[other, pl.ds(j * CW, CW)]
            copy = remote(block, block, on_send.at[j], on_recv.at[j], peer(*CORE))
            copy.start()
            self.on_copies.append(copy)
        for copy in self.own_copies + self.on_copies:
            copy.wait_recv()
        for copy in self.far_copies + self.own_copies + self.on_copies:
            copy.wait_send()


def gather_rows(out, sems):
    gather = Gather(out, sems)
    gather.begin()
    gather.finish()


REDUCE_SCRATCH = [
    pltpu.VMEM((2, OWN, D), BF16),
    pltpu.VMEM((OWN, D), BF16),
    pltpu.VMEM((OWN, D), BF16),
    pltpu.VMEM((OWN, D), F32),
    pltpu.SemaphoreType.DMA((2, NC)),
    pltpu.SemaphoreType.DMA((2, NC)),
    pltpu.SemaphoreType.DMA((NC,)),
    pltpu.SemaphoreType.DMA((NC,)),
]
GATHER_SCRATCH = [pltpu.SemaphoreType.DMA((NC,))] * 6


def norm_scale(v):
    return lax.rsqrt(jnp.mean(v * v, axis=1, keepdims=True) + EPS)


def norm_back(v, r, g, dy):
    column_sum = jnp.sum(dy * g * v, axis=1, keepdims=True)
    return r * g * dy - v * (r * r * r) * (column_sum / D)


def input_tile(ref, j):
    return ref[:, pl.ds(pl.multiple_of(j * CW, CW), CW)]


def forward_kernel(r):
    yh, core, _, _ = place()
    t = yh * 2 + core
    greet(FF_PEERS)

    def begin(name, src, dst):
        return FF_MOVES[name].start(src, dst, *r.moves[name])

    load_count = iter(range(32))

    def load(src, dst):
        copy = pltpu.make_async_copy(src, dst, r.load_sems.at[next(load_count)])
        copy.start()
        return copy

    width = 4 * HD
    places = [r.down_vmem.at[:, pl.ds(n * width, width)] for n in range(3)]
    features_load = load(r.features, r.features_vmem)
    value_load = load(r.w_value, places[0])
    key_load = load(r.w_key, places[1])
    query_load = load(r.w_query, places[2])
    features_own_load = load(r.features.at[rows_of(t, OWN)], r.features_own)
    top_own_load = load(r.cotangent.at[rows_of(t, OWN)], r.top_own)

    def projected(n):
        return dot(
            r.features_vmem[...], r.down_vmem[:, n * width : (n + 1) * width], ((1,), (0,))
        )

    wait([features_load, value_load])
    r.value[...] = projected(0).astype(BF16)
    greeted(FF_PEERS)

    def project():
        key_load.wait()
        r.k_raw[...] = projected(1)
        query_load.wait()
        r.q_raw[...] = projected(2)

    weights = attend_part(
        project, r.q_raw, r.k_raw, r.value, r.seg, r.q_gain, r.k_gain,
        r.attended, r.q_head, r.k_head, r.v_head, r.probs, r.scales, *r.attend,
        lambda: [
            load(r.w_out, r.out_vmem),
            load(r.w_gate, r.gate_vmem),
            load(r.w_up, r.up_vmem),
            load(r.w_down, r.down_vmem),
        ],
    )
    saved = [
        load(r.q_head, r.q_head_out),
        load(r.k_head, r.k_head_out),
        load(r.v_head, r.v_head_out),
        load(r.probs, r.probs_out),
        load(r.q_raw, r.q_raw_out),
        load(r.k_raw, r.k_raw_out),
        load(r.scales, r.scales_out),
    ]
    weights[0].wait()

    def attn_part(j):
        r.part[:, j * CW : (j + 1) * CW] = dot(
            r.attended[...], r.out_vmem[:, j * CW : (j + 1) * CW], ((1,), (0,))
        ).astype(BF16)

    Reduce(r.part, *r.reduce).run(attn_part)
    features_own_load.wait()
    v = r.reduce[3][...]
    state = r.features_own[...].astype(F32) + v * norm_scale(v) * r.attn_gain[...]
    r.hidden[rows_of(t, OWN), :] = state.astype(BF16)
    r.attn_own[...] = v
    r.hidden_own[...] = state
    features_copies = begin(FF.features_half, r.features, r.features_half)
    attended_copies = begin(FF.attended_all, r.attended, r.attended_all)
    gather_rows(r.hidden, r.gather)
    hidden_copies = begin(FF.hidden_half, r.hidden, r.hidden_half)

    wait(weights[1:])

    def hidden_units(j, _):
        cols = pl.ds(pl.multiple_of(j * CW, CW), CW)
        gate = dot(r.hidden[...], r.gate_vmem[:, cols], ((1,), (0,)))
        upward = dot(r.hidden[...], r.up_vmem[:, cols], ((1,), (0,)))
        sigma = jax.nn.sigmoid(gate)
        activated = gate * sigma
        r.mixed[:, cols] = (activated * upward).astype(BF16)
        r.act[:, cols] = activated
        r.slope[:, cols] = upward * sigma * (1.0 + gate * (1.0 - sigma))
        return 0

    lax.fori_loop(0, NC, hidden_units, 0)
    mixed_copies = begin(FF.mixed_right, r.mixed, r.mixed_right)

    def mlp_part(j):
        r.part[:, j * CW : (j + 1) * CW] = dot(
            r.mixed[...], r.down_vmem[:, j * CW : (j + 1) * CW], ((1,), (0,))
        ).astype(BF16)

    Reduce(r.part, *r.reduce).run(mlp_part)
    top_own_load.wait()
    v = r.reduce[3][...]
    z = norm_scale(v)
    dy = r.top_own[...].astype(F32)
    g = r.mlp_gain[...]
    r.d_mlp[rows_of(t, OWN), :] = norm_back(v, z, g, dy).astype(BF16)
    r.result_own[...] = (r.hidden_own[...] + v * z * g).astype(BF16)
    mlp_gain_grad = jnp.sum(dy * v * z, axis=0, keepdims=True)
    gather_rows(r.d_mlp, r.gather)
    top_copies = begin(FF.top_half, r.d_mlp, r.top_half)

    def hidden_units_back(j, _):
        cols = pl.ds(pl.multiple_of(j * CW, CW), CW)
        d_mixed = dot(r.d_mlp[...], r.down_vmem[cols, :], ((1,), (1,)))
        r.d_up[:, cols] = (d_mixed * r.act[:, cols]).astype(BF16)
        r.d_gate[:, cols] = (d_mixed * r.slope[:, cols]).astype(BF16)
        return 0

    lax.fori_loop(0, NC, hidden_units_back, 0)
    right_copies = begin(FF.gate_right, r.d_gate, r.gate_right) + begin(FF.up_right, r.d_up, r.up_right)
    wait(features_copies)
    features_copies = begin(FF.features_rest, r.features_half, r.features_rest)

    def back_part(j):
        rows = pl.ds(j * CW, CW)
        r.part[:, j * CW : (j + 1) * CW] = (
            dot(r.d_gate[...], r.gate_vmem[rows, :], ((1,), (1,)))
            + dot(r.d_up[...], r.up_vmem[rows, :], ((1,), (1,)))
        ).astype(BF16)

    Reduce(r.part, *r.reduce).run(back_part)
    wait(hidden_copies)
    hidden_copies = begin(FF.hidden_rest, r.hidden_half, r.hidden_rest)
    dy = r.top_own[...].astype(F32) + r.reduce[3][...]
    v = r.attn_own[...]
    a = norm_scale(v)
    g = r.attn_gain[...]
    r.d_attn[rows_of(t, OWN), :] = norm_back(v, a, g, dy).astype(BF16)
    r.d_hidden_own[...] = dy
    row = lax.broadcasted_iota(jnp.int32, (8, D), 0)
    attn_grad = jnp.sum(dy * v * a, axis=0, keepdims=True)
    r.gain_rows[...] = jnp.where(row == 0, attn_grad, mlp_gain_grad)
    gather_rows(r.d_attn, r.gather)
    r.d_attended[...] = dot(r.d_attn[...], r.out_vmem[...], ((1,), (1,))).astype(BF16)
    wait(right_copies + hidden_copies + features_copies + attended_copies)
    wait(mixed_copies + top_copies + saved)


WIDE = jax.ShapeDtypeStruct((T, D), BF16)
NARROW = jax.ShapeDtypeStruct((T, 4 * HD), BF16)
HALVES = jax.ShapeDtypeStruct((4, T, D // 2), BF16)
FF_MOVES = dict(
    features_half=half_move(WIDE, "x"),
    features_rest=core_move(HALVES),
    attended_all=full_move(NARROW, "z"),
    hidden_half=half_move(WIDE, "z"),
    hidden_rest=core_move(HALVES),
    gate_right=quarter_move(WIDE, "z"),
    up_right=quarter_move(WIDE, "z"),
    mixed_right=quarter_move(WIDE, "x"),
    top_half=half_move(WIDE, "x"),
)
FF = Names(**{name: name for name in FF_MOVES})
FF_PEERS = distinct(
    [CORE, FAR]
    + [(0, dy, dx, 0, 0) for dy in range(2) for dx in range(4) if dy or dx]
    + peers_of(FF_MOVES)
)


def attend_scratch():
    dma = pltpu.SemaphoreType.DMA
    return [
        pltpu.VMEM((8, 8, T), F32),
        pltpu.VMEM((T, 4 * HD), BF16),
        pltpu.VMEM((T, 4 * HD), BF16),
        pltpu.VMEM((2, T, HD), F32),
        pltpu.VMEM((T, HD), F32),
        pltpu.VMEM((T, HD), F32),
        pltpu.VMEM((4, T, HD), BF16),
        dma((4, 4)),
        dma((4, 4)),
        dma((4,)),
        dma((4,)),
        dma((8,)),
        dma((8,)),
        dma((2,)),
        dma((2,)),
        dma((4,)),
        dma((4,)),
    ]


def forward(small, large):
    weight, wide = pltpu.VMEM((D, D), BF16), pltpu.VMEM((T, D), BF16)
    own, tall = pltpu.VMEM((OWN, D), F32), pltpu.VMEM((T, D), F32)
    own_low = pltpu.VMEM((OWN, D), BF16)
    saved = dict(
        q_head=((4 * T, HD), BF16),
        k_head=((8 * T, HD), BF16),
        v_head=((8 * T, HD), BF16),
        probs=((4, T, 8 * T), BF16),
        q_raw=((T, 4 * HD), F32),
        k_raw=((T, 4 * HD), F32),
        scales=((T, HD), F32),
    )
    scratch = dict(
        out_vmem=pltpu.VMEM((4 * HD, D), BF16),
        gate_vmem=weight,
        up_vmem=weight,
        down_vmem=weight,
        features_own=own_low,
        top_own=own_low,
        part=wide,
        hidden=wide,
        act=tall,
        slope=tall,
        d_gate=wide,
        d_up=wide,
        d_mlp=wide,
        mixed=wide,
        attn_own=own,
        hidden_own=own,
        load_sems=pltpu.SemaphoreType.DMA((32,)),
        reduce=REDUCE_SCRATCH,
        gather=GATHER_SCRATCH,
        moves=move_scratch(FF_MOVES),
        features_vmem=wide,
        value=pltpu.VMEM((T, 4 * HD), BF16),
        attended=pltpu.VMEM((T, 4 * HD), BF16),
        attend=attend_scratch(),
        **{name: pltpu.VMEM(*saved[name]) for name in saved},
    )
    outs = dict(
        d_attended=((T, 4 * HD), BF16),
        d_hidden_own=((OWN, D), F32),
        result_own=((OWN, D), BF16),
        gain_rows=((8, D), F32),
        d_attn=((T, D), BF16),
    )
    large_outs = {name: move.out for name, move in FF_MOVES.items()}
    large_outs |= {name + "_out": out for name, out in saved.items()}
    return run_kernel(forward_kernel, 1, small, large, outs, large_outs, scratch, 62)


def row_device(yl, x):
    return {"ctx": yl * 4 + x}


ATTEND_PEERS = [CORE, FAR] + [(0, dy, dx, 0, 0) for dy in range(2) for dx in range(4) if dy or dx]


def tensor_sum(own, near, far, send, recv):
    yh, core, _, _ = place()
    copy = remote(own.at[0], near, send.at[0], recv.at[0], peer(*CORE))
    copy.start()
    copy.wait_recv()
    own[1] = own[0] + near[...]
    again = remote(own.at[1], far, send.at[1], recv.at[1], peer(*FAR))
    again.start()
    again.wait_recv()
    total = own[1] + far[...]
    copy.wait_send()
    again.wait_send()
    return total


def two_columns(first, second):
    lane = lax.broadcasted_iota(jnp.int32, (T, HD), 1)
    return jnp.where(lane < HD // 2, first, second)


class Spread:
    def __init__(self, src, dst, sems):
        self.src, self.dst = src, dst
        self.send, self.recv, self.down_send, self.down_recv = sems

    def row_copy(self, s):
        _, _, yl, x = place()
        h = lax.rem(x + s, 4)
        return remote(
            self.src.at[:, pl.ds(pl.multiple_of(h * HD, HD), HD)],
            self.dst.at[rows_of(yl * 4 + x, T)],
            self.send.at[s],
            self.recv.at[s],
            row_device(yl, h),
        )

    def down_copy(self, s):
        _, _, yl, x = place()
        h = lax.rem(x + s, 4)
        return remote(
            self.src.at[:, pl.ds(pl.multiple_of(h * HD, HD), HD)],
            self.dst.at[rows_of(x, T)],
            self.down_send.at[s],
            self.down_recv.at[s],
            row_device(1, h),
        )


def keep_own(src, dst, block):
    _, _, _, x = place()
    dst[rows_of(block, T), :] = src[:, pl.ds(pl.multiple_of(x * HD, HD), HD)]


def attend_part(
    project, q_raw, k_raw, value, seg, q_gain, k_gain,
    attended, q_head, k_head, v_head, probs_out, scale_out,
    seg_all, q_low, k_low, sums, near, far, result,
    v_sems, k_sems, q_send, q_recv, s_send, s_recv, sum_send, sum_recv, a_send, a_recv,
    load_weights,
):
    yh, core, yl, x = place()
    me = yl * 4 + x
    v_sems = [v_sems.at[i] for i in range(4)]
    k_sems = [k_sems.at[i] for i in range(4)]
    values = Spread(value, v_head, v_sems)
    keys = Spread(k_low, k_head, k_sems)

    @pl.when(yl == 0)
    def _():
        for s in range(4):
            values.down_copy(s).start()

    for s in (1, 2, 3):
        values.row_copy(s).start()
    seg_all[me] = jnp.broadcast_to(seg[...].astype(F32), (8, T))

    def seg_copy(s):
        dx, dy = s % 4, s // 4
        to = row_device(lax.rem(yl + dy, 2), lax.rem(x + dx, 4))
        return remote(seg_all.at[me], seg_all.at[me], s_send.at[s], s_recv.at[s], to)

    for s in range(1, 8):
        seg_copy(s).start()

    project()
    qr, kr = q_raw[...], k_raw[...]
    sums[0] = two_columns(
        jnp.sum(qr * qr, axis=1, keepdims=True), jnp.sum(kr * kr, axis=1, keepdims=True)
    )
    keep_own(value, v_head, me)
    weights = load_weights()
    scales = lax.rsqrt(tensor_sum(sums, near, far, sum_send, sum_recv) / D + EPS)
    scale_out[...] = scales
    k_low[...] = (kr * scales[:, HD // 2 : HD // 2 + 1] * k_gain[...]).astype(BF16)

    @pl.when(yl == 0)
    def _():
        for s in range(4):
            keys.down_copy(s).start()

    for s in (1, 2, 3):
        keys.row_copy(s).start()
    q_low[...] = (qr * scales[:, :1] * q_gain[...]).astype(BF16)

    def q_copy(s):
        h = lax.rem(x + s, 4)
        return remote(
            q_low.at[:, pl.ds(pl.multiple_of(h * HD, HD), HD)],
            q_head.at[rows_of(x, T)],
            q_send.at[s],
            q_recv.at[s],
            row_device(yl, h),
        )

    for s in (1, 2, 3):
        q_copy(s).start()
    keep_own(k_low, k_head, me)
    keep_own(q_low, q_head, x)
    for s in range(1, 8):
        seg_copy(s).wait()
    for s in (1, 2, 3):
        values.row_copy(s).wait()
        keys.row_copy(s).wait()
        q_copy(s).wait()

    @pl.when(yl == 0)
    def _():
        for s in range(4):
            values.down_copy(s).wait_send()
            keys.down_copy(s).wait_send()

    @pl.when(yl == 1)
    def _():
        for s in range(4):
            values.down_copy(s).wait_recv()
            keys.down_copy(s).wait_recv()

    lane = lax.broadcasted_iota(jnp.int32, (8, HD), 0)
    pick = jnp.where(lane == 0, 1.0, 0.0)

    def attend(row, i):
        blocks = row * 4 + i + 1
        width = blocks * T
        q = q_head[i * T : (i + 1) * T, :]
        scores = dot(q, k_head[:width, :], ((1,), (1,))) * HD ** (-0.5)
        own_seg = dot(seg_all[row * 4 + i], pick, ((0,), (0,)))[:, :1]
        seg_keys = jnp.concatenate([seg_all[b, :1, :] for b in range(blocks)], axis=1)
        q_place = lax.broadcasted_iota(jnp.int32, (T, width), 0) + (blocks - 1) * T
        k_place = lax.broadcasted_iota(jnp.int32, (T, width), 1)
        counted = (k_place <= q_place) & (seg_keys == own_seg)
        scores = jnp.where(counted, scores, -1e30)
        exps = jnp.exp(scores - jnp.max(scores, axis=1, keepdims=True))
        probs = (exps * (1.0 / jnp.sum(exps, axis=1, keepdims=True))).astype(BF16)
        probs_out[i, :, :width] = probs
        result[i] = dot(probs, v_head[:width, :], ((1,), (0,))).astype(BF16)

    def back_copy(i):
        return remote(
            result.at[i],
            attended.at[:, pl.ds(pl.multiple_of(x * HD, HD), HD)],
            a_send.at[i],
            a_recv.at[x],
            row_device(yl, i),
        )

    for i in range(4):
        for row in range(2):

            @pl.when(yl == row)
            def _():
                attend(row, i)

        @pl.when(x == i)
        def _():
            attended[:, i * HD : (i + 1) * HD] = result[i]

        @pl.when(x != i)
        def _():
            back_copy(i).start()

    for h in range(4):

        @pl.when(x != h)
        def _():
            back_copy(h).wait_send()
            remote(
                result.at[h],
                attended.at[:, h * HD : (h + 1) * HD],
                a_send.at[h],
                a_recv.at[h],
                row_device(yl, h),
            ).wait_recv()
    return weights


def product_rows(left, right):
    return dot(
        left.reshape(4 * T, left.shape[2]), right.reshape(4 * T, right.shape[2]), ((0,), (0,))
    ).astype(BF16)


def blocks_out(partial, slots, send, recv, axis, piece=None):
    me = spot(axis)
    made = []
    for s in (1, 2, 3):
        source, target = partial.at[lax.rem(me + s, 4)], slots.at[s - 1]
        send_sem, recv_sem = send.at[s - 1], recv.at[s - 1]
        if piece is not None:
            source, target = source.at[:, piece], target.at[:, piece]
            send_sem, recv_sem = send.at[s - 1, piece], recv.at[s - 1, piece]
        made.append(remote(source, target, send_sem, recv_sem, peer(*along(axis, s))))
    return made


def add_blocks(total, partial, slots, axis):
    me = spot(axis)
    for y in range(2):
        for j in range(4):
            block = partial[me, y, j].astype(F32)
            for s in range(3):
                block += slots[s, y, j].astype(F32)
            total[y, j] = block.astype(BF16)


HALF_GRID = (2, 4, 64)
BACK_MOVES = dict(
    attn_left=quarter_move(WIDE, "z"),
    q_right=quarter_move(NARROW, "x"),
    k_right=quarter_move(NARROW, "x"),
    v_right=quarter_move(NARROW, "x"),
    mlp_in=final_move(jax.ShapeDtypeStruct(HALF_GRID + (1024,), BF16), "z"),
    mlp_down=final_move(jax.ShapeDtypeStruct(HALF_GRID + (512,), BF16), "x"),
    qkv=final_move(jax.ShapeDtypeStruct(HALF_GRID + (384,), BF16), "x"),
    out=final_move(jax.ShapeDtypeStruct(HALF_GRID + (512,), BF16), "x"),
    tiles=rank_move(jax.ShapeDtypeStruct((32, 16, HD), F32)),
)
BACK = Names(**{name: name for name in BACK_MOVES})
BACK_PEERS = distinct(ATTEND_PEERS + peers_of(BACK_MOVES))


def back_scratch():
    dma = pltpu.SemaphoreType.DMA

    def vmem(*shape, kind=BF16):
        return pltpu.VMEM(shape, kind)

    rows = (2, 4, 64)
    return dict(
        q_head=vmem(4 * T, HD),
        k_head=vmem(8 * T, HD),
        v_head=vmem(8 * T, HD),
        probs=vmem(2, T, 8 * T),
        q_raw=vmem(T, 4 * HD, kind=F32),
        k_raw=vmem(T, 4 * HD, kind=F32),
        scales=vmem(T, HD, kind=F32),
        wq=vmem(D, 4 * HD),
        wk=vmem(D, 4 * HD),
        wv=vmem(D, 4 * HD),
        left=vmem(2, 4, T, D // 2),
        top=vmem(2, 4, T, D // 2),
        gate_right=vmem(4, T, 512),
        up_right=vmem(4, T, 512),
        mixed_right=vmem(4, T, 512),
        attn_left=vmem(4, T, 512),
        attended_all=vmem(4, T, 512),
        q_right=vmem(4, T, HD),
        k_right=vmem(4, T, HD),
        v_right=vmem(4, T, HD),
        in_part=vmem(4, *rows, 1024),
        in_slots=vmem(3, *rows, 1024),
        in_sum=vmem(*rows, 1024),
        down_part=vmem(4, *rows, 512),
        down_slots=vmem(3, *rows, 512),
        down_sum=vmem(*rows, 512),
        qkv_part=vmem(4, *rows, 384),
        qkv_slots=vmem(3, *rows, 384),
        qkv_sum=vmem(*rows, 384),
        out_part=vmem(*rows, 512),
        tile_part=vmem(32, 16, HD, kind=F32),
        d_q=vmem(T, 4 * HD),
        d_k=vmem(T, 4 * HD),
        d_v=vmem(T, 4 * HD),
        part=vmem(T, D),
        d_out=vmem(4 * T, HD),
        dq_buf=vmem(4, T, HD),
        dk_buf=vmem(8, T, HD),
        dv_buf=vmem(8, T, HD),
        dk_acc=vmem(8 * T, HD, kind=F32),
        dv_acc=vmem(8 * T, HD, kind=F32),
        dq_got=vmem(4, T, HD),
        dk_got=vmem(2, 4, T, HD),
        dv_got=vmem(2, 4, T, HD),
        sums=vmem(2, T, HD, kind=F32),
        near=vmem(T, HD, kind=F32),
        far=vmem(T, HD, kind=F32),
        gain_near=vmem(8, D, kind=F32),
        gain_far=vmem(8, D, kind=F32),
        gain_sum=vmem(8, D, kind=F32),
        load_sems=dma((32,)),
        in_send=dma((3, 4)),
        in_recv=dma((3, 4)),
        down_send=dma((3,)),
        down_recv=dma((3,)),
        qkv_send=dma((3,)),
        qkv_recv=dma((3,)),
        o_send=dma((4,)),
        o_recv=dma((4,)),
        dq_send=dma((4,)),
        dq_recv=dma((4,)),
        dk_send=dma((8,)),
        dk_recv=dma((2, 4)),
        dv_send=dma((8,)),
        dv_recv=dma((2, 4)),
        sum_send=dma((2,)),
        sum_recv=dma((2,)),
        gain_send=dma((2,)),
        gain_recv=dma((2,)),
        top_send=dma((1,)),
        top_recv=dma((1,)),
        result_send=dma((3,)),
        result_recv=dma((3,)),
        reduce=REDUCE_SCRATCH,
        gather=GATHER_SCRATCH,
        moves=move_scratch(BACK_MOVES),
    )


def backward_kernel(r):
    yh, core, yl, x = place()
    t = yh * 2 + core
    scale = HD ** (-0.5)
    greet(BACK_PEERS)
    greeted(BACK_PEERS)

    def begin(name, src, dst):
        return BACK_MOVES[name].start(src, dst, *r.moves[name])

    load_count = iter(range(32))

    def load(src, dst):
        copy = pltpu.make_async_copy(src, dst, r.load_sems.at[next(load_count)])
        copy.start()
        return copy

    def o_copy(s):
        h = lax.rem(x + s, 4)
        return remote(
            r.d_attended.at[:, pl.ds(pl.multiple_of(h * HD, HD), HD)],
            r.d_out.at[rows_of(x, T)],
            r.o_send.at[s],
            r.o_recv.at[s],
            row_device(yl, h),
        )

    for s in (1, 2, 3):
        o_copy(s).start()
    hidden0_load = load(r.hidden_half, r.left.at[core])
    gate_right_load = load(r.gate_right_in, r.gate_right)
    up_right_load = load(r.up_right_in, r.up_right)
    hidden1_load = load(r.hidden_rest, r.left.at[1 - core])
    q_head_load = load(r.q_head_in, r.q_head)
    k_head_load = load(r.k_head_in, r.k_head)
    v_head_load = load(r.v_head_in, r.v_head)
    probs_loads = [load(r.probs_in.at[i], r.probs.at[i]) for i in range(2)]
    q_raw_load = load(r.q_raw_in, r.q_raw)
    k_raw_load = load(r.k_raw_in, r.k_raw)
    scales_load = load(r.scales_in, r.scales)
    mixed_right_load = load(r.mixed_right_in, r.mixed_right)
    top_load = load(r.top_half, r.top.at[core])
    attended_all_load = load(r.attended_all_in, r.attended_all)
    w_query_load = load(r.w_query, r.wq)
    w_key_load = load(r.w_key, r.wk)
    w_value_load = load(r.w_value, r.wv)
    gain_near_copy = remote(
        r.gains, r.gain_near, r.gain_send.at[0], r.gain_recv.at[0], peer(*CORE)
    )
    gain_near_copy.start()
    top_copy = remote(
        r.top_half, r.top.at[core], r.top_send.at[0], r.top_recv.at[0], peer(*CORE)
    )
    top_copy.start()
    mine, other = rows_of(t, OWN), rows_of((1 - yh) * 2 + core, OWN)
    result_load = load(r.result_own, r.outputs.at[mine])
    result_copies = [
        remote(
            r.result_own, r.outputs.at[mine], r.result_send.at[n], r.result_recv.at[n], to
        )
        for n, to in enumerate((peer(*FAR), peer(*CORE)))
    ]
    for copy in result_copies:
        copy.start()
    attn_left = begin(BACK.attn_left, r.d_attn, r.attn_left)
    keep_own(r.d_attended, r.d_out, x)
    r.dk_acc[...] = jnp.zeros_like(r.dk_acc)
    r.dv_acc[...] = jnp.zeros_like(r.dv_acc)

    wait([hidden0_load, gate_right_load, up_right_load, hidden1_load])
    in_copies = []

    def in_piece(piece):
        copies = blocks_out(r.in_part, r.in_slots, r.in_send, r.in_recv, "x", piece)
        for copy in copies:
            copy.start()
        in_copies.extend(copies)

    for i in range(4):
        left = r.left[i // 2, :, :, (i % 2) * 512 : (i % 2 + 1) * 512]
        for n, right in enumerate((r.gate_right, r.up_right)):
            got = product_rows(left, right[...])
            for y in range(2):
                for j in range(4):
                    r.in_part[j, y, i, :, n * 512 : (n + 1) * 512] = got[
                        (y * 4 + j) * 64 : (y * 4 + j + 1) * 64
                    ]
        if i < 2:
            in_piece(i)
    features0_load = load(r.features_half, r.left.at[core])
    features1_load = load(r.features_rest, r.left.at[1 - core])
    gain_near_copy.wait()
    r.gain_sum[...] = r.gains[...] + r.gain_near[...]
    gain_far_copy = remote(
        r.gain_sum, r.gain_far, r.gain_send.at[1], r.gain_recv.at[1], peer(*FAR)
    )
    gain_far_copy.start()

    for s in (1, 2, 3):
        o_copy(s).wait()
    wait([q_head_load, k_head_load, v_head_load])

    def back(row, i):
        width = (row * 4 + i + 1) * T
        q = r.q_head[i * T : (i + 1) * T, :]
        do = r.d_out[i * T : (i + 1) * T, :]
        probs_low = r.probs[i % 2, :, :width]
        probs = probs_low.astype(F32)
        d_probs = dot(do, r.v_head[:width, :], ((1,), (1,)))
        delta = jnp.sum(probs * d_probs, axis=1, keepdims=True)
        d_scores = (probs * (d_probs - delta)).astype(BF16)
        r.dq_buf[i] = (dot(d_scores, r.k_head[:width, :], ((1,), (0,))) * scale).astype(BF16)
        r.dk_acc[:width, :] += dot(d_scores, q, ((0,), (0,)))
        r.dv_acc[:width, :] += dot(probs_low, do, ((0,), (0,)))

    def dq_copy(i):
        return remote(
            r.dq_buf.at[i], r.dq_got.at[x], r.dq_send.at[i], r.dq_recv.at[x], row_device(yl, i)
        )

    for i in range(4):
        probs_loads[i].wait()
        for row in range(2):

            @pl.when(yl == row)
            def _():
                back(row, i)

        if i < 2:
            probs_loads.append(load(r.probs_in.at[i + 2], r.probs.at[i]))

        @pl.when(x == i)
        def _():
            r.dq_got[i] = r.dq_buf[i]

        @pl.when(x != i)
        def _():
            dq_copy(i).start()

    def kv_copy(j, buf, got, send, recv):
        return remote(
            buf.at[j], got.at[yl, x], send.at[j], recv.at[yl, x], row_device(j // 4, j % 4)
        )

    dk_args = (r.dk_buf, r.dk_got, r.dk_send, r.dk_recv)
    dv_args = (r.dv_buf, r.dv_got, r.dv_send, r.dv_recv)
    for j in range(8):
        r.dk_buf[j] = (r.dk_acc[j * T : (j + 1) * T, :] * scale).astype(BF16)
        r.dv_buf[j] = r.dv_acc[j * T : (j + 1) * T, :].astype(BF16)
        here = (yl == j // 4) & (x == j % 4)

        @pl.when(here)
        def _():
            r.dk_got[j // 4, j % 4] = r.dk_buf[j]
            r.dv_got[j // 4, j % 4] = r.dv_buf[j]

        sends = (yl >= j // 4) & ~here

        @pl.when(sends)
        def _():
            kv_copy(j, *dk_args).start()
            kv_copy(j, *dv_args).start()

    in_piece(2)
    in_piece(3)

    result_copies[0].wait_recv()
    result_copies.append(
        remote(
            r.outputs.at[other],
            r.outputs.at[other],
            r.result_send.at[2],
            r.result_recv.at[2],
            peer(*CORE),
        )
    )
    result_copies[2].start()

    mixed_right_load.wait()
    top_load.wait()
    top_copy.wait()
    for i in range(4):
        left = r.top[i // 2, :, :, (i % 2) * 512 : (i % 2 + 1) * 512]
        r.down_part[i] = product_rows(left, r.mixed_right[...]).reshape(2, 4, 64, 512)
    down_copies = blocks_out(r.down_part, r.down_slots, r.down_send, r.down_recv, "z")
    for copy in down_copies:
        copy.start()
    attended_all_load.wait()
    wait(attn_left)
    r.out_part[...] = product_rows(r.attn_left[...], r.attended_all[...]).reshape(2, 4, 64, 512)

    for h in range(4):

        @pl.when(x != h)
        def _():
            dq_copy(h).wait_send()
            remote(
                r.dq_buf.at[h], r.dq_got.at[h], r.dq_send.at[h], r.dq_recv.at[h],
                row_device(yl, h),
            ).wait_recv()

        for row in range(2):
            comes = (row >= yl) & ~((yl == row) & (x == h))

            @pl.when(comes)
            def _():
                for buf, got, send, recv in (dk_args, dv_args):
                    remote(
                        buf.at[0],
                        got.at[row, h],
                        send.at[0],
                        recv.at[row, h],
                        row_device(row, h),
                    ).wait_recv()

    for j in range(8):
        here = (yl == j // 4) & (x == j % 4)
        sends = (yl >= j // 4) & ~here

        @pl.when(sends)
        def _():
            kv_copy(j, *dk_args).wait_send()
            kv_copy(j, *dv_args).wait_send()

    @pl.when(yl == 1)
    def _():
        for h in range(4):
            r.dk_got[0, h] = jnp.zeros((T, HD), BF16)
            r.dv_got[0, h] = jnp.zeros((T, HD), BF16)

    wait([q_raw_load, k_raw_load, scales_load])
    q_sum = jnp.zeros((T, 1), F32)
    k_sum = jnp.zeros((T, 1), F32)
    for h in range(4):
        cols = slice(h * HD, (h + 1) * HD)
        dq = r.dq_got[h].astype(F32)
        dk = r.dk_got[0, h].astype(F32) + r.dk_got[1, h].astype(F32)
        r.d_v[:, cols] = (r.dv_got[0, h].astype(F32) + r.dv_got[1, h].astype(F32)).astype(BF16)
        q_sum += jnp.sum(dq * r.q_raw[:, cols] * r.q_gain[:, cols], axis=1, keepdims=True)
        k_sum += jnp.sum(dk * r.k_raw[:, cols] * r.k_gain[:, cols], axis=1, keepdims=True)
    r.sums[0] = two_columns(q_sum, k_sum)
    v_copies = begin(BACK.v_right, r.d_v, r.v_right)
    total = tensor_sum(r.sums, r.near, r.far, r.sum_send, r.sum_recv)
    qs, ks = r.scales[:, :1], r.scales[:, HD // 2 : HD // 2 + 1]
    q_coef = qs * qs * qs * (total[:, :1] / D)
    k_coef = ks * ks * ks * (total[:, HD // 2 : HD // 2 + 1] / D)
    gain_far_copy.wait()
    both = r.gain_sum[...] + r.gain_far[...]
    tile = []
    for h in range(4):
        cols = slice(h * HD, (h + 1) * HD)
        dq = r.dq_got[h].astype(F32)
        dk = r.dk_got[0, h].astype(F32) + r.dk_got[1, h].astype(F32)
        qr, kr = r.q_raw[:, cols], r.k_raw[:, cols]
        r.d_q[:, cols] = (qs * r.q_gain[:, cols] * dq - qr * q_coef).astype(BF16)
        r.d_k[:, cols] = (ks * r.k_gain[:, cols] * dk - kr * k_coef).astype(BF16)
        tile.append((jnp.sum(dq * qr * qs, axis=0, keepdims=True), jnp.sum(dk * kr * ks, axis=0, keepdims=True)))
    qk_copies = begin(BACK.q_right, r.d_q, r.q_right) + begin(BACK.k_right, r.d_k, r.k_right)
    row = lax.broadcasted_iota(jnp.int32, (8, HD), 0)
    top_tile = jnp.zeros((8, HD), F32)
    for h in range(4):
        top_tile = jnp.where(row == h, tile[h][0], top_tile)
        top_tile = jnp.where(row == h + 4, tile[h][1], top_tile)
    for rank in range(32):
        r.tile_part[rank, :8] = top_tile
        r.tile_part[rank, 8:] = both[:, (rank // 2) * HD : (rank // 2 + 1) * HD]
    tile_copies = begin(BACK.tiles, r.tile_part, r.tiles)

    wait([w_query_load, w_key_load, w_value_load])

    def input_part(j):
        rows = pl.ds(j * CW, CW)
        r.part[:, j * CW : (j + 1) * CW] = (
            dot(r.d_q[...], r.wq[rows, :], ((1,), (1,)))
            + dot(r.d_k[...], r.wk[rows, :], ((1,), (1,)))
            + dot(r.d_v[...], r.wv[rows, :], ((1,), (1,)))
        ).astype(BF16)

    reduce = Reduce(r.part, *r.reduce)
    reduce.begin(input_part)
    out_copies = begin(BACK.out, r.out_part, r.out)
    wait(v_copies + qk_copies)
    features0_load.wait()
    features1_load.wait()
    for i in range(4):
        left = r.left[i // 2, :, :, (i % 2) * 512 : (i % 2 + 1) * 512]
        for n, right in enumerate((r.q_right, r.k_right, r.v_right)):
            r.qkv_part[i, :, :, :, n * HD : (n + 1) * HD] = product_rows(left, right[...]).reshape(
                2, 4, 64, HD
            )
    qkv_copies = blocks_out(r.qkv_part, r.qkv_slots, r.qkv_send, r.qkv_recv, "z")
    for copy in qkv_copies:
        copy.start()
    reduce.finish()
    r.input_grad[mine, :] = (r.d_hidden_own[...] + r.reduce[3][...]).astype(BF16)
    gather = Gather(r.input_grad, r.gather)
    gather.begin()

    wait(down_copies)
    add_blocks(r.down_sum, r.down_part, r.down_slots, "z")
    down_final = begin(BACK.mlp_down, r.down_sum, r.mlp_down)
    wait(in_copies)
    add_blocks(r.in_sum, r.in_part, r.in_slots, "x")
    in_final = begin(BACK.mlp_in, r.in_sum, r.mlp_in)
    gather.finish()
    wait(qkv_copies)
    add_blocks(r.qkv_sum, r.qkv_part, r.qkv_slots, "z")
    qkv_final = begin(BACK.qkv, r.qkv_sum, r.qkv)
    result_load.wait()
    result_copies[0].wait_send()
    result_copies[1].wait()
    result_copies[2].wait()
    wait(tile_copies + out_copies + down_final + in_final + qkv_final)


def backward(small, large):
    large_outs = dict(
        outputs=((T, D), BF16),
        tiles=((32, 16, HD), F32),
        mlp_in=(HALF_GRID + (1024,), BF16),
        mlp_down=(HALF_GRID + (512,), BF16),
        qkv=(HALF_GRID + (384,), BF16),
        out=(HALF_GRID + (512,), BF16),
    )
    outs = dict(input_grad=((T, D), BF16))
    return run_kernel(backward_kernel, 6, small, large, outs, large_outs, back_scratch(), 62)


def add_up(blocks):
    return jnp.sum(blocks.astype(F32), axis=0)


def rows_out(final):
    return add_up(final).transpose(1, 0, 2)


def per_device(
    inputs, segments, w_query, w_key, w_value, w_out, q_gain, k_gain, attn_gain,
    w_gate, w_up, w_down, mlp_gain, cotangent,
):
    features, top = inputs[0], cotangent[0]
    q_row, k_row = q_gain.reshape(1, -1), k_gain.reshape(1, -1)
    a_row, m_row = attn_gain.reshape(1, -1), mlp_gain.reshape(1, -1)

    ff = forward(
        dict(seg=segments, q_gain=q_row, k_gain=k_row, attn_gain=a_row, mlp_gain=m_row),
        dict(
            features=features, cotangent=top, w_query=w_query, w_key=w_key, w_value=w_value,
            w_out=w_out, w_gate=w_gate, w_up=w_up, w_down=w_down,
        ),
    )
    got = backward(
        dict(
            d_attended=ff.d_attended, q_gain=q_row, k_gain=k_row, gains=ff.gain_rows,
            d_hidden_own=ff.d_hidden_own, result_own=ff.result_own,
        ),
        dict(
            q_head_in=ff.q_head_out, k_head_in=ff.k_head_out, v_head_in=ff.v_head_out,
            probs_in=ff.probs_out, q_raw_in=ff.q_raw_out, k_raw_in=ff.k_raw_out,
            scales_in=ff.scales_out,
            w_query=w_query, w_key=w_key, w_value=w_value,
            hidden_half=ff.hidden_half, hidden_rest=ff.hidden_rest, gate_right_in=ff.gate_right,
            up_right_in=ff.up_right, top_half=ff.top_half, mixed_right_in=ff.mixed_right,
            features_half=ff.features_half, features_rest=ff.features_rest,
            attended_all_in=ff.attended_all, d_attn=ff.d_attn,
        ),
    )
    gains = add_up(got.tiles)
    rank = lax.axis_index("dp") * 8 + lax.axis_index("ctx")
    heads = lax.dynamic_slice_in_dim(gains[:8], rank * 4, 4, 1)
    columns = lax.dynamic_slice_in_dim(gains[8:10], lax.rem(rank, 2) * 64, 64, 1)
    qkv, mlp_in, mlp_down = rows_out(got.qkv), rows_out(got.mlp_in), rows_out(got.mlp_down)
    out_grad = add_up(got.out.reshape(8, 64, 512))

    def joined(block):
        return block.reshape(64, -1)

    return (
        got.outputs[None],
        got.input_grad[None],
        joined(qkv[:, :, :128]),
        joined(qkv[:, :, 128:256]),
        joined(qkv[:, :, 256:]),
        out_grad.T,
        heads[:4],
        heads[4:],
        columns[0],
        joined(mlp_in[:, :, :512]),
        joined(mlp_in[:, :, 512:]),
        joined(mlp_down).T,
        columns[1],
    )


def solution(mesh):
    rows, full = P("dp", "ctx", None), P()
    down, across = P("tensor", None), P(None, "tensor")
    in_specs = (
        rows, P("dp", "ctx"), across, across, across, down, down, down, full,
        across, across, down, full, rows,
    )
    split = ("dp", "ctx")
    out_specs = (
        rows, rows, P(split, "tensor"), P(split, "tensor"), P(split, "tensor"), P("tensor", split),
        P("tensor", split), P("tensor", split), P(split), P(split, "tensor"), P(split, "tensor"),
        P("tensor", split), P(split),
    )
    return jax.shard_map(
        per_device, mesh=mesh, in_specs=in_specs, out_specs=out_specs, check_vma=False
    )
```

```python
import functools
import jax
import jax.numpy as jnp
from jax import lax
from jax.experimental import pallas as pl
from jax.experimental.pallas import tpu as pltpu
from jax.sharding import PartitionSpec as P

MESH = pl.DeviceIdType.MESH
F32 = jnp.float32
BF16 = jnp.bfloat16
EPS = 1e-06
T = 256
D = 2048
HD = 128
OWN = 64
NC = 4
CW = D // NC
VMEM = pl.BlockSpec(memory_space=pltpu.VMEM)
ANY = pl.BlockSpec(memory_space=pltpu.HBM)


def place():
    t = lax.axis_index("tensor")
    ctx = lax.axis_index("ctx")
    return t // 2, lax.rem(t, 2), ctx // 4, lax.rem(ctx, 4)


def peer(dz=0, dy=0, dx=0, dh=0, dc=0):
    yh, core, yl, x = place()
    z = lax.rem(lax.axis_index("dp") + dz, 4)
    ctx = lax.rem(yl + dy, 2) * 4 + lax.rem(x + dx, 4)
    return {"dp": z, "ctx": ctx, "tensor": lax.rem(yh + dh, 2) * 2 + lax.rem(core + dc, 2)}


CORE, FAR = (0, 0, 0, 0, 1), (0, 0, 0, 1, 0)


def along(axis, s):
    return (s, 0, 0, 0, 0) if axis == "z" else (0, 0, s, 0, 0)


def spot(axis):
    return lax.axis_index("dp") if axis == "z" else place()[3]


def remote(src, dst, send_sem, recv_sem, device):
    return pltpu.make_async_remote_copy(
        src_ref=src,
        dst_ref=dst,
        send_sem=send_sem,
        recv_sem=recv_sem,
        device_id=device,
        device_id_type=MESH,
    )


def greet(offsets):
    barrier = pltpu.get_barrier_semaphore()
    for offset in offsets:
        pl.semaphore_signal(barrier, inc=1, device_id=peer(*offset), device_id_type=MESH)


def greeted(offsets):
    pl.semaphore_wait(pltpu.get_barrier_semaphore(), len(offsets))


def wait(copies):
    for copy in copies:
        copy.wait()


def dot(a, b, dims):
    return lax.dot_general(a, b, (dims, ((), ())), preferred_element_type=F32)


def rows_of(index, count):
    return pl.ds(pl.multiple_of(index * count, count), count)


class Move:
    def __init__(self, source, shape, offsets, pairs):
        self.source, self.shape, self.offsets, self.pairs = source, shape, offsets, pairs
        self.out = (shape, source.dtype)

    def scratch(self):
        dma = pltpu.SemaphoreType.DMA
        return [dma((len(self.offsets),)), dma((len(self.offsets),)), dma((1,))]

    def copies(self, src, dst, send, recv, local):
        made = []
        at = 0
        for a, b, offset in self.pairs(src, dst):
            if offset is None:
                made.append(pltpu.make_async_copy(a, b, local.at[0]))
            else:
                made.append(remote(a, b, send.at[at], recv.at[at], peer(*offset)))
                at += 1
        return made

    def start(self, src, dst, *sems):
        copies = self.copies(src, dst, *sems)
        for copy in copies:
            copy.start()
        return copies


def half_move(a, axis):
    half = a.shape[1] // 2
    offsets = [along(axis, s) for s in (1, 2, 3)]

    def pairs(src, dst):
        mine = src.at[:, pl.ds(pl.multiple_of(place()[1] * half, half), half)]
        me = spot(axis)
        return [(mine, dst.at[me], offset) for offset in offsets + [None]]

    return Move(a, (4, T, half), offsets, pairs)


def core_move(a):
    return Move(a, a.shape, [CORE], lambda src, dst: [(src, dst, CORE)])


def quarter_move(b, axis):
    width = b.shape[1] // 4
    offsets = [along(axis, s) for s in (1, 2, 3)]

    def pairs(src, dst):
        me = spot(axis)

        def part(s):
            return src.at[:, pl.ds(pl.multiple_of(lax.rem(me + s, 4) * width, width), width)]

        made = [(part(s), dst.at[me], along(axis, s)) for s in (1, 2, 3)]
        return made + [(part(0), dst.at[me], None)]

    return Move(b, (4, T, width), offsets, pairs)


def full_move(b, axis):
    offsets = [along(axis, s) for s in (1, 2, 3)]

    def pairs(src, dst):
        return [(src, dst.at[spot(axis)], offset) for offset in offsets + [None]]

    return Move(b, (4,) + b.shape, offsets, pairs)


def block_move(p, axis):
    offsets = [along(axis, s) for s in (1, 2, 3)]

    def pairs(src, dst):
        me = spot(axis)
        made = [(src.at[lax.rem(me + s, 4)], dst.at[me], along(axis, s)) for s in (1, 2, 3)]
        return made + [(src.at[me], dst.at[me], None)]

    return Move(p, p.shape, offsets, pairs)


def final_move(p, axis):
    steps = [(dy, s) for dy in range(2) for s in range(4) if dy or s]

    def offset(dy, s):
        return (s, dy, 0, 0, 0) if axis == "z" else (0, dy, s, 0, 0)

    def pairs(src, dst):
        yl, me = place()[2], spot(axis)
        made = [
            (src.at[lax.rem(yl + dy, 2), lax.rem(me + s, 4)], dst.at[yl, me], offset(dy, s))
            for dy, s in steps
        ]
        return made + [(src.at[yl, me], dst.at[yl, me], None)]

    return Move(p, p.shape, [offset(*step) for step in steps], pairs)


def rank_move(p):
    steps = [(dz, dy, dx, 0, 0) for dz in range(4) for dy in range(2) for dx in range(4)][1:]

    def pairs(src, dst):
        _, _, yl, x = place()
        z = lax.axis_index("dp")
        me = z * 8 + yl * 4 + x

        def rank(dz, dy, dx, *_):
            return lax.rem(z + dz, 4) * 8 + lax.rem(yl + dy, 2) * 4 + lax.rem(x + dx, 4)

        made = [(src.at[rank(*step)], dst.at[me], step) for step in steps]
        return made + [(src.at[me], dst.at[me], None)]

    return Move(p, p.shape, steps, pairs)


class Names:
    def __init__(self, **names):
        self.__dict__.update(names)


def run_kernel(body, collective_id, small, large, small_outs, large_outs, scratch, vmem):
    ins = [jax.tree.flatten(small), jax.tree.flatten(large)]
    shapes = [
        jax.tree.flatten({name: jax.ShapeDtypeStruct(*out) for name, out in outs.items()})
        for outs in (small_outs, large_outs)
    ]
    own = jax.tree.flatten(scratch)

    def kernel(*refs):
        names, at = {}, 0
        for leaves, tree in ins + shapes + [own]:
            names.update(tree.unflatten(refs[at : at + len(leaves)]))
            at += len(leaves)
        body(Names(**names))

    got = pl.pallas_call(
        kernel,
        name=body.__name__,
        out_shape=shapes[0][0] + shapes[1][0],
        in_specs=[VMEM] * len(ins[0][0]) + [ANY] * len(ins[1][0]),
        out_specs=[VMEM] * len(shapes[0][0]) + [ANY] * len(shapes[1][0]),
        scratch_shapes=own[0],
        compiler_params=pltpu.CompilerParams(
            collective_id=collective_id, has_side_effects=True, vmem_limit_bytes=vmem * 2**20
        ),
    )(*ins[0][0], *ins[1][0])
    n = len(shapes[0][0])
    return Names(**shapes[0][1].unflatten(got[:n]), **shapes[1][1].unflatten(got[n:]))


def move_scratch(moves):
    return {name: move.scratch() for name, move in moves.items()}


def peers_of(moves):
    return [offset for move in moves.values() for offset in move.offsets]


def distinct(offsets):
    return list(dict.fromkeys(offsets))


class Reduce:
    def __init__(self, part, near, far, out_low, acc, *sems):
        self.part, self.near, self.far, self.out_low, self.acc = part, near, far, out_low, acc
        self.sems = sems
        self.near_copies, self.far_copies = [], []

    def send(self, j):
        yh, core, _, _ = place()
        near_send, near_recv, _, _ = self.sems
        cols = pl.ds(j * CW, CW)
        for slot, row in ((0, (1 - yh) * 2 + (1 - core)), (1, yh * 2 + (1 - core))):
            copy = remote(
                self.part.at[rows_of(row, OWN), cols],
                self.near.at[slot, :, cols],
                near_send.at[slot, j],
                near_recv.at[slot, j],
                peer(*CORE),
            )
            copy.start()
            self.near_copies.append(copy)

    def forward(self, j):
        yh, core, _, _ = place()
        _, _, far_send, far_recv = self.sems
        cols = pl.ds(j * CW, CW)
        self.near_copies[2 * j].wait_recv()
        self.out_low[:, cols] = (
            self.part[rows_of((1 - yh) * 2 + core, OWN), cols].astype(F32)
            + self.near[0, :, cols].astype(F32)
        ).astype(BF16)
        copy = remote(
            self.out_low.at[:, cols], self.far.at[:, cols], far_send.at[j], far_recv.at[j],
            peer(*FAR),
        )
        copy.start()
        self.far_copies.append(copy)

    def finish(self):
        yh, core, _, _ = place()
        for j in range(NC):
            cols = pl.ds(j * CW, CW)
            self.near_copies[2 * j + 1].wait_recv()
            self.acc[:, cols] = self.part[rows_of(yh * 2 + core, OWN), cols].astype(
                F32
            ) + self.near[1, :, cols].astype(F32)
        for j in range(NC):
            cols = pl.ds(j * CW, CW)
            self.far_copies[j].wait_recv()
            self.acc[:, cols] = self.acc[:, cols] + self.far[:, cols].astype(F32)
        for copy in self.near_copies + self.far_copies:
            copy.wait_send()

    def begin(self, produce):
        for j in range(NC):
            produce(j)
            self.send(j)
            if j > 0:
                self.forward(j - 1)
        self.forward(NC - 1)

    def run(self, produce):
        self.begin(produce)
        self.finish()


class Gather:
    def __init__(self, out, sems):
        self.out, self.sems = out, sems

    def begin(self):
        yh, core, _, _ = place()
        own_send, own_recv, far_send, far_recv, _, _ = self.sems
        mine = rows_of(yh * 2 + core, OWN)
        self.far_copies, self.own_copies, self.on_copies = [], [], []
        for j in range(NC):
            block = self.out.at[mine, pl.ds(j * CW, CW)]
            copy = remote(block, block, far_send.at[j], far_recv.at[j], peer(*FAR))
            copy.start()
            self.far_copies.append(copy)
        for j in range(NC):
            block = self.out.at[mine, pl.ds(j * CW, CW)]
            copy = remote(block, block, own_send.at[j], own_recv.at[j], peer(*CORE))
            copy.start()
            self.own_copies.append(copy)

    def finish(self):
        yh, core, _, _ = place()
        on_send, on_recv = self.sems[4:]
        other = rows_of((1 - yh) * 2 + core, OWN)
        for j in range(NC):
            self.far_copies[j].wait_recv()
            block = self.out.at[other, pl.ds(j * CW, CW)]
            copy = remote(block, block, on_send.at[j], on_recv.at[j], peer(*CORE))
            copy.start()
            self.on_copies.append(copy)
        for copy in self.own_copies + self.on_copies:
            copy.wait_recv()
        for copy in self.far_copies + self.own_copies + self.on_copies:
            copy.wait_send()


def gather_rows(out, sems):
    gather = Gather(out, sems)
    gather.begin()
    gather.finish()


REDUCE_SCRATCH = [
    pltpu.VMEM((2, OWN, D), BF16),
    pltpu.VMEM((OWN, D), BF16),
    pltpu.VMEM((OWN, D), BF16),
    pltpu.VMEM((OWN, D), F32),
    pltpu.SemaphoreType.DMA((2, NC)),
    pltpu.SemaphoreType.DMA((2, NC)),
    pltpu.SemaphoreType.DMA((NC,)),
    pltpu.SemaphoreType.DMA((NC,)),
]
GATHER_SCRATCH = [pltpu.SemaphoreType.DMA((NC,))] * 6


def norm_scale(v):
    return lax.rsqrt(jnp.mean(v * v, axis=1, keepdims=True) + EPS)


def norm_back(v, r, g, dy):
    column_sum = jnp.sum(dy * g * v, axis=1, keepdims=True)
    return r * g * dy - v * (r * r * r) * (column_sum / D)


def input_tile(ref, j):
    return ref[:, pl.ds(pl.multiple_of(j * CW, CW), CW)]


def forward_kernel(r):
    yh, core, _, _ = place()
    t = yh * 2 + core
    greet(FF_PEERS)

    def begin(name, src, dst):
        return FF_MOVES[name].start(src, dst, *r.moves[name])

    load_count = iter(range(32))

    def load(src, dst):
        copy = pltpu.make_async_copy(src, dst, r.load_sems.at[next(load_count)])
        copy.start()
        return copy

    width = 4 * HD
    places = [r.down_vmem.at[:, pl.ds(n * width, width)] for n in range(3)]
    features_load = load(r.features, r.features_vmem)
    value_load = load(r.w_value, places[0])
    key_load = load(r.w_key, places[1])
    query_load = load(r.w_query, places[2])
    features_own_load = load(r.features.at[rows_of(t, OWN)], r.features_own)
    top_own_load = load(r.cotangent.at[rows_of(t, OWN)], r.top_own)

    def projected(n):
        return dot(
            r.features_vmem[...], r.down_vmem[:, n * width : (n + 1) * width], ((1,), (0,))
        )

    wait([features_load, value_load])
    r.value[...] = projected(0).astype(BF16)
    greeted(FF_PEERS)

    def project():
        key_load.wait()
        r.k_raw[...] = projected(1)
        query_load.wait()
        r.q_raw[...] = projected(2)

    weights = attend_part(
        project, r.q_raw, r.k_raw, r.value, r.seg, r.q_gain, r.k_gain,
        r.attended, r.q_head, r.k_head, r.v_head, r.probs, r.scales, *r.attend,
        lambda: [
            load(r.w_out, r.out_vmem),
            load(r.w_gate, r.gate_vmem),
            load(r.w_up, r.up_vmem),
            load(r.w_down, r.down_vmem),
        ],
    )
    saved = [
        load(r.q_head, r.q_head_out),
        load(r.k_head, r.k_head_out),
        load(r.v_head, r.v_head_out),
        load(r.probs, r.probs_out),
        load(r.q_raw, r.q_raw_out),
        load(r.k_raw, r.k_raw_out),
        load(r.scales, r.scales_out),
    ]
    weights[0].wait()

    def attn_part(j):
        r.part[:, j * CW : (j + 1) * CW] = dot(
            r.attended[...], r.out_vmem[:, j * CW : (j + 1) * CW], ((1,), (0,))
        ).astype(BF16)

    Reduce(r.part, *r.reduce).run(attn_part)
    features_own_load.wait()
    v = r.reduce[3][...]
    state = r.features_own[...].astype(F32) + v * norm_scale(v) * r.attn_gain[...]
    r.hidden[rows_of(t, OWN), :] = state.astype(BF16)
    r.attn_own[...] = v
    r.hidden_own[...] = state
    features_copies = begin(FF.features_half, r.features, r.features_half)
    attended_copies = begin(FF.attended_all, r.attended, r.attended_all)
    gather_rows(r.hidden, r.gather)
    hidden_copies = begin(FF.hidden_half, r.hidden, r.hidden_half)

    wait(weights[1:])

    def hidden_units(j, _):
        cols = pl.ds(pl.multiple_of(j * CW, CW), CW)
        gate = dot(r.hidden[...], r.gate_vmem[:, cols], ((1,), (0,)))
        upward = dot(r.hidden[...], r.up_vmem[:, cols], ((1,), (0,)))
        sigma = jax.nn.sigmoid(gate)
        activated = gate * sigma
        r.mixed[:, cols] = (activated * upward).astype(BF16)
        r.act[:, cols] = activated
        r.slope[:, cols] = upward * sigma * (1.0 + gate * (1.0 - sigma))
        return 0

    lax.fori_loop(0, NC, hidden_units, 0)
    mixed_copies = begin(FF.mixed_right, r.mixed, r.mixed_right)

    def mlp_part(j):
        r.part[:, j * CW : (j + 1) * CW] = dot(
            r.mixed[...], r.down_vmem[:, j * CW : (j + 1) * CW], ((1,), (0,))
        ).astype(BF16)

    Reduce(r.part, *r.reduce).run(mlp_part)
    top_own_load.wait()
    v = r.reduce[3][...]
    z = norm_scale(v)
    dy = r.top_own[...].astype(F32)
    g = r.mlp_gain[...]
    r.d_mlp[rows_of(t, OWN), :] = norm_back(v, z, g, dy).astype(BF16)
    r.result_own[...] = (r.hidden_own[...] + v * z * g).astype(BF16)
    mlp_gain_grad = jnp.sum(dy * v * z, axis=0, keepdims=True)
    gather_rows(r.d_mlp, r.gather)
    top_copies = begin(FF.top_half, r.d_mlp, r.top_half)

    def hidden_units_back(j, _):
        cols = pl.ds(pl.multiple_of(j * CW, CW), CW)
        d_mixed = dot(r.d_mlp[...], r.down_vmem[cols, :], ((1,), (1,)))
        r.d_up[:, cols] = (d_mixed * r.act[:, cols]).astype(BF16)
        r.d_gate[:, cols] = (d_mixed * r.slope[:, cols]).astype(BF16)
        return 0

    lax.fori_loop(0, NC, hidden_units_back, 0)
    right_copies = begin(FF.gate_right, r.d_gate, r.gate_right) + begin(FF.up_right, r.d_up, r.up_right)
    wait(features_copies)
    features_copies = begin(FF.features_rest, r.features_half, r.features_rest)

    def back_part(j):
        rows = pl.ds(j * CW, CW)
        r.part[:, j * CW : (j + 1) * CW] = (
            dot(r.d_gate[...], r.gate_vmem[rows, :], ((1,), (1,)))
            + dot(r.d_up[...], r.up_vmem[rows, :], ((1,), (1,)))
        ).astype(BF16)

    Reduce(r.part, *r.reduce).run(back_part)
    wait(hidden_copies)
    hidden_copies = begin(FF.hidden_rest, r.hidden_half, r.hidden_rest)
    dy = r.top_own[...].astype(F32) + r.reduce[3][...]
    v = r.attn_own[...]
    a = norm_scale(v)
    g = r.attn_gain[...]
    r.d_attn[rows_of(t, OWN), :] = norm_back(v, a, g, dy).astype(BF16)
    r.d_hidden_own[...] = dy
    row = lax.broadcasted_iota(jnp.int32, (8, D), 0)
    attn_grad = jnp.sum(dy * v * a, axis=0, keepdims=True)
    r.gain_rows[...] = jnp.where(row == 0, attn_grad, mlp_gain_grad)
    gather_rows(r.d_attn, r.gather)
    r.d_attended[...] = dot(r.d_attn[...], r.out_vmem[...], ((1,), (1,))).astype(BF16)
    wait(right_copies + hidden_copies + features_copies + attended_copies)
    wait(mixed_copies + top_copies + saved)


WIDE = jax.ShapeDtypeStruct((T, D), BF16)
NARROW = jax.ShapeDtypeStruct((T, 4 * HD), BF16)
HALVES = jax.ShapeDtypeStruct((4, T, D // 2), BF16)
FF_MOVES = dict(
    features_half=half_move(WIDE, "x"),
    features_rest=core_move(HALVES),
    attended_all=full_move(NARROW, "z"),
    hidden_half=half_move(WIDE, "z"),
    hidden_rest=core_move(HALVES),
    gate_right=quarter_move(WIDE, "z"),
    up_right=quarter_move(WIDE, "z"),
    mixed_right=quarter_move(WIDE, "x"),
    top_half=half_move(WIDE, "x"),
)
FF = Names(**{name: name for name in FF_MOVES})
FF_PEERS = distinct(
    [CORE, FAR]
    + [(0, dy, dx, 0, 0) for dy in range(2) for dx in range(4) if dy or dx]
    + peers_of(FF_MOVES)
)


def attend_scratch():
    dma = pltpu.SemaphoreType.DMA
    return [
        pltpu.VMEM((8, 8, T), F32),
        pltpu.VMEM((T, 4 * HD), BF16),
        pltpu.VMEM((T, 4 * HD), BF16),
        pltpu.VMEM((2, T, HD), F32),
        pltpu.VMEM((T, HD), F32),
        pltpu.VMEM((T, HD), F32),
        pltpu.VMEM((4, T, HD), BF16),
        dma((4, 4)),
        dma((4, 4)),
        dma((4,)),
        dma((4,)),
        dma((8,)),
        dma((8,)),
        dma((2,)),
        dma((2,)),
        dma((4,)),
        dma((4,)),
    ]


def forward(small, large):
    weight, wide = pltpu.VMEM((D, D), BF16), pltpu.VMEM((T, D), BF16)
    own, tall = pltpu.VMEM((OWN, D), F32), pltpu.VMEM((T, D), F32)
    own_low = pltpu.VMEM((OWN, D), BF16)
    saved = dict(
        q_head=((4 * T, HD), BF16),
        k_head=((8 * T, HD), BF16),
        v_head=((8 * T, HD), BF16),
        probs=((4, T, 8 * T), BF16),
        q_raw=((T, 4 * HD), F32),
        k_raw=((T, 4 * HD), F32),
        scales=((T, HD), F32),
    )
    scratch = dict(
        out_vmem=pltpu.VMEM((4 * HD, D), BF16),
        gate_vmem=weight,
        up_vmem=weight,
        down_vmem=weight,
        features_own=own_low,
        top_own=own_low,
        part=wide,
        hidden=wide,
        act=tall,
        slope=tall,
        d_gate=wide,
        d_up=wide,
        d_mlp=wide,
        mixed=wide,
        attn_own=own,
        hidden_own=own,
        load_sems=pltpu.SemaphoreType.DMA((32,)),
        reduce=REDUCE_SCRATCH,
        gather=GATHER_SCRATCH,
        moves=move_scratch(FF_MOVES),
        features_vmem=wide,
        value=pltpu.VMEM((T, 4 * HD), BF16),
        attended=pltpu.VMEM((T, 4 * HD), BF16),
        attend=attend_scratch(),
        **{name: pltpu.VMEM(*saved[name]) for name in saved},
    )
    outs = dict(
        d_attended=((T, 4 * HD), BF16),
        d_hidden_own=((OWN, D), F32),
        result_own=((OWN, D), BF16),
        gain_rows=((8, D), F32),
        d_attn=((T, D), BF16),
    )
    large_outs = {name: move.out for name, move in FF_MOVES.items()}
    large_outs |= {name + "_out": out for name, out in saved.items()}
    return run_kernel(forward_kernel, 1, small, large, outs, large_outs, scratch, 62)


def row_device(yl, x):
    return {"ctx": yl * 4 + x}


ATTEND_PEERS = [CORE, FAR] + [(0, dy, dx, 0, 0) for dy in range(2) for dx in range(4) if dy or dx]


def tensor_sum(own, near, far, send, recv):
    yh, core, _, _ = place()
    copy = remote(own.at[0], near, send.at[0], recv.at[0], peer(*CORE))
    copy.start()
    copy.wait_recv()
    own[1] = own[0] + near[...]
    again = remote(own.at[1], far, send.at[1], recv.at[1], peer(*FAR))
    again.start()
    again.wait_recv()
    total = own[1] + far[...]
    copy.wait_send()
    again.wait_send()
    return total


def two_columns(first, second):
    lane = lax.broadcasted_iota(jnp.int32, (T, HD), 1)
    return jnp.where(lane < HD // 2, first, second)


class Spread:
    def __init__(self, src, dst, sems):
        self.src, self.dst = src, dst
        self.send, self.recv, self.down_send, self.down_recv = sems

    def row_copy(self, s):
        _, _, yl, x = place()
        h = lax.rem(x + s, 4)
        return remote(
            self.src.at[:, pl.ds(pl.multiple_of(h * HD, HD), HD)],
            self.dst.at[rows_of(yl * 4 + x, T)],
            self.send.at[s],
            self.recv.at[s],
            row_device(yl, h),
        )

    def down_copy(self, s):
        _, _, yl, x = place()
        h = lax.rem(x + s, 4)
        return remote(
            self.src.at[:, pl.ds(pl.multiple_of(h * HD, HD), HD)],
            self.dst.at[rows_of(x, T)],
            self.down_send.at[s],
            self.down_recv.at[s],
            row_device(1, h),
        )


def keep_own(src, dst, block):
    _, _, _, x = place()
    dst[rows_of(block, T), :] = src[:, pl.ds(pl.multiple_of(x * HD, HD), HD)]


def attend_part(
    project, q_raw, k_raw, value, seg, q_gain, k_gain,
    attended, q_head, k_head, v_head, probs_out, scale_out,
    seg_all, q_low, k_low, sums, near, far, result,
    v_sems, k_sems, q_send, q_recv, s_send, s_recv, sum_send, sum_recv, a_send, a_recv,
    load_weights,
):
    yh, core, yl, x = place()
    me = yl * 4 + x
    v_sems = [v_sems.at[i] for i in range(4)]
    k_sems = [k_sems.at[i] for i in range(4)]
    values = Spread(value, v_head, v_sems)
    keys = Spread(k_low, k_head, k_sems)

    @pl.when(yl == 0)
    def _():
        for s in range(4):
            values.down_copy(s).start()

    for s in (1, 2, 3):
        values.row_copy(s).start()
    seg_all[me] = jnp.broadcast_to(seg[...].astype(F32), (8, T))

    def seg_copy(s):
        dx, dy = s % 4, s // 4
        to = row_device(lax.rem(yl + dy, 2), lax.rem(x + dx, 4))
        return remote(seg_all.at[me], seg_all.at[me], s_send.at[s], s_recv.at[s], to)

    for s in range(1, 8):
        seg_copy(s).start()

    project()
    qr, kr = q_raw[...], k_raw[...]
    sums[0] = two_columns(
        jnp.sum(qr * qr, axis=1, keepdims=True), jnp.sum(kr * kr, axis=1, keepdims=True)
    )
    keep_own(value, v_head, me)
    weights = load_weights()
    scales = lax.rsqrt(tensor_sum(sums, near, far, sum_send, sum_recv) / D + EPS)
    scale_out[...] = scales
    k_low[...] = (kr * scales[:, HD // 2 : HD // 2 + 1] * k_gain[...]).astype(BF16)

    @pl.when(yl == 0)
    def _():
        for s in range(4):
            keys.down_copy(s).start()

    for s in (1, 2, 3):
        keys.row_copy(s).start()
    q_low[...] = (qr * scales[:, :1] * q_gain[...]).astype(BF16)

    def q_copy(s):
        h = lax.rem(x + s, 4)
        return remote(
            q_low.at[:, pl.ds(pl.multiple_of(h * HD, HD), HD)],
            q_head.at[rows_of(x, T)],
            q_send.at[s],
            q_recv.at[s],
            row_device(yl, h),
        )

    for s in (1, 2, 3):
        q_copy(s).start()
    keep_own(k_low, k_head, me)
    keep_own(q_low, q_head, x)
    for s in range(1, 8):
        seg_copy(s).wait()
    for s in (1, 2, 3):
        values.row_copy(s).wait()
        keys.row_copy(s).wait()
        q_copy(s).wait()

    @pl.when(yl == 0)
    def _():
        for s in range(4):
            values.down_copy(s).wait_send()
            keys.down_copy(s).wait_send()

    @pl.when(yl == 1)
    def _():
        for s in range(4):
            values.down_copy(s).wait_recv()
            keys.down_copy(s).wait_recv()

    lane = lax.broadcasted_iota(jnp.int32, (8, HD), 0)
    pick = jnp.where(lane == 0, 1.0, 0.0)

    def attend(row, i):
        blocks = row * 4 + i + 1
        width = blocks * T
        q = q_head[i * T : (i + 1) * T, :]
        scores = dot(q, k_head[:width, :], ((1,), (1,))) * HD ** (-0.5)
        own_seg = dot(seg_all[row * 4 + i], pick, ((0,), (0,)))[:, :1]
        seg_keys = jnp.concatenate([seg_all[b, :1, :] for b in range(blocks)], axis=1)
        q_place = lax.broadcasted_iota(jnp.int32, (T, width), 0) + (blocks - 1) * T
        k_place = lax.broadcasted_iota(jnp.int32, (T, width), 1)
        counted = (k_place <= q_place) & (seg_keys == own_seg)
        scores = jnp.where(counted, scores, -1e30)
        exps = jnp.exp(scores - jnp.max(scores, axis=1, keepdims=True))
        probs = (exps * (1.0 / jnp.sum(exps, axis=1, keepdims=True))).astype(BF16)
        probs_out[i, :, :width] = probs
        result[i] = dot(probs, v_head[:width, :], ((1,), (0,))).astype(BF16)

    def back_copy(i):
        return remote(
            result.at[i],
            attended.at[:, pl.ds(pl.multiple_of(x * HD, HD), HD)],
            a_send.at[i],
            a_recv.at[x],
            row_device(yl, i),
        )

    for i in range(4):
        for row in range(2):

            @pl.when(yl == row)
            def _():
                attend(row, i)

        @pl.when(x == i)
        def _():
            attended[:, i * HD : (i + 1) * HD] = result[i]

        @pl.when(x != i)
        def _():
            back_copy(i).start()

    for h in range(4):

        @pl.when(x != h)
        def _():
            back_copy(h).wait_send()
            remote(
                result.at[h],
                attended.at[:, h * HD : (h + 1) * HD],
                a_send.at[h],
                a_recv.at[h],
                row_device(yl, h),
            ).wait_recv()
    return weights


def product_rows(left, right):
    return dot(
        left.reshape(4 * T, left.shape[2]), right.reshape(4 * T, right.shape[2]), ((0,), (0,))
    ).astype(BF16)


def blocks_out(partial, slots, send, recv, axis):
    me = spot(axis)
    return [
        remote(
            partial.at[lax.rem(me + s, 4)], slots.at[s - 1], send.at[s - 1], recv.at[s - 1],
            peer(*along(axis, s)),
        )
        for s in (1, 2, 3)
    ]


def add_blocks(total, partial, slots, axis):
    me = spot(axis)
    for y in range(2):
        for j in range(4):
            block = partial[me, y, j].astype(F32)
            for s in range(3):
                block += slots[s, y, j].astype(F32)
            total[y, j] = block.astype(BF16)


HALF_GRID = (2, 4, 64)
BACK_MOVES = dict(
    attn_left=quarter_move(WIDE, "z"),
    q_right=quarter_move(NARROW, "x"),
    k_right=quarter_move(NARROW, "x"),
    v_right=quarter_move(NARROW, "x"),
    mlp_in=final_move(jax.ShapeDtypeStruct(HALF_GRID + (1024,), BF16), "z"),
    mlp_down=final_move(jax.ShapeDtypeStruct(HALF_GRID + (512,), BF16), "x"),
    qkv=final_move(jax.ShapeDtypeStruct(HALF_GRID + (384,), BF16), "x"),
    out=final_move(jax.ShapeDtypeStruct(HALF_GRID + (512,), BF16), "x"),
    tiles=rank_move(jax.ShapeDtypeStruct((32, 16, HD), F32)),
)
BACK = Names(**{name: name for name in BACK_MOVES})
BACK_PEERS = distinct(ATTEND_PEERS + peers_of(BACK_MOVES))


def back_scratch():
    dma = pltpu.SemaphoreType.DMA

    def vmem(*shape, kind=BF16):
        return pltpu.VMEM(shape, kind)

    rows = (2, 4, 64)
    return dict(
        q_head=vmem(4 * T, HD),
        k_head=vmem(8 * T, HD),
        v_head=vmem(8 * T, HD),
        probs=vmem(2, T, 8 * T),
        q_raw=vmem(T, 4 * HD, kind=F32),
        k_raw=vmem(T, 4 * HD, kind=F32),
        scales=vmem(T, HD, kind=F32),
        wq=vmem(D, 4 * HD),
        wk=vmem(D, 4 * HD),
        wv=vmem(D, 4 * HD),
        left=vmem(2, 4, T, D // 2),
        top=vmem(2, 4, T, D // 2),
        gate_right=vmem(4, T, 512),
        up_right=vmem(4, T, 512),
        mixed_right=vmem(4, T, 512),
        attn_left=vmem(4, T, 512),
        attended_all=vmem(4, T, 512),
        q_right=vmem(4, T, HD),
        k_right=vmem(4, T, HD),
        v_right=vmem(4, T, HD),
        in_part=vmem(4, *rows, 1024),
        in_slots=vmem(2, *rows, 1024),
        in_across=vmem(2, 2, 2, 64, 1024),
        in_sum=vmem(*rows, 1024),
        down_part=vmem(4, *rows, 512),
        down_slots=vmem(3, *rows, 512),
        down_sum=vmem(*rows, 512),
        qkv_part=vmem(4, *rows, 384),
        qkv_slots=vmem(3, *rows, 384),
        qkv_sum=vmem(*rows, 384),
        out_part=vmem(*rows, 512),
        tile_part=vmem(32, 16, HD, kind=F32),
        d_q=vmem(T, 4 * HD),
        d_k=vmem(T, 4 * HD),
        d_v=vmem(T, 4 * HD),
        part=vmem(T, D),
        d_out=vmem(4 * T, HD),
        dq_buf=vmem(4, T, HD),
        dk_buf=vmem(8, T, HD),
        dv_buf=vmem(8, T, HD),
        dk_acc=vmem(8 * T, HD, kind=F32),
        dv_acc=vmem(8 * T, HD, kind=F32),
        dq_got=vmem(4, T, HD),
        dk_got=vmem(2, 4, T, HD),
        dv_got=vmem(2, 4, T, HD),
        sums=vmem(2, T, HD, kind=F32),
        near=vmem(T, HD, kind=F32),
        far=vmem(T, HD, kind=F32),
        gain_near=vmem(8, D, kind=F32),
        gain_far=vmem(8, D, kind=F32),
        gain_sum=vmem(8, D, kind=F32),
        load_sems=dma((32,)),
        in_send=dma((2, 4)),
        in_recv=dma((2, 4)),
        across_send=dma((2,)),
        across_recv=dma((2,)),
        down_send=dma((3,)),
        down_recv=dma((3,)),
        qkv_send=dma((3,)),
        qkv_recv=dma((3,)),
        o_send=dma((4,)),
        o_recv=dma((4,)),
        dq_send=dma((4,)),
        dq_recv=dma((4,)),
        dk_send=dma((8,)),
        dk_recv=dma((2, 4)),
        dv_send=dma((8,)),
        dv_recv=dma((2, 4)),
        sum_send=dma((2,)),
        sum_recv=dma((2,)),
        gain_send=dma((2,)),
        gain_recv=dma((2,)),
        top_send=dma((1,)),
        top_recv=dma((1,)),
        result_send=dma((3,)),
        result_recv=dma((3,)),
        reduce=REDUCE_SCRATCH,
        gather=GATHER_SCRATCH,
        moves=move_scratch(BACK_MOVES),
    )


def backward_kernel(r):
    yh, core, yl, x = place()
    t = yh * 2 + core
    scale = HD ** (-0.5)
    greet(BACK_PEERS)
    greeted(BACK_PEERS)

    def begin(name, src, dst):
        return BACK_MOVES[name].start(src, dst, *r.moves[name])

    load_count = iter(range(32))

    def load(src, dst):
        copy = pltpu.make_async_copy(src, dst, r.load_sems.at[next(load_count)])
        copy.start()
        return copy

    def o_copy(s):
        h = lax.rem(x + s, 4)
        return remote(
            r.d_attended.at[:, pl.ds(pl.multiple_of(h * HD, HD), HD)],
            r.d_out.at[rows_of(x, T)],
            r.o_send.at[s],
            r.o_recv.at[s],
            row_device(yl, h),
        )

    for s in (1, 2, 3):
        o_copy(s).start()
    hidden0_load = load(r.hidden_half, r.left.at[core])
    gate_right_load = load(r.gate_right_in, r.gate_right)
    up_right_load = load(r.up_right_in, r.up_right)
    hidden1_load = load(r.hidden_rest, r.left.at[1 - core])
    gain_near_copy = remote(
        r.gains, r.gain_near, r.gain_send.at[0], r.gain_recv.at[0], peer(*CORE)
    )
    gain_near_copy.start()
    top_copy = remote(
        r.top_half, r.top.at[core], r.top_send.at[0], r.top_recv.at[0], peer(*CORE)
    )
    top_copy.start()
    mine, other = rows_of(t, OWN), rows_of((1 - yh) * 2 + core, OWN)
    result_load = load(r.result_own, r.outputs.at[mine])
    result_copies = [
        remote(
            r.result_own, r.outputs.at[mine], r.result_send.at[n], r.result_recv.at[n], to
        )
        for n, to in enumerate((peer(*FAR), peer(*CORE)))
    ]
    for copy in result_copies:
        copy.start()
    attn_left = begin(BACK.attn_left, r.d_attn, r.attn_left)
    keep_own(r.d_attended, r.d_out, x)
    r.dk_acc[...] = jnp.zeros_like(r.dk_acc)
    r.dv_acc[...] = jnp.zeros_like(r.dv_acc)

    wait([hidden0_load, gate_right_load, up_right_load, hidden1_load])
    q_head_load = load(r.q_head_in, r.q_head)
    k_head_load = load(r.k_head_in, r.k_head)
    v_head_load = load(r.v_head_in, r.v_head)
    probs_loads = [load(r.probs_in.at[i], r.probs.at[i]) for i in range(2)]
    q_raw_load = load(r.q_raw_in, r.q_raw)
    k_raw_load = load(r.k_raw_in, r.k_raw)
    scales_load = load(r.scales_in, r.scales)
    mixed_right_load = load(r.mixed_right_in, r.mixed_right)
    top_load = load(r.top_half, r.top.at[core])
    attended_all_load = load(r.attended_all_in, r.attended_all)
    w_query_load = load(r.w_query, r.wq)
    w_key_load = load(r.w_key, r.wk)
    w_value_load = load(r.w_value, r.wv)
    onward, backward_way = along("x", 1), along("x", 3)
    after, before = lax.rem(x + 1, 4), lax.rem(x + 3, 4)
    opposite = lax.rem(x + 2, 4)
    across = [
        remote(
            r.in_part.at[opposite, :, pl.ds(2 * n, 2)], r.in_across.at[n], r.across_send.at[n],
            r.across_recv.at[n], peer(*way),
        )
        for n, way in enumerate((onward, backward_way))
    ]
    in_copies = []

    def in_piece(piece):
        for n, (block, way) in enumerate(((after, onward), (before, backward_way))):
            copy = remote(
                r.in_part.at[block, :, piece], r.in_slots.at[n, :, piece],
                r.in_send.at[n, piece], r.in_recv.at[n, piece], peer(*way),
            )
            copy.start()
            in_copies.append(copy)

    for i in range(4):
        rows = r.left[i // 2, :, :, (i % 2) * 512 : (i % 2 + 1) * 512]
        for n, half in enumerate((r.gate_right, r.up_right)):
            got = product_rows(rows, half[...])
            for y in range(2):
                for j in range(4):
                    r.in_part[j, y, i, :, n * 512 : (n + 1) * 512] = got[
                        (y * 4 + j) * 64 : (y * 4 + j + 1) * 64
                    ]
        if i % 2 == 1:
            across[i // 2].start()
    features0_load = load(r.features_half, r.left.at[core])
    features1_load = load(r.features_rest, r.left.at[1 - core])
    gain_near_copy.wait()
    r.gain_sum[...] = r.gains[...] + r.gain_near[...]
    gain_far_copy = remote(
        r.gain_sum, r.gain_far, r.gain_send.at[1], r.gain_recv.at[1], peer(*FAR)
    )
    gain_far_copy.start()

    for s in (1, 2, 3):
        o_copy(s).wait()
    wait([q_head_load, k_head_load, v_head_load])

    def back(row, i):
        width = (row * 4 + i + 1) * T
        q = r.q_head[i * T : (i + 1) * T, :]
        do = r.d_out[i * T : (i + 1) * T, :]
        probs_low = r.probs[i % 2, :, :width]
        probs = probs_low.astype(F32)
        d_probs = dot(do, r.v_head[:width, :], ((1,), (1,)))
        delta = jnp.sum(probs * d_probs, axis=1, keepdims=True)
        d_scores = (probs * (d_probs - delta)).astype(BF16)
        r.dq_buf[i] = (dot(d_scores, r.k_head[:width, :], ((1,), (0,))) * scale).astype(BF16)
        r.dk_acc[:width, :] += dot(d_scores, q, ((0,), (0,)))
        r.dv_acc[:width, :] += dot(probs_low, do, ((0,), (0,)))

    def dq_copy(i):
        return remote(
            r.dq_buf.at[i], r.dq_got.at[x], r.dq_send.at[i], r.dq_recv.at[x], row_device(yl, i)
        )

    for i in range(4):
        probs_loads[i].wait()
        for row in range(2):

            @pl.when(yl == row)
            def _():
                back(row, i)

        if i < 2:
            probs_loads.append(load(r.probs_in.at[i + 2], r.probs.at[i]))

        @pl.when(x == i)
        def _():
            r.dq_got[i] = r.dq_buf[i]

        @pl.when(x != i)
        def _():
            dq_copy(i).start()

    def kv_copy(j, buf, got, send, recv):
        return remote(
            buf.at[j], got.at[yl, x], send.at[j], recv.at[yl, x], row_device(j // 4, j % 4)
        )

    dk_args = (r.dk_buf, r.dk_got, r.dk_send, r.dk_recv)
    dv_args = (r.dv_buf, r.dv_got, r.dv_send, r.dv_recv)
    for j in range(8):
        r.dk_buf[j] = (r.dk_acc[j * T : (j + 1) * T, :] * scale).astype(BF16)
        r.dv_buf[j] = r.dv_acc[j * T : (j + 1) * T, :].astype(BF16)
        here = (yl == j // 4) & (x == j % 4)

        @pl.when(here)
        def _():
            r.dk_got[j // 4, j % 4] = r.dk_buf[j]
            r.dv_got[j // 4, j % 4] = r.dv_buf[j]

        sends = (yl >= j // 4) & ~here

        @pl.when(sends)
        def _():
            kv_copy(j, *dk_args).start()
            kv_copy(j, *dv_args).start()

    result_copies[0].wait_recv()
    result_copies.append(
        remote(
            r.outputs.at[other],
            r.outputs.at[other],
            r.result_send.at[2],
            r.result_recv.at[2],
            peer(*CORE),
        )
    )
    result_copies[2].start()

    mixed_right_load.wait()
    top_load.wait()
    top_copy.wait()
    for i in range(4):
        left = r.top[i // 2, :, :, (i % 2) * 512 : (i % 2 + 1) * 512]
        r.down_part[i] = product_rows(left, r.mixed_right[...]).reshape(2, 4, 64, 512)
    down_copies = blocks_out(r.down_part, r.down_slots, r.down_send, r.down_recv, "z")
    for copy in down_copies:
        copy.start()
    attended_all_load.wait()
    wait(attn_left)
    r.out_part[...] = product_rows(r.attn_left[...], r.attended_all[...]).reshape(2, 4, 64, 512)

    for n, block in enumerate((after, before)):
        across[n].wait()
        for y in range(2):
            for m in range(2):
                mine_too = r.in_part[block, y, 2 * n + m].astype(F32)
                r.in_part[block, y, 2 * n + m] = (
                    mine_too + r.in_across[n, y, m].astype(F32)
                ).astype(BF16)

    for h in range(4):

        @pl.when(x != h)
        def _():
            dq_copy(h).wait_send()
            remote(
                r.dq_buf.at[h], r.dq_got.at[h], r.dq_send.at[h], r.dq_recv.at[h],
                row_device(yl, h),
            ).wait_recv()

        for row in range(2):
            comes = (row >= yl) & ~((yl == row) & (x == h))

            @pl.when(comes)
            def _():
                for buf, got, send, recv in (dk_args, dv_args):
                    remote(
                        buf.at[0],
                        got.at[row, h],
                        send.at[0],
                        recv.at[row, h],
                        row_device(row, h),
                    ).wait_recv()

    for j in range(8):
        here = (yl == j // 4) & (x == j % 4)
        sends = (yl >= j // 4) & ~here

        @pl.when(sends)
        def _():
            kv_copy(j, *dk_args).wait_send()
            kv_copy(j, *dv_args).wait_send()

    @pl.when(yl == 1)
    def _():
        for h in range(4):
            r.dk_got[0, h] = jnp.zeros((T, HD), BF16)
            r.dv_got[0, h] = jnp.zeros((T, HD), BF16)

    in_piece(0)
    in_piece(1)
    wait([q_raw_load, k_raw_load, scales_load])
    q_sum = jnp.zeros((T, 1), F32)
    k_sum = jnp.zeros((T, 1), F32)
    for h in range(4):
        cols = slice(h * HD, (h + 1) * HD)
        dq = r.dq_got[h].astype(F32)
        dk = r.dk_got[0, h].astype(F32) + r.dk_got[1, h].astype(F32)
        r.d_v[:, cols] = (r.dv_got[0, h].astype(F32) + r.dv_got[1, h].astype(F32)).astype(BF16)
        q_sum += jnp.sum(dq * r.q_raw[:, cols] * r.q_gain[:, cols], axis=1, keepdims=True)
        k_sum += jnp.sum(dk * r.k_raw[:, cols] * r.k_gain[:, cols], axis=1, keepdims=True)
    r.sums[0] = two_columns(q_sum, k_sum)
    v_copies = begin(BACK.v_right, r.d_v, r.v_right)
    total = tensor_sum(r.sums, r.near, r.far, r.sum_send, r.sum_recv)
    qs, ks = r.scales[:, :1], r.scales[:, HD // 2 : HD // 2 + 1]
    q_coef = qs * qs * qs * (total[:, :1] / D)
    k_coef = ks * ks * ks * (total[:, HD // 2 : HD // 2 + 1] / D)
    gain_far_copy.wait()
    both = r.gain_sum[...] + r.gain_far[...]
    tile = []
    for h in range(4):
        cols = slice(h * HD, (h + 1) * HD)
        dq = r.dq_got[h].astype(F32)
        dk = r.dk_got[0, h].astype(F32) + r.dk_got[1, h].astype(F32)
        qr, kr = r.q_raw[:, cols], r.k_raw[:, cols]
        r.d_q[:, cols] = (qs * r.q_gain[:, cols] * dq - qr * q_coef).astype(BF16)
        r.d_k[:, cols] = (ks * r.k_gain[:, cols] * dk - kr * k_coef).astype(BF16)
        tile.append((jnp.sum(dq * qr * qs, axis=0, keepdims=True), jnp.sum(dk * kr * ks, axis=0, keepdims=True)))
    qk_copies = begin(BACK.q_right, r.d_q, r.q_right) + begin(BACK.k_right, r.d_k, r.k_right)
    row = lax.broadcasted_iota(jnp.int32, (8, HD), 0)
    top_tile = jnp.zeros((8, HD), F32)
    for h in range(4):
        top_tile = jnp.where(row == h, tile[h][0], top_tile)
        top_tile = jnp.where(row == h + 4, tile[h][1], top_tile)
    for rank in range(32):
        r.tile_part[rank, :8] = top_tile
        r.tile_part[rank, 8:] = both[:, (rank // 2) * HD : (rank // 2 + 1) * HD]
    tile_copies = begin(BACK.tiles, r.tile_part, r.tiles)

    wait([w_query_load, w_key_load, w_value_load])

    def input_part(j):
        rows = pl.ds(j * CW, CW)
        r.part[:, j * CW : (j + 1) * CW] = (
            dot(r.d_q[...], r.wq[rows, :], ((1,), (1,)))
            + dot(r.d_k[...], r.wk[rows, :], ((1,), (1,)))
            + dot(r.d_v[...], r.wv[rows, :], ((1,), (1,)))
        ).astype(BF16)

    reduce = Reduce(r.part, *r.reduce)
    reduce.begin(input_part)
    out_copies = begin(BACK.out, r.out_part, r.out)
    wait(v_copies + qk_copies)
    in_piece(2)
    in_piece(3)
    features0_load.wait()
    features1_load.wait()
    for i in range(4):
        left = r.left[i // 2, :, :, (i % 2) * 512 : (i % 2 + 1) * 512]
        for n, right in enumerate((r.q_right, r.k_right, r.v_right)):
            r.qkv_part[i, :, :, :, n * HD : (n + 1) * HD] = product_rows(left, right[...]).reshape(
                2, 4, 64, HD
            )
    qkv_copies = blocks_out(r.qkv_part, r.qkv_slots, r.qkv_send, r.qkv_recv, "z")
    for copy in qkv_copies:
        copy.start()
    reduce.finish()
    r.input_grad[mine, :] = (r.d_hidden_own[...] + r.reduce[3][...]).astype(BF16)
    gather = Gather(r.input_grad, r.gather)
    gather.begin()

    wait(down_copies)
    add_blocks(r.down_sum, r.down_part, r.down_slots, "z")
    down_final = begin(BACK.mlp_down, r.down_sum, r.mlp_down)
    wait(in_copies)
    for y in range(2):
        for j in range(4):
            r.in_sum[y, j] = (
                r.in_part[x, y, j].astype(F32)
                + r.in_slots[0, y, j].astype(F32)
                + r.in_slots[1, y, j].astype(F32)
            ).astype(BF16)
    in_final = begin(BACK.mlp_in, r.in_sum, r.mlp_in)
    gather.finish()
    wait(qkv_copies)
    add_blocks(r.qkv_sum, r.qkv_part, r.qkv_slots, "z")
    qkv_final = begin(BACK.qkv, r.qkv_sum, r.qkv)
    result_load.wait()
    result_copies[0].wait_send()
    result_copies[1].wait()
    result_copies[2].wait()
    wait(tile_copies + out_copies + down_final + in_final + qkv_final)


def backward(small, large):
    large_outs = dict(
        outputs=((T, D), BF16),
        tiles=((32, 16, HD), F32),
        mlp_in=(HALF_GRID + (1024,), BF16),
        mlp_down=(HALF_GRID + (512,), BF16),
        qkv=(HALF_GRID + (384,), BF16),
        out=(HALF_GRID + (512,), BF16),
    )
    outs = dict(input_grad=((T, D), BF16))
    return run_kernel(backward_kernel, 6, small, large, outs, large_outs, back_scratch(), 62)


def results_kernel(
    rank_ref, tiles_in, mlp_in_in, mlp_down_in, qkv_in, out_in, outputs_in, input_grad_in,
    outputs, input_grad, query, key, value, out_grad, q_gain, k_gain, attn_gain, gate, up, down,
    mlp_gain, mlp_in, mlp_down, qkv, out, tiles, sems,
):
    pairs = [
        (mlp_in_in, mlp_in), (mlp_down_in, mlp_down), (qkv_in, qkv), (out_in, out),
        (tiles_in, tiles), (outputs_in, outputs), (input_grad_in, input_grad),
    ]
    copies = [pltpu.make_async_copy(a, b, sems.at[n]) for n, (a, b) in enumerate(pairs)]
    for copy in copies:
        copy.start()
    copies[0].wait()
    rank = rank_ref[0]
    for j in range(4):
        both = mlp_in[0, j].astype(F32) + mlp_in[1, j].astype(F32)
        gate[:, j * 512 : (j + 1) * 512] = both[:, :512]
        up[:, j * 512 : (j + 1) * 512] = both[:, 512:]
    wait(copies[1:3])
    for j in range(4):
        down[:, j * 512 : (j + 1) * 512] = mlp_down[0, j].astype(F32) + mlp_down[1, j].astype(F32)
        heads = qkv[0, j].astype(F32) + qkv[1, j].astype(F32)
        for n, grad in enumerate((query, key, value)):
            grad[:, j * HD : (j + 1) * HD] = heads[:, n * HD : (n + 1) * HD]
    copies[3].wait()
    total = out[0, 0].astype(F32)
    for n in range(1, 8):
        total += out[n // 4, n % 4].astype(F32)
    out_grad[...] = total
    copies[4].wait()
    gains = tiles[0]
    for n in range(1, 32):
        gains += tiles[n]
    heads = pltpu.roll(gains[:8], HD - rank * 4, 1)
    q_gain[...] = heads[:4, :4]
    k_gain[...] = heads[4:, :4]
    columns = pltpu.roll(gains[8:], HD - lax.rem(rank, 2) * 64, 1)
    attn_gain[...] = columns[:1, :64]
    mlp_gain[...] = columns[1:2, :64]
    wait(copies[5:])


def results(got):
    rank = lax.axis_index("dp") * 8 + lax.axis_index("ctx")
    narrow, wide, low = ((64, 4 * HD), F32), ((64, D), F32), ((T, D), BF16)
    outs = [low, low, narrow, narrow, narrow, narrow, ((4, 4), F32), ((4, 4), F32), ((1, 64), F32)]
    outs += [wide, wide, wide, ((1, 64), F32)]
    return pl.pallas_call(
        results_kernel,
        name=results.__name__,
        out_shape=[jax.ShapeDtypeStruct(*out) for out in outs],
        in_specs=[pl.BlockSpec(memory_space=pltpu.SMEM)] + [ANY] * 7,
        out_specs=[ANY] * 2 + [VMEM] * 11,
        scratch_shapes=[
            pltpu.VMEM(HALF_GRID + (1024,), BF16),
            pltpu.VMEM(HALF_GRID + (512,), BF16),
            pltpu.VMEM(HALF_GRID + (384,), BF16),
            pltpu.VMEM(HALF_GRID + (512,), BF16),
            pltpu.VMEM((32, 16, HD), F32),
            pltpu.SemaphoreType.DMA((7,)),
        ],
        compiler_params=pltpu.CompilerParams(vmem_limit_bytes=40 * 2**20),
    )(
        rank.reshape(1), got.tiles, got.mlp_in, got.mlp_down, got.qkv, got.out,
        got.outputs, got.input_grad,
    )


def per_device(
    inputs, segments, w_query, w_key, w_value, w_out, q_gain, k_gain, attn_gain,
    w_gate, w_up, w_down, mlp_gain, cotangent,
):
    features, top = inputs[0], cotangent[0]
    q_row, k_row = q_gain.reshape(1, -1), k_gain.reshape(1, -1)
    a_row, m_row = attn_gain.reshape(1, -1), mlp_gain.reshape(1, -1)

    ff = forward(
        dict(seg=segments, q_gain=q_row, k_gain=k_row, attn_gain=a_row, mlp_gain=m_row),
        dict(
            features=features, cotangent=top, w_query=w_query, w_key=w_key, w_value=w_value,
            w_out=w_out, w_gate=w_gate, w_up=w_up, w_down=w_down,
        ),
    )
    got = backward(
        dict(
            d_attended=ff.d_attended, q_gain=q_row, k_gain=k_row, gains=ff.gain_rows,
            d_hidden_own=ff.d_hidden_own, result_own=ff.result_own,
        ),
        dict(
            q_head_in=ff.q_head_out, k_head_in=ff.k_head_out, v_head_in=ff.v_head_out,
            probs_in=ff.probs_out, q_raw_in=ff.q_raw_out, k_raw_in=ff.k_raw_out,
            scales_in=ff.scales_out,
            w_query=w_query, w_key=w_key, w_value=w_value,
            hidden_half=ff.hidden_half, hidden_rest=ff.hidden_rest, gate_right_in=ff.gate_right,
            up_right_in=ff.up_right, top_half=ff.top_half, mixed_right_in=ff.mixed_right,
            features_half=ff.features_half, features_rest=ff.features_rest,
            attended_all_in=ff.attended_all, d_attn=ff.d_attn,
        ),
    )
    (
        outputs, input_grad, query, key, value, out_grad, q_gain_grad, k_gain_grad,
        attn_gain_grad, gate, up, down, mlp_gain_grad,
    ) = results(got)
    return (
        outputs[None],
        input_grad[None],
        query,
        key,
        value,
        out_grad.T,
        q_gain_grad,
        k_gain_grad,
        attn_gain_grad[0],
        gate,
        up,
        down.T,
        mlp_gain_grad[0],
    )


def solution(mesh):
    rows, full = P("dp", "ctx", None), P()
    down, across = P("tensor", None), P(None, "tensor")
    in_specs = (
        rows, P("dp", "ctx"), across, across, across, down, down, down, full,
        across, across, down, full, rows,
    )
    split = ("dp", "ctx")
    out_specs = (
        rows, rows, P(split, "tensor"), P(split, "tensor"), P(split, "tensor"), P("tensor", split),
        P("tensor", split), P("tensor", split), P(split), P(split, "tensor"), P(split, "tensor"),
        P("tensor", split), P(split),
    )
    return jax.shard_map(
        per_device, mesh=mesh, in_specs=in_specs, out_specs=out_specs, check_vma=False
    )
```

```python
import functools
import jax
import jax.numpy as jnp
from jax import lax
from jax.experimental import pallas as pl
from jax.experimental.pallas import tpu as pltpu
from jax.sharding import PartitionSpec as P

MESH = pl.DeviceIdType.MESH
F32 = jnp.float32
BF16 = jnp.bfloat16
EPS = 1e-06
T = 256
D = 2048
HD = 128
OWN = 64
NC = 4
CW = D // NC
VMEM = pl.BlockSpec(memory_space=pltpu.VMEM)
ANY = pl.BlockSpec(memory_space=pltpu.HBM)


def place():
    t = lax.axis_index("tensor")
    ctx = lax.axis_index("ctx")
    return t // 2, lax.rem(t, 2), ctx // 4, lax.rem(ctx, 4)


def peer(dz=0, dy=0, dx=0, dh=0, dc=0):
    yh, core, yl, x = place()
    z = lax.rem(lax.axis_index("dp") + dz, 4)
    ctx = lax.rem(yl + dy, 2) * 4 + lax.rem(x + dx, 4)
    return {"dp": z, "ctx": ctx, "tensor": lax.rem(yh + dh, 2) * 2 + lax.rem(core + dc, 2)}


CORE, FAR = (0, 0, 0, 0, 1), (0, 0, 0, 1, 0)


def along(axis, s):
    return (s, 0, 0, 0, 0) if axis == "z" else (0, 0, s, 0, 0)


def spot(axis):
    return lax.axis_index("dp") if axis == "z" else place()[3]


def remote(src, dst, send_sem, recv_sem, device):
    return pltpu.make_async_remote_copy(
        src_ref=src,
        dst_ref=dst,
        send_sem=send_sem,
        recv_sem=recv_sem,
        device_id=device,
        device_id_type=MESH,
    )


def greet(offsets):
    barrier = pltpu.get_barrier_semaphore()
    for offset in offsets:
        pl.semaphore_signal(barrier, inc=1, device_id=peer(*offset), device_id_type=MESH)


def greeted(offsets):
    pl.semaphore_wait(pltpu.get_barrier_semaphore(), len(offsets))


def wait(copies):
    for copy in copies:
        copy.wait()


def dot(a, b, dims):
    return lax.dot_general(a, b, (dims, ((), ())), preferred_element_type=F32)


def rows_of(index, count):
    return pl.ds(pl.multiple_of(index * count, count), count)


class Move:
    def __init__(self, source, shape, offsets, pairs):
        self.source, self.shape, self.offsets, self.pairs = source, shape, offsets, pairs
        self.out = (shape, source.dtype)

    def scratch(self):
        dma = pltpu.SemaphoreType.DMA
        return [dma((len(self.offsets),)), dma((len(self.offsets),)), dma((1,))]

    def copies(self, src, dst, send, recv, local):
        made = []
        at = 0
        for a, b, offset in self.pairs(src, dst):
            if offset is None:
                made.append(pltpu.make_async_copy(a, b, local.at[0]))
            else:
                made.append(remote(a, b, send.at[at], recv.at[at], peer(*offset)))
                at += 1
        return made

    def start(self, src, dst, *sems):
        copies = self.copies(src, dst, *sems)
        for copy in copies:
            copy.start()
        return copies


def half_move(a, axis):
    half = a.shape[1] // 2
    offsets = [along(axis, s) for s in (1, 2, 3)]

    def pairs(src, dst):
        mine = src.at[:, pl.ds(pl.multiple_of(place()[1] * half, half), half)]
        me = spot(axis)
        return [(mine, dst.at[me], offset) for offset in offsets + [None]]

    return Move(a, (4, T, half), offsets, pairs)


def core_move(a):
    return Move(a, a.shape, [CORE], lambda src, dst: [(src, dst, CORE)])


def quarter_move(b, axis):
    width = b.shape[1] // 4
    offsets = [along(axis, s) for s in (1, 2, 3)]

    def pairs(src, dst):
        me = spot(axis)

        def part(s):
            return src.at[:, pl.ds(pl.multiple_of(lax.rem(me + s, 4) * width, width), width)]

        made = [(part(s), dst.at[me], along(axis, s)) for s in (1, 2, 3)]
        return made + [(part(0), dst.at[me], None)]

    return Move(b, (4, T, width), offsets, pairs)


def full_move(b, axis):
    offsets = [along(axis, s) for s in (1, 2, 3)]

    def pairs(src, dst):
        return [(src, dst.at[spot(axis)], offset) for offset in offsets + [None]]

    return Move(b, (4,) + b.shape, offsets, pairs)


def block_move(p, axis):
    offsets = [along(axis, s) for s in (1, 2, 3)]

    def pairs(src, dst):
        me = spot(axis)
        made = [(src.at[lax.rem(me + s, 4)], dst.at[me], along(axis, s)) for s in (1, 2, 3)]
        return made + [(src.at[me], dst.at[me], None)]

    return Move(p, p.shape, offsets, pairs)


def final_move(p, axis):
    steps = [(dy, s) for dy in range(2) for s in range(4) if dy or s]

    def offset(dy, s):
        return (s, dy, 0, 0, 0) if axis == "z" else (0, dy, s, 0, 0)

    def pairs(src, dst):
        yl, me = place()[2], spot(axis)
        made = [
            (src.at[lax.rem(yl + dy, 2), lax.rem(me + s, 4)], dst.at[yl, me], offset(dy, s))
            for dy, s in steps
        ]
        return made + [(src.at[yl, me], dst.at[yl, me], None)]

    return Move(p, p.shape, [offset(*step) for step in steps], pairs)


class Names:
    def __init__(self, **names):
        self.__dict__.update(names)


def run_kernel(body, collective_id, small, large, small_outs, large_outs, scratch, vmem):
    ins = [jax.tree.flatten(small), jax.tree.flatten(large)]
    shapes = [
        jax.tree.flatten({name: jax.ShapeDtypeStruct(*out) for name, out in outs.items()})
        for outs in (small_outs, large_outs)
    ]
    own = jax.tree.flatten(scratch)

    def kernel(*refs):
        names, at = {}, 0
        for leaves, tree in ins + shapes + [own]:
            names.update(tree.unflatten(refs[at : at + len(leaves)]))
            at += len(leaves)
        body(Names(**names))

    got = pl.pallas_call(
        kernel,
        name=body.__name__,
        out_shape=shapes[0][0] + shapes[1][0],
        in_specs=[VMEM] * len(ins[0][0]) + [ANY] * len(ins[1][0]),
        out_specs=[VMEM] * len(shapes[0][0]) + [ANY] * len(shapes[1][0]),
        scratch_shapes=own[0],
        compiler_params=pltpu.CompilerParams(
            collective_id=collective_id, has_side_effects=True, vmem_limit_bytes=vmem * 2**20
        ),
    )(*ins[0][0], *ins[1][0])
    n = len(shapes[0][0])
    return Names(**shapes[0][1].unflatten(got[:n]), **shapes[1][1].unflatten(got[n:]))


def move_scratch(moves):
    return {name: move.scratch() for name, move in moves.items()}


def peers_of(moves):
    return [offset for move in moves.values() for offset in move.offsets]


def distinct(offsets):
    return list(dict.fromkeys(offsets))


class Reduce:
    def __init__(self, part, near, far, out_low, acc, *sems):
        self.part, self.near, self.far, self.out_low, self.acc = part, near, far, out_low, acc
        self.sems = sems
        self.near_copies, self.far_copies = [], []

    def send(self, j):
        yh, core, _, _ = place()
        near_send, near_recv, _, _ = self.sems
        cols = pl.ds(j * CW, CW)
        for slot, row in ((0, (1 - yh) * 2 + (1 - core)), (1, yh * 2 + (1 - core))):
            copy = remote(
                self.part.at[rows_of(row, OWN), cols],
                self.near.at[slot, :, cols],
                near_send.at[slot, j],
                near_recv.at[slot, j],
                peer(*CORE),
            )
            copy.start()
            self.near_copies.append(copy)

    def forward(self, j):
        yh, core, _, _ = place()
        _, _, far_send, far_recv = self.sems
        cols = pl.ds(j * CW, CW)
        self.near_copies[2 * j].wait_recv()
        self.out_low[:, cols] = (
            self.part[rows_of((1 - yh) * 2 + core, OWN), cols].astype(F32)
            + self.near[0, :, cols].astype(F32)
        ).astype(BF16)
        copy = remote(
            self.out_low.at[:, cols], self.far.at[:, cols], far_send.at[j], far_recv.at[j],
            peer(*FAR),
        )
        copy.start()
        self.far_copies.append(copy)

    def finish(self):
        yh, core, _, _ = place()
        for j in range(NC):
            cols = pl.ds(j * CW, CW)
            self.near_copies[2 * j + 1].wait_recv()
            self.acc[:, cols] = self.part[rows_of(yh * 2 + core, OWN), cols].astype(
                F32
            ) + self.near[1, :, cols].astype(F32)
        for j in range(NC):
            cols = pl.ds(j * CW, CW)
            self.far_copies[j].wait_recv()
            self.acc[:, cols] = self.acc[:, cols] + self.far[:, cols].astype(F32)
        for copy in self.near_copies + self.far_copies:
            copy.wait_send()

    def begin(self, produce):
        for j in range(NC):
            produce(j)
            self.send(j)
            if j > 0:
                self.forward(j - 1)
        self.forward(NC - 1)

    def run(self, produce):
        self.begin(produce)
        self.finish()


class Gather:
    def __init__(self, out, sems):
        self.out, self.sems = out, sems

    def begin(self):
        yh, core, _, _ = place()
        own_send, own_recv, far_send, far_recv, _, _ = self.sems
        mine = rows_of(yh * 2 + core, OWN)
        self.far_copies, self.own_copies, self.on_copies = [], [], []
        for j in range(NC):
            block = self.out.at[mine, pl.ds(j * CW, CW)]
            copy = remote(block, block, far_send.at[j], far_recv.at[j], peer(*FAR))
            copy.start()
            self.far_copies.append(copy)
        for j in range(NC):
            block = self.out.at[mine, pl.ds(j * CW, CW)]
            copy = remote(block, block, own_send.at[j], own_recv.at[j], peer(*CORE))
            copy.start()
            self.own_copies.append(copy)

    def finish(self, use=lambda j: None):
        yh, core, _, _ = place()
        on_send, on_recv = self.sems[4:]
        other = rows_of((1 - yh) * 2 + core, OWN)

        def whole(j):
            self.own_copies[j].wait_recv()
            self.on_copies[j].wait_recv()
            use(j)

        for j in range(NC):
            self.far_copies[j].wait_recv()
            block = self.out.at[other, pl.ds(j * CW, CW)]
            copy = remote(block, block, on_send.at[j], on_recv.at[j], peer(*CORE))
            copy.start()
            self.on_copies.append(copy)
            if j > 0:
                whole(j - 1)
        whole(NC - 1)
        for copy in self.far_copies + self.own_copies + self.on_copies:
            copy.wait_send()


def gather_rows(out, sems, use=lambda j: None):
    gather = Gather(out, sems)
    gather.begin()
    gather.finish(use)


REDUCE_SCRATCH = [
    pltpu.VMEM((2, OWN, D), BF16),
    pltpu.VMEM((OWN, D), BF16),
    pltpu.VMEM((OWN, D), BF16),
    pltpu.VMEM((OWN, D), F32),
    pltpu.SemaphoreType.DMA((2, NC)),
    pltpu.SemaphoreType.DMA((2, NC)),
    pltpu.SemaphoreType.DMA((NC,)),
    pltpu.SemaphoreType.DMA((NC,)),
]
GATHER_SCRATCH = [pltpu.SemaphoreType.DMA((NC,))] * 6


def norm_scale(v):
    return lax.rsqrt(jnp.mean(v * v, axis=1, keepdims=True) + EPS)


def norm_back(v, r, g, dy):
    column_sum = jnp.sum(dy * g * v, axis=1, keepdims=True)
    return r * g * dy - v * (r * r * r) * (column_sum / D)


def input_tile(ref, j):
    return ref[:, pl.ds(pl.multiple_of(j * CW, CW), CW)]


def forward_kernel(r):
    yh, core, _, _ = place()
    t = yh * 2 + core
    greet(FF_PEERS)

    def begin(name, src, dst):
        return FF_MOVES[name].start(src, dst, *r.moves[name])

    load_count = iter(range(32))

    def load(src, dst):
        copy = pltpu.make_async_copy(src, dst, r.load_sems.at[next(load_count)])
        copy.start()
        return copy

    width = 4 * HD
    places = [r.down_vmem.at[:, pl.ds(n * width, width)] for n in range(3)]
    features_load = load(r.features, r.features_vmem)
    value_load = load(r.w_value, places[0])
    key_load = load(r.w_key, places[1])
    query_load = load(r.w_query, places[2])
    features_own_load = load(r.features.at[rows_of(t, OWN)], r.features_own)
    top_own_load = load(r.cotangent.at[rows_of(t, OWN)], r.top_own)

    def projected(n):
        return dot(
            r.features_vmem[...], r.down_vmem[:, n * width : (n + 1) * width], ((1,), (0,))
        )

    wait([features_load, value_load])
    r.value[...] = projected(0).astype(BF16)
    greeted(FF_PEERS)
    features_copies = begin(FF.features_half, r.features_vmem, r.features_half)

    def project():
        key_load.wait()
        r.k_raw[...] = projected(1)
        query_load.wait()
        r.q_raw[...] = projected(2)

    weights = attend_part(
        project, r.q_raw, r.k_raw, r.value, r.seg, r.q_gain, r.k_gain,
        r.attended, r.q_head, r.k_head, r.v_head, r.probs, r.scales, *r.attend,
        lambda: [
            load(r.w_out, r.out_vmem),
            load(r.w_gate, r.gate_vmem),
            load(r.w_up, r.up_vmem),
            load(r.w_down, r.down_vmem),
        ],
    )
    saved = [
        load(r.q_head, r.q_head_out),
        load(r.k_head, r.k_head_out),
        load(r.v_head, r.v_head_out),
        load(r.probs, r.probs_out),
        load(r.q_raw, r.q_raw_out),
        load(r.k_raw, r.k_raw_out),
        load(r.scales, r.scales_out),
    ]
    weights[0].wait()

    def attn_part(j):
        r.part[:, j * CW : (j + 1) * CW] = dot(
            r.attended[...], r.out_vmem[:, j * CW : (j + 1) * CW], ((1,), (0,))
        ).astype(BF16)

    Reduce(r.part, *r.reduce).run(attn_part)
    features_own_load.wait()
    v = r.reduce[3][...]
    state = r.features_own[...].astype(F32) + v * norm_scale(v) * r.attn_gain[...]
    r.hidden[rows_of(t, OWN), :] = state.astype(BF16)
    r.attn_own[...] = v
    r.hidden_own[...] = state
    attended_copies = begin(FF.attended_all, r.attended, r.attended_all)
    wait(weights[1:])

    def hidden_units(k):
        rows = pl.ds(k * CW, CW)

        def some(j, _):
            cols = pl.ds(pl.multiple_of(j * CW, CW), CW)
            gate = dot(r.hidden[:, rows], r.gate_vmem[rows, cols], ((1,), (0,)))
            upward = dot(r.hidden[:, rows], r.up_vmem[rows, cols], ((1,), (0,)))
            if k > 0:
                gate += r.act[:, cols]
                upward += r.slope[:, cols]
            if k < NC - 1:
                r.act[:, cols] = gate
                r.slope[:, cols] = upward
            else:
                sigma = jax.nn.sigmoid(gate)
                activated = gate * sigma
                r.mixed[:, cols] = (activated * upward).astype(BF16)
                r.act[:, cols] = activated
                r.slope[:, cols] = upward * sigma * (1.0 + gate * (1.0 - sigma))
            return 0

        lax.fori_loop(0, NC, some, 0)

    gather_rows(r.hidden, r.gather, hidden_units)
    hidden_copies = begin(FF.hidden_half, r.hidden, r.hidden_half)
    mixed_copies = begin(FF.mixed_right, r.mixed, r.mixed_right)

    def mlp_part(j):
        r.part[:, j * CW : (j + 1) * CW] = dot(
            r.mixed[...], r.down_vmem[:, j * CW : (j + 1) * CW], ((1,), (0,))
        ).astype(BF16)

    Reduce(r.part, *r.reduce).run(mlp_part)
    top_own_load.wait()
    v = r.reduce[3][...]
    z = norm_scale(v)
    dy = r.top_own[...].astype(F32)
    g = r.mlp_gain[...]
    r.d_mlp[rows_of(t, OWN), :] = norm_back(v, z, g, dy).astype(BF16)
    r.result_own[...] = (r.hidden_own[...] + v * z * g).astype(BF16)
    mlp_gain_grad = jnp.sum(dy * v * z, axis=0, keepdims=True)
    z = lax.axis_index("dp")
    gate_copies = FF_MOVES[FF.gate_right].copies(
        r.d_gate, r.gate_right, *r.moves[FF.gate_right]
    )
    up_copies = FF_MOVES[FF.up_right].copies(r.d_up, r.up_right, *r.moves[FF.up_right])

    gather_rows(r.d_mlp, r.gather)
    for s in (2, 1, 3, 0):
        cols = pl.ds(pl.multiple_of(lax.rem(z + s, 4) * CW, CW), CW)
        d_mixed = dot(r.d_mlp[...], r.down_vmem[cols, :], ((1,), (1,)))
        r.d_up[:, cols] = (d_mixed * r.act[:, cols]).astype(BF16)
        r.d_gate[:, cols] = (d_mixed * r.slope[:, cols]).astype(BF16)
        gate_copies[s - 1].start()
        up_copies[s - 1].start()
    right_copies = gate_copies + up_copies
    top_copies = begin(FF.top_half, r.d_mlp, r.top_half)
    wait(features_copies)
    features_copies = begin(FF.features_rest, r.features_half, r.features_rest)

    def back_part(j):
        rows = pl.ds(j * CW, CW)
        r.part[:, j * CW : (j + 1) * CW] = (
            dot(r.d_gate[...], r.gate_vmem[rows, :], ((1,), (1,)))
            + dot(r.d_up[...], r.up_vmem[rows, :], ((1,), (1,)))
        ).astype(BF16)

    Reduce(r.part, *r.reduce).run(back_part)
    wait(hidden_copies)
    hidden_copies = begin(FF.hidden_rest, r.hidden_half, r.hidden_rest)
    dy = r.top_own[...].astype(F32) + r.reduce[3][...]
    v = r.attn_own[...]
    a = norm_scale(v)
    g = r.attn_gain[...]
    r.d_attn[rows_of(t, OWN), :] = norm_back(v, a, g, dy).astype(BF16)
    r.d_hidden_own[...] = dy
    row = lax.broadcasted_iota(jnp.int32, (8, D), 0)
    attn_grad = jnp.sum(dy * v * a, axis=0, keepdims=True)
    r.gain_rows[...] = jnp.where(row == 0, attn_grad, mlp_gain_grad)
    gather_rows(r.d_attn, r.gather)
    r.d_attended[...] = dot(r.d_attn[...], r.out_vmem[...], ((1,), (1,))).astype(BF16)
    wait(right_copies + hidden_copies + features_copies + attended_copies)
    wait(mixed_copies + top_copies + saved)


WIDE = jax.ShapeDtypeStruct((T, D), BF16)
NARROW = jax.ShapeDtypeStruct((T, 4 * HD), BF16)
HALVES = jax.ShapeDtypeStruct((4, T, D // 2), BF16)
FF_MOVES = dict(
    features_half=half_move(WIDE, "z"),
    features_rest=core_move(HALVES),
    attended_all=full_move(NARROW, "z"),
    hidden_half=half_move(WIDE, "z"),
    hidden_rest=core_move(HALVES),
    gate_right=quarter_move(WIDE, "z"),
    up_right=quarter_move(WIDE, "z"),
    mixed_right=quarter_move(WIDE, "x"),
    top_half=half_move(WIDE, "x"),
)
FF = Names(**{name: name for name in FF_MOVES})
FF_PEERS = distinct(
    [CORE, FAR]
    + [(0, dy, dx, 0, 0) for dy in range(2) for dx in range(4) if dy or dx]
    + peers_of(FF_MOVES)
)


def attend_scratch():
    dma = pltpu.SemaphoreType.DMA
    return [
        pltpu.VMEM((8, 8, T), F32),
        pltpu.VMEM((T, 4 * HD), BF16),
        pltpu.VMEM((T, 4 * HD), BF16),
        pltpu.VMEM((2, 8, T), F32),
        pltpu.VMEM((8, T), F32),
        pltpu.VMEM((8, T), F32),
        pltpu.VMEM((4, T, HD), BF16),
        dma((4, 4)),
        dma((4, 4)),
        dma((4,)),
        dma((4,)),
        dma((8,)),
        dma((8,)),
        dma((2,)),
        dma((2,)),
        dma((4,)),
        dma((4,)),
    ]


def forward(small, large):
    weight, wide = pltpu.VMEM((D, D), BF16), pltpu.VMEM((T, D), BF16)
    own, tall = pltpu.VMEM((OWN, D), F32), pltpu.VMEM((T, D), F32)
    own_low = pltpu.VMEM((OWN, D), BF16)
    saved = dict(
        q_head=((4 * T, HD), BF16),
        k_head=((8 * T, HD), BF16),
        v_head=((8 * T, HD), BF16),
        probs=((4, T, 8 * T), BF16),
        q_raw=((T, 4 * HD), F32),
        k_raw=((T, 4 * HD), F32),
        scales=((T, HD), F32),
    )
    scratch = dict(
        out_vmem=pltpu.VMEM((4 * HD, D), BF16),
        gate_vmem=weight,
        up_vmem=weight,
        down_vmem=weight,
        features_own=own_low,
        top_own=own_low,
        part=wide,
        hidden=wide,
        act=tall,
        slope=tall,
        d_gate=wide,
        d_up=wide,
        d_mlp=wide,
        mixed=wide,
        attn_own=own,
        hidden_own=own,
        load_sems=pltpu.SemaphoreType.DMA((32,)),
        reduce=REDUCE_SCRATCH,
        gather=GATHER_SCRATCH,
        moves=move_scratch(FF_MOVES),
        features_vmem=wide,
        value=pltpu.VMEM((T, 4 * HD), BF16),
        attended=pltpu.VMEM((T, 4 * HD), BF16),
        attend=attend_scratch(),
        **{name: pltpu.VMEM(*saved[name]) for name in saved},
    )
    outs = dict(
        d_attended=((T, 4 * HD), BF16),
        d_hidden_own=((OWN, D), F32),
        result_own=((OWN, D), BF16),
        gain_rows=((8, D), F32),
        d_attn=((T, D), BF16),
    )
    large_outs = {name: move.out for name, move in FF_MOVES.items()}
    large_outs |= {name + "_out": out for name, out in saved.items()}
    return run_kernel(forward_kernel, 1, small, large, outs, large_outs, scratch, 62)


def row_device(yl, x):
    return {"ctx": yl * 4 + x}


ATTEND_PEERS = [CORE, FAR] + [(0, dy, dx, 0, 0) for dy in range(2) for dx in range(4) if dy or dx]


def tensor_sum(own, near, far, send, recv):
    copy = remote(own.at[0], near, send.at[0], recv.at[0], peer(*CORE))
    copy.start()
    copy.wait_recv()
    own[1] = own[0] + near[...]
    again = remote(own.at[1], far, send.at[1], recv.at[1], peer(*FAR))
    again.start()
    again.wait_recv()
    total = own[1] + far[...]
    copy.wait_send()
    again.wait_send()
    return total


def exact_dot(a, b, dims):
    return lax.dot_general(
        a, b, (dims, ((), ())), preferred_element_type=F32, precision=lax.Precision.HIGHEST
    )


def token_rows(values, row):
    pick = lax.broadcasted_iota(jnp.int32, (8, values.shape[1]), 0) == row
    return exact_dot(jnp.where(pick, 1.0, 0.0), values, ((1,), (1,)))


def token_columns(rows):
    lane = lax.broadcasted_iota(jnp.int32, (8, HD), 1) // (HD // 2)
    pick = lax.broadcasted_iota(jnp.int32, (8, HD), 0) == lane
    return exact_dot(rows, jnp.where(pick, 1.0, 0.0), ((0,), (0,)))


class Spread:
    def __init__(self, src, dst, sems):
        self.src, self.dst = src, dst
        self.send, self.recv, self.down_send, self.down_recv = sems

    def row_copy(self, s):
        _, _, yl, x = place()
        h = lax.rem(x + s, 4)
        return remote(
            self.src.at[:, pl.ds(pl.multiple_of(h * HD, HD), HD)],
            self.dst.at[rows_of(yl * 4 + x, T)],
            self.send.at[s],
            self.recv.at[s],
            row_device(yl, h),
        )

    def down_copy(self, s):
        _, _, yl, x = place()
        h = lax.rem(x + s, 4)
        return remote(
            self.src.at[:, pl.ds(pl.multiple_of(h * HD, HD), HD)],
            self.dst.at[rows_of(x, T)],
            self.down_send.at[s],
            self.down_recv.at[s],
            row_device(1, h),
        )


def keep_own(src, dst, block):
    _, _, _, x = place()
    dst[rows_of(block, T), :] = src[:, pl.ds(pl.multiple_of(x * HD, HD), HD)]


def attend_part(
    project, q_raw, k_raw, value, seg, q_gain, k_gain,
    attended, q_head, k_head, v_head, probs_out, scale_out,
    seg_all, q_low, k_low, sums, near, far, result,
    v_sems, k_sems, q_send, q_recv, s_send, s_recv, sum_send, sum_recv, a_send, a_recv,
    load_weights,
):
    yh, core, yl, x = place()
    me = yl * 4 + x
    v_sems = [v_sems.at[i] for i in range(4)]
    k_sems = [k_sems.at[i] for i in range(4)]
    values = Spread(value, v_head, v_sems)
    keys = Spread(k_low, k_head, k_sems)

    @pl.when(yl == 0)
    def _():
        for s in range(4):
            values.down_copy(s).start()

    for s in (1, 2, 3):
        values.row_copy(s).start()
    seg_all[me] = jnp.broadcast_to(seg[...].astype(F32), (8, T))

    def seg_copy(s):
        dx, dy = s % 4, s // 4
        to = row_device(lax.rem(yl + dy, 2), lax.rem(x + dx, 4))
        return remote(seg_all.at[me], seg_all.at[me], s_send.at[s], s_recv.at[s], to)

    for s in range(1, 8):
        seg_copy(s).start()

    project()
    qr, kr = q_raw[...], k_raw[...]
    sums[0] = token_rows(qr * qr, 0) + token_rows(kr * kr, 1)
    keep_own(value, v_head, me)
    weights = load_weights()
    scales = token_columns(
        lax.rsqrt(tensor_sum(sums, near, far, sum_send, sum_recv) / D + EPS)
    )
    scale_out[...] = scales
    k_low[...] = (kr * scales[:, HD // 2 : HD // 2 + 1] * k_gain[...]).astype(BF16)

    @pl.when(yl == 0)
    def _():
        for s in range(4):
            keys.down_copy(s).start()

    for s in (1, 2, 3):
        keys.row_copy(s).start()
    q_low[...] = (qr * scales[:, :1] * q_gain[...]).astype(BF16)

    def q_copy(s):
        h = lax.rem(x + s, 4)
        return remote(
            q_low.at[:, pl.ds(pl.multiple_of(h * HD, HD), HD)],
            q_head.at[rows_of(x, T)],
            q_send.at[s],
            q_recv.at[s],
            row_device(yl, h),
        )

    for s in (1, 2, 3):
        q_copy(s).start()
    keep_own(k_low, k_head, me)
    keep_own(q_low, q_head, x)
    for s in range(1, 8):
        seg_copy(s).wait()
    for s in (1, 2, 3):
        values.row_copy(s).wait()
        keys.row_copy(s).wait()
        q_copy(s).wait()

    @pl.when(yl == 0)
    def _():
        for s in range(4):
            values.down_copy(s).wait_send()
            keys.down_copy(s).wait_send()

    @pl.when(yl == 1)
    def _():
        for s in range(4):
            values.down_copy(s).wait_recv()
            keys.down_copy(s).wait_recv()

    lane = lax.broadcasted_iota(jnp.int32, (8, HD), 0)
    pick = jnp.where(lane == 0, 1.0, 0.0)

    def attend(row, i):
        blocks = row * 4 + i + 1
        width = blocks * T
        q = q_head[i * T : (i + 1) * T, :]
        scores = dot(q, k_head[:width, :], ((1,), (1,))) * HD ** (-0.5)
        own_seg = dot(seg_all[row * 4 + i], pick, ((0,), (0,)))[:, :1]
        seg_keys = jnp.concatenate([seg_all[b, :1, :] for b in range(blocks)], axis=1)
        q_place = lax.broadcasted_iota(jnp.int32, (T, width), 0) + (blocks - 1) * T
        k_place = lax.broadcasted_iota(jnp.int32, (T, width), 1)
        counted = (k_place <= q_place) & (seg_keys == own_seg)
        scores = jnp.where(counted, scores, -1e30)
        exps = jnp.exp(scores - jnp.max(scores, axis=1, keepdims=True))
        probs = (exps * (1.0 / jnp.sum(exps, axis=1, keepdims=True))).astype(BF16)
        probs_out[i, :, :width] = probs
        result[i] = dot(probs, v_head[:width, :], ((1,), (0,))).astype(BF16)

    def back_copy(i):
        return remote(
            result.at[i],
            attended.at[:, pl.ds(pl.multiple_of(x * HD, HD), HD)],
            a_send.at[i],
            a_recv.at[x],
            row_device(yl, i),
        )

    for i in range(4):
        for row in range(2):

            @pl.when(yl == row)
            def _():
                attend(row, i)

        @pl.when(x == i)
        def _():
            attended[:, i * HD : (i + 1) * HD] = result[i]

        @pl.when(x != i)
        def _():
            back_copy(i).start()

    for h in range(4):

        @pl.when(x != h)
        def _():
            back_copy(h).wait_send()
            remote(
                result.at[h],
                attended.at[:, h * HD : (h + 1) * HD],
                a_send.at[h],
                a_recv.at[h],
                row_device(yl, h),
            ).wait_recv()
    return weights


def product_rows(left, right):
    return dot(
        left.reshape(4 * T, left.shape[2]), right.reshape(4 * T, right.shape[2]), ((0,), (0,))
    ).astype(BF16)


def blocks_out(partial, slots, send, recv, axis, start=0, width=None):
    me = spot(axis)
    cols = pl.ds(start, partial.shape[-1] if width is None else width)
    copies = [
        remote(
            partial.at[lax.rem(me + s, 4), :, :, :, cols], slots.at[s - 1, :, :, :, cols],
            send.at[s - 1], recv.at[s - 1], peer(*along(axis, s)),
        )
        for s in (1, 2, 3)
    ]
    for copy in copies:
        copy.start()
    return copies


def add_blocks(total, partial, slots, axis):
    me = spot(axis)
    for y in range(2):
        for j in range(4):
            block = partial[me, y, j].astype(F32)
            for s in range(3):
                block += slots[s, y, j].astype(F32)
            total[y, j] = block.astype(total.dtype)


HALF_GRID = (2, 4, 64)
BACK_MOVES = dict(
    attn_left=quarter_move(WIDE, "z"),
    q_right=quarter_move(NARROW, "z"),
    k_right=quarter_move(NARROW, "z"),
    v_right=quarter_move(NARROW, "z"),
    mlp_in=final_move(jax.ShapeDtypeStruct(HALF_GRID + (1024,), BF16), "z"),
    mlp_down=final_move(jax.ShapeDtypeStruct(HALF_GRID + (512,), BF16), "x"),
    qkv=final_move(jax.ShapeDtypeStruct(HALF_GRID + (384,), BF16), "z"),
    out=final_move(jax.ShapeDtypeStruct(HALF_GRID + (512,), BF16), "x"),
    tiles=final_move(jax.ShapeDtypeStruct((2, 4, 16, HD), F32), "x"),
)
BACK = Names(**{name: name for name in BACK_MOVES})
BACK_PEERS = distinct(ATTEND_PEERS + peers_of(BACK_MOVES))


def back_scratch():
    dma = pltpu.SemaphoreType.DMA

    def vmem(*shape, kind=BF16):
        return pltpu.VMEM(shape, kind)

    rows = (2, 4, 64)
    return dict(
        q_head=vmem(4 * T, HD),
        k_head=vmem(8 * T, HD),
        v_head=vmem(8 * T, HD),
        probs=vmem(2, T, 8 * T),
        q_raw=vmem(T, 4 * HD, kind=F32),
        k_raw=vmem(T, 4 * HD, kind=F32),
        scales=vmem(T, HD, kind=F32),
        wq=vmem(D, 4 * HD),
        wk=vmem(D, 4 * HD),
        wv=vmem(D, 4 * HD),
        left=vmem(2, 4, T, D // 2),
        top=vmem(2, 4, T, D // 2),
        gate_right=vmem(4, T, 512),
        up_right=vmem(4, T, 512),
        mixed_right=vmem(4, T, 512),
        attn_left=vmem(4, T, 512),
        attended_all=vmem(4, T, 512),
        q_right=vmem(4, T, HD),
        k_right=vmem(4, T, HD),
        v_right=vmem(4, T, HD),
        in_part=vmem(4, *rows, 1024),
        in_slots=vmem(2, *rows, 1024),
        in_across=vmem(2, 2, 2, 64, 1024),
        in_sum=vmem(*rows, 1024),
        down_part=vmem(4, *rows, 512),
        down_slots=vmem(3, *rows, 512),
        down_sum=vmem(*rows, 512),
        qkv_part=vmem(4, *rows, 384),
        qkv_slots=vmem(3, *rows, 384),
        qkv_sum=vmem(*rows, 384),
        out_part=vmem(*rows, 512),
        tile_part=vmem(4, 2, 4, 16, HD, kind=F32),
        tile_slots=vmem(3, 2, 4, 16, HD, kind=F32),
        tile_sum=vmem(2, 4, 16, HD, kind=F32),
        d_q=vmem(T, 4 * HD),
        d_k=vmem(T, 4 * HD),
        d_v=vmem(T, 4 * HD),
        part=vmem(T, D),
        d_out=vmem(4 * T, HD),
        dq_buf=vmem(4, T, HD),
        dk_buf=vmem(8, T, HD),
        dv_buf=vmem(8, T, HD),
        dk_acc=vmem(8 * T, HD, kind=F32),
        dv_acc=vmem(8 * T, HD, kind=F32),
        dq_got=vmem(4, T, HD),
        dk_got=vmem(2, 4, T, HD),
        dv_got=vmem(2, 4, T, HD),
        sums=vmem(2, 8, T, kind=F32),
        near=vmem(8, T, kind=F32),
        far=vmem(8, T, kind=F32),
        gain_near=vmem(8, D, kind=F32),
        gain_far=vmem(8, D, kind=F32),
        gain_sum=vmem(8, D, kind=F32),
        load_sems=dma((32,)),
        in_send=dma((2, 4)),
        in_recv=dma((2, 4)),
        across_send=dma((2,)),
        across_recv=dma((2,)),
        down_send=dma((3,)),
        down_recv=dma((3,)),
        qkv_send=dma((3,)),
        qkv_recv=dma((3,)),
        v_send=dma((3,)),
        v_recv=dma((3,)),
        tile_send=dma((3,)),
        tile_recv=dma((3,)),
        o_send=dma((4,)),
        o_recv=dma((4,)),
        dq_send=dma((4,)),
        dq_recv=dma((4,)),
        dk_send=dma((8,)),
        dk_recv=dma((2, 4)),
        dv_send=dma((8,)),
        dv_recv=dma((2, 4)),
        sum_send=dma((2,)),
        sum_recv=dma((2,)),
        gain_send=dma((2,)),
        gain_recv=dma((2,)),
        top_send=dma((1,)),
        top_recv=dma((1,)),
        result_send=dma((3,)),
        result_recv=dma((3,)),
        reduce=REDUCE_SCRATCH,
        gather=GATHER_SCRATCH,
        moves=move_scratch(BACK_MOVES),
    )


def backward_kernel(r):
    yh, core, yl, x = place()
    t = yh * 2 + core
    scale = HD ** (-0.5)
    greet(BACK_PEERS)

    def begin(name, src, dst):
        return BACK_MOVES[name].start(src, dst, *r.moves[name])

    load_count = iter(range(32))

    def load(src, dst):
        copy = pltpu.make_async_copy(src, dst, r.load_sems.at[next(load_count)])
        copy.start()
        return copy

    hidden0_load = load(r.hidden_half, r.left.at[core])
    gate_right_load = load(r.gate_right_in, r.gate_right)
    up_right_load = load(r.up_right_in, r.up_right)
    hidden1_load = load(r.hidden_rest, r.left.at[1 - core])
    greeted(BACK_PEERS)

    def o_copy(s):
        h = lax.rem(x + s, 4)
        return remote(
            r.d_attended.at[:, pl.ds(pl.multiple_of(h * HD, HD), HD)],
            r.d_out.at[rows_of(x, T)],
            r.o_send.at[s],
            r.o_recv.at[s],
            row_device(yl, h),
        )

    for s in (1, 2, 3):
        o_copy(s).start()
    gain_near_copy = remote(
        r.gains, r.gain_near, r.gain_send.at[0], r.gain_recv.at[0], peer(*CORE)
    )
    gain_near_copy.start()
    top_copy = remote(
        r.top_half, r.top.at[core], r.top_send.at[0], r.top_recv.at[0], peer(*CORE)
    )
    top_copy.start()
    mine, other = rows_of(t, OWN), rows_of((1 - yh) * 2 + core, OWN)
    result_load = load(r.result_own, r.outputs.at[mine])
    result_copies = [
        remote(
            r.result_own, r.outputs.at[mine], r.result_send.at[n], r.result_recv.at[n], to
        )
        for n, to in enumerate((peer(*FAR), peer(*CORE)))
    ]
    for copy in result_copies:
        copy.start()
    attn_left = begin(BACK.attn_left, r.d_attn, r.attn_left)
    keep_own(r.d_attended, r.d_out, x)
    r.dk_acc[...] = jnp.zeros_like(r.dk_acc)
    r.dv_acc[...] = jnp.zeros_like(r.dv_acc)

    wait([hidden0_load, gate_right_load, up_right_load, hidden1_load])
    q_head_load = load(r.q_head_in, r.q_head)
    k_head_load = load(r.k_head_in, r.k_head)
    v_head_load = load(r.v_head_in, r.v_head)
    probs_loads = [load(r.probs_in.at[i], r.probs.at[i]) for i in range(2)]
    q_raw_load = load(r.q_raw_in, r.q_raw)
    k_raw_load = load(r.k_raw_in, r.k_raw)
    scales_load = load(r.scales_in, r.scales)
    mixed_right_load = load(r.mixed_right_in, r.mixed_right)
    top_load = load(r.top_half, r.top.at[core])
    attended_all_load = load(r.attended_all_in, r.attended_all)
    w_query_load = load(r.w_query, r.wq)
    w_key_load = load(r.w_key, r.wk)
    w_value_load = load(r.w_value, r.wv)
    onward, backward_way = along("x", 1), along("x", 3)
    after, before = lax.rem(x + 1, 4), lax.rem(x + 3, 4)
    opposite = lax.rem(x + 2, 4)
    across = [
        remote(
            r.in_part.at[opposite, :, pl.ds(2 * n, 2)], r.in_across.at[n], r.across_send.at[n],
            r.across_recv.at[n], peer(*way),
        )
        for n, way in enumerate((onward, backward_way))
    ]
    in_copies = []

    z = lax.axis_index("dp")

    def in_piece(step):
        piece = lax.rem(z + step, 4)
        for n, (block, way) in enumerate(((after, onward), (before, backward_way))):
            copy = remote(
                r.in_part.at[block, :, piece], r.in_slots.at[n, :, piece],
                r.in_send.at[n, step], r.in_recv.at[n, step], peer(*way),
            )
            copy.start()
            in_copies.append(copy)

    in_final = BACK_MOVES[BACK.mlp_in].copies(r.in_sum, r.mlp_in, *r.moves[BACK.mlp_in])

    def in_place(step):
        piece = lax.rem(z + step, 4)
        wait(in_copies[2 * step : 2 * step + 2])
        for y in range(2):
            r.in_sum[y, piece] = (
                r.in_part[x, y, piece].astype(F32)
                + r.in_slots[0, y, piece].astype(F32)
                + r.in_slots[1, y, piece].astype(F32)
            ).astype(BF16)
        for n in ((3, 7), (0, 4), (1, 5), (2, 6))[step]:
            in_final[n].start()

    for i in range(4):
        rows = r.left[i // 2, :, :, (i % 2) * 512 : (i % 2 + 1) * 512]
        for n, half in enumerate((r.gate_right, r.up_right)):
            got = product_rows(rows, half[...])
            for y in range(2):
                for j in range(4):
                    r.in_part[j, y, i, :, n * 512 : (n + 1) * 512] = got[
                        (y * 4 + j) * 64 : (y * 4 + j + 1) * 64
                    ]
        if i % 2 == 1:
            across[i // 2].start()
    features0_load = load(r.features_half, r.left.at[core])
    features1_load = load(r.features_rest, r.left.at[1 - core])
    gain_near_copy.wait()
    r.gain_sum[...] = r.gains[...] + r.gain_near[...]
    gain_far_copy = remote(
        r.gain_sum, r.gain_far, r.gain_send.at[1], r.gain_recv.at[1], peer(*FAR)
    )
    gain_far_copy.start()

    for s in (1, 2, 3):
        o_copy(s).wait()
    wait([q_head_load, k_head_load, v_head_load])

    def back(row, i):
        width = (row * 4 + i + 1) * T
        q = r.q_head[i * T : (i + 1) * T, :]
        do = r.d_out[i * T : (i + 1) * T, :]
        probs_low = r.probs[i % 2, :, :width]
        probs = probs_low.astype(F32)
        d_probs = dot(do, r.v_head[:width, :], ((1,), (1,)))
        delta = jnp.sum(probs * d_probs, axis=1, keepdims=True)
        d_scores = (probs * (d_probs - delta)).astype(BF16)
        r.dq_buf[i] = (dot(d_scores, r.k_head[:width, :], ((1,), (0,))) * scale).astype(BF16)
        r.dk_acc[:width, :] += dot(d_scores, q, ((0,), (0,)))
        r.dv_acc[:width, :] += dot(probs_low, do, ((0,), (0,)))

    def dq_copy(i):
        return remote(
            r.dq_buf.at[i], r.dq_got.at[x], r.dq_send.at[i], r.dq_recv.at[x], row_device(yl, i)
        )

    for i in range(4):
        probs_loads[i].wait()
        for row in range(2):

            @pl.when(yl == row)
            def _():
                back(row, i)

        if i < 2:
            probs_loads.append(load(r.probs_in.at[i + 2], r.probs.at[i]))

        @pl.when(x == i)
        def _():
            r.dq_got[i] = r.dq_buf[i]

        @pl.when(x != i)
        def _():
            dq_copy(i).start()

    def kv_copy(j, buf, got, send, recv):
        return remote(
            buf.at[j], got.at[yl, x], send.at[j], recv.at[yl, x], row_device(j // 4, j % 4)
        )

    dk_args = (r.dk_buf, r.dk_got, r.dk_send, r.dk_recv)
    dv_args = (r.dv_buf, r.dv_got, r.dv_send, r.dv_recv)
    for j in range(8):
        r.dk_buf[j] = (r.dk_acc[j * T : (j + 1) * T, :] * scale).astype(BF16)
        r.dv_buf[j] = r.dv_acc[j * T : (j + 1) * T, :].astype(BF16)
        here = (yl == j // 4) & (x == j % 4)

        @pl.when(here)
        def _():
            r.dk_got[j // 4, j % 4] = r.dk_buf[j]
            r.dv_got[j // 4, j % 4] = r.dv_buf[j]

        sends = (yl >= j // 4) & ~here

        @pl.when(sends)
        def _():
            kv_copy(j, *dk_args).start()
            kv_copy(j, *dv_args).start()

    result_copies[0].wait_recv()
    result_copies.append(
        remote(
            r.outputs.at[other],
            r.outputs.at[other],
            r.result_send.at[2],
            r.result_recv.at[2],
            peer(*CORE),
        )
    )
    result_copies[2].start()

    mixed_right_load.wait()
    top_load.wait()
    top_copy.wait()
    for i in range(4):
        left = r.top[i // 2, :, :, (i % 2) * 512 : (i % 2 + 1) * 512]
        r.down_part[i] = product_rows(left, r.mixed_right[...]).reshape(2, 4, 64, 512)
    down_copies = blocks_out(r.down_part, r.down_slots, r.down_send, r.down_recv, "z")
    attended_all_load.wait()
    wait(attn_left)
    r.out_part[...] = product_rows(r.attn_left[...], r.attended_all[...]).reshape(2, 4, 64, 512)

    for n, block in enumerate((after, before)):
        across[n].wait()
        for y in range(2):
            for m in range(2):
                mine_too = r.in_part[block, y, 2 * n + m].astype(F32)
                r.in_part[block, y, 2 * n + m] = (
                    mine_too + r.in_across[n, y, m].astype(F32)
                ).astype(BF16)

    for h in range(4):

        @pl.when(x != h)
        def _():
            dq_copy(h).wait_send()
            remote(
                r.dq_buf.at[h], r.dq_got.at[h], r.dq_send.at[h], r.dq_recv.at[h],
                row_device(yl, h),
            ).wait_recv()

        for row in range(2):
            comes = (row >= yl) & ~((yl == row) & (x == h))

            @pl.when(comes)
            def _():
                for buf, got, send, recv in (dk_args, dv_args):
                    remote(
                        buf.at[0],
                        got.at[row, h],
                        send.at[0],
                        recv.at[row, h],
                        row_device(row, h),
                    ).wait_recv()

    for j in range(8):
        here = (yl == j // 4) & (x == j % 4)
        sends = (yl >= j // 4) & ~here

        @pl.when(sends)
        def _():
            kv_copy(j, *dk_args).wait_send()
            kv_copy(j, *dv_args).wait_send()

    @pl.when(yl == 1)
    def _():
        for h in range(4):
            r.dk_got[0, h] = jnp.zeros((T, HD), BF16)
            r.dv_got[0, h] = jnp.zeros((T, HD), BF16)

    for step in range(4):
        in_piece(step)
    out_copies = begin(BACK.out, r.out_part, r.out)
    wait([q_raw_load, k_raw_load, scales_load])
    sums = jnp.zeros((8, T), F32)
    for h in range(4):
        cols = slice(h * HD, (h + 1) * HD)
        dq = r.dq_got[h].astype(F32)
        dk = r.dk_got[0, h].astype(F32) + r.dk_got[1, h].astype(F32)
        r.d_v[:, cols] = (r.dv_got[0, h].astype(F32) + r.dv_got[1, h].astype(F32)).astype(BF16)
        sums += token_rows(dq * r.q_raw[:, cols] * r.q_gain[:, cols], 0)
        sums += token_rows(dk * r.k_raw[:, cols] * r.k_gain[:, cols], 1)
    r.sums[0] = sums
    v_copies = begin(BACK.v_right, r.d_v, r.v_right)
    total = token_columns(tensor_sum(r.sums, r.near, r.far, r.sum_send, r.sum_recv))
    qs, ks = r.scales[:, :1], r.scales[:, HD // 2 : HD // 2 + 1]
    q_coef = qs * qs * qs * (total[:, :1] / D)
    k_coef = ks * ks * ks * (total[:, HD // 2 : HD // 2 + 1] / D)
    gain_far_copy.wait()
    both = r.gain_sum[...] + r.gain_far[...]
    tile = []
    for h in range(4):
        cols = slice(h * HD, (h + 1) * HD)
        dq = r.dq_got[h].astype(F32)
        dk = r.dk_got[0, h].astype(F32) + r.dk_got[1, h].astype(F32)
        qr, kr = r.q_raw[:, cols], r.k_raw[:, cols]
        r.d_q[:, cols] = (qs * r.q_gain[:, cols] * dq - qr * q_coef).astype(BF16)
        r.d_k[:, cols] = (ks * r.k_gain[:, cols] * dk - kr * k_coef).astype(BF16)
        tile.append((jnp.sum(dq * qr * qs, axis=0, keepdims=True), jnp.sum(dk * kr * ks, axis=0, keepdims=True)))
    qk_copies = begin(BACK.q_right, r.d_q, r.q_right) + begin(BACK.k_right, r.d_k, r.k_right)
    row = lax.broadcasted_iota(jnp.int32, (8, HD), 0)
    top_tile = jnp.zeros((8, HD), F32)
    for h in range(4):
        top_tile = jnp.where(row == h, tile[h][0], top_tile)
        top_tile = jnp.where(row == h + 4, tile[h][1], top_tile)
    for rank in range(32):
        to = (rank // 8, rank // 4 % 2, rank % 4)
        r.tile_part[(*to, slice(0, 8))] = top_tile
        r.tile_part[(*to, slice(8, 16))] = both[:, (rank // 2) * HD : (rank // 2 + 1) * HD]
    tile_copies = blocks_out(r.tile_part, r.tile_slots, r.tile_send, r.tile_recv, "z")

    wait([w_query_load, w_key_load, w_value_load])

    def input_part(j):
        rows = pl.ds(j * CW, CW)
        r.part[:, j * CW : (j + 1) * CW] = (
            dot(r.d_q[...], r.wq[rows, :], ((1,), (1,)))
            + dot(r.d_k[...], r.wk[rows, :], ((1,), (1,)))
            + dot(r.d_v[...], r.wv[rows, :], ((1,), (1,)))
        ).astype(BF16)

    reduce = Reduce(r.part, *r.reduce)
    reduce.begin(input_part)
    wait(down_copies)
    add_blocks(r.down_sum, r.down_part, r.down_slots, "z")
    down_final = begin(BACK.mlp_down, r.down_sum, r.mlp_down)
    in_place(0)

    def qkv_product(n, right):
        for i in range(4):
            left = r.left[i // 2, :, :, (i % 2) * 512 : (i % 2 + 1) * 512]
            got = product_rows(left, right[...])
            for y in range(2):
                for j in range(4):
                    r.qkv_part[j, y, i, :, n * HD : (n + 1) * HD] = got[
                        (y * 4 + j) * 64 : (y * 4 + j + 1) * 64
                    ]

    wait([features0_load, features1_load])
    wait(v_copies)
    qkv_product(2, r.v_right)
    qkv_args = (r.qkv_part, r.qkv_slots)
    qkv_copies = blocks_out(*qkv_args, r.v_send, r.v_recv, "x", 2 * HD, HD)
    in_place(1)
    wait(qk_copies)
    qkv_product(0, r.q_right)
    qkv_product(1, r.k_right)
    qkv_copies += blocks_out(*qkv_args, r.qkv_send, r.qkv_recv, "x", 0, 2 * HD)
    in_place(2)
    wait(tile_copies)
    add_blocks(r.tile_sum, r.tile_part, r.tile_slots, "z")
    tile_final = begin(BACK.tiles, r.tile_sum, r.tiles)
    reduce.finish()
    r.input_grad[mine, :] = (r.d_hidden_own[...] + r.reduce[3][...]).astype(BF16)
    gather = Gather(r.input_grad, r.gather)
    gather.begin()

    in_place(3)
    wait(qkv_copies)
    add_blocks(r.qkv_sum, r.qkv_part, r.qkv_slots, "x")
    qkv_final = begin(BACK.qkv, r.qkv_sum, r.qkv)
    gather.finish()
    result_load.wait()
    result_copies[0].wait_send()
    result_copies[1].wait()
    result_copies[2].wait()
    wait(tile_final + out_copies + down_final + in_final + qkv_final)


def backward(small, large):
    large_outs = dict(
        outputs=((T, D), BF16),
        tiles=((2, 4, 16, HD), F32),
        mlp_in=(HALF_GRID + (1024,), BF16),
        mlp_down=(HALF_GRID + (512,), BF16),
        qkv=(HALF_GRID + (384,), BF16),
        out=(HALF_GRID + (512,), BF16),
    )
    outs = dict(input_grad=((T, D), BF16))
    return run_kernel(backward_kernel, 6, small, large, outs, large_outs, back_scratch(), 62)


def results_kernel(
    rank_ref, tiles_in, mlp_in_in, mlp_down_in, qkv_in, out_in, outputs_in, input_grad_in,
    outputs, input_grad, query, key, value, out_grad, q_gain, k_gain, attn_gain, gate, up, down,
    mlp_gain, mlp_in, mlp_down, qkv, out, tiles, staged, sems,
):
    pairs = [
        (outputs_in, staged.at[0]), (input_grad_in, staged.at[1]),
        (mlp_in_in, mlp_in), (mlp_down_in, mlp_down), (qkv_in, qkv), (out_in, out),
        (tiles_in, tiles),
    ]
    copies = [pltpu.make_async_copy(a, b, sems.at[n]) for n, (a, b) in enumerate(pairs)]
    for copy in copies:
        copy.start()
    wait(copies[:2])
    onward = [
        pltpu.make_async_copy(staged.at[0], outputs, sems.at[7]),
        pltpu.make_async_copy(staged.at[1], input_grad, sems.at[8]),
    ]
    for copy in onward:
        copy.start()
    copies[2].wait()
    rank = rank_ref[0]
    for j in range(4):
        both = mlp_in[0, j].astype(F32) + mlp_in[1, j].astype(F32)
        gate[:, j * 512 : (j + 1) * 512] = both[:, :512]
        up[:, j * 512 : (j + 1) * 512] = both[:, 512:]
    wait(copies[3:5])
    for j in range(4):
        down[:, j * 512 : (j + 1) * 512] = mlp_down[0, j].astype(F32) + mlp_down[1, j].astype(F32)
        heads = qkv[0, j].astype(F32) + qkv[1, j].astype(F32)
        for n, grad in enumerate((query, key, value)):
            grad[:, j * HD : (j + 1) * HD] = heads[:, n * HD : (n + 1) * HD]
    copies[5].wait()
    total = out[0, 0].astype(F32)
    for n in range(1, 8):
        total += out[n // 4, n % 4].astype(F32)
    out_grad[...] = total
    copies[6].wait()
    gains = tiles[0, 0]
    for n in range(1, 8):
        gains += tiles[n // 4, n % 4]
    heads = pltpu.roll(gains[:8], HD - rank * 4, 1)
    q_gain[...] = heads[:4, :4]
    k_gain[...] = heads[4:, :4]
    columns = pltpu.roll(gains[8:], HD - lax.rem(rank, 2) * 64, 1)
    attn_gain[...] = columns[:1, :64]
    mlp_gain[...] = columns[1:2, :64]
    wait(onward)


def results(got):
    rank = lax.axis_index("dp") * 8 + lax.axis_index("ctx")
    narrow, wide, low = ((64, 4 * HD), F32), ((64, D), F32), ((T, D), BF16)
    outs = [low, low, narrow, narrow, narrow, narrow, ((4, 4), F32), ((4, 4), F32), ((1, 64), F32)]
    outs += [wide, wide, wide, ((1, 64), F32)]
    return pl.pallas_call(
        results_kernel,
        name=results.__name__,
        out_shape=[jax.ShapeDtypeStruct(*out) for out in outs],
        in_specs=[pl.BlockSpec(memory_space=pltpu.SMEM)] + [ANY] * 7,
        out_specs=[ANY] * 2 + [VMEM] * 11,
        scratch_shapes=[
            pltpu.VMEM(HALF_GRID + (1024,), BF16),
            pltpu.VMEM(HALF_GRID + (512,), BF16),
            pltpu.VMEM(HALF_GRID + (384,), BF16),
            pltpu.VMEM(HALF_GRID + (512,), BF16),
            pltpu.VMEM((2, 4, 16, HD), F32),
            pltpu.VMEM((2, T, D), BF16),
            pltpu.SemaphoreType.DMA((9,)),
        ],
        compiler_params=pltpu.CompilerParams(vmem_limit_bytes=62 * 2**20),
    )(
        rank.reshape(1), got.tiles, got.mlp_in, got.mlp_down, got.qkv, got.out,
        got.outputs, got.input_grad,
    )


def per_device(
    inputs, segments, w_query, w_key, w_value, w_out, q_gain, k_gain, attn_gain,
    w_gate, w_up, w_down, mlp_gain, cotangent,
):
    features, top = inputs[0], cotangent[0]
    q_row, k_row = q_gain.reshape(1, -1), k_gain.reshape(1, -1)
    a_row, m_row = attn_gain.reshape(1, -1), mlp_gain.reshape(1, -1)

    ff = forward(
        dict(seg=segments, q_gain=q_row, k_gain=k_row, attn_gain=a_row, mlp_gain=m_row),
        dict(
            features=features, cotangent=top, w_query=w_query, w_key=w_key, w_value=w_value,
            w_out=w_out, w_gate=w_gate, w_up=w_up, w_down=w_down,
        ),
    )
    got = backward(
        dict(
            d_attended=ff.d_attended, q_gain=q_row, k_gain=k_row, gains=ff.gain_rows,
            d_hidden_own=ff.d_hidden_own, result_own=ff.result_own,
        ),
        dict(
            q_head_in=ff.q_head_out, k_head_in=ff.k_head_out, v_head_in=ff.v_head_out,
            probs_in=ff.probs_out, q_raw_in=ff.q_raw_out, k_raw_in=ff.k_raw_out,
            scales_in=ff.scales_out,
            w_query=w_query, w_key=w_key, w_value=w_value,
            hidden_half=ff.hidden_half, hidden_rest=ff.hidden_rest, gate_right_in=ff.gate_right,
            up_right_in=ff.up_right, top_half=ff.top_half, mixed_right_in=ff.mixed_right,
            features_half=ff.features_half, features_rest=ff.features_rest,
            attended_all_in=ff.attended_all, d_attn=ff.d_attn,
        ),
    )
    (
        outputs, input_grad, query, key, value, out_grad, q_gain_grad, k_gain_grad,
        attn_gain_grad, gate, up, down, mlp_gain_grad,
    ) = results(got)
    return (
        outputs[None],
        input_grad[None],
        query,
        key,
        value,
        out_grad.T,
        q_gain_grad,
        k_gain_grad,
        attn_gain_grad[0],
        gate,
        up,
        down.T,
        mlp_gain_grad[0],
    )


def solution(mesh):
    rows, full = P("dp", "ctx", None), P()
    down, across = P("tensor", None), P(None, "tensor")
    in_specs = (
        rows, P("dp", "ctx"), across, across, across, down, down, down, full,
        across, across, down, full, rows,
    )
    split = ("dp", "ctx")
    out_specs = (
        rows, rows, P(split, "tensor"), P(split, "tensor"), P(split, "tensor"), P("tensor", split),
        P("tensor", split), P("tensor", split), P(split), P(split, "tensor"), P(split, "tensor"),
        P("tensor", split), P(split),
    )
    return jax.shard_map(
        per_device, mesh=mesh, in_specs=in_specs, out_specs=out_specs, check_vma=False
    )
```

```python
import functools
import jax
import jax.numpy as jnp
from jax import lax
from jax.experimental import pallas as pl
from jax.experimental.pallas import tpu as pltpu
from jax.sharding import PartitionSpec as P

MESH = pl.DeviceIdType.MESH
F32 = jnp.float32
BF16 = jnp.bfloat16
EPS = 1e-06
T = 256
D = 2048
HD = 128
OWN = 64
NC = 4
CW = D // NC
VMEM = pl.BlockSpec(memory_space=pltpu.VMEM)
ANY = pl.BlockSpec(memory_space=pltpu.HBM)


def place():
    t = lax.axis_index("tensor")
    ctx = lax.axis_index("ctx")
    return t // 2, lax.rem(t, 2), ctx // 4, lax.rem(ctx, 4)


def peer(dz=0, dy=0, dx=0, dh=0, dc=0):
    yh, core, yl, x = place()
    z = lax.rem(lax.axis_index("dp") + dz, 4)
    ctx = lax.rem(yl + dy, 2) * 4 + lax.rem(x + dx, 4)
    return {"dp": z, "ctx": ctx, "tensor": lax.rem(yh + dh, 2) * 2 + lax.rem(core + dc, 2)}


CORE, FAR = (0, 0, 0, 0, 1), (0, 0, 0, 1, 0)


def along(axis, s):
    return (s, 0, 0, 0, 0) if axis == "z" else (0, 0, s, 0, 0)


def spot(axis):
    return lax.axis_index("dp") if axis == "z" else place()[3]


def remote(src, dst, send_sem, recv_sem, device):
    return pltpu.make_async_remote_copy(
        src_ref=src,
        dst_ref=dst,
        send_sem=send_sem,
        recv_sem=recv_sem,
        device_id=device,
        device_id_type=MESH,
    )


def greet(offsets):
    barrier = pltpu.get_barrier_semaphore()
    for offset in offsets:
        pl.semaphore_signal(barrier, inc=1, device_id=peer(*offset), device_id_type=MESH)


def greeted(offsets):
    pl.semaphore_wait(pltpu.get_barrier_semaphore(), len(offsets))


def wait(copies):
    for copy in copies:
        copy.wait()


def dot(a, b, dims):
    return lax.dot_general(a, b, (dims, ((), ())), preferred_element_type=F32)


def rows_of(index, count):
    return pl.ds(pl.multiple_of(index * count, count), count)


class Move:
    def __init__(self, source, shape, offsets, pairs):
        self.source, self.shape, self.offsets, self.pairs = source, shape, offsets, pairs
        self.out = (shape, source.dtype)

    def scratch(self):
        dma = pltpu.SemaphoreType.DMA
        return [dma((len(self.offsets),)), dma((len(self.offsets),)), dma((1,))]

    def copies(self, src, dst, send, recv, local):
        made = []
        at = 0
        for a, b, offset in self.pairs(src, dst):
            if offset is None:
                made.append(pltpu.make_async_copy(a, b, local.at[0]))
            else:
                made.append(remote(a, b, send.at[at], recv.at[at], peer(*offset)))
                at += 1
        return made

    def start(self, src, dst, *sems):
        copies = self.copies(src, dst, *sems)
        for copy in copies:
            copy.start()
        return copies


def half_move(a, axis):
    half = a.shape[1] // 2
    offsets = [along(axis, s) for s in (1, 2, 3)]

    def pairs(src, dst):
        mine = src.at[:, pl.ds(pl.multiple_of(place()[1] * half, half), half)]
        me = spot(axis)
        return [(mine, dst.at[me], offset) for offset in offsets + [None]]

    return Move(a, (4, T, half), offsets, pairs)


def core_move(a):
    return Move(a, a.shape, [CORE], lambda src, dst: [(src, dst, CORE)])


def quarter_move(b, axis):
    width = b.shape[1] // 4
    offsets = [along(axis, s) for s in (1, 2, 3)]

    def pairs(src, dst):
        me = spot(axis)

        def part(s):
            return src.at[:, pl.ds(pl.multiple_of(lax.rem(me + s, 4) * width, width), width)]

        made = [(part(s), dst.at[me], along(axis, s)) for s in (1, 2, 3)]
        return made + [(part(0), dst.at[me], None)]

    return Move(b, (4, T, width), offsets, pairs)


def full_move(b, axis):
    offsets = [along(axis, s) for s in (1, 2, 3)]

    def pairs(src, dst):
        return [(src, dst.at[spot(axis)], offset) for offset in offsets + [None]]

    return Move(b, (4,) + b.shape, offsets, pairs)


def block_move(p, axis):
    offsets = [along(axis, s) for s in (1, 2, 3)]

    def pairs(src, dst):
        me = spot(axis)
        made = [(src.at[lax.rem(me + s, 4)], dst.at[me], along(axis, s)) for s in (1, 2, 3)]
        return made + [(src.at[me], dst.at[me], None)]

    return Move(p, p.shape, offsets, pairs)


def final_move(p, axis):
    steps = [(dy, s) for dy in range(2) for s in range(4) if dy or s]

    def offset(dy, s):
        return (s, dy, 0, 0, 0) if axis == "z" else (0, dy, s, 0, 0)

    def pairs(src, dst):
        yl, me = place()[2], spot(axis)
        made = [
            (src.at[lax.rem(yl + dy, 2), lax.rem(me + s, 4)], dst.at[yl, me], offset(dy, s))
            for dy, s in steps
        ]
        return made + [(src.at[yl, me], dst.at[yl, me], None)]

    return Move(p, p.shape, [offset(*step) for step in steps], pairs)


class Names:
    def __init__(self, **names):
        self.__dict__.update(names)


def run_kernel(body, collective_id, small, large, small_outs, large_outs, scratch, vmem):
    ins = [jax.tree.flatten(small), jax.tree.flatten(large)]
    shapes = [
        jax.tree.flatten({name: jax.ShapeDtypeStruct(*out) for name, out in outs.items()})
        for outs in (small_outs, large_outs)
    ]
    own = jax.tree.flatten(scratch)

    def kernel(*refs):
        names, at = {}, 0
        for leaves, tree in ins + shapes + [own]:
            names.update(tree.unflatten(refs[at : at + len(leaves)]))
            at += len(leaves)
        body(Names(**names))

    got = pl.pallas_call(
        kernel,
        name=body.__name__,
        out_shape=shapes[0][0] + shapes[1][0],
        in_specs=[VMEM] * len(ins[0][0]) + [ANY] * len(ins[1][0]),
        out_specs=[VMEM] * len(shapes[0][0]) + [ANY] * len(shapes[1][0]),
        scratch_shapes=own[0],
        compiler_params=pltpu.CompilerParams(
            collective_id=collective_id, has_side_effects=True, vmem_limit_bytes=vmem * 2**20
        ),
    )(*ins[0][0], *ins[1][0])
    n = len(shapes[0][0])
    return Names(**shapes[0][1].unflatten(got[:n]), **shapes[1][1].unflatten(got[n:]))


def move_scratch(moves):
    return {name: move.scratch() for name, move in moves.items()}


def peers_of(moves):
    return [offset for move in moves.values() for offset in move.offsets]


def distinct(offsets):
    return list(dict.fromkeys(offsets))


class Reduce:
    def __init__(self, part, near, far, out_low, acc, *sems):
        self.part, self.near, self.far, self.out_low, self.acc = part, near, far, out_low, acc
        self.sems = sems
        self.near_copies, self.far_copies = [], []

    def send(self, j):
        yh, core, _, _ = place()
        near_send, near_recv, _, _ = self.sems
        cols = pl.ds(j * CW, CW)
        for slot, row in ((0, (1 - yh) * 2 + (1 - core)), (1, yh * 2 + (1 - core))):
            copy = remote(
                self.part.at[rows_of(row, OWN), cols],
                self.near.at[slot, :, cols],
                near_send.at[slot, j],
                near_recv.at[slot, j],
                peer(*CORE),
            )
            copy.start()
            self.near_copies.append(copy)

    def forward(self, j):
        yh, core, _, _ = place()
        _, _, far_send, far_recv = self.sems
        cols = pl.ds(j * CW, CW)
        self.near_copies[2 * j].wait_recv()
        self.out_low[:, cols] = (
            self.part[rows_of((1 - yh) * 2 + core, OWN), cols].astype(F32)
            + self.near[0, :, cols].astype(F32)
        ).astype(BF16)
        copy = remote(
            self.out_low.at[:, cols], self.far.at[:, cols], far_send.at[j], far_recv.at[j],
            peer(*FAR),
        )
        copy.start()
        self.far_copies.append(copy)

    def finish(self):
        yh, core, _, _ = place()
        for j in range(NC):
            cols = pl.ds(j * CW, CW)
            self.near_copies[2 * j + 1].wait_recv()
            self.acc[:, cols] = self.part[rows_of(yh * 2 + core, OWN), cols].astype(
                F32
            ) + self.near[1, :, cols].astype(F32)
        for j in range(NC):
            cols = pl.ds(j * CW, CW)
            self.far_copies[j].wait_recv()
            self.acc[:, cols] = self.acc[:, cols] + self.far[:, cols].astype(F32)
        for copy in self.near_copies + self.far_copies:
            copy.wait_send()

    def begin(self, produce):
        for j in range(NC):
            produce(j)
            self.send(j)
            if j > 0:
                self.forward(j - 1)
        self.forward(NC - 1)

    def run(self, produce):
        self.begin(produce)
        self.finish()


class Gather:
    def __init__(self, out, sems):
        self.out, self.sems = out, sems

    def begin(self):
        yh, core, _, _ = place()
        own_send, own_recv, far_send, far_recv, _, _ = self.sems
        mine = rows_of(yh * 2 + core, OWN)
        self.far_copies, self.own_copies, self.on_copies = [], [], []
        for j in range(NC):
            block = self.out.at[mine, pl.ds(j * CW, CW)]
            copy = remote(block, block, far_send.at[j], far_recv.at[j], peer(*FAR))
            copy.start()
            self.far_copies.append(copy)
        for j in range(NC):
            block = self.out.at[mine, pl.ds(j * CW, CW)]
            copy = remote(block, block, own_send.at[j], own_recv.at[j], peer(*CORE))
            copy.start()
            self.own_copies.append(copy)

    def finish(self, use=lambda j: None):
        yh, core, _, _ = place()
        on_send, on_recv = self.sems[4:]
        other = rows_of((1 - yh) * 2 + core, OWN)

        def whole(j):
            self.own_copies[j].wait_recv()
            self.on_copies[j].wait_recv()
            use(j)

        for j in range(NC):
            self.far_copies[j].wait_recv()
            block = self.out.at[other, pl.ds(j * CW, CW)]
            copy = remote(block, block, on_send.at[j], on_recv.at[j], peer(*CORE))
            copy.start()
            self.on_copies.append(copy)
            if j > 0:
                whole(j - 1)
        whole(NC - 1)
        for copy in self.far_copies + self.own_copies + self.on_copies:
            copy.wait_send()


def gather_rows(out, sems, use=lambda j: None):
    gather = Gather(out, sems)
    gather.begin()
    gather.finish(use)


REDUCE_SCRATCH = [
    pltpu.VMEM((2, OWN, D), BF16),
    pltpu.VMEM((OWN, D), BF16),
    pltpu.VMEM((OWN, D), BF16),
    pltpu.VMEM((OWN, D), F32),
    pltpu.SemaphoreType.DMA((2, NC)),
    pltpu.SemaphoreType.DMA((2, NC)),
    pltpu.SemaphoreType.DMA((NC,)),
    pltpu.SemaphoreType.DMA((NC,)),
]
GATHER_SCRATCH = [pltpu.SemaphoreType.DMA((NC,))] * 6


def norm_scale(v):
    return lax.rsqrt(jnp.mean(v * v, axis=1, keepdims=True) + EPS)


def norm_back(v, r, g, dy):
    column_sum = jnp.sum(dy * g * v, axis=1, keepdims=True)
    return r * g * dy - v * (r * r * r) * (column_sum / D)


def input_tile(ref, j):
    return ref[:, pl.ds(pl.multiple_of(j * CW, CW), CW)]


def forward_kernel(r):
    yh, core, _, _ = place()
    t = yh * 2 + core
    greet(FF_PEERS)

    def begin(name, src, dst):
        return FF_MOVES[name].start(src, dst, *r.moves[name])

    load_count = iter(range(32))

    def load(src, dst):
        copy = pltpu.make_async_copy(src, dst, r.load_sems.at[next(load_count)])
        copy.start()
        return copy

    width = 4 * HD
    places = [r.down_vmem.at[:, pl.ds(n * width, width)] for n in range(3)]
    features_load = load(r.features, r.features_vmem)
    value_load = load(r.w_value, places[0])
    key_load = load(r.w_key, places[1])
    query_load = load(r.w_query, places[2])
    features_own_load = load(r.features.at[rows_of(t, OWN)], r.features_own)
    top_own_load = load(r.cotangent.at[rows_of(t, OWN)], r.top_own)

    def projected(n):
        return dot(
            r.features_vmem[...], r.down_vmem[:, n * width : (n + 1) * width], ((1,), (0,))
        )

    wait([features_load, value_load])
    r.value[...] = projected(0).astype(BF16)
    greeted(FF_PEERS)

    def project():
        key_load.wait()
        r.k_raw[...] = projected(1)
        query_load.wait()
        r.q_raw[...] = projected(2)

    weights = attend_part(
        project, r.q_raw, r.k_raw, r.value, r.seg, r.q_gain, r.k_gain,
        r.attended, r.q_head, r.k_head, r.v_head, r.probs, r.scales, *r.attend,
        lambda: [
            load(r.w_out, r.out_vmem),
            load(r.w_gate, r.gate_vmem),
            load(r.w_up, r.up_vmem),
            load(r.w_down, r.down_vmem),
        ],
    )
    saved = [
        load(r.q_head, r.q_head_out),
        load(r.k_head, r.k_head_out),
        load(r.v_head, r.v_head_out),
        load(r.probs, r.probs_out),
        load(r.q_raw, r.q_raw_out),
        load(r.k_raw, r.k_raw_out),
        load(r.scales, r.scales_out),
    ]
    weights[0].wait()

    def attn_part(j):
        r.part[:, j * CW : (j + 1) * CW] = dot(
            r.attended[...], r.out_vmem[:, j * CW : (j + 1) * CW], ((1,), (0,))
        ).astype(BF16)

    Reduce(r.part, *r.reduce).run(attn_part)
    features_own_load.wait()
    v = r.reduce[3][...]
    state = r.features_own[...].astype(F32) + v * norm_scale(v) * r.attn_gain[...]
    r.hidden[rows_of(t, OWN), :] = state.astype(BF16)
    r.attn_own[...] = v
    r.hidden_own[...] = state
    features_copies = begin(FF.features_half, r.features_vmem, r.features_half)
    attended_copies = begin(FF.attended_all, r.attended, r.attended_all)
    wait(weights[1:])

    def hidden_units(k):
        rows = pl.ds(k * CW, CW)

        def some(j, _):
            cols = pl.ds(pl.multiple_of(j * CW, CW), CW)
            gate = dot(r.hidden[:, rows], r.gate_vmem[rows, cols], ((1,), (0,)))
            upward = dot(r.hidden[:, rows], r.up_vmem[rows, cols], ((1,), (0,)))
            if k > 0:
                gate += r.act[:, cols]
                upward += r.slope[:, cols]
            if k < NC - 1:
                r.act[:, cols] = gate
                r.slope[:, cols] = upward
            else:
                sigma = jax.nn.sigmoid(gate)
                activated = gate * sigma
                r.mixed[:, cols] = (activated * upward).astype(BF16)
                r.act[:, cols] = activated
                r.slope[:, cols] = upward * sigma * (1.0 + gate * (1.0 - sigma))
            return 0

        lax.fori_loop(0, NC, some, 0)

    gather_rows(r.hidden, r.gather, hidden_units)
    hidden_copies = begin(FF.hidden_half, r.hidden, r.hidden_half)
    mixed_copies = begin(FF.mixed_right, r.mixed, r.mixed_right)

    def mlp_part(j):
        r.part[:, j * CW : (j + 1) * CW] = dot(
            r.mixed[...], r.down_vmem[:, j * CW : (j + 1) * CW], ((1,), (0,))
        ).astype(BF16)

    Reduce(r.part, *r.reduce).run(mlp_part)
    top_own_load.wait()
    v = r.reduce[3][...]
    z = norm_scale(v)
    dy = r.top_own[...].astype(F32)
    g = r.mlp_gain[...]
    r.d_mlp[rows_of(t, OWN), :] = norm_back(v, z, g, dy).astype(BF16)
    r.result_own[...] = (r.hidden_own[...] + v * z * g).astype(BF16)
    mlp_gain_grad = jnp.sum(dy * v * z, axis=0, keepdims=True)
    z = lax.axis_index("dp")
    gate_copies = FF_MOVES[FF.gate_right].copies(
        r.d_gate, r.gate_right, *r.moves[FF.gate_right]
    )
    up_copies = FF_MOVES[FF.up_right].copies(r.d_up, r.up_right, *r.moves[FF.up_right])

    gather_rows(r.d_mlp, r.gather)
    for s in (2, 1, 3, 0):
        cols = pl.ds(pl.multiple_of(lax.rem(z + s, 4) * CW, CW), CW)
        d_mixed = dot(r.d_mlp[...], r.down_vmem[cols, :], ((1,), (1,)))
        r.d_up[:, cols] = (d_mixed * r.act[:, cols]).astype(BF16)
        r.d_gate[:, cols] = (d_mixed * r.slope[:, cols]).astype(BF16)
        gate_copies[s - 1].start()
        up_copies[s - 1].start()
    right_copies = gate_copies + up_copies
    top_copies = begin(FF.top_half, r.d_mlp, r.top_half)
    wait(features_copies)
    features_copies = begin(FF.features_rest, r.features_half, r.features_rest)

    def back_part(j):
        rows = pl.ds(j * CW, CW)
        r.part[:, j * CW : (j + 1) * CW] = (
            dot(r.d_gate[...], r.gate_vmem[rows, :], ((1,), (1,)))
            + dot(r.d_up[...], r.up_vmem[rows, :], ((1,), (1,)))
        ).astype(BF16)

    Reduce(r.part, *r.reduce).run(back_part)
    wait(hidden_copies)
    hidden_copies = begin(FF.hidden_rest, r.hidden_half, r.hidden_rest)
    dy = r.top_own[...].astype(F32) + r.reduce[3][...]
    v = r.attn_own[...]
    a = norm_scale(v)
    g = r.attn_gain[...]
    r.d_attn[rows_of(t, OWN), :] = norm_back(v, a, g, dy).astype(BF16)
    r.d_hidden_own[...] = dy
    row = lax.broadcasted_iota(jnp.int32, (8, D), 0)
    attn_grad = jnp.sum(dy * v * a, axis=0, keepdims=True)
    r.gain_rows[...] = jnp.where(row == 0, attn_grad, mlp_gain_grad)
    gather_rows(r.d_attn, r.gather)
    r.d_attended[...] = dot(r.d_attn[...], r.out_vmem[...], ((1,), (1,))).astype(BF16)
    wait(right_copies + hidden_copies + features_copies + attended_copies)
    wait(mixed_copies + top_copies + saved)


WIDE = jax.ShapeDtypeStruct((T, D), BF16)
NARROW = jax.ShapeDtypeStruct((T, 4 * HD), BF16)
HALVES = jax.ShapeDtypeStruct((4, T, D // 2), BF16)
FF_MOVES = dict(
    features_half=half_move(WIDE, "x"),
    features_rest=core_move(HALVES),
    attended_all=full_move(NARROW, "z"),
    hidden_half=half_move(WIDE, "z"),
    hidden_rest=core_move(HALVES),
    gate_right=quarter_move(WIDE, "z"),
    up_right=quarter_move(WIDE, "z"),
    mixed_right=quarter_move(WIDE, "x"),
    top_half=half_move(WIDE, "x"),
)
FF = Names(**{name: name for name in FF_MOVES})
FF_PEERS = distinct(
    [CORE, FAR]
    + [(0, dy, dx, 0, 0) for dy in range(2) for dx in range(4) if dy or dx]
    + peers_of(FF_MOVES)
)


def attend_scratch():
    dma = pltpu.SemaphoreType.DMA
    return [
        pltpu.VMEM((8, 8, T), F32),
        pltpu.VMEM((T, 4 * HD), BF16),
        pltpu.VMEM((T, 4 * HD), BF16),
        pltpu.VMEM((2, 8, T), F32),
        pltpu.VMEM((8, T), F32),
        pltpu.VMEM((8, T), F32),
        pltpu.VMEM((4, T, HD), BF16),
        dma((4, 4)),
        dma((4, 4)),
        dma((4,)),
        dma((4,)),
        dma((8,)),
        dma((8,)),
        dma((2,)),
        dma((2,)),
        dma((4,)),
        dma((4,)),
    ]


def forward(small, large):
    weight, wide = pltpu.VMEM((D, D), BF16), pltpu.VMEM((T, D), BF16)
    own, tall = pltpu.VMEM((OWN, D), F32), pltpu.VMEM((T, D), F32)
    own_low = pltpu.VMEM((OWN, D), BF16)
    saved = dict(
        q_head=((4 * T, HD), BF16),
        k_head=((8 * T, HD), BF16),
        v_head=((8 * T, HD), BF16),
        probs=((4, T, 8 * T), BF16),
        q_raw=((T, 4 * HD), F32),
        k_raw=((T, 4 * HD), F32),
        scales=((T, HD), F32),
    )
    scratch = dict(
        out_vmem=pltpu.VMEM((4 * HD, D), BF16),
        gate_vmem=weight,
        up_vmem=weight,
        down_vmem=weight,
        features_own=own_low,
        top_own=own_low,
        part=wide,
        hidden=wide,
        act=tall,
        slope=tall,
        d_gate=wide,
        d_up=wide,
        d_mlp=wide,
        mixed=wide,
        attn_own=own,
        hidden_own=own,
        load_sems=pltpu.SemaphoreType.DMA((32,)),
        reduce=REDUCE_SCRATCH,
        gather=GATHER_SCRATCH,
        moves=move_scratch(FF_MOVES),
        features_vmem=wide,
        value=pltpu.VMEM((T, 4 * HD), BF16),
        attended=pltpu.VMEM((T, 4 * HD), BF16),
        attend=attend_scratch(),
        **{name: pltpu.VMEM(*saved[name]) for name in saved},
    )
    outs = dict(
        d_attended=((T, 4 * HD), BF16),
        d_hidden_own=((OWN, D), F32),
        result_own=((OWN, D), BF16),
        gain_rows=((8, D), F32),
        d_attn=((T, D), BF16),
    )
    large_outs = {name: move.out for name, move in FF_MOVES.items()}
    large_outs |= {name + "_out": out for name, out in saved.items()}
    return run_kernel(forward_kernel, 1, small, large, outs, large_outs, scratch, 62)


def row_device(yl, x):
    return {"ctx": yl * 4 + x}


ATTEND_PEERS = [CORE, FAR] + [(0, dy, dx, 0, 0) for dy in range(2) for dx in range(4) if dy or dx]


def tensor_sum(own, near, far, send, recv):
    copy = remote(own.at[0], near, send.at[0], recv.at[0], peer(*CORE))
    copy.start()
    copy.wait_recv()
    own[1] = own[0] + near[...]
    again = remote(own.at[1], far, send.at[1], recv.at[1], peer(*FAR))
    again.start()
    again.wait_recv()
    total = own[1] + far[...]
    copy.wait_send()
    again.wait_send()
    return total


def exact_dot(a, b, dims):
    return lax.dot_general(
        a, b, (dims, ((), ())), preferred_element_type=F32, precision=lax.Precision.HIGHEST
    )


def token_rows(values, row):
    pick = lax.broadcasted_iota(jnp.int32, (8, values.shape[1]), 0) == row
    return exact_dot(jnp.where(pick, 1.0, 0.0), values, ((1,), (1,)))


def token_columns(rows):
    lane = lax.broadcasted_iota(jnp.int32, (8, HD), 1) // (HD // 2)
    pick = lax.broadcasted_iota(jnp.int32, (8, HD), 0) == lane
    return exact_dot(rows, jnp.where(pick, 1.0, 0.0), ((0,), (0,)))


class Spread:
    def __init__(self, src, dst, sems):
        self.src, self.dst = src, dst
        self.send, self.recv, self.down_send, self.down_recv = sems

    def row_copy(self, s):
        _, _, yl, x = place()
        h = lax.rem(x + s, 4)
        return remote(
            self.src.at[:, pl.ds(pl.multiple_of(h * HD, HD), HD)],
            self.dst.at[rows_of(yl * 4 + x, T)],
            self.send.at[s],
            self.recv.at[s],
            row_device(yl, h),
        )

    def down_copy(self, s):
        _, _, yl, x = place()
        h = lax.rem(x + s, 4)
        return remote(
            self.src.at[:, pl.ds(pl.multiple_of(h * HD, HD), HD)],
            self.dst.at[rows_of(x, T)],
            self.down_send.at[s],
            self.down_recv.at[s],
            row_device(1, h),
        )


def keep_own(src, dst, block):
    _, _, _, x = place()
    dst[rows_of(block, T), :] = src[:, pl.ds(pl.multiple_of(x * HD, HD), HD)]


def attend_part(
    project, q_raw, k_raw, value, seg, q_gain, k_gain,
    attended, q_head, k_head, v_head, probs_out, scale_out,
    seg_all, q_low, k_low, sums, near, far, result,
    v_sems, k_sems, q_send, q_recv, s_send, s_recv, sum_send, sum_recv, a_send, a_recv,
    load_weights,
):
    yh, core, yl, x = place()
    me = yl * 4 + x
    v_sems = [v_sems.at[i] for i in range(4)]
    k_sems = [k_sems.at[i] for i in range(4)]
    values = Spread(value, v_head, v_sems)
    keys = Spread(k_low, k_head, k_sems)

    @pl.when(yl == 0)
    def _():
        for s in range(4):
            values.down_copy(s).start()

    for s in (1, 2, 3):
        values.row_copy(s).start()
    seg_all[me] = jnp.broadcast_to(seg[...].astype(F32), (8, T))

    def seg_copy(s):
        dx, dy = s % 4, s // 4
        to = row_device(lax.rem(yl + dy, 2), lax.rem(x + dx, 4))
        return remote(seg_all.at[me], seg_all.at[me], s_send.at[s], s_recv.at[s], to)

    for s in range(1, 8):
        seg_copy(s).start()

    project()
    qr, kr = q_raw[...], k_raw[...]
    sums[0] = token_rows(qr * qr, 0) + token_rows(kr * kr, 1)
    keep_own(value, v_head, me)
    weights = load_weights()
    scales = token_columns(
        lax.rsqrt(tensor_sum(sums, near, far, sum_send, sum_recv) / D + EPS)
    )
    scale_out[...] = scales
    k_low[...] = (kr * scales[:, HD // 2 : HD // 2 + 1] * k_gain[...]).astype(BF16)

    @pl.when(yl == 0)
    def _():
        for s in range(4):
            keys.down_copy(s).start()

    for s in (1, 2, 3):
        keys.row_copy(s).start()
    q_low[...] = (qr * scales[:, :1] * q_gain[...]).astype(BF16)

    def q_copy(s):
        h = lax.rem(x + s, 4)
        return remote(
            q_low.at[:, pl.ds(pl.multiple_of(h * HD, HD), HD)],
            q_head.at[rows_of(x, T)],
            q_send.at[s],
            q_recv.at[s],
            row_device(yl, h),
        )

    for s in (1, 2, 3):
        q_copy(s).start()
    keep_own(k_low, k_head, me)
    keep_own(q_low, q_head, x)
    for s in range(1, 8):
        seg_copy(s).wait()
    for s in (1, 2, 3):
        values.row_copy(s).wait()
        keys.row_copy(s).wait()
        q_copy(s).wait()

    @pl.when(yl == 0)
    def _():
        for s in range(4):
            values.down_copy(s).wait_send()
            keys.down_copy(s).wait_send()

    @pl.when(yl == 1)
    def _():
        for s in range(4):
            values.down_copy(s).wait_recv()
            keys.down_copy(s).wait_recv()

    lane = lax.broadcasted_iota(jnp.int32, (8, HD), 0)
    pick = jnp.where(lane == 0, 1.0, 0.0)

    def attend(row, i):
        blocks = row * 4 + i + 1
        width = blocks * T
        q = q_head[i * T : (i + 1) * T, :]
        scores = dot(q, k_head[:width, :], ((1,), (1,))) * HD ** (-0.5)
        own_seg = dot(seg_all[row * 4 + i], pick, ((0,), (0,)))[:, :1]
        seg_keys = jnp.concatenate([seg_all[b, :1, :] for b in range(blocks)], axis=1)
        q_place = lax.broadcasted_iota(jnp.int32, (T, width), 0) + (blocks - 1) * T
        k_place = lax.broadcasted_iota(jnp.int32, (T, width), 1)
        counted = (k_place <= q_place) & (seg_keys == own_seg)
        scores = jnp.where(counted, scores, -1e30)
        exps = jnp.exp(scores - jnp.max(scores, axis=1, keepdims=True))
        probs = (exps * (1.0 / jnp.sum(exps, axis=1, keepdims=True))).astype(BF16)
        probs_out[i, :, :width] = probs
        result[i] = dot(probs, v_head[:width, :], ((1,), (0,))).astype(BF16)

    def back_copy(i):
        return remote(
            result.at[i],
            attended.at[:, pl.ds(pl.multiple_of(x * HD, HD), HD)],
            a_send.at[i],
            a_recv.at[x],
            row_device(yl, i),
        )

    for i in range(4):
        for row in range(2):

            @pl.when(yl == row)
            def _():
                attend(row, i)

        @pl.when(x == i)
        def _():
            attended[:, i * HD : (i + 1) * HD] = result[i]

        @pl.when(x != i)
        def _():
            back_copy(i).start()

    for h in range(4):

        @pl.when(x != h)
        def _():
            back_copy(h).wait_send()
            remote(
                result.at[h],
                attended.at[:, h * HD : (h + 1) * HD],
                a_send.at[h],
                a_recv.at[h],
                row_device(yl, h),
            ).wait_recv()
    return weights


def product_rows(left, right):
    return dot(
        left.reshape(4 * T, left.shape[2]), right.reshape(4 * T, right.shape[2]), ((0,), (0,))
    ).astype(BF16)


def blocks_out(partial, slots, send, recv, axis, start=0, width=None):
    me = spot(axis)
    cols = pl.ds(start, partial.shape[-1] if width is None else width)
    copies = [
        remote(
            partial.at[lax.rem(me + s, 4), :, :, :, cols], slots.at[s - 1, :, :, :, cols],
            send.at[s - 1], recv.at[s - 1], peer(*along(axis, s)),
        )
        for s in (1, 2, 3)
    ]
    for copy in copies:
        copy.start()
    return copies


def add_blocks(total, partial, slots, axis):
    me = spot(axis)
    for y in range(2):
        for j in range(4):
            block = partial[me, y, j].astype(F32)
            for s in range(3):
                block += slots[s, y, j].astype(F32)
            total[y, j] = block.astype(total.dtype)


HALF_GRID = (2, 4, 64)
BACK_MOVES = dict(
    attn_left=quarter_move(WIDE, "z"),
    q_right=quarter_move(NARROW, "x"),
    k_right=quarter_move(NARROW, "x"),
    v_right=quarter_move(NARROW, "x"),
    mlp_in=final_move(jax.ShapeDtypeStruct(HALF_GRID + (1024,), BF16), "z"),
    mlp_down=final_move(jax.ShapeDtypeStruct(HALF_GRID + (512,), BF16), "x"),
    qkv=final_move(jax.ShapeDtypeStruct(HALF_GRID + (384,), BF16), "x"),
    out=final_move(jax.ShapeDtypeStruct(HALF_GRID + (512,), BF16), "x"),
    tiles=final_move(jax.ShapeDtypeStruct((2, 4, 16, HD), F32), "x"),
)
BACK = Names(**{name: name for name in BACK_MOVES})
BACK_PEERS = distinct(ATTEND_PEERS + peers_of(BACK_MOVES))


def back_scratch():
    dma = pltpu.SemaphoreType.DMA

    def vmem(*shape, kind=BF16):
        return pltpu.VMEM(shape, kind)

    rows = (2, 4, 64)
    return dict(
        q_head=vmem(4 * T, HD),
        k_head=vmem(8 * T, HD),
        v_head=vmem(8 * T, HD),
        probs=vmem(2, T, 8 * T),
        q_raw=vmem(T, 4 * HD, kind=F32),
        k_raw=vmem(T, 4 * HD, kind=F32),
        scales=vmem(T, HD, kind=F32),
        wq=vmem(D, 4 * HD),
        wk=vmem(D, 4 * HD),
        wv=vmem(D, 4 * HD),
        left=vmem(2, 4, T, D // 2),
        top=vmem(2, 4, T, D // 2),
        gate_right=vmem(4, T, 512),
        up_right=vmem(4, T, 512),
        mixed_right=vmem(4, T, 512),
        attn_left=vmem(4, T, 512),
        attended_all=vmem(4, T, 512),
        q_right=vmem(4, T, HD),
        k_right=vmem(4, T, HD),
        v_right=vmem(4, T, HD),
        in_part=vmem(4, *rows, 1024),
        in_slots=vmem(2, *rows, 1024),
        in_across=vmem(2, 2, 2, 64, 1024),
        in_sum=vmem(*rows, 1024),
        down_part=vmem(4, *rows, 512),
        down_slots=vmem(3, *rows, 512),
        down_sum=vmem(*rows, 512),
        qkv_part=vmem(4, *rows, 384),
        qkv_slots=vmem(3, *rows, 384),
        qkv_sum=vmem(*rows, 384),
        out_part=vmem(*rows, 512),
        tile_part=vmem(4, 2, 4, 16, HD, kind=F32),
        tile_slots=vmem(3, 2, 4, 16, HD, kind=F32),
        tile_sum=vmem(2, 4, 16, HD, kind=F32),
        d_q=vmem(T, 4 * HD),
        d_k=vmem(T, 4 * HD),
        d_v=vmem(T, 4 * HD),
        part=vmem(T, D),
        d_out=vmem(4 * T, HD),
        dq_buf=vmem(4, T, HD),
        dk_buf=vmem(8, T, HD),
        dv_buf=vmem(8, T, HD),
        dk_acc=vmem(8 * T, HD, kind=F32),
        dv_acc=vmem(8 * T, HD, kind=F32),
        dq_got=vmem(4, T, HD),
        dk_got=vmem(2, 4, T, HD),
        dv_got=vmem(2, 4, T, HD),
        sums=vmem(2, 8, T, kind=F32),
        near=vmem(8, T, kind=F32),
        far=vmem(8, T, kind=F32),
        gain_near=vmem(8, D, kind=F32),
        gain_far=vmem(8, D, kind=F32),
        gain_sum=vmem(8, D, kind=F32),
        load_sems=dma((32,)),
        in_send=dma((2, 4)),
        in_recv=dma((2, 4)),
        across_send=dma((2,)),
        across_recv=dma((2,)),
        down_send=dma((3,)),
        down_recv=dma((3,)),
        qkv_send=dma((3,)),
        qkv_recv=dma((3,)),
        v_send=dma((3,)),
        v_recv=dma((3,)),
        tile_send=dma((3,)),
        tile_recv=dma((3,)),
        o_send=dma((4,)),
        o_recv=dma((4,)),
        dq_send=dma((4,)),
        dq_recv=dma((4,)),
        dk_send=dma((8,)),
        dk_recv=dma((2, 4)),
        dv_send=dma((8,)),
        dv_recv=dma((2, 4)),
        sum_send=dma((2,)),
        sum_recv=dma((2,)),
        gain_send=dma((2,)),
        gain_recv=dma((2,)),
        top_send=dma((1,)),
        top_recv=dma((1,)),
        result_send=dma((3,)),
        result_recv=dma((3,)),
        reduce=REDUCE_SCRATCH,
        gather=GATHER_SCRATCH,
        moves=move_scratch(BACK_MOVES),
    )


def backward_kernel(r):
    yh, core, yl, x = place()
    t = yh * 2 + core
    scale = HD ** (-0.5)
    greet(BACK_PEERS)

    def begin(name, src, dst):
        return BACK_MOVES[name].start(src, dst, *r.moves[name])

    load_count = iter(range(32))

    def load(src, dst):
        copy = pltpu.make_async_copy(src, dst, r.load_sems.at[next(load_count)])
        copy.start()
        return copy

    hidden0_load = load(r.hidden_half, r.left.at[core])
    gate_right_load = load(r.gate_right_in, r.gate_right)
    up_right_load = load(r.up_right_in, r.up_right)
    hidden1_load = load(r.hidden_rest, r.left.at[1 - core])
    greeted(BACK_PEERS)

    def o_copy(s):
        h = lax.rem(x + s, 4)
        return remote(
            r.d_attended.at[:, pl.ds(pl.multiple_of(h * HD, HD), HD)],
            r.d_out.at[rows_of(x, T)],
            r.o_send.at[s],
            r.o_recv.at[s],
            row_device(yl, h),
        )

    for s in (1, 2, 3):
        o_copy(s).start()
    gain_near_copy = remote(
        r.gains, r.gain_near, r.gain_send.at[0], r.gain_recv.at[0], peer(*CORE)
    )
    gain_near_copy.start()
    top_copy = remote(
        r.top_half, r.top.at[core], r.top_send.at[0], r.top_recv.at[0], peer(*CORE)
    )
    top_copy.start()
    mine, other = rows_of(t, OWN), rows_of((1 - yh) * 2 + core, OWN)
    result_load = load(r.result_own, r.outputs.at[mine])
    result_copies = [
        remote(
            r.result_own, r.outputs.at[mine], r.result_send.at[n], r.result_recv.at[n], to
        )
        for n, to in enumerate((peer(*FAR), peer(*CORE)))
    ]
    for copy in result_copies:
        copy.start()
    attn_left = begin(BACK.attn_left, r.d_attn, r.attn_left)
    keep_own(r.d_attended, r.d_out, x)
    r.dk_acc[...] = jnp.zeros_like(r.dk_acc)
    r.dv_acc[...] = jnp.zeros_like(r.dv_acc)

    wait([hidden0_load, gate_right_load, up_right_load, hidden1_load])
    q_head_load = load(r.q_head_in, r.q_head)
    k_head_load = load(r.k_head_in, r.k_head)
    v_head_load = load(r.v_head_in, r.v_head)
    probs_loads = [load(r.probs_in.at[i], r.probs.at[i]) for i in range(2)]
    q_raw_load = load(r.q_raw_in, r.q_raw)
    k_raw_load = load(r.k_raw_in, r.k_raw)
    scales_load = load(r.scales_in, r.scales)
    mixed_right_load = load(r.mixed_right_in, r.mixed_right)
    top_load = load(r.top_half, r.top.at[core])
    attended_all_load = load(r.attended_all_in, r.attended_all)
    w_query_load = load(r.w_query, r.wq)
    w_key_load = load(r.w_key, r.wk)
    w_value_load = load(r.w_value, r.wv)
    onward, backward_way = along("x", 1), along("x", 3)
    after, before = lax.rem(x + 1, 4), lax.rem(x + 3, 4)
    opposite = lax.rem(x + 2, 4)
    across = [
        remote(
            r.in_part.at[opposite, :, pl.ds(2 * n, 2)], r.in_across.at[n], r.across_send.at[n],
            r.across_recv.at[n], peer(*way),
        )
        for n, way in enumerate((onward, backward_way))
    ]
    in_copies = []

    z = lax.axis_index("dp")

    def in_piece(step):
        piece = lax.rem(z + step, 4)
        for n, (block, way) in enumerate(((after, onward), (before, backward_way))):
            copy = remote(
                r.in_part.at[block, :, piece], r.in_slots.at[n, :, piece],
                r.in_send.at[n, step], r.in_recv.at[n, step], peer(*way),
            )
            copy.start()
            in_copies.append(copy)

    in_final = BACK_MOVES[BACK.mlp_in].copies(r.in_sum, r.mlp_in, *r.moves[BACK.mlp_in])

    def in_place(step):
        piece = lax.rem(z + step, 4)
        wait(in_copies[2 * step : 2 * step + 2])
        for y in range(2):
            r.in_sum[y, piece] = (
                r.in_part[x, y, piece].astype(F32)
                + r.in_slots[0, y, piece].astype(F32)
                + r.in_slots[1, y, piece].astype(F32)
            ).astype(BF16)
        for n in ((3, 7), (0, 4), (1, 5), (2, 6))[step]:
            in_final[n].start()

    for i in range(4):
        rows = r.left[i // 2, :, :, (i % 2) * 512 : (i % 2 + 1) * 512]
        for n, half in enumerate((r.gate_right, r.up_right)):
            got = product_rows(rows, half[...])
            for y in range(2):
                for j in range(4):
                    r.in_part[j, y, i, :, n * 512 : (n + 1) * 512] = got[
                        (y * 4 + j) * 64 : (y * 4 + j + 1) * 64
                    ]
        if i % 2 == 1:
            across[i // 2].start()
    features0_load = load(r.features_half, r.left.at[core])
    features1_load = load(r.features_rest, r.left.at[1 - core])
    gain_near_copy.wait()
    r.gain_sum[...] = r.gains[...] + r.gain_near[...]
    gain_far_copy = remote(
        r.gain_sum, r.gain_far, r.gain_send.at[1], r.gain_recv.at[1], peer(*FAR)
    )
    gain_far_copy.start()

    for s in (1, 2, 3):
        o_copy(s).wait()
    wait([q_head_load, k_head_load, v_head_load])

    def back(row, i):
        width = (row * 4 + i + 1) * T
        q = r.q_head[i * T : (i + 1) * T, :]
        do = r.d_out[i * T : (i + 1) * T, :]
        probs_low = r.probs[i % 2, :, :width]
        probs = probs_low.astype(F32)
        d_probs = dot(do, r.v_head[:width, :], ((1,), (1,)))
        delta = jnp.sum(probs * d_probs, axis=1, keepdims=True)
        d_scores = (probs * (d_probs - delta)).astype(BF16)
        r.dq_buf[i] = (dot(d_scores, r.k_head[:width, :], ((1,), (0,))) * scale).astype(BF16)
        r.dk_acc[:width, :] += dot(d_scores, q, ((0,), (0,)))
        r.dv_acc[:width, :] += dot(probs_low, do, ((0,), (0,)))

    def dq_copy(i):
        return remote(
            r.dq_buf.at[i], r.dq_got.at[x], r.dq_send.at[i], r.dq_recv.at[x], row_device(yl, i)
        )

    for i in range(4):
        probs_loads[i].wait()
        for row in range(2):

            @pl.when(yl == row)
            def _():
                back(row, i)

        if i < 2:
            probs_loads.append(load(r.probs_in.at[i + 2], r.probs.at[i]))

        @pl.when(x == i)
        def _():
            r.dq_got[i] = r.dq_buf[i]

        @pl.when(x != i)
        def _():
            dq_copy(i).start()

    def kv_copy(j, buf, got, send, recv):
        return remote(
            buf.at[j], got.at[yl, x], send.at[j], recv.at[yl, x], row_device(j // 4, j % 4)
        )

    dk_args = (r.dk_buf, r.dk_got, r.dk_send, r.dk_recv)
    dv_args = (r.dv_buf, r.dv_got, r.dv_send, r.dv_recv)
    for j in range(8):
        r.dk_buf[j] = (r.dk_acc[j * T : (j + 1) * T, :] * scale).astype(BF16)
        r.dv_buf[j] = r.dv_acc[j * T : (j + 1) * T, :].astype(BF16)
        here = (yl == j // 4) & (x == j % 4)

        @pl.when(here)
        def _():
            r.dk_got[j // 4, j % 4] = r.dk_buf[j]
            r.dv_got[j // 4, j % 4] = r.dv_buf[j]

        sends = (yl >= j // 4) & ~here

        @pl.when(sends)
        def _():
            kv_copy(j, *dk_args).start()
            kv_copy(j, *dv_args).start()

    result_copies[0].wait_recv()
    result_copies.append(
        remote(
            r.outputs.at[other],
            r.outputs.at[other],
            r.result_send.at[2],
            r.result_recv.at[2],
            peer(*CORE),
        )
    )
    result_copies[2].start()

    mixed_right_load.wait()
    top_load.wait()
    top_copy.wait()
    for i in range(4):
        left = r.top[i // 2, :, :, (i % 2) * 512 : (i % 2 + 1) * 512]
        r.down_part[i] = product_rows(left, r.mixed_right[...]).reshape(2, 4, 64, 512)
    down_copies = blocks_out(r.down_part, r.down_slots, r.down_send, r.down_recv, "z")
    attended_all_load.wait()
    wait(attn_left)
    r.out_part[...] = product_rows(r.attn_left[...], r.attended_all[...]).reshape(2, 4, 64, 512)

    for n, block in enumerate((after, before)):
        across[n].wait()
        for y in range(2):
            for m in range(2):
                mine_too = r.in_part[block, y, 2 * n + m].astype(F32)
                r.in_part[block, y, 2 * n + m] = (
                    mine_too + r.in_across[n, y, m].astype(F32)
                ).astype(BF16)

    for h in range(4):

        @pl.when(x != h)
        def _():
            dq_copy(h).wait_send()
            remote(
                r.dq_buf.at[h], r.dq_got.at[h], r.dq_send.at[h], r.dq_recv.at[h],
                row_device(yl, h),
            ).wait_recv()

        for row in range(2):
            comes = (row >= yl) & ~((yl == row) & (x == h))

            @pl.when(comes)
            def _():
                for buf, got, send, recv in (dk_args, dv_args):
                    remote(
                        buf.at[0],
                        got.at[row, h],
                        send.at[0],
                        recv.at[row, h],
                        row_device(row, h),
                    ).wait_recv()

    for j in range(8):
        here = (yl == j // 4) & (x == j % 4)
        sends = (yl >= j // 4) & ~here

        @pl.when(sends)
        def _():
            kv_copy(j, *dk_args).wait_send()
            kv_copy(j, *dv_args).wait_send()

    @pl.when(yl == 1)
    def _():
        for h in range(4):
            r.dk_got[0, h] = jnp.zeros((T, HD), BF16)
            r.dv_got[0, h] = jnp.zeros((T, HD), BF16)

    in_piece(0)
    out_copies = begin(BACK.out, r.out_part, r.out)
    wait([q_raw_load, k_raw_load, scales_load])
    sums = jnp.zeros((8, T), F32)
    for h in range(4):
        cols = slice(h * HD, (h + 1) * HD)
        dq = r.dq_got[h].astype(F32)
        dk = r.dk_got[0, h].astype(F32) + r.dk_got[1, h].astype(F32)
        r.d_v[:, cols] = (r.dv_got[0, h].astype(F32) + r.dv_got[1, h].astype(F32)).astype(BF16)
        sums += token_rows(dq * r.q_raw[:, cols] * r.q_gain[:, cols], 0)
        sums += token_rows(dk * r.k_raw[:, cols] * r.k_gain[:, cols], 1)
    r.sums[0] = sums
    v_copies = begin(BACK.v_right, r.d_v, r.v_right)
    total = token_columns(tensor_sum(r.sums, r.near, r.far, r.sum_send, r.sum_recv))
    qs, ks = r.scales[:, :1], r.scales[:, HD // 2 : HD // 2 + 1]
    q_coef = qs * qs * qs * (total[:, :1] / D)
    k_coef = ks * ks * ks * (total[:, HD // 2 : HD // 2 + 1] / D)
    gain_far_copy.wait()
    both = r.gain_sum[...] + r.gain_far[...]
    tile = []
    for h in range(4):
        cols = slice(h * HD, (h + 1) * HD)
        dq = r.dq_got[h].astype(F32)
        dk = r.dk_got[0, h].astype(F32) + r.dk_got[1, h].astype(F32)
        qr, kr = r.q_raw[:, cols], r.k_raw[:, cols]
        r.d_q[:, cols] = (qs * r.q_gain[:, cols] * dq - qr * q_coef).astype(BF16)
        r.d_k[:, cols] = (ks * r.k_gain[:, cols] * dk - kr * k_coef).astype(BF16)
        tile.append((jnp.sum(dq * qr * qs, axis=0, keepdims=True), jnp.sum(dk * kr * ks, axis=0, keepdims=True)))
    qk_copies = begin(BACK.q_right, r.d_q, r.q_right) + begin(BACK.k_right, r.d_k, r.k_right)
    row = lax.broadcasted_iota(jnp.int32, (8, HD), 0)
    top_tile = jnp.zeros((8, HD), F32)
    for h in range(4):
        top_tile = jnp.where(row == h, tile[h][0], top_tile)
        top_tile = jnp.where(row == h + 4, tile[h][1], top_tile)
    for rank in range(32):
        to = (rank // 8, rank // 4 % 2, rank % 4)
        r.tile_part[(*to, slice(0, 8))] = top_tile
        r.tile_part[(*to, slice(8, 16))] = both[:, (rank // 2) * HD : (rank // 2 + 1) * HD]
    tile_copies = blocks_out(r.tile_part, r.tile_slots, r.tile_send, r.tile_recv, "z")

    wait([w_query_load, w_key_load, w_value_load])

    def input_part(j):
        rows = pl.ds(j * CW, CW)
        r.part[:, j * CW : (j + 1) * CW] = (
            dot(r.d_q[...], r.wq[rows, :], ((1,), (1,)))
            + dot(r.d_k[...], r.wk[rows, :], ((1,), (1,)))
            + dot(r.d_v[...], r.wv[rows, :], ((1,), (1,)))
        ).astype(BF16)

    reduce = Reduce(r.part, *r.reduce)
    reduce.begin(input_part)

    def qkv_product(n, right):
        for i in range(4):
            left = r.left[i // 2, :, :, (i % 2) * 512 : (i % 2 + 1) * 512]
            r.qkv_part[i, :, :, :, n * HD : (n + 1) * HD] = product_rows(left, right[...]).reshape(
                2, 4, 64, HD
            )

    wait([features0_load, features1_load])
    wait(v_copies)
    qkv_product(2, r.v_right)
    qkv_args = (r.qkv_part, r.qkv_slots)
    qkv_copies = blocks_out(*qkv_args, r.v_send, r.v_recv, "z", 2 * HD, HD)
    wait(qk_copies)
    for step in (1, 2, 3):
        in_piece(step)
    qkv_product(0, r.q_right)
    qkv_product(1, r.k_right)
    qkv_copies += blocks_out(*qkv_args, r.qkv_send, r.qkv_recv, "z", 0, 2 * HD)
    reduce.finish()
    r.input_grad[mine, :] = (r.d_hidden_own[...] + r.reduce[3][...]).astype(BF16)
    gather = Gather(r.input_grad, r.gather)
    gather.begin()

    for step in range(4):
        in_place(step)
    wait(down_copies)
    add_blocks(r.down_sum, r.down_part, r.down_slots, "z")
    down_final = begin(BACK.mlp_down, r.down_sum, r.mlp_down)
    wait(tile_copies)
    add_blocks(r.tile_sum, r.tile_part, r.tile_slots, "z")
    tile_final = begin(BACK.tiles, r.tile_sum, r.tiles)
    wait(qkv_copies)
    add_blocks(r.qkv_sum, r.qkv_part, r.qkv_slots, "z")
    qkv_final = begin(BACK.qkv, r.qkv_sum, r.qkv)
    gather.finish()
    result_load.wait()
    result_copies[0].wait_send()
    result_copies[1].wait()
    result_copies[2].wait()
    wait(tile_final + out_copies + down_final + in_final + qkv_final)


def backward(small, large):
    large_outs = dict(
        outputs=((T, D), BF16),
        tiles=((2, 4, 16, HD), F32),
        mlp_in=(HALF_GRID + (1024,), BF16),
        mlp_down=(HALF_GRID + (512,), BF16),
        qkv=(HALF_GRID + (384,), BF16),
        out=(HALF_GRID + (512,), BF16),
    )
    outs = dict(input_grad=((T, D), BF16))
    return run_kernel(backward_kernel, 6, small, large, outs, large_outs, back_scratch(), 62)


def results_kernel(
    rank_ref, tiles_in, mlp_in_in, mlp_down_in, qkv_in, out_in, outputs_in, input_grad_in,
    outputs, input_grad, query, key, value, out_grad, q_gain, k_gain, attn_gain, gate, up, down,
    mlp_gain, mlp_in, mlp_down, qkv, out, tiles, staged, sems,
):
    pairs = [
        (outputs_in, staged.at[0]), (input_grad_in, staged.at[1]),
        (mlp_in_in, mlp_in), (mlp_down_in, mlp_down), (qkv_in, qkv), (out_in, out),
        (tiles_in, tiles),
    ]
    copies = [pltpu.make_async_copy(a, b, sems.at[n]) for n, (a, b) in enumerate(pairs)]
    for copy in copies:
        copy.start()
    wait(copies[:2])
    onward = [
        pltpu.make_async_copy(staged.at[0], outputs, sems.at[7]),
        pltpu.make_async_copy(staged.at[1], input_grad, sems.at[8]),
    ]
    for copy in onward:
        copy.start()
    copies[2].wait()
    rank = rank_ref[0]
    for j in range(4):
        both = mlp_in[0, j].astype(F32) + mlp_in[1, j].astype(F32)
        gate[:, j * 512 : (j + 1) * 512] = both[:, :512]
        up[:, j * 512 : (j + 1) * 512] = both[:, 512:]
    wait(copies[3:5])
    for j in range(4):
        down[:, j * 512 : (j + 1) * 512] = mlp_down[0, j].astype(F32) + mlp_down[1, j].astype(F32)
        heads = qkv[0, j].astype(F32) + qkv[1, j].astype(F32)
        for n, grad in enumerate((query, key, value)):
            grad[:, j * HD : (j + 1) * HD] = heads[:, n * HD : (n + 1) * HD]
    copies[5].wait()
    total = out[0, 0].astype(F32)
    for n in range(1, 8):
        total += out[n // 4, n % 4].astype(F32)
    out_grad[...] = total
    copies[6].wait()
    gains = tiles[0, 0]
    for n in range(1, 8):
        gains += tiles[n // 4, n % 4]
    heads = pltpu.roll(gains[:8], HD - rank * 4, 1)
    q_gain[...] = heads[:4, :4]
    k_gain[...] = heads[4:, :4]
    columns = pltpu.roll(gains[8:], HD - lax.rem(rank, 2) * 64, 1)
    attn_gain[...] = columns[:1, :64]
    mlp_gain[...] = columns[1:2, :64]
    wait(onward)


def results(got):
    rank = lax.axis_index("dp") * 8 + lax.axis_index("ctx")
    narrow, wide, low = ((64, 4 * HD), F32), ((64, D), F32), ((T, D), BF16)
    outs = [low, low, narrow, narrow, narrow, narrow, ((4, 4), F32), ((4, 4), F32), ((1, 64), F32)]
    outs += [wide, wide, wide, ((1, 64), F32)]
    return pl.pallas_call(
        results_kernel,
        name=results.__name__,
        out_shape=[jax.ShapeDtypeStruct(*out) for out in outs],
        in_specs=[pl.BlockSpec(memory_space=pltpu.SMEM)] + [ANY] * 7,
        out_specs=[ANY] * 2 + [VMEM] * 11,
        scratch_shapes=[
            pltpu.VMEM(HALF_GRID + (1024,), BF16),
            pltpu.VMEM(HALF_GRID + (512,), BF16),
            pltpu.VMEM(HALF_GRID + (384,), BF16),
            pltpu.VMEM(HALF_GRID + (512,), BF16),
            pltpu.VMEM((2, 4, 16, HD), F32),
            pltpu.VMEM((2, T, D), BF16),
            pltpu.SemaphoreType.DMA((9,)),
        ],
        compiler_params=pltpu.CompilerParams(vmem_limit_bytes=62 * 2**20),
    )(
        rank.reshape(1), got.tiles, got.mlp_in, got.mlp_down, got.qkv, got.out,
        got.outputs, got.input_grad,
    )


def per_device(
    inputs, segments, w_query, w_key, w_value, w_out, q_gain, k_gain, attn_gain,
    w_gate, w_up, w_down, mlp_gain, cotangent,
):
    features, top = inputs[0], cotangent[0]
    q_row, k_row = q_gain.reshape(1, -1), k_gain.reshape(1, -1)
    a_row, m_row = attn_gain.reshape(1, -1), mlp_gain.reshape(1, -1)

    ff = forward(
        dict(seg=segments, q_gain=q_row, k_gain=k_row, attn_gain=a_row, mlp_gain=m_row),
        dict(
            features=features, cotangent=top, w_query=w_query, w_key=w_key, w_value=w_value,
            w_out=w_out, w_gate=w_gate, w_up=w_up, w_down=w_down,
        ),
    )
    got = backward(
        dict(
            d_attended=ff.d_attended, q_gain=q_row, k_gain=k_row, gains=ff.gain_rows,
            d_hidden_own=ff.d_hidden_own, result_own=ff.result_own,
        ),
        dict(
            q_head_in=ff.q_head_out, k_head_in=ff.k_head_out, v_head_in=ff.v_head_out,
            probs_in=ff.probs_out, q_raw_in=ff.q_raw_out, k_raw_in=ff.k_raw_out,
            scales_in=ff.scales_out,
            w_query=w_query, w_key=w_key, w_value=w_value,
            hidden_half=ff.hidden_half, hidden_rest=ff.hidden_rest, gate_right_in=ff.gate_right,
            up_right_in=ff.up_right, top_half=ff.top_half, mixed_right_in=ff.mixed_right,
            features_half=ff.features_half, features_rest=ff.features_rest,
            attended_all_in=ff.attended_all, d_attn=ff.d_attn,
        ),
    )
    (
        outputs, input_grad, query, key, value, out_grad, q_gain_grad, k_gain_grad,
        attn_gain_grad, gate, up, down, mlp_gain_grad,
    ) = results(got)
    return (
        outputs[None],
        input_grad[None],
        query,
        key,
        value,
        out_grad.T,
        q_gain_grad,
        k_gain_grad,
        attn_gain_grad[0],
        gate,
        up,
        down.T,
        mlp_gain_grad[0],
    )


def solution(mesh):
    rows, full = P("dp", "ctx", None), P()
    down, across = P("tensor", None), P(None, "tensor")
    in_specs = (
        rows, P("dp", "ctx"), across, across, across, down, down, down, full,
        across, across, down, full, rows,
    )
    split = ("dp", "ctx")
    out_specs = (
        rows, rows, P(split, "tensor"), P(split, "tensor"), P(split, "tensor"), P("tensor", split),
        P("tensor", split), P("tensor", split), P(split), P(split, "tensor"), P(split, "tensor"),
        P("tensor", split), P(split),
    )
    return jax.shard_map(
        per_device, mesh=mesh, in_specs=in_specs, out_specs=out_specs, check_vma=False
    )
```
